32 devices in a mesh: seq: 16 (over z, y, core), mlp: 2 (over x).
Axes of the slice: x: 2, y: 2, z: 4, core: 2. Of those that a mesh axis runs over, the one named last changes fastest.
Arguments:
- tokens: bfloat16 [3, 2, 1024, 768], P(None, 'mlp', 'seq'), may hold values from -6 to 6
- upstream: bfloat16 [3, 2, 1024, 768], P(None, 'mlp', 'seq'), may hold values from -6 to 6
- token_mask: int32 [3, 2, 1024], P(None, 'mlp', 'seq'), may hold values 0 or 1
- time_index: int32 [3, 2], P(None, 'mlp'), may hold values from 0 to 127
- weight_index: int32 [3, 2], P(None, 'mlp'), may hold values from 0 to 127
- time_table: bfloat16 [128, 128], replicated, may hold values from -6 to 6
- weight_grid: float32 [128], replicated, may hold values from 0.3 to 3
- w_ada: bfloat16 [128, 4608], P(None, 'seq'), may hold values from -0.5 to 0.5
- b_ada: bfloat16 [4608], P('seq'), may hold values from -3 to 3
- gain_one: bfloat16 [768], P('seq'), may hold values from 0.5 to 1.5
- gain_two: bfloat16 [768], P('seq'), may hold values from 0.5 to 1.5
- w_qkv: bfloat16 [768, 2304], P('seq'), may hold values from -0.21875 to 0.21875
- w_proj: bfloat16 [768, 768], P('seq'), may hold values from -6 to 6
- w_up: bfloat16 [768, 3072], P('seq', 'mlp'), may hold values from -0.21875 to 0.21875
- b_up: bfloat16 [3072], P('mlp'), may hold values from -3 to 3
- w_down: bfloat16 [3072, 768], P('mlp', 'seq'), may hold values from -0.109375 to 0.109375
- b_down: bfloat16 [768], P('seq'), may hold values from -3 to 3
Outputs:
- result: bfloat16 [3, 2, 1024, 768], P(None, 'mlp', 'seq')
- d_tokens: float32 [3, 2, 1024, 768], P(None, 'mlp', 'seq')
- d_time_table: float32 [128, 128], P('seq')
- d_w_ada: float32 [128, 4608], P(None, 'seq')
- d_b_ada: float32 [4608], P('seq')
- d_gain_one: float32 [768], P('seq')
- d_gain_two: float32 [768], P('seq')
- d_w_qkv: float32 [768, 2304], P('seq')
- d_w_proj: float32 [768, 768], P('seq')
- d_w_up: float32 [768, 3072], P('seq', 'mlp')
- d_b_up: float32 [3072], P('mlp')
- d_w_down: float32 [3072, 768], P('mlp', 'seq')
- d_b_down: float32 [768], P('seq')
The draws below stay inside these ranges and needn't reach their ends.
All inputs are finite; a program needn't handle non-finite values. No bound on the sum of `token_mask` on one device may be relied on, other than what follows from the above.
Results may differ from the reference program's by a relative error of at most 0.012.
The reference program's roundings to bfloat16 on the way count: a program that leaves them out, or rounds other values in their place, can miss the bound.
Values may be sent and summed in bfloat16 or wider, within the bound.
No kernel may reach another device: no remote copies, remote signals or barrier semaphores. Data moves between devices by JAX's collectives and lax.ppermute only.
A program may use at most 256 MiB of HBM per device.

```python
import math
import jax
import jax.numpy as jnp
from jax import lax

HEADS = 12
HEAD = 64
D = 768
FF = 3072
COND = 128
GRID = 128
MICRO = 3
LENGTH = 1024
BATCH = 2


def with_ends(values, own_key, low, largest):
    index_at = [jax.random.randint(jax.random.fold_in(own_key, axis), (), 0, length) for axis, length in enumerate(values.shape)]
    main_axis = values.shape.index(max(values.shape))
    beside = index_at[:main_axis] + [(index_at[main_axis] + 1) % values.shape[main_axis]] + index_at[main_axis + 1:]
    return values.at[tuple(index_at)].set(low).at[tuple(beside)].set(largest)


def level_of(rng, dims, pieces, least, high):
    factor_of, own = 1.0, jax.random.fold_in(rng, 6)
    for axis_at, parts in pieces:
        steps = jnp.exp(jax.random.uniform(jax.random.fold_in(own, axis_at), (parts,), jnp.float32, least / len(pieces), high / len(pieces)))
        factor_of = factor_of * jnp.repeat(steps, dims[axis_at] // parts).reshape([-1 if axis == axis_at else 1 for axis in range(len(dims))])
    return factor_of


def gaussian(rng, dims, deviation, most, shards=(), dtype=jnp.bfloat16):
    loudness = level_of(rng, dims, shards, -0.22, 0.18) if shards else 1.0
    values = jax.random.normal(rng, dims, jnp.float32) * deviation * loudness
    return jnp.minimum(jnp.maximum(values, -most), most).astype(dtype)


def setup_inputs(seed: int = 0) -> dict:
    streams_of = jax.random.split(jax.random.key(seed), 18)
    return {
        "tokens": gaussian(streams_of[0], (MICRO, BATCH, LENGTH, D), 1.0, 6.0, ((1, 2), (2, 16))),
        "upstream": gaussian(streams_of[1], (MICRO, BATCH, LENGTH, D), 1.0, 6.0, ((1, 2), (2, 16))),
        "token_mask": with_ends((jax.random.randint(streams_of[2], (MICRO, BATCH, LENGTH), 0, 4) < 3).astype(jnp.int32), jax.random.fold_in(streams_of[2], 1), 0, 1),
        "time_index": with_ends(jax.random.randint(streams_of[3], (MICRO, BATCH), 0, GRID), jax.random.fold_in(streams_of[3], 1), 0, GRID - 1).astype(jnp.int32),
        "weight_index": with_ends(jax.random.randint(streams_of[4], (MICRO, BATCH), 0, GRID), jax.random.fold_in(streams_of[4], 1), 0, GRID - 1).astype(jnp.int32),
        "time_table": gaussian(streams_of[5], (GRID, COND), 1.0, 6.0),
        "weight_grid": jnp.clip(jnp.exp(jax.random.uniform(streams_of[6], (GRID,), jnp.float32, math.log(0.3), math.log(3.0))), 0.3, 3.0),
        "w_ada": gaussian(streams_of[7], (COND, 6 * D), COND ** -0.5, 0.5, ((1, 16),)),
        "b_ada": gaussian(streams_of[8], (6 * D,), 0.5, 3.0, ((0, 16),)),
        "gain_one": jnp.clip(1.0 + 0.1 * jax.random.normal(streams_of[9], (D,), jnp.float32), 0.5, 1.5).astype(jnp.bfloat16),
        "gain_two": jnp.clip(1.0 + 0.1 * jax.random.normal(streams_of[10], (D,), jnp.float32), 0.5, 1.5).astype(jnp.bfloat16),
        "w_qkv": gaussian(streams_of[11], (D, 3 * D), D ** -0.5, 0.21875, ((0, 16),)),
        "w_proj": gaussian(streams_of[12], (D, D), 1 ** -0.5, 6.0, ((0, 16),)),
        "w_up": gaussian(streams_of[13], (D, FF), D ** -0.5, 0.21875, ((0, 16), (1, 2))),
        "b_up": gaussian(streams_of[14], (FF,), 0.5, 3.0, ((0, 2),)),
        "w_down": gaussian(streams_of[15], (FF, D), FF ** -0.5, 0.109375, ((0, 2), (1, 16))),
        "b_down": gaussian(streams_of[16], (D,), 0.5, 3.0, ((0, 16),)),
    }


highest = lax.Precision.HIGHEST

@jax.custom_vjp
def low(v):
    return lax.optimization_barrier(v.astype(jnp.bfloat16)).astype(jnp.float32)

@jax.custom_vjp
def low_back(v):
    return v

def low_keep(v):
    return (low(v), None)

def low_pass(kept, grad):
    return (grad,)

def back_keep(v):
    return (v, None)

def back_low(kept, grad):
    return (low(grad),)
low.defvjp(low_keep, low_pass)
low_back.defvjp(back_keep, back_low)

def matmul(left, right):
    return jnp.dot(left, right, precision=highest)

def norm_mod(inputs, gain_vec, shifts, scales):
    average = lax.optimization_barrier(jnp.mean(inputs, -1, keepdims=True))
    centred = inputs - average
    spread = lax.optimization_barrier(jnp.mean(centred * centred, -1, keepdims=True))
    return centred * lax.rsqrt(spread + 1e-06) * gain_vec * (1.0 + scales) + shifts

def rotate(inputs, cosine, sines):
    half_size = inputs.shape[-1] // 2
    turned = jnp.concatenate([-inputs[..., half_size:], inputs[..., :half_size]], -1)
    return inputs * cosine + turned * sines

def rotary_tables(positions):
    frequency = 10000.0 ** (-jnp.arange(0, HEAD, 2).astype(jnp.float32) / HEAD)
    angles = positions.astype(jnp.float32)[:, None] * frequency[None, :]
    angles = jnp.concatenate([angles, angles], -1)[:, None, :]
    return (jnp.cos(angles), jnp.sin(angles))

def layer_sequence(params, inputs, cond_row, cosine, sines):
    w_ada, b_ada, gain_one, gain_two, w_qkv, w_proj, w_up, b_up, w_down, b_down = params
    length = inputs.shape[0]
    model_width = inputs.shape[1]
    scaling = HEAD ** (-0.5)
    modulation = matmul(cond_row[None, :], w_ada)[0] + b_ada
    shift_one, scale_one, gate_one, shift_two, scale_two, gate_two = jnp.split(modulation, 6)
    normed = low(norm_mod(inputs, gain_one, shift_one, scale_one))
    project = low_back(matmul(normed, w_qkv))
    queries = low(rotate(project[:, :model_width].reshape(length, HEADS, HEAD), cosine, sines))
    keys = low(rotate(project[:, model_width:2 * model_width].reshape(length, HEADS, HEAD), cosine, sines))
    values = low(project[:, 2 * model_width:].reshape(length, HEADS, HEAD))
    scores = low_back(jnp.einsum('qhe,khe->hqk', queries, keys, precision=highest) * scaling)
    attn_probs = low(jax.nn.softmax(scores, axis=-1))
    mixed = jnp.einsum('hqk,khe->qhe', attn_probs, values, precision=highest).reshape(length, model_width)
    mixed = low(low_back(mixed))
    attended = low_back(matmul(mixed, w_proj))
    middle = inputs + gate_one * attended
    normed_two = low(norm_mod(middle, gain_two, shift_two, scale_two))
    hidden = low_back(matmul(normed_two, w_up) + b_up)
    active = low(jax.nn.gelu(hidden, approximate=True))
    output = low_back(matmul(active, w_down)) + b_down
    return middle + gate_two * output

def reference(tokens, upstream, token_mask, time_index, weight_index, time_table, weight_grid, w_ada, b_ada, gain_one, gain_two, w_qkv, w_proj, w_up, b_up, w_down, b_down):
    params = tuple((member.astype(jnp.float32) for member in (w_ada, b_ada, gain_one, gain_two, w_qkv, w_proj, w_up, b_up, w_down, b_down)))
    time_rows = time_table.astype(jnp.float32)
    inputs = tokens.astype(jnp.float32).reshape(MICRO * BATCH, LENGTH, D)
    cosine, sines = rotary_tables(jnp.arange(LENGTH).astype(jnp.int32))
    flat_index = time_index.reshape(MICRO * BATCH)

    def forward(params, inputs, time_rows):
        cond_rows = time_rows[flat_index]

        def per_sequence(operands):
            return layer_sequence(params, operands[0], operands[1], cosine, sines)
        return lax.map(jax.checkpoint(per_sequence), (inputs, cond_rows))
    outputs, pullback = jax.vjp(forward, params, inputs, time_rows)
    loss_weights = weight_grid[weight_index]
    cotangent = upstream.astype(jnp.float32) * token_mask.astype(jnp.float32)[..., None] * loss_weights[:, :, None, None]
    grad_params, grad_inputs, grad_table = pullback(cotangent.reshape(MICRO * BATCH, LENGTH, D))
    result = outputs.reshape(MICRO, BATCH, LENGTH, D).astype(jnp.bfloat16)
    d_tokens = grad_inputs.reshape(MICRO, BATCH, LENGTH, D)
    return (result, d_tokens, grad_table, grad_params[0], grad_params[1], grad_params[2], grad_params[3], grad_params[4], grad_params[5], grad_params[6], grad_params[7], grad_params[8], grad_params[9])
```

```python
import functools

import jax
import jax.numpy as jnp
from jax import lax
from jax.experimental import pallas as pl
from jax.experimental.pallas import tpu as pltpu
from jax.sharding import PartitionSpec as P

HEADS = 12
HEAD = 64
MICRO = 3
PLANES = 4
GROUPS = 4
PER_GROUP = HEADS // GROUPS
WIDTH = PER_GROUP * HEAD
QUERY_BLOCK = 256
SCALING = HEAD ** (-0.5)
BF16 = jnp.bfloat16
F32 = jnp.float32
highest = lax.Precision.HIGHEST

VMEM = pl.BlockSpec(memory_space=pltpu.VMEM)
SMEM = pl.BlockSpec(memory_space=pltpu.SMEM)


def nn(left, right):
    return lax.dot_general(left, right, (((1,), (0,)), ((), ())), preferred_element_type=F32)


def nt(left, right):
    return lax.dot_general(left, right, (((1,), (1,)), ((), ())), preferred_element_type=F32)


def standardize(inputs):
    average = jnp.mean(inputs, -1, keepdims=True)
    centred = inputs - average
    spread = jnp.mean(centred * centred, -1, keepdims=True)
    root = lax.rsqrt(spread + 1e-06)
    return centred * root, root


def forward_kernel(place, *refs, blocks):
    tokens, refs = refs[:blocks], refs[blocks:]
    weights, refs = refs[:PLANES], refs[PLANES:]
    (gain, shift, cosine, sines), refs = refs[:4], refs[4:]
    mixed, refs = refs[:blocks], refs[blocks:]
    heads, log_total, normed, weight, keys, mixed_turned = refs
    plane = place[0]
    rows = weights[0].shape[0]
    count = tokens[0].shape[0]
    for distance in range(PLANES):
        first = pl.multiple_of((plane ^ distance) * rows, 16)
        weight[pl.ds(first, rows), :] = weights[distance][...]
    for block in range(blocks):
        xhat, _ = standardize(tokens[block][...].astype(F32))
        normed[block * count : (block + 1) * count, :] = (xhat * gain[...] + shift[...]).astype(BF16)
    project = nt(weight[...].T, normed[...])
    cos, sin = cosine[...], sines[...]
    half = HEAD // 2
    for part in range(2):
        for head in range(PER_GROUP):
            start = part * WIDTH + head * HEAD
            first, second = project[start : start + half], project[start + half : start + HEAD]
            turned = jnp.concatenate([first * cos - second * sin, second * cos + first * sin], 0).astype(BF16)
            if part == 0:
                turned = turned * jnp.asarray(SCALING, BF16)
            else:
                keys[head] = turned.T
            heads[start : start + HEAD, :] = turned
    heads[2 * WIDTH :, :] = project[2 * WIDTH :].astype(BF16)
    length = heads.shape[1]
    for head in range(PER_GROUP):
        start = head * HEAD

        def queries_step(step, carry):
            columns = pl.ds(pl.multiple_of(step * QUERY_BLOCK, QUERY_BLOCK), QUERY_BLOCK)
            scores = nn(keys[head], heads[start : start + HEAD, columns])
            peak = jnp.max(scores, 0, keepdims=True)
            exps = jnp.exp(scores - peak)
            total = jnp.sum(exps, 0, keepdims=True)
            log_total[head : head + 1, columns] = peak + jnp.log(total)
            probs = (exps * (1.0 / total)).astype(BF16)
            values = heads[2 * WIDTH + start : 2 * WIDTH + start + HEAD, :]
            mixed_turned[start : start + HEAD, columns] = nn(values, probs).astype(BF16)
            return carry

        lax.fori_loop(0, length // QUERY_BLOCK, queries_step, 0)
    for block in range(blocks):
        mixed[block][...] = mixed_turned[:, block * count : (block + 1) * count].T


def backward_kernel(place, share, *refs, blocks):
    tokens, refs = refs[:blocks], refs[blocks:]
    d_mixed, refs = refs[:blocks], refs[blocks:]
    (heads, log_total, normed, weight, cosine, sines), refs = refs[:6], refs[6:]
    d_normed, refs = refs[:blocks], refs[blocks:]
    d_weight, refs = refs[:PLANES], refs[PLANES:]
    sums, d_turned, d_keys, d_values, d_project, d_whole, keys, values = refs
    plane, active = place[0], share[0]
    count = tokens[0].shape[0]
    length = heads.shape[1]
    for block in range(blocks):
        d_turned[:, block * count : (block + 1) * count] = d_mixed[block][...].T
    cos, sin = cosine[...], sines[...]
    half = HEAD // 2
    d_keys[...] = jnp.zeros_like(d_keys)
    d_values[...] = jnp.zeros_like(d_values)
    for head in range(PER_GROUP):
        start = head * HEAD
        keys_turned = heads.at[WIDTH + start : WIDTH + start + HEAD]
        keys[...] = keys_turned[...].T
        values[...] = heads[2 * WIDTH + start : 2 * WIDTH + start + HEAD, :].T

        def queries_step(step, carry):
            columns = pl.ds(pl.multiple_of(step * QUERY_BLOCK, QUERY_BLOCK), QUERY_BLOCK)
            queries = heads[start : start + HEAD, columns]
            incoming = d_turned[start : start + HEAD, columns]
            scores = nn(keys[...], queries)
            probs = jnp.exp(scores - log_total[head : head + 1, columns])
            d_probs = nn(values[...], incoming)
            delta = jnp.sum(probs * d_probs, 0, keepdims=True)
            d_scores = (probs * (d_probs - delta)).astype(BF16)
            d_values[start : start + HEAD, :] += nt(incoming, probs.astype(BF16))
            d_keys[start : start + HEAD, :] += nt(queries, d_scores)
            d_queries = nn(keys_turned[...], d_scores) * SCALING
            first, second = d_queries[:half], d_queries[half:]
            cos_here, sin_here = cosine[:, columns], sines[:, columns]
            d_project[start : start + half, columns] = (first * cos_here + second * sin_here).astype(BF16)
            d_project[start + half : start + HEAD, columns] = (second * cos_here - first * sin_here).astype(BF16)
            return carry

        lax.fori_loop(0, length // QUERY_BLOCK, queries_step, 0)
        first, second = d_keys[start : start + half, :], d_keys[start + half : start + HEAD, :]
        d_project[WIDTH + start : WIDTH + start + half, :] = (first * cos + second * sin).astype(BF16)
        d_project[WIDTH + start + half : WIDTH + start + HEAD, :] = (second * cos - first * sin).astype(BF16)
    d_project[2 * WIDTH :, :] = d_values[...].astype(BF16)
    d_shift = jnp.zeros((1, normed.shape[1]), F32)
    d_xhat = jnp.zeros((1, normed.shape[1]), F32)
    for block in range(blocks):
        part = nt(d_project[:, block * count : (block + 1) * count].T, weight[...]) * active
        d_normed[block][...] = part.astype(BF16)
        xhat, _ = standardize(tokens[block][...].astype(F32))
        d_shift = d_shift + jnp.sum(part, 0, keepdims=True)
        d_xhat = d_xhat + jnp.sum(part * xhat, 0, keepdims=True)
    sums[0:1, :] = d_shift
    sums[1:2, :] = d_xhat
    d_whole[...] = (nn(d_project[...], normed[...]) * active).astype(BF16).T
    rows = d_weight[0].shape[0]
    for distance in range(PLANES):
        first = pl.multiple_of((plane ^ distance) * rows, 16)
        d_weight[distance][...] = d_whole[pl.ds(first, rows), :]


def shape_of(dims, dtype):
    return jax.ShapeDtypeStruct(dims, dtype)


def attend_forward(place, tokens, weights, gain, shift, cosine, sines):
    blocks, (count, width) = len(tokens), tokens[0].shape
    length = blocks * count
    columns = weights[0].shape[1]
    outs = pl.pallas_call(
        functools.partial(forward_kernel, blocks=blocks),
        out_shape=[shape_of((count, WIDTH), BF16)] * blocks
        + [
            shape_of((columns, length), BF16),
            shape_of((8, length), F32),
            shape_of((length, width), BF16),
            shape_of((width, columns), BF16),
        ],
        in_specs=[SMEM] + [VMEM] * (blocks + PLANES + 4),
        out_specs=[VMEM] * (blocks + 4),
        scratch_shapes=[pltpu.VMEM((PER_GROUP, length, HEAD), BF16), pltpu.VMEM((WIDTH, length), BF16)],
        compiler_params=pltpu.CompilerParams(vmem_limit_bytes=56 * 1024 * 1024),
        name="attend_forward",
    )(place, *tokens, *weights, gain, shift, cosine, sines)
    return outs[:blocks], outs[blocks:]


def attend_backward(place, active, tokens, d_mixed, kept, cosine, sines):
    blocks, (count, width) = len(tokens), tokens[0].shape
    length = blocks * count
    columns = 3 * WIDTH
    rows = width // PLANES
    outs = pl.pallas_call(
        functools.partial(backward_kernel, blocks=blocks),
        out_shape=[shape_of((count, width), BF16)] * blocks
        + [shape_of((rows, columns), BF16)] * PLANES
        + [shape_of((8, width), F32)],
        in_specs=[SMEM, SMEM] + [VMEM] * (2 * blocks + 6),
        out_specs=[VMEM] * (blocks + PLANES + 1),
        scratch_shapes=[
            pltpu.VMEM((WIDTH, length), BF16),
            pltpu.VMEM((WIDTH, length), F32),
            pltpu.VMEM((WIDTH, length), F32),
            pltpu.VMEM((columns, length), BF16),
            pltpu.VMEM((width, columns), BF16),
            pltpu.VMEM((length, HEAD), BF16),
            pltpu.VMEM((length, HEAD), BF16),
        ],
        compiler_params=pltpu.CompilerParams(vmem_limit_bytes=56 * 1024 * 1024),
        name="attend_backward",
    )(place, active, *tokens, *d_mixed, *kept, cosine, sines)
    return outs[:blocks], outs[blocks : blocks + PLANES], outs[-1]


def pick(stack, index):
    return lax.dynamic_index_in_dim(stack, index, 0, keepdims=False)


def gelu_tanh(hidden_in):
    return jax.nn.gelu(hidden_in, approximate=True)


def bits_of(count):
    return [1 << bit for bit in range(count.bit_length() - 1)]


def body(
    tokens,
    upstream,
    token_mask,
    time_index,
    weight_index,
    time_table,
    weight_grid,
    w_ada,
    b_ada,
    gain_one,
    gain_two,
    w_qkv,
    w_proj,
    w_up,
    b_up,
    w_down,
    b_down,
    *,
    n,
    m,
):
    side = n // PLANES
    me = lax.axis_index("seq")
    plane, spot = me // side, me % side
    shard, width = tokens.shape[2], tokens.shape[3]
    rows = w_qkv.shape[0]
    hidden_count = w_up.shape[1]
    grid_size = time_table.shape[0]
    count = MICRO * shard

    def swap(value, distance, to=None, frm=None):
        pairs = [
            (i, i ^ distance)
            for i in range(n)
            if (to is None or (i ^ distance) // side < to) and (frm is None or i // side < frm)
        ]
        return lax.ppermute(value, "seq", pairs)

    def swap_mlp(value, distance):
        return lax.ppermute(value, "mlp", [(i, i ^ distance) for i in range(m)])

    packed = jnp.concatenate(
        [w_up, w_down.T, w_proj.reshape(-1, hidden_count), w_ada.reshape(-1, hidden_count)], 0
    )
    gathered = lax.all_gather(packed, "seq", axis=0)

    x_low = tokens[:, 0]
    last = jnp.minimum(plane, MICRO - 1)
    pieces = [pick(x_low, last)]
    for distance in range(1, PLANES):
        pieces.append(
            swap(pick(x_low, jnp.minimum(plane ^ distance, MICRO - 1)), distance * side, to=MICRO)
        )
    token_blocks = {0: jnp.concatenate(pieces, 0)}
    for bit in reversed(bits_of(side)):
        for known in list(token_blocks):
            token_blocks[known | bit] = swap(token_blocks[known], bit, to=MICRO)
    token_blocks = [token_blocks[at] for at in range(side)]

    by_group = w_qkv.reshape(rows, 3, GROUPS, WIDTH).transpose(2, 0, 1, 3).reshape(GROUPS, rows, 3 * WIDTH)
    received = jnp.stack(
        [pick(by_group, spot % GROUPS)]
        + [swap(pick(by_group, (spot ^ e) % GROUPS), e) for e in range(1, side)]
    )
    weight_blocks = {0: jnp.concatenate([pick(received, spot ^ at) for at in range(side)], 0)}
    for bit in (2, 1):
        for known in list(weight_blocks):
            weight_blocks[known | bit] = swap(
                weight_blocks[known], bit * side, to=MICRO if bit == 1 else None
            )
    weight_blocks = [weight_blocks[at] for at in range(PLANES)]

    index_here = time_index[:, 0]
    onehot_here = (index_here[:, None] == jnp.arange(grid_size)[None, :]).astype(BF16)
    cond_here = jnp.dot(onehot_here, time_table, preferred_element_type=F32).astype(BF16)
    ada_part = jnp.dot(cond_here, w_ada, preferred_element_type=F32) + b_ada.astype(F32)
    ada_columns = w_ada.shape[1]
    small = jnp.concatenate(
        [ada_part.reshape(-1), gain_one.astype(F32), gain_two.astype(F32), b_down.astype(F32)]
    )[None]
    for bit in bits_of(n):
        small = jnp.concatenate([small, swap(small, bit)], 0)
    for bit in bits_of(n):
        halves = small.reshape(n // (2 * bit), 2, bit, -1)
        small = jnp.where((me & bit) != 0, halves[:, ::-1], halves).reshape(n, -1)
    cut = MICRO * ada_columns
    modulation = small[:, :cut].reshape(n, MICRO, ada_columns).transpose(1, 0, 2).reshape(MICRO, -1)
    full_gain_one = small[:, cut : cut + rows].reshape(1, width)
    full_gain_two = small[:, cut + rows : cut + 2 * rows].reshape(1, width)
    full_bias_down = small[:, cut + 2 * rows :].reshape(1, width)
    parts = [modulation[:, at * width : (at + 1) * width] for at in range(6)]
    shift_one, scale_one, gate_one, shift_two, scale_two, gate_two = parts
    wide = [jnp.broadcast_to(part[:, None], (MICRO, shard, width)).reshape(count, width) for part in parts]

    order = ((plane ^ jnp.arange(PLANES))[None, :] * side + (spot ^ jnp.arange(side))[:, None]) * shard
    positions = (order[:, :, None] + jnp.arange(shard)).reshape(1, -1).astype(F32)
    frequency = 10000.0 ** (-jnp.arange(0, HEAD, 2).astype(F32) / HEAD)
    angles = frequency[:, None] * positions
    cosine, sines = jnp.cos(angles), jnp.sin(angles)

    place = plane.astype(jnp.int32).reshape(1)
    active = ((plane < MICRO) & (spot < GROUPS)).astype(F32).reshape(1)
    mixed_blocks, kept = attend_forward(
        place,
        token_blocks,
        weight_blocks,
        full_gain_one * (1.0 + pick(scale_one, last))[None],
        pick(shift_one, last)[None],
        cosine,
        sines,
    )

    received = jnp.stack(
        [mixed_blocks[0]] + [swap(mixed_blocks[e], e, to=MICRO) for e in range(1, side)]
    )
    block = jnp.concatenate([pick(received, spot ^ group) for group in range(GROUPS)], -1)

    def to_tokens(block):
        received = jnp.stack(
            [block[:shard]]
            + [
                swap(block[d * shard : (d + 1) * shard], d * side, frm=MICRO)
                for d in range(1, PLANES)
            ]
        )
        return jnp.concatenate([pick(received, plane ^ at) for at in range(MICRO)], 0)

    mixed = to_tokens(block)

    weights_at = gathered[:, : 2 * rows]
    full_up = weights_at[:, :rows].reshape(width, hidden_count)
    full_down = weights_at[:, rows:].reshape(width, hidden_count)
    proj_rows = rows * width // hidden_count
    full_proj = gathered[:, 2 * rows : 2 * rows + proj_rows].reshape(width, width)
    full_ada = gathered[:, 2 * rows + proj_rows :].reshape(n, w_ada.shape[0], ada_columns)

    onehot_weight = weight_index[:, 0][:, None] == jnp.arange(grid_size)[None, :]
    loss_weights = jnp.sum(jnp.where(onehot_weight, weight_grid[None, :], 0.0), -1)
    d_result = (
        upstream[:, 0].astype(F32)
        * token_mask[:, 0].astype(F32)[..., None]
        * loss_weights[:, None, None]
    ).reshape(count, width)
    d_output = wide[5] * d_result
    rows_grad = [d_output.astype(BF16)]
    rows_grad = jnp.concatenate(rows_grad + [swap_mlp(rows_grad[0], d) for d in range(1, m)], 0)

    x = x_low.astype(F32).reshape(count, width)
    attended = nn(mixed, full_proj)
    middle = x + wide[2] * attended
    xhat_two, root_two = standardize(middle)
    normed_two = (xhat_two * (full_gain_two * (1.0 + wide[4])) + wide[3]).astype(BF16)
    rows_all = jnp.concatenate([normed_two] + [swap_mlp(normed_two, d) for d in range(1, m)], 0)

    hidden = nn(rows_all, full_up) + b_up.astype(F32)
    active_wide, pull_gelu = jax.vjp(gelu_tanh, hidden)
    active_low = active_wide.astype(BF16)
    d_active = nn(rows_grad, full_down)
    d_hidden = pull_gelu(d_active)[0].astype(BF16)

    def sum_mlp(partial):
        total = partial[:count]
        for d in range(1, m):
            total = total + swap_mlp(partial[d * count : (d + 1) * count].astype(BF16), d).astype(F32)
        return total

    d_normed_two = sum_mlp(nt(d_hidden, full_up))
    output = sum_mlp(nt(active_low, full_down)) + full_bias_down
    result = (middle + wide[5] * output).astype(BF16)

    def by_sequence(value):
        return jnp.sum(value.reshape(MICRO, shard, width), 1)

    def pull_norm(d_normed, gains, xhat, root):
        e = d_normed * gains
        return root * (
            e - jnp.mean(e, -1, keepdims=True) - xhat * jnp.mean(e * xhat, -1, keepdims=True)
        )

    d_middle = d_result + pull_norm(d_normed_two, full_gain_two * (1.0 + wide[4]), xhat_two, root_two)
    d_attended_low = (wide[2] * d_middle).astype(BF16)
    d_mixed = nt(d_attended_low, full_proj).astype(BF16).reshape(MICRO, shard, width)

    pieces = [pick(d_mixed, last)]
    for distance in range(1, PLANES):
        pieces.append(
            swap(pick(d_mixed, jnp.minimum(plane ^ distance, MICRO - 1)), distance * side, to=MICRO)
        )
    block = jnp.concatenate(pieces, 0)
    by_group = jnp.stack([block[:, at * WIDTH : (at + 1) * WIDTH] for at in range(GROUPS)])
    d_mixed_blocks = [pick(by_group, spot % GROUPS)]
    for e in range(1, side):
        d_mixed_blocks.append(swap(pick(by_group, (spot ^ e) % GROUPS), e, to=MICRO))

    def tn(left, right):
        return lax.dot_general(left, right, (((0,), (0,)), ((), ())), preferred_element_type=F32)

    grads = jnp.concatenate(
        [
            tn(rows_all, d_hidden).astype(BF16).reshape(n, rows, hidden_count),
            tn(rows_grad, active_low).astype(BF16).reshape(n, rows, hidden_count),
            tn(mixed, d_attended_low).astype(BF16).reshape(n, proj_rows, hidden_count),
        ],
        1,
    )
    grads = lax.psum_scatter(grads, "seq", scatter_dimension=0, tiled=True)[0].astype(F32)
    grad_up = grads[:rows]
    grad_down = grads[rows : 2 * rows].T
    grad_proj = grads[2 * rows :].reshape(rows, width)
    for bit in bits_of(m):
        grad_proj = grad_proj + swap_mlp(grad_proj.astype(BF16), bit).astype(F32)

    d_normed_blocks, d_weight_blocks, sums = attend_backward(
        place, active, token_blocks, d_mixed_blocks, kept, cosine, sines
    )

    blocks = dict(enumerate(d_normed_blocks))
    for bit in bits_of(side):
        for at in [at for at in blocks if at & bit]:
            arrived = swap(blocks.pop(at), bit, to=MICRO)
            blocks[at ^ bit] = (blocks[at ^ bit].astype(F32) + arrived.astype(F32)).astype(BF16)
    d_normed = to_tokens(blocks[0]).astype(F32)
    xhat_one, root_one = standardize(x)
    d_tokens = d_middle + pull_norm(d_normed, full_gain_one * (1.0 + wide[1]), xhat_one, root_one)

    total = d_weight_blocks[0].astype(F32)
    for distance in range(1, PLANES):
        total = total + swap(d_weight_blocks[distance], distance * side, frm=MICRO).astype(F32)
    by_spot = total.astype(BF16).reshape(side, rows, 3 * WIDTH)
    received = jnp.stack(
        [pick(by_spot, spot)] + [swap(pick(by_spot, spot ^ e), e) for e in range(1, side)]
    )
    grad_qkv = jnp.stack([pick(received, spot ^ group) for group in range(GROUPS)])
    grad_qkv = grad_qkv.reshape(GROUPS, rows, 3, WIDTH).transpose(1, 2, 0, 3).reshape(rows, 3 * width)
    grad_qkv = grad_qkv.astype(F32)
    for bit in bits_of(m):
        grad_qkv = grad_qkv + swap_mlp(grad_qkv.astype(BF16), bit).astype(F32)

    xhat_sums = by_sequence(d_normed_two * xhat_two)
    own = (jnp.arange(MICRO) == plane)[:, None]
    bias_up_rows = -(-hidden_count // width)
    bias_up_sum = jnp.sum(d_hidden.astype(F32), 0)
    bias_up_sum = jnp.pad(bias_up_sum, (0, bias_up_rows * width - hidden_count)).reshape(-1, width)
    small = jnp.concatenate(
        [
            jnp.where(own, sums[0:1], 0.0),
            jnp.where(own, sums[1:2], 0.0),
            by_sequence(d_middle * attended),
            by_sequence(d_normed_two),
            full_gain_two * xhat_sums,
            by_sequence(d_result * output),
            jnp.sum((1.0 + scale_two) * xhat_sums, 0, keepdims=True),
            jnp.sum(d_output, 0, keepdims=True),
            bias_up_sum,
        ],
        0,
    )
    for bit in bits_of(n):
        small = small + swap(small, bit)
    d_xhat = small[MICRO : 2 * MICRO]
    at = 6 * MICRO
    grad_bias_up = small[at + 2 :].reshape(-1)[:hidden_count]
    index_row = jnp.pad(index_here.astype(F32), (0, width - MICRO))[None]
    small = jnp.concatenate(
        [
            small[:MICRO],
            full_gain_one * d_xhat,
            small[2 * MICRO : at + 2],
            jnp.sum((1.0 + scale_one) * d_xhat, 0, keepdims=True),
            index_row,
        ],
        0,
    )[None]
    for bit in bits_of(m):
        small = jnp.concatenate([small, swap_mlp(small, bit)], 0)
    d_modulation = small[:, :at].reshape(m, 6, MICRO, width).transpose(0, 2, 1, 3)
    d_modulation = d_modulation.reshape(m * MICRO, n, ada_columns)
    vectors = jnp.sum(small[:, at : at + 3], 0)
    index_all = small[:, at + 3, :MICRO].reshape(-1).astype(jnp.int32)
    onehot = (index_all[:, None] == jnp.arange(grid_size)[None, :]).astype(BF16)
    cond = jnp.dot(onehot, time_table, preferred_element_type=F32)
    d_modulation_own = lax.dynamic_index_in_dim(d_modulation, me, 1, keepdims=False)
    grad_ada = jnp.dot(cond.T, d_modulation_own, precision=highest)
    grad_bias_ada = jnp.sum(d_modulation_own, 0)
    d_cond = jnp.einsum("bic,idc->bd", d_modulation, full_ada.astype(F32), precision=highest)
    table_rows = grid_size // n
    onehot_own = index_all[None, :] == (me * table_rows + jnp.arange(table_rows))[:, None]
    grad_table = jnp.dot(onehot_own.astype(F32), d_cond, precision=highest)
    vectors = lax.dynamic_slice_in_dim(vectors, me * rows, rows, 1)
    return (
        result.reshape(MICRO, 1, shard, width),
        d_tokens.reshape(MICRO, 1, shard, width),
        grad_table,
        grad_ada,
        grad_bias_ada,
        vectors[2],
        vectors[0],
        grad_qkv,
        grad_proj,
        grad_up,
        grad_bias_up,
        grad_down,
        vectors[1],
    )


def solution(mesh):
    in_specs = (
        P(None, "mlp", "seq", None),
        P(None, "mlp", "seq", None),
        P(None, "mlp", "seq"),
        P(None, "mlp"),
        P(None, "mlp"),
        P(),
        P(),
        P(None, "seq"),
        P("seq"),
        P("seq"),
        P("seq"),
        P("seq", None),
        P("seq", None),
        P("seq", "mlp"),
        P("mlp"),
        P("mlp", "seq"),
        P("seq"),
    )
    out_specs = (
        P(None, "mlp", "seq", None),
        P(None, "mlp", "seq", None),
        P("seq", None),
        P(None, "seq"),
        P("seq"),
        P("seq"),
        P("seq"),
        P("seq", None),
        P("seq", None),
        P("seq", "mlp"),
        P("mlp"),
        P("mlp", "seq"),
        P("seq"),
    )
    run = functools.partial(body, n=mesh.shape["seq"], m=mesh.shape["mlp"])
    return jax.shard_map(run, mesh=mesh, in_specs=in_specs, out_specs=out_specs, check_vma=False)
```

```python
import functools

import jax
import jax.numpy as jnp
from jax import lax
from jax.experimental import pallas as pl
from jax.experimental.pallas import tpu as pltpu
from jax.sharding import PartitionSpec as P

HEADS = 12
HEAD = 64
MICRO = 3
PLANES = 4
GROUPS = 4
PER_GROUP = HEADS // GROUPS
WIDTH = PER_GROUP * HEAD
QUERY_BLOCK = 256
SCALING = HEAD ** (-0.5)
BF16 = jnp.bfloat16
F32 = jnp.float32
highest = lax.Precision.HIGHEST

VMEM = pl.BlockSpec(memory_space=pltpu.VMEM)
SMEM = pl.BlockSpec(memory_space=pltpu.SMEM)


def nn(left, right):
    return lax.dot_general(left, right, (((1,), (0,)), ((), ())), preferred_element_type=F32)


def nt(left, right):
    return lax.dot_general(left, right, (((1,), (1,)), ((), ())), preferred_element_type=F32)


def standardize(inputs):
    average = jnp.mean(inputs, -1, keepdims=True)
    centred = inputs - average
    spread = jnp.mean(centred * centred, -1, keepdims=True)
    root = lax.rsqrt(spread + 1e-06)
    return centred * root, root


def forward_kernel(tokens, weight, gain, shift, cosine, sines, mixed, heads, log_total, normed, keys, mixed_turned):
    length = tokens.shape[0]
    for start in range(0, length, QUERY_BLOCK):
        rows = slice(start, start + QUERY_BLOCK)
        xhat, _ = standardize(tokens[rows].astype(F32))
        normed[rows, :] = (xhat * gain[...] + shift[...]).astype(BF16)
    project = nt(weight[...].T, normed[...])
    cos, sin = cosine[...], sines[...]
    half = HEAD // 2
    for part in range(2):
        for head in range(PER_GROUP):
            start = part * WIDTH + head * HEAD
            first, second = project[start : start + half], project[start + half : start + HEAD]
            turned = jnp.concatenate([first * cos - second * sin, second * cos + first * sin], 0).astype(BF16)
            if part == 0:
                turned = turned * jnp.asarray(SCALING, BF16)
            else:
                keys[head] = turned.T
            heads[start : start + HEAD, :] = turned
    heads[2 * WIDTH :, :] = project[2 * WIDTH :].astype(BF16)
    for head in range(PER_GROUP):
        start = head * HEAD

        def queries_step(step, carry):
            columns = pl.ds(pl.multiple_of(step * QUERY_BLOCK, QUERY_BLOCK), QUERY_BLOCK)
            scores = nn(keys[head], heads[start : start + HEAD, columns])
            peak = jnp.max(scores, 0, keepdims=True)
            exps = jnp.exp(scores - peak)
            total = jnp.sum(exps, 0, keepdims=True)
            log_total[head : head + 1, columns] = peak + jnp.log(total)
            probs = (exps * (1.0 / total)).astype(BF16)
            values = heads[2 * WIDTH + start : 2 * WIDTH + start + HEAD, :]
            mixed_turned[start : start + HEAD, columns] = nn(values, probs).astype(BF16)
            return carry

        lax.fori_loop(0, length // QUERY_BLOCK, queries_step, 0)
    mixed[...] = mixed_turned[...].T


def backward_kernel(
    tokens,
    d_mixed,
    heads,
    log_total,
    normed,
    weight,
    cosine,
    sines,
    d_normed,
    d_weight,
    sums,
    d_turned,
    d_keys,
    d_values,
    d_project,
    keys,
    values,
):
    length = heads.shape[1]
    d_turned[...] = d_mixed[...].T
    cos, sin = cosine[...], sines[...]
    half = HEAD // 2
    d_keys[...] = jnp.zeros_like(d_keys)
    d_values[...] = jnp.zeros_like(d_values)
    for head in range(PER_GROUP):
        start = head * HEAD
        keys_turned = heads.at[WIDTH + start : WIDTH + start + HEAD]
        keys[...] = keys_turned[...].T
        values[...] = heads[2 * WIDTH + start : 2 * WIDTH + start + HEAD, :].T

        def queries_step(step, carry):
            columns = pl.ds(pl.multiple_of(step * QUERY_BLOCK, QUERY_BLOCK), QUERY_BLOCK)
            queries = heads[start : start + HEAD, columns]
            incoming = d_turned[start : start + HEAD, columns]
            scores = nn(keys[...], queries)
            probs = jnp.exp(scores - log_total[head : head + 1, columns])
            d_probs = nn(values[...], incoming)
            delta = jnp.sum(probs * d_probs, 0, keepdims=True)
            d_scores = (probs * (d_probs - delta)).astype(BF16)
            d_values[start : start + HEAD, :] += nt(incoming, probs.astype(BF16))
            d_keys[start : start + HEAD, :] += nt(queries, d_scores)
            d_queries = nn(keys_turned[...], d_scores) * SCALING
            first, second = d_queries[:half], d_queries[half:]
            cos_here, sin_here = cosine[:, columns], sines[:, columns]
            d_project[start : start + half, columns] = (first * cos_here + second * sin_here).astype(BF16)
            d_project[start + half : start + HEAD, columns] = (second * cos_here - first * sin_here).astype(BF16)
            return carry

        lax.fori_loop(0, length // QUERY_BLOCK, queries_step, 0)
        first, second = d_keys[start : start + half, :], d_keys[start + half : start + HEAD, :]
        d_project[WIDTH + start : WIDTH + start + half, :] = (first * cos + second * sin).astype(BF16)
        d_project[WIDTH + start + half : WIDTH + start + HEAD, :] = (second * cos - first * sin).astype(BF16)
    d_project[2 * WIDTH :, :] = d_values[...].astype(BF16)
    d_shift = jnp.zeros((1, normed.shape[1]), F32)
    d_xhat = jnp.zeros((1, normed.shape[1]), F32)
    for start in range(0, length, QUERY_BLOCK):
        rows = slice(start, start + QUERY_BLOCK)
        part = nt(d_project[:, rows].T, weight[...])
        d_normed[rows, :] = part.astype(BF16)
        xhat, _ = standardize(tokens[rows].astype(F32))
        d_shift = d_shift + jnp.sum(part, 0, keepdims=True)
        d_xhat = d_xhat + jnp.sum(part * xhat, 0, keepdims=True)
    sums[0:1, :] = d_shift
    sums[1:2, :] = d_xhat
    d_weight[...] = nn(d_project[...], normed[...]).astype(BF16).T


def shape_of(dims, dtype):
    return jax.ShapeDtypeStruct(dims, dtype)


def attend_forward(tokens, weight, gain, shift, cosine, sines):
    length, width = tokens.shape
    columns = weight.shape[1]
    return pl.pallas_call(
        forward_kernel,
        out_shape=[
            shape_of((length, WIDTH), BF16),
            shape_of((columns, length), BF16),
            shape_of((8, length), F32),
            shape_of((length, width), BF16),
        ],
        in_specs=[VMEM] * 6,
        out_specs=[VMEM] * 4,
        scratch_shapes=[pltpu.VMEM((PER_GROUP, length, HEAD), BF16), pltpu.VMEM((WIDTH, length), BF16)],
        compiler_params=pltpu.CompilerParams(vmem_limit_bytes=56 * 1024 * 1024),
        name="attend_forward",
    )(tokens, weight, gain, shift, cosine, sines)


def attend_backward(tokens, d_mixed, heads, log_total, normed, weight, cosine, sines):
    length, width = tokens.shape
    columns = weight.shape[1]
    return pl.pallas_call(
        backward_kernel,
        out_shape=[
            shape_of((length, width), BF16),
            shape_of((width, columns), BF16),
            shape_of((8, width), F32),
        ],
        in_specs=[VMEM] * 8,
        out_specs=[VMEM] * 3,
        scratch_shapes=[
            pltpu.VMEM((WIDTH, length), BF16),
            pltpu.VMEM((WIDTH, length), F32),
            pltpu.VMEM((WIDTH, length), F32),
            pltpu.VMEM((columns, length), BF16),
            pltpu.VMEM((length, HEAD), BF16),
            pltpu.VMEM((length, HEAD), BF16),
        ],
        compiler_params=pltpu.CompilerParams(vmem_limit_bytes=56 * 1024 * 1024),
        name="attend_backward",
    )(tokens, d_mixed, heads, log_total, normed, weight, cosine, sines)


def pick(stack, index):
    return lax.dynamic_index_in_dim(stack, index, 0, keepdims=False)


def gelu_tanh(hidden_in):
    return jax.nn.gelu(hidden_in, approximate=True)


def bits_of(count):
    return [1 << bit for bit in range(count.bit_length() - 1)]


def body(
    tokens,
    upstream,
    token_mask,
    time_index,
    weight_index,
    time_table,
    weight_grid,
    w_ada,
    b_ada,
    gain_one,
    gain_two,
    w_qkv,
    w_proj,
    w_up,
    b_up,
    w_down,
    b_down,
    *,
    n,
    m,
):
    side = n // PLANES
    me = lax.axis_index("seq")
    plane, spot = me // side, me % side
    shard, width = tokens.shape[2], tokens.shape[3]
    rows = w_qkv.shape[0]
    hidden_count = w_up.shape[1]
    grid_size = time_table.shape[0]
    count = MICRO * shard

    def exchange(slots):
        return lax.all_to_all(slots, "seq", 0, 0, tiled=True)

    def everywhere(value):
        return exchange(jnp.broadcast_to(value[None], (n,) + value.shape))

    def to_planes(parts):
        return [parts[min(at, MICRO - 1)] for at in range(PLANES)]

    def swap_mlp(value, distance):
        return lax.ppermute(value, "mlp", [(i, i ^ distance) for i in range(m)])

    packed = jnp.concatenate(
        [w_up, w_down.T, w_proj.reshape(-1, hidden_count), w_ada.reshape(-1, hidden_count)], 0
    )
    gathered = lax.all_gather(packed, "seq", axis=0)

    x_low = tokens[:, 0]
    last = jnp.minimum(plane, MICRO - 1)
    slots = jnp.stack(to_planes(x_low))[:, None]
    slots = jnp.broadcast_to(slots, (PLANES, side, shard, width)).reshape(n, shard, width)
    token_block = exchange(slots).reshape(n * shard, width)
    by_group = w_qkv.reshape(rows, 3, GROUPS, WIDTH).transpose(2, 0, 1, 3).reshape(1, GROUPS, rows, 3 * WIDTH)
    slots = jnp.broadcast_to(by_group, (n // GROUPS, GROUPS, rows, 3 * WIDTH)).reshape(n, rows, 3 * WIDTH)
    weight_block = exchange(slots).reshape(width, 3 * WIDTH)

    index_here = time_index[:, 0]
    onehot_here = (index_here[:, None] == jnp.arange(grid_size)[None, :]).astype(BF16)
    cond_here = jnp.dot(onehot_here, time_table, preferred_element_type=F32).astype(BF16)
    ada_part = jnp.dot(cond_here, w_ada, preferred_element_type=F32) + b_ada.astype(F32)
    ada_columns = w_ada.shape[1]
    small = jnp.concatenate(
        [ada_part.reshape(-1), gain_one.astype(F32), gain_two.astype(F32), b_down.astype(F32)]
    )
    small = everywhere(small)
    cut = MICRO * ada_columns
    modulation = small[:, :cut].reshape(n, MICRO, ada_columns).transpose(1, 0, 2).reshape(MICRO, -1)
    full_gain_one = small[:, cut : cut + rows].reshape(1, width)
    full_gain_two = small[:, cut + rows : cut + 2 * rows].reshape(1, width)
    full_bias_down = small[:, cut + 2 * rows :].reshape(1, width)
    parts = [modulation[:, at * width : (at + 1) * width] for at in range(6)]
    shift_one, scale_one, gate_one, shift_two, scale_two, gate_two = parts
    wide = [jnp.broadcast_to(part[:, None], (MICRO, shard, width)).reshape(count, width) for part in parts]

    positions = jnp.arange(n * shard).astype(F32)[None, :]
    frequency = 10000.0 ** (-jnp.arange(0, HEAD, 2).astype(F32) / HEAD)
    angles = frequency[:, None] * positions
    cosine, sines = jnp.cos(angles), jnp.sin(angles)

    mixed_block, heads, log_total, normed = attend_forward(
        token_block,
        weight_block,
        full_gain_one * (1.0 + pick(scale_one, last))[None],
        pick(shift_one, last)[None],
        cosine,
        sines,
    )

    received = exchange(mixed_block.reshape(n, shard, WIDTH)).reshape(PLANES, side, shard, WIDTH)
    mixed = received[:MICRO, :GROUPS].transpose(0, 2, 1, 3).reshape(count, width)

    weights_at = gathered[:, : 2 * rows]
    full_up = weights_at[:, :rows].reshape(width, hidden_count)
    full_down = weights_at[:, rows:].reshape(width, hidden_count)
    proj_rows = rows * width // hidden_count
    full_proj = gathered[:, 2 * rows : 2 * rows + proj_rows].reshape(width, width)
    full_ada = gathered[:, 2 * rows + proj_rows :].reshape(n, w_ada.shape[0], ada_columns)

    onehot_weight = weight_index[:, 0][:, None] == jnp.arange(grid_size)[None, :]
    loss_weights = jnp.sum(jnp.where(onehot_weight, weight_grid[None, :], 0.0), -1)
    d_result = (
        upstream[:, 0].astype(F32)
        * token_mask[:, 0].astype(F32)[..., None]
        * loss_weights[:, None, None]
    ).reshape(count, width)
    d_output = wide[5] * d_result
    rows_grad = [d_output.astype(BF16)]
    rows_grad = jnp.concatenate(rows_grad + [swap_mlp(rows_grad[0], d) for d in range(1, m)], 0)

    x = x_low.astype(F32).reshape(count, width)
    attended = nn(mixed, full_proj)
    middle = x + wide[2] * attended
    xhat_two, root_two = standardize(middle)
    normed_two = (xhat_two * (full_gain_two * (1.0 + wide[4])) + wide[3]).astype(BF16)
    rows_all = jnp.concatenate([normed_two] + [swap_mlp(normed_two, d) for d in range(1, m)], 0)

    hidden = nn(rows_all, full_up) + b_up.astype(F32)
    active_wide, pull_gelu = jax.vjp(gelu_tanh, hidden)
    active_low = active_wide.astype(BF16)
    d_active = nn(rows_grad, full_down)
    d_hidden = pull_gelu(d_active)[0].astype(BF16)

    def sum_mlp(partial):
        total = partial[:count]
        for d in range(1, m):
            total = total + swap_mlp(partial[d * count : (d + 1) * count].astype(BF16), d).astype(F32)
        return total

    d_normed_two = sum_mlp(nt(d_hidden, full_up))
    output = sum_mlp(nt(active_low, full_down)) + full_bias_down
    result = (middle + wide[5] * output).astype(BF16)

    def by_sequence(value):
        return jnp.sum(value.reshape(MICRO, shard, width), 1)

    def pull_norm(d_normed, gains, xhat, root):
        e = d_normed * gains
        return root * (
            e - jnp.mean(e, -1, keepdims=True) - xhat * jnp.mean(e * xhat, -1, keepdims=True)
        )

    d_middle = d_result + pull_norm(d_normed_two, full_gain_two * (1.0 + wide[4]), xhat_two, root_two)
    d_attended_low = (wide[2] * d_middle).astype(BF16)
    d_mixed = nt(d_attended_low, full_proj).astype(BF16).reshape(MICRO, shard, width)

    by_group = d_mixed.reshape(MICRO, shard, GROUPS, WIDTH).transpose(0, 2, 1, 3)
    slots = jnp.stack(to_planes(by_group))[:, None]
    slots = jnp.broadcast_to(slots, (PLANES, side // GROUPS, GROUPS, shard, WIDTH))
    d_mixed_block = exchange(slots.reshape(n, shard, WIDTH)).reshape(n * shard, WIDTH)

    def tn(left, right):
        return lax.dot_general(left, right, (((0,), (0,)), ((), ())), preferred_element_type=F32)

    grads = jnp.concatenate(
        [
            tn(rows_all, d_hidden).astype(BF16).reshape(n, rows, hidden_count),
            tn(rows_grad, active_low).astype(BF16).reshape(n, rows, hidden_count),
            tn(mixed, d_attended_low).astype(BF16).reshape(n, proj_rows, hidden_count),
        ],
        1,
    )
    grads = lax.psum_scatter(grads, "seq", scatter_dimension=0, tiled=True)[0].astype(F32)
    grad_up = grads[:rows]
    grad_down = grads[rows : 2 * rows].T
    grad_proj = grads[2 * rows :].reshape(rows, width)
    for bit in bits_of(m):
        grad_proj = grad_proj + swap_mlp(grad_proj.astype(BF16), bit).astype(F32)

    d_normed_block, d_weight, sums = attend_backward(
        token_block, d_mixed_block, heads, log_total, normed, weight_block, cosine, sines
    )

    received = exchange(d_normed_block.reshape(n, shard, width)).reshape(PLANES, side, shard, width)
    d_normed = jnp.sum(received[:MICRO, :GROUPS].astype(F32), 1).reshape(count, width)
    xhat_one, root_one = standardize(x)
    d_tokens = d_middle + pull_norm(d_normed, full_gain_one * (1.0 + wide[1]), xhat_one, root_one)

    received = exchange(d_weight.reshape(n, rows, 3 * WIDTH)).reshape(PLANES, side, rows, 3 * WIDTH)
    grad_qkv = jnp.sum(received[:MICRO, :GROUPS].astype(F32), 0)
    grad_qkv = grad_qkv.reshape(GROUPS, rows, 3, WIDTH).transpose(1, 2, 0, 3).reshape(rows, 3 * width)
    for bit in bits_of(m):
        grad_qkv = grad_qkv + swap_mlp(grad_qkv.astype(BF16), bit).astype(F32)

    xhat_sums = by_sequence(d_normed_two * xhat_two)
    own = ((jnp.arange(MICRO) == plane) & (spot < GROUPS))[:, None]
    bias_up_rows = -(-hidden_count // width)
    bias_up_sum = jnp.sum(d_hidden.astype(F32), 0)
    bias_up_sum = jnp.pad(bias_up_sum, (0, bias_up_rows * width - hidden_count)).reshape(-1, width)
    small = jnp.concatenate(
        [
            jnp.where(own, sums[0:1], 0.0),
            jnp.where(own, sums[1:2], 0.0),
            by_sequence(d_middle * attended),
            by_sequence(d_normed_two),
            full_gain_two * xhat_sums,
            by_sequence(d_result * output),
            jnp.sum((1.0 + scale_two) * xhat_sums, 0, keepdims=True),
            jnp.sum(d_output, 0, keepdims=True),
            bias_up_sum,
        ],
        0,
    )
    lines = small.shape[0]
    small = jnp.sum(exchange(small.reshape(lines, n, rows).transpose(1, 0, 2)), 0)
    small = everywhere(small).transpose(1, 0, 2).reshape(lines, width)
    d_xhat = small[MICRO : 2 * MICRO]
    at = 6 * MICRO
    grad_bias_up = small[at + 2 :].reshape(-1)[:hidden_count]
    index_row = jnp.pad(index_here.astype(F32), (0, width - MICRO))[None]
    small = jnp.concatenate(
        [
            small[:MICRO],
            full_gain_one * d_xhat,
            small[2 * MICRO : at + 2],
            jnp.sum((1.0 + scale_one) * d_xhat, 0, keepdims=True),
            index_row,
        ],
        0,
    )[None]
    for bit in bits_of(m):
        small = jnp.concatenate([small, swap_mlp(small, bit)], 0)
    d_modulation = small[:, :at].reshape(m, 6, MICRO, width).transpose(0, 2, 1, 3)
    d_modulation = d_modulation.reshape(m * MICRO, n, ada_columns)
    vectors = jnp.sum(small[:, at : at + 3], 0)
    index_all = small[:, at + 3, :MICRO].reshape(-1).astype(jnp.int32)
    onehot = (index_all[:, None] == jnp.arange(grid_size)[None, :]).astype(BF16)
    cond = jnp.dot(onehot, time_table, preferred_element_type=F32)
    d_modulation_own = lax.dynamic_index_in_dim(d_modulation, me, 1, keepdims=False)
    grad_ada = jnp.dot(cond.T, d_modulation_own, precision=highest)
    grad_bias_ada = jnp.sum(d_modulation_own, 0)
    d_cond = jnp.einsum("bic,idc->bd", d_modulation, full_ada.astype(F32), precision=highest)
    table_rows = grid_size // n
    onehot_own = index_all[None, :] == (me * table_rows + jnp.arange(table_rows))[:, None]
    grad_table = jnp.dot(onehot_own.astype(F32), d_cond, precision=highest)
    vectors = lax.dynamic_slice_in_dim(vectors, me * rows, rows, 1)
    return (
        result.reshape(MICRO, 1, shard, width),
        d_tokens.reshape(MICRO, 1, shard, width),
        grad_table,
        grad_ada,
        grad_bias_ada,
        vectors[2],
        vectors[0],
        grad_qkv,
        grad_proj,
        grad_up,
        grad_bias_up,
        grad_down,
        vectors[1],
    )


def solution(mesh):
    in_specs = (
        P(None, "mlp", "seq", None),
        P(None, "mlp", "seq", None),
        P(None, "mlp", "seq"),
        P(None, "mlp"),
        P(None, "mlp"),
        P(),
        P(),
        P(None, "seq"),
        P("seq"),
        P("seq"),
        P("seq"),
        P("seq", None),
        P("seq", None),
        P("seq", "mlp"),
        P("mlp"),
        P("mlp", "seq"),
        P("seq"),
    )
    out_specs = (
        P(None, "mlp", "seq", None),
        P(None, "mlp", "seq", None),
        P("seq", None),
        P(None, "seq"),
        P("seq"),
        P("seq"),
        P("seq"),
        P("seq", None),
        P("seq", None),
        P("seq", "mlp"),
        P("mlp"),
        P("mlp", "seq"),
        P("seq"),
    )
    run = functools.partial(body, n=mesh.shape["seq"], m=mesh.shape["mlp"])
    return jax.shard_map(run, mesh=mesh, in_specs=in_specs, out_specs=out_specs, check_vma=False)
```

```python
import functools

import jax
import jax.numpy as jnp
from jax import lax
from jax.experimental import pallas as pl
from jax.experimental.pallas import tpu as pltpu
from jax.sharding import PartitionSpec as P

HEADS = 12
HEAD = 64
MICRO = 3
PLANES = 4
GROUPS = 4
PER_GROUP = HEADS // GROUPS
WIDTH = PER_GROUP * HEAD
QUERY_BLOCK = 256
SCALING = HEAD ** (-0.5)
BF16 = jnp.bfloat16
F32 = jnp.float32
highest = lax.Precision.HIGHEST

VMEM = pl.BlockSpec(memory_space=pltpu.VMEM)
SMEM = pl.BlockSpec(memory_space=pltpu.SMEM)


def nn(left, right):
    return lax.dot_general(left, right, (((1,), (0,)), ((), ())), preferred_element_type=F32)


def nt(left, right):
    return lax.dot_general(left, right, (((1,), (1,)), ((), ())), preferred_element_type=F32)


def standardize(inputs):
    average = jnp.mean(inputs, -1, keepdims=True)
    centred = inputs - average
    spread = jnp.mean(centred * centred, -1, keepdims=True)
    root = lax.rsqrt(spread + 1e-06)
    return centred * root, root


def forward_kernel(place, *refs, blocks):
    tokens, refs = refs[:blocks], refs[blocks:]
    weights, refs = refs[:PLANES], refs[PLANES:]
    (gain, shift, cosine, sines), refs = refs[:4], refs[4:]
    mixed, refs = refs[:blocks], refs[blocks:]
    heads, log_total, normed, weight, keys, mixed_turned = refs
    plane = place[0]
    rows = weights[0].shape[0]
    count = tokens[0].shape[0]
    for distance in range(PLANES):
        first = pl.multiple_of((plane ^ distance) * rows, 16)
        weight[pl.ds(first, rows), :] = weights[distance][...]
    for block in range(blocks):
        xhat, _ = standardize(tokens[block][...].astype(F32))
        normed[block * count : (block + 1) * count, :] = (xhat * gain[...] + shift[...]).astype(BF16)
    project = nt(weight[...].T, normed[...])
    cos, sin = cosine[...], sines[...]
    half = HEAD // 2
    for part in range(2):
        for head in range(PER_GROUP):
            start = part * WIDTH + head * HEAD
            first, second = project[start : start + half], project[start + half : start + HEAD]
            turned = jnp.concatenate([first * cos - second * sin, second * cos + first * sin], 0).astype(BF16)
            if part == 0:
                turned = turned * jnp.asarray(SCALING, BF16)
            else:
                keys[head] = turned.T
            heads[start : start + HEAD, :] = turned
    heads[2 * WIDTH :, :] = project[2 * WIDTH :].astype(BF16)
    length = heads.shape[1]
    for head in range(PER_GROUP):
        start = head * HEAD

        def queries_step(step, carry):
            columns = pl.ds(pl.multiple_of(step * QUERY_BLOCK, QUERY_BLOCK), QUERY_BLOCK)
            scores = nn(keys[head], heads[start : start + HEAD, columns])
            peak = jnp.max(scores, 0, keepdims=True)
            exps = jnp.exp(scores - peak)
            total = jnp.sum(exps, 0, keepdims=True)
            log_total[head : head + 1, columns] = peak + jnp.log(total)
            probs = (exps * (1.0 / total)).astype(BF16)
            values = heads[2 * WIDTH + start : 2 * WIDTH + start + HEAD, :]
            mixed_turned[start : start + HEAD, columns] = nn(values, probs).astype(BF16)
            return carry

        lax.fori_loop(0, length // QUERY_BLOCK, queries_step, 0)
    for block in range(blocks):
        mixed[block][...] = mixed_turned[:, block * count : (block + 1) * count].T


def backward_kernel(place, *refs, blocks):
    tokens, refs = refs[:blocks], refs[blocks:]
    d_mixed, refs = refs[:blocks], refs[blocks:]
    (heads, log_total, normed, weight, cosine, sines), refs = refs[:6], refs[6:]
    d_normed, refs = refs[:blocks], refs[blocks:]
    d_weight, refs = refs[:PLANES], refs[PLANES:]
    sums, d_turned, d_keys, d_values, d_project, d_whole, keys, values = refs
    plane = place[0]
    count = tokens[0].shape[0]
    length = heads.shape[1]
    for block in range(blocks):
        d_turned[:, block * count : (block + 1) * count] = d_mixed[block][...].T
    cos, sin = cosine[...], sines[...]
    half = HEAD // 2
    d_keys[...] = jnp.zeros_like(d_keys)
    d_values[...] = jnp.zeros_like(d_values)
    for head in range(PER_GROUP):
        start = head * HEAD
        keys_turned = heads.at[WIDTH + start : WIDTH + start + HEAD]
        keys[...] = keys_turned[...].T
        values[...] = heads[2 * WIDTH + start : 2 * WIDTH + start + HEAD, :].T

        def queries_step(step, carry):
            columns = pl.ds(pl.multiple_of(step * QUERY_BLOCK, QUERY_BLOCK), QUERY_BLOCK)
            queries = heads[start : start + HEAD, columns]
            incoming = d_turned[start : start + HEAD, columns]
            scores = nn(keys[...], queries)
            probs = jnp.exp(scores - log_total[head : head + 1, columns])
            d_probs = nn(values[...], incoming)
            delta = jnp.sum(probs * d_probs, 0, keepdims=True)
            d_scores = (probs * (d_probs - delta)).astype(BF16)
            d_values[start : start + HEAD, :] += nt(incoming, probs.astype(BF16))
            d_keys[start : start + HEAD, :] += nt(queries, d_scores)
            d_queries = nn(keys_turned[...], d_scores) * SCALING
            first, second = d_queries[:half], d_queries[half:]
            cos_here, sin_here = cosine[:, columns], sines[:, columns]
            d_project[start : start + half, columns] = (first * cos_here + second * sin_here).astype(BF16)
            d_project[start + half : start + HEAD, columns] = (second * cos_here - first * sin_here).astype(BF16)
            return carry

        lax.fori_loop(0, length // QUERY_BLOCK, queries_step, 0)
        first, second = d_keys[start : start + half, :], d_keys[start + half : start + HEAD, :]
        d_project[WIDTH + start : WIDTH + start + half, :] = (first * cos + second * sin).astype(BF16)
        d_project[WIDTH + start + half : WIDTH + start + HEAD, :] = (second * cos - first * sin).astype(BF16)
    d_project[2 * WIDTH :, :] = d_values[...].astype(BF16)
    d_shift = jnp.zeros((1, normed.shape[1]), F32)
    d_xhat = jnp.zeros((1, normed.shape[1]), F32)
    for block in range(blocks):
        part = nt(d_project[:, block * count : (block + 1) * count].T, weight[...])
        d_normed[block][...] = part.astype(BF16)
        xhat, _ = standardize(tokens[block][...].astype(F32))
        d_shift = d_shift + jnp.sum(part, 0, keepdims=True)
        d_xhat = d_xhat + jnp.sum(part * xhat, 0, keepdims=True)
    sums[0:1, :] = d_shift
    sums[1:2, :] = d_xhat
    d_whole[...] = nn(d_project[...], normed[...]).astype(BF16).T
    rows = d_weight[0].shape[0]
    for distance in range(PLANES):
        first = pl.multiple_of((plane ^ distance) * rows, 16)
        d_weight[distance][...] = d_whole[pl.ds(first, rows), :]


def shape_of(dims, dtype):
    return jax.ShapeDtypeStruct(dims, dtype)


def attend_forward(place, tokens, weights, gain, shift, cosine, sines):
    blocks, (count, width) = len(tokens), tokens[0].shape
    length = blocks * count
    columns = weights[0].shape[1]
    outs = pl.pallas_call(
        functools.partial(forward_kernel, blocks=blocks),
        out_shape=[shape_of((count, WIDTH), BF16)] * blocks
        + [
            shape_of((columns, length), BF16),
            shape_of((8, length), F32),
            shape_of((length, width), BF16),
            shape_of((width, columns), BF16),
        ],
        in_specs=[SMEM] + [VMEM] * (blocks + PLANES + 4),
        out_specs=[VMEM] * (blocks + 4),
        scratch_shapes=[pltpu.VMEM((PER_GROUP, length, HEAD), BF16), pltpu.VMEM((WIDTH, length), BF16)],
        compiler_params=pltpu.CompilerParams(vmem_limit_bytes=56 * 1024 * 1024),
        name="attend_forward",
    )(place, *tokens, *weights, gain, shift, cosine, sines)
    return outs[:blocks], outs[blocks:]


def attend_backward(place, tokens, d_mixed, kept, cosine, sines):
    blocks, (count, width) = len(tokens), tokens[0].shape
    length = blocks * count
    columns = 3 * WIDTH
    rows = width // PLANES
    outs = pl.pallas_call(
        functools.partial(backward_kernel, blocks=blocks),
        out_shape=[shape_of((count, width), BF16)] * blocks
        + [shape_of((rows, columns), BF16)] * PLANES
        + [shape_of((8, width), F32)],
        in_specs=[SMEM] + [VMEM] * (2 * blocks + 6),
        out_specs=[VMEM] * (blocks + PLANES + 1),
        scratch_shapes=[
            pltpu.VMEM((WIDTH, length), BF16),
            pltpu.VMEM((WIDTH, length), F32),
            pltpu.VMEM((WIDTH, length), F32),
            pltpu.VMEM((columns, length), BF16),
            pltpu.VMEM((width, columns), BF16),
            pltpu.VMEM((length, HEAD), BF16),
            pltpu.VMEM((length, HEAD), BF16),
        ],
        compiler_params=pltpu.CompilerParams(vmem_limit_bytes=56 * 1024 * 1024),
        name="attend_backward",
    )(place, *tokens, *d_mixed, *kept, cosine, sines)
    return outs[:blocks], outs[blocks : blocks + PLANES], outs[-1]


def pick(stack, index):
    return lax.dynamic_index_in_dim(stack, index, 0, keepdims=False)


def gelu_tanh(hidden_in):
    return jax.nn.gelu(hidden_in, approximate=True)


def bits_of(count):
    return [1 << bit for bit in range(count.bit_length() - 1)]


def body(
    tokens,
    upstream,
    token_mask,
    time_index,
    weight_index,
    time_table,
    weight_grid,
    w_ada,
    b_ada,
    gain_one,
    gain_two,
    w_qkv,
    w_proj,
    w_up,
    b_up,
    w_down,
    b_down,
    *,
    n,
    m,
):
    side = n // PLANES
    me = lax.axis_index("seq")
    plane, spot, core = me // side, me % side, me % 2
    shard, width = tokens.shape[2], tokens.shape[3]
    rows = w_qkv.shape[0]
    hidden_count = w_up.shape[1]
    grid_size = time_table.shape[0]
    count = PLANES * shard
    same_core = [list(range(at, n, 2)) for at in range(2)]

    def swap(value, distance):
        return lax.ppermute(value, "seq", [(i, i ^ distance) for i in range(n)])

    def swap_mlp(value, distance):
        return lax.ppermute(value, "mlp", [(i, i ^ distance) for i in range(m)])

    def between_planes(pieces):
        return [pieces[0]] + [swap(pieces[d], d * side) for d in range(1, PLANES)]

    def in_plane(pieces):
        return [pieces[0]] + [swap(pieces[e], e) for e in range(1, side)]

    def in_order(blocks, axis):
        halves = jnp.stack(blocks)
        for bit in bits_of(len(blocks)):
            here = halves.reshape((len(blocks) // (2 * bit), 2, bit) + halves.shape[1:])
            halves = jnp.where((axis & bit) != 0, here[:, ::-1], here).reshape(halves.shape)
        return halves

    proj_rows = rows * width // hidden_count
    packed = jnp.concatenate(
        [w_up, w_down.T, w_proj.reshape(-1, hidden_count), w_ada.reshape(-1, hidden_count)], 0
    )
    gathered = lax.all_gather(packed, "seq", axis=0, axis_index_groups=same_core)

    x_low = tokens[:, 0]

    def for_plane(values):
        return [pick(values, jnp.minimum(plane ^ d, MICRO - 1)) for d in range(PLANES)]

    own_low = jnp.concatenate(between_planes(for_plane(x_low)), 0)
    token_blocks = {0: own_low}
    for bit in reversed(bits_of(side)):
        for known in list(token_blocks):
            token_blocks[known | bit] = swap(token_blocks[known], bit)
    token_blocks = [token_blocks[at] for at in range(side)]

    by_group = w_qkv.reshape(rows, 3, GROUPS, WIDTH).transpose(2, 0, 1, 3).reshape(GROUPS, rows, 3 * WIDTH)
    received = in_plane([pick(by_group, (spot ^ e) % GROUPS) for e in range(side)])
    received = jnp.stack(received)
    weight_blocks = {0: jnp.concatenate([pick(received, spot ^ at) for at in range(side)], 0)}
    for bit in (2, 1):
        for known in list(weight_blocks):
            weight_blocks[known | bit] = swap(weight_blocks[known], bit * side)
    weight_blocks = [weight_blocks[at] for at in range(PLANES)]

    index_here = time_index[:, 0]
    onehot_here = (index_here[:, None] == jnp.arange(grid_size)[None, :]).astype(BF16)
    cond_here = jnp.dot(onehot_here, time_table, preferred_element_type=F32).astype(BF16)
    ada_part = jnp.dot(cond_here, w_ada, preferred_element_type=F32) + b_ada.astype(F32)
    ada_columns = w_ada.shape[1]
    small = jnp.concatenate(
        [
            ada_part.reshape(-1),
            jnp.concatenate([gain_one, gain_two, b_down]).astype(F32),
            token_mask[:, 0].astype(F32).reshape(-1),
        ]
    )[None]
    for bit in bits_of(n):
        small = jnp.concatenate([small, swap(small, bit)], 0)
    small = in_order(list(small), me)
    last = jnp.minimum(plane, MICRO - 1)
    cut = MICRO * ada_columns
    modulation = small[:, :cut].reshape(n, MICRO, ada_columns).transpose(1, 0, 2).reshape(MICRO, -1)
    full_gain_one = small[:, cut : cut + rows].reshape(1, width)
    full_gain_two = small[:, cut + rows : cut + 2 * rows].reshape(1, width)
    full_bias_down = small[:, cut + 2 * rows : cut + 3 * rows].reshape(1, width)
    mask = small[:, cut + 3 * rows :].reshape(PLANES, side, MICRO, shard)
    mask = pick(mask.transpose(1, 2, 0, 3).reshape(side * MICRO, PLANES, shard), spot * MICRO + last)
    mask = jnp.concatenate([pick(mask, plane ^ d) for d in range(PLANES)])[:, None]
    scale_one_all = modulation[:, width : 2 * width]
    mine = pick(modulation, last)[None]
    parts = [mine[:, at * width : (at + 1) * width] for at in range(6)]
    shift_one, scale_one, gate_one, shift_two, scale_two, gate_two = parts

    order = ((plane ^ jnp.arange(PLANES))[None, :] * side + (spot ^ jnp.arange(side))[:, None]) * shard
    positions = (order[:, :, None] + jnp.arange(shard)).reshape(1, -1).astype(F32)
    frequency = 10000.0 ** (-jnp.arange(0, HEAD, 2).astype(F32) / HEAD)
    angles = frequency[:, None] * positions
    cosine, sines = jnp.cos(angles), jnp.sin(angles)

    place = plane.astype(jnp.int32).reshape(1)
    gains_one = full_gain_one * (1.0 + scale_one)
    mixed_blocks, kept = attend_forward(
        place, token_blocks, weight_blocks, gains_one, shift_one, cosine, sines
    )

    received = jnp.stack(in_plane(mixed_blocks))
    mixed = jnp.concatenate([pick(received, spot ^ group) for group in range(GROUPS)], -1)

    gathered = jnp.stack([gathered, swap(gathered, 1)])
    gathered = jnp.stack([pick(gathered, core), pick(gathered, 1 - core)], 1)
    full_up = gathered[:, :, :rows].reshape(width, hidden_count)
    full_down = gathered[:, :, rows : 2 * rows].reshape(width, hidden_count)
    full_proj = gathered[:, :, 2 * rows : 2 * rows + proj_rows].reshape(width, width)
    full_ada = gathered[:, :, 2 * rows + proj_rows :].reshape(n, w_ada.shape[0], ada_columns)

    onehot_weight = weight_index[:, 0][:, None] == jnp.arange(grid_size)[None, :]
    loss_weights = jnp.sum(jnp.where(onehot_weight, weight_grid[None, :], 0.0), -1)
    loss_weight = jnp.where(plane < MICRO, pick(loss_weights, last), 0.0)
    own_upstream = jnp.concatenate(between_planes(for_plane(upstream[:, 0])), 0)
    d_result = own_upstream.astype(F32) * (mask * loss_weight)
    d_output = gate_two * d_result
    rows_grad = [d_output.astype(BF16)]
    rows_grad = jnp.concatenate(rows_grad + [swap_mlp(rows_grad[0], d) for d in range(1, m)], 0)

    x = own_low.astype(F32)
    attended = nn(mixed, full_proj)
    middle = x + gate_one * attended
    xhat_two, root_two = standardize(middle)
    gains_two = full_gain_two * (1.0 + scale_two)
    normed_two = (xhat_two * gains_two + shift_two).astype(BF16)
    rows_all = jnp.concatenate([normed_two] + [swap_mlp(normed_two, d) for d in range(1, m)], 0)

    hidden = nn(rows_all, full_up) + b_up.astype(F32)
    active_wide, pull_gelu = jax.vjp(gelu_tanh, hidden)
    active_low = active_wide.astype(BF16)
    d_active = nn(rows_grad, full_down)
    d_hidden = pull_gelu(d_active)[0].astype(BF16)

    def sum_mlp(partial):
        total = partial[:count]
        for d in range(1, m):
            total = total + swap_mlp(partial[d * count : (d + 1) * count].astype(BF16), d).astype(F32)
        return total

    d_normed_two = sum_mlp(nt(d_hidden, full_up))
    output = sum_mlp(nt(active_low, full_down)) + full_bias_down
    result = (middle + gate_two * output).astype(BF16)

    def over_tokens(value):
        return jnp.sum(value, 0, keepdims=True)

    def pull_norm(d_normed, gains, xhat, root):
        e = d_normed * gains
        return root * (
            e - jnp.mean(e, -1, keepdims=True) - xhat * jnp.mean(e * xhat, -1, keepdims=True)
        )

    def back_to_tokens(value):
        received = between_planes([value[d * shard : (d + 1) * shard] for d in range(PLANES)])
        received = jnp.stack(received)
        return jnp.stack([pick(received, plane ^ at) for at in range(MICRO)])[:, None]

    d_middle = d_result + pull_norm(d_normed_two, gains_two, xhat_two, root_two)
    d_attended_low = (gate_one * d_middle).astype(BF16)
    d_mixed = nt(d_attended_low, full_proj).astype(BF16)

    by_group = jnp.stack([d_mixed[:, at * WIDTH : (at + 1) * WIDTH] for at in range(GROUPS)])
    d_mixed_blocks = in_plane([pick(by_group, (spot ^ e) % GROUPS) for e in range(side)])
    if side > GROUPS:
        share = (spot < GROUPS).astype(BF16)
        d_mixed_blocks = [block * share for block in d_mixed_blocks]

    def tn(left, right):
        return lax.dot_general(left, right, (((0,), (0,)), ((), ())), preferred_element_type=F32)

    grads = jnp.concatenate(
        [
            tn(rows_all, d_hidden).astype(BF16).reshape(n // 2, 2, rows, hidden_count),
            tn(rows_grad, active_low).astype(BF16).reshape(n // 2, 2, rows, hidden_count),
            tn(mixed, d_attended_low).astype(BF16).reshape(n // 2, 2, proj_rows, hidden_count),
        ],
        2,
    )
    arrived = swap(lax.dynamic_index_in_dim(grads, 1 - core, 1, keepdims=False), 1)
    grads = lax.dynamic_index_in_dim(grads, core, 1, keepdims=False)
    grads = (grads.astype(F32) + arrived.astype(F32)).astype(BF16)
    grads = lax.psum_scatter(grads, "seq", scatter_dimension=0, axis_index_groups=same_core, tiled=True)
    grads = grads[0].astype(F32)
    grad_up = grads[:rows]
    grad_down = grads[rows : 2 * rows].T
    grad_proj = grads[2 * rows :].reshape(rows, width)
    for bit in bits_of(m):
        grad_proj = grad_proj + swap_mlp(grad_proj.astype(BF16), bit).astype(F32)

    d_normed_blocks, d_weight_blocks, sums = attend_backward(
        place, token_blocks, d_mixed_blocks, kept, cosine, sines
    )

    blocks = dict(enumerate(d_normed_blocks))
    for bit in bits_of(side):
        for at in [at for at in blocks if at & bit]:
            arrived = swap(blocks.pop(at), bit)
            blocks[at ^ bit] = (blocks[at ^ bit].astype(F32) + arrived.astype(F32)).astype(BF16)
    d_normed = blocks[0].astype(F32)
    xhat_one, root_one = standardize(x)
    d_tokens = (d_middle + pull_norm(d_normed, gains_one, xhat_one, root_one)).astype(BF16)

    total = sum(piece.astype(F32) for piece in between_planes(d_weight_blocks))
    by_spot = total.astype(BF16).reshape(side, rows, 3 * WIDTH)
    received = jnp.stack(in_plane([pick(by_spot, spot ^ e) for e in range(side)]))
    grad_qkv = jnp.stack([pick(received, spot ^ group) for group in range(GROUPS)])
    grad_qkv = grad_qkv.reshape(GROUPS, rows, 3, WIDTH).transpose(1, 2, 0, 3).reshape(rows, 3 * width)
    grad_qkv = grad_qkv.astype(F32)
    for bit in bits_of(m):
        grad_qkv = grad_qkv + swap_mlp(grad_qkv.astype(BF16), bit).astype(F32)

    xhat_sums = over_tokens(d_normed_two * xhat_two)
    bias_up_rows = -(-hidden_count // width)
    bias_up_sum = jnp.sum(d_hidden.astype(F32), 0)
    bias_up_sum = jnp.pad(bias_up_sum, (0, bias_up_rows * width - hidden_count)).reshape(-1, width)
    small = jnp.concatenate(
        [
            sums[0:1],
            sums[1:2],
            over_tokens(d_middle * attended),
            over_tokens(d_normed_two),
            full_gain_two * xhat_sums,
            over_tokens(d_result * output),
            (1.0 + scale_two) * xhat_sums,
            over_tokens(d_output),
            bias_up_sum,
        ],
        0,
    )
    for bit in bits_of(side):
        small = small + swap(small, bit)
    small = small[None]
    for bit in bits_of(PLANES):
        small = jnp.concatenate([small, swap(small, bit * side)], 0)
    small = in_order(list(small), plane)[:MICRO]
    grad_bias_up = jnp.sum(small[:, 8:], 0).reshape(-1)[:hidden_count]
    d_xhat = small[:, 1]
    vectors = jnp.stack(
        [
            jnp.sum((1.0 + scale_one_all) * d_xhat, 0),
            jnp.sum(small[:, 6], 0),
            jnp.sum(small[:, 7], 0),
            jnp.pad(index_here.astype(F32), (0, width - MICRO)),
        ]
    )
    small = jnp.concatenate(
        [small[:, :1], (full_gain_one * d_xhat)[:, None], small[:, 2:6]], 1
    ).reshape(6 * MICRO, width)
    small = jnp.concatenate([small, vectors], 0)[None]
    for bit in bits_of(m):
        small = jnp.concatenate([small, swap_mlp(small, bit)], 0)
    at = 6 * MICRO
    d_modulation = small[:, :at].reshape(m * MICRO, n, ada_columns)
    vectors = jnp.sum(small[:, at : at + 3], 0)
    index_all = small[:, at + 3, :MICRO].reshape(-1).astype(jnp.int32)
    onehot = (index_all[:, None] == jnp.arange(grid_size)[None, :]).astype(BF16)
    cond = jnp.dot(onehot, time_table, preferred_element_type=F32)
    d_modulation_own = lax.dynamic_index_in_dim(d_modulation, me, 1, keepdims=False)
    grad_ada = jnp.dot(cond.T, d_modulation_own, precision=highest)
    grad_bias_ada = jnp.sum(d_modulation_own, 0)
    d_cond = jnp.einsum("bic,idc->bd", d_modulation, full_ada.astype(F32), precision=highest)
    table_rows = grid_size // n
    onehot_own = index_all[None, :] == (me * table_rows + jnp.arange(table_rows))[:, None]
    grad_table = jnp.dot(onehot_own.astype(F32), d_cond, precision=highest)
    vectors = lax.dynamic_slice_in_dim(vectors, me * rows, rows, 1)
    return (
        back_to_tokens(result),
        back_to_tokens(d_tokens).astype(F32),
        grad_table,
        grad_ada,
        grad_bias_ada,
        vectors[0],
        vectors[1],
        grad_qkv,
        grad_proj,
        grad_up,
        grad_bias_up,
        grad_down,
        vectors[2],
    )


def solution(mesh):
    in_specs = (
        P(None, "mlp", "seq", None),
        P(None, "mlp", "seq", None),
        P(None, "mlp", "seq"),
        P(None, "mlp"),
        P(None, "mlp"),
        P(),
        P(),
        P(None, "seq"),
        P("seq"),
        P("seq"),
        P("seq"),
        P("seq", None),
        P("seq", None),
        P("seq", "mlp"),
        P("mlp"),
        P("mlp", "seq"),
        P("seq"),
    )
    out_specs = (
        P(None, "mlp", "seq", None),
        P(None, "mlp", "seq", None),
        P("seq", None),
        P(None, "seq"),
        P("seq"),
        P("seq"),
        P("seq"),
        P("seq", None),
        P("seq", None),
        P("seq", "mlp"),
        P("mlp"),
        P("mlp", "seq"),
        P("seq"),
    )
    run = functools.partial(body, n=mesh.shape["seq"], m=mesh.shape["mlp"])
    return jax.shard_map(run, mesh=mesh, in_specs=in_specs, out_specs=out_specs, check_vma=False)
```

```python
import functools
import math

import jax
import jax.numpy as jnp
from jax import lax
from jax.experimental import pallas as pl
from jax.experimental.pallas import tpu as pltpu
from jax.sharding import PartitionSpec as P

HEADS = 12
HEAD = 64
MICRO = 3
PLANES = 4
GROUPS = 4
PER_GROUP = HEADS // GROUPS
WIDTH = PER_GROUP * HEAD
QUERY_BLOCK = 256
SCALING = HEAD ** (-0.5)
BF16 = jnp.bfloat16
F32 = jnp.float32
highest = lax.Precision.HIGHEST
SLOPE = math.sqrt(2.0 / math.pi)
CUBIC = 0.044715
SMALL = 384

SHIFT_ONE, SCALE_ONE, GATE_ONE, SHIFT_TWO, SCALE_TWO, GATE_TWO, GAIN_ONE, GAIN_TWO, BIAS_DOWN = range(9)
SCALES_ALL, GAINS_ONE, GAINS_TWO = 9, 12, 13

VMEM = pl.BlockSpec(memory_space=pltpu.VMEM)
SMEM = pl.BlockSpec(memory_space=pltpu.SMEM)


def nn(left, right):
    return lax.dot_general(left, right, (((1,), (0,)), ((), ())), preferred_element_type=F32)


def nt(left, right):
    return lax.dot_general(left, right, (((1,), (1,)), ((), ())), preferred_element_type=F32)


def standardize(inputs):
    average = jnp.mean(inputs, -1, keepdims=True)
    centred = inputs - average
    spread = jnp.mean(centred * centred, -1, keepdims=True)
    root = lax.rsqrt(spread + 1e-06)
    return centred * root, root


def pull_norm(d_normed, gains, xhat, root):
    e = d_normed * gains
    return root * (e - jnp.mean(e, -1, keepdims=True) - xhat * jnp.mean(e * xhat, -1, keepdims=True))


def over_tokens(value):
    return jnp.sum(value, 0, keepdims=True)


def shape_of(dims, dtype):
    return jax.ShapeDtypeStruct(dims, dtype)


def call(kernel, name, operands, scalars, outs, scratch=(), flops=0, aliases=None):
    moved = sum(math.prod(o.shape) * o.dtype.itemsize for o in list(operands) + list(outs))
    return pl.pallas_call(
        kernel,
        out_shape=list(outs),
        in_specs=[SMEM] * len(scalars) + [VMEM] * len(operands),
        out_specs=[VMEM] * len(outs),
        scratch_shapes=list(scratch),
        input_output_aliases=aliases or {},
        compiler_params=pltpu.CompilerParams(vmem_limit_bytes=56 * 1024 * 1024),
        cost_estimate=pl.CostEstimate(flops=flops, bytes_accessed=moved, transcendentals=0),
        name=name,
    )(*scalars, *operands)


def modulation_kernel(times, table, w_ada, b_ada, gain_one, gain_two, b_down, mask, small):
    columns = w_ada.shape[1]
    rows = gain_one.shape[1]
    at = lax.broadcasted_iota(jnp.int32, (8, table.shape[0]), 1)
    line = lax.broadcasted_iota(jnp.int32, (8, table.shape[0]), 0)
    wanted = jnp.where(line == 0, times[0, 0], jnp.where(line == 1, times[1, 0], times[2, 0]))
    cond = nn((at == wanted).astype(F32).astype(BF16), table[...]).astype(BF16)
    part = nn(cond, w_ada[...]) + b_ada[...].astype(F32)
    small[...] = jnp.zeros_like(small)
    small[0:MICRO, 0:columns] = part[0:MICRO]
    small[3:4, 0:rows] = gain_one[...].astype(F32)
    small[3:4, 128 : 128 + rows] = gain_two[...].astype(F32)
    small[3:4, 256 : 256 + rows] = b_down[...].astype(F32)
    small[4 : 4 + MICRO, 0 : mask.shape[1]] = mask[...].astype(F32)


def vectors_kernel(place, weight_index, weight_grid, small, vectors, scale, line):
    n = small.shape[0]
    width = vectors.shape[1]
    columns, rows, shard = 6 * width // n, width // n, scale.shape[0] // PLANES
    plane, spot = place[0], place[1]
    side = n // PLANES
    me = plane * side + spot
    last = jnp.minimum(plane, MICRO - 1)

    def one_of(three):
        return jnp.where(last == 0, three[0:1], jnp.where(last == 1, three[1:2], three[2:3]))

    def pieces(first, size):
        start = first
        while start < first + size:
            stop = min(first + size, (start // width + 1) * width)
            yield start // width, start % width, start - first, stop - start
            start = stop

    vectors[...] = jnp.zeros_like(vectors)
    for i in range(n):
        here = small.at[me ^ i]
        mine = one_of(here[0:MICRO, 0:columns])
        for part, column, offset, size in pieces(i * columns, columns):
            vectors[part : part + 1, column : column + size] = mine[:, offset : offset + size]
            if part == SCALE_ONE:
                vectors[SCALES_ALL : SCALES_ALL + MICRO, column : column + size] = here[
                    0:MICRO, offset : offset + size
                ]
        for row, offset in ((GAIN_ONE, 0), (GAIN_TWO, 128), (BIAS_DOWN, 256)):
            vectors[row : row + 1, i * rows : (i + 1) * rows] = here[3:4, offset : offset + rows]
    for to, gain, by in ((GAINS_ONE, GAIN_ONE, SCALE_ONE), (GAINS_TWO, GAIN_TWO, SCALE_TWO)):
        vectors[to : to + 1, :] = vectors[gain : gain + 1, :] * (1.0 + vectors[by : by + 1, :])
    line[...] = jnp.zeros_like(line)
    for d in range(PLANES):
        line[0:1, d * shard : (d + 1) * shard] = one_of(small[d * side, 4 : 4 + MICRO, 0:shard])
    weight = jnp.where(plane < MICRO, weight_grid[weight_index[last, 0]], 0.0)
    scale[...] = line[...].T[:, 0:1] * weight


def project_kernel(place, gathered, tokens, vectors, *refs, chunks):
    side = len(refs) - 4
    mixed, (attended, middle, normed, weight) = refs[:side], refs[side:]
    spot = place[1]
    unit = gathered.shape[3]
    width = tokens.shape[1]
    for at in range(width // unit):
        weight[:, at * unit : (at + 1) * unit] = gathered[:, chunks + at].reshape(width, unit)
    total = jnp.zeros(attended.shape, F32)
    for e in range(side):
        other = spot ^ e
        block = mixed[e][...]
        if side > GROUPS:
            block = jnp.where(other < GROUPS, block, jnp.zeros_like(block))
        first = pl.multiple_of((other % GROUPS) * WIDTH, WIDTH)
        total = total + nn(block, weight[pl.ds(first, WIDTH), :])
    attended[...] = total
    after = tokens[...].astype(F32) + vectors[GATE_ONE : GATE_ONE + 1] * total
    middle[...] = after
    xhat, _ = standardize(after)
    normed[...] = (xhat * vectors[GAINS_TWO : GAINS_TWO + 1] + vectors[SHIFT_TWO : SHIFT_TWO + 1]).astype(BF16)


def feed_kernel(gathered, rows, d_rows, bias, output, d_normed, active, d_hidden):
    width, unit = rows.shape[1], gathered.shape[3]
    parts = bias.shape[1] // unit
    out = jnp.zeros(output.shape, F32)
    back = jnp.zeros(output.shape, F32)
    for at in range(parts):
        columns = slice(at * unit, (at + 1) * unit)
        up = gathered[:, at].reshape(width, unit)
        down = gathered[:, parts + at].reshape(width, unit)
        u = nn(rows[...], up) + bias[:, columns]
        square = u * u
        bent = jnp.tanh(SLOPE * u * (1.0 + CUBIC * square))
        half = 0.5 * (1.0 + bent)
        on = (u * half).astype(BF16)
        active[:, columns] = on
        slope = half + 0.5 * u * (1.0 - bent * bent) * (SLOPE * (1.0 + 3.0 * CUBIC * square))
        d_on = (nn(d_rows[...], down) * slope).astype(BF16)
        d_hidden[:, columns] = d_on
        out = out + nt(on, down)
        back = back + nt(d_on, up)
    output[...] = out.astype(output.dtype)
    d_normed[...] = back.astype(d_normed.dtype)


def feed_grads_kernel(*refs, blocks):
    rows, d_rows = refs[:blocks], refs[blocks : 2 * blocks]
    active, d_hidden = refs[2 * blocks : 3 * blocks], refs[3 * blocks : 4 * blocks]
    packed, bias = refs[4 * blocks :]
    unit = packed.shape[3]
    shape = (packed.shape[0],) + packed.shape[2:]
    parts = bias.shape[1] // unit
    turned = [ref[...].T for ref in rows]
    d_turned = [ref[...].T for ref in d_rows]
    for at in range(parts):
        columns = slice(at * unit, (at + 1) * unit)
        up = sum(nn(turned[b], d_hidden[b][:, columns]) for b in range(blocks))
        packed[:, at] = up.astype(BF16).reshape(shape)
        down = sum(nn(d_turned[b], active[b][:, columns]) for b in range(blocks))
        packed[:, parts + at] = down.astype(BF16).reshape(shape)
        bias[:, columns] = sum(over_tokens(d_hidden[b][:, columns].astype(F32)) for b in range(blocks))


def middle_kernel(place, gathered, vectors, upstream, scale, attended, middle, d_own, *refs, chunks, others):
    arrived, refs = refs[:others], refs[others:]
    d_mixed, (d_middle, d_attended, sums, weight) = refs[:-4], refs[-4:]
    spot = place[1]
    unit = gathered.shape[3]
    width = middle.shape[1]
    for at in range(width // unit):
        weight[:, at * unit : (at + 1) * unit] = gathered[:, chunks + at].reshape(width, unit)
    d_normed = d_own[...]
    for ref in arrived:
        d_normed = d_normed + ref[...].astype(F32)
    xhat, root = standardize(middle[...])
    d_result = upstream[...].astype(F32) * scale[...]
    d_after = d_result + pull_norm(d_normed, vectors[GAINS_TWO : GAINS_TWO + 1], xhat, root)
    d_middle[...] = d_after
    low = (vectors[GATE_ONE : GATE_ONE + 1] * d_after).astype(BF16)
    d_attended[...] = low
    for e in range(len(d_mixed)):
        first = pl.multiple_of(((spot ^ e) % GROUPS) * WIDTH, WIDTH)
        d_mixed[e][...] = nt(low, weight[pl.ds(first, WIDTH), :]).astype(BF16)
    sums[0:1, :] = over_tokens(d_after * attended[...])
    sums[1:2, :] = over_tokens(d_normed)
    sums[2:3, :] = over_tokens(d_normed * xhat)
    sums[3:8, :] = jnp.zeros((5, width), F32)


def project_grads_kernel(place, d_attended, *refs, chunks):
    side = len(refs) - 5
    mixed, (_, packed, whole, ready, done) = refs[:side], refs[side:]
    spot = place[1]
    unit = packed.shape[3]
    width = d_attended.shape[1]
    if side > GROUPS:
        whole[...] = jnp.zeros_like(whole)
    for e in range(side):
        other = spot ^ e
        first = pl.multiple_of((other % GROUPS) * WIDTH, WIDTH)
        grad = nn(mixed[e][...].T, d_attended[...]).astype(BF16)
        if side > GROUPS:
            grad = whole[pl.ds(first, WIDTH), :] + jnp.where(other < GROUPS, grad, jnp.zeros_like(grad))
        whole[pl.ds(first, WIDTH), :] = grad
    copies = []
    for at in range(width // unit):
        ready[at] = whole[:, at * unit : (at + 1) * unit].reshape(ready.shape[1:])
        copies.append(pltpu.make_async_copy(ready.at[at], packed.at[:, chunks + at], done.at[at]))
        copies[-1].start()
    for copy in copies:
        copy.wait()


def output_kernel(vectors, upstream, scale, middle, own, *refs, others):
    arrived, (result, sums) = refs[:others], refs[others:]
    output = own[...] + vectors[BIAS_DOWN : BIAS_DOWN + 1]
    for ref in arrived:
        output = output + ref[...].astype(F32)
    gate = vectors[GATE_TWO : GATE_TWO + 1]
    result[...] = (middle[...] + gate * output).astype(BF16)
    d_result = upstream[...].astype(F32) * scale[...]
    sums[0:1, :] = over_tokens(d_result * output)
    sums[1:2, :] = over_tokens(gate * d_result)
    sums[2:8, :] = jnp.zeros((6, middle.shape[1]), F32)


def tokens_kernel(vectors, tokens, d_middle, own, arrived, d_tokens):
    xhat, root = standardize(tokens[...].astype(F32))
    d_normed = own[...].astype(F32) + arrived[...].astype(F32)
    back = pull_norm(d_normed, vectors[GAINS_ONE : GAINS_ONE + 1], xhat, root)
    d_tokens[...] = (d_middle[...] + back).astype(BF16)


def forward_kernel(place, *refs, blocks):
    tokens, refs = refs[:blocks], refs[blocks:]
    weights, refs = refs[:PLANES], refs[PLANES:]
    (vectors, cosine, sines), refs = refs[:3], refs[3:]
    gain, shift = vectors[GAINS_ONE : GAINS_ONE + 1], vectors[SHIFT_ONE : SHIFT_ONE + 1]
    mixed, refs = refs[:blocks], refs[blocks:]
    heads, log_total, normed, weight, keys, mixed_turned = refs
    plane = place[0]
    rows = weights[0].shape[0]
    count = tokens[0].shape[0]
    for distance in range(PLANES):
        first = pl.multiple_of((plane ^ distance) * rows, 16)
        weight[pl.ds(first, rows), :] = weights[distance][...]
    for block in range(blocks):
        xhat, _ = standardize(tokens[block][...].astype(F32))
        normed[block * count : (block + 1) * count, :] = (xhat * gain + shift).astype(BF16)
    project = nt(weight[...].T, normed[...])
    cos, sin = cosine[...], sines[...]
    half = HEAD // 2
    for part in range(2):
        for head in range(PER_GROUP):
            start = part * WIDTH + head * HEAD
            first, second = project[start : start + half], project[start + half : start + HEAD]
            turned = jnp.concatenate([first * cos - second * sin, second * cos + first * sin], 0).astype(BF16)
            if part == 0:
                turned = turned * jnp.asarray(SCALING, BF16)
            else:
                keys[head] = turned.T
            heads[start : start + HEAD, :] = turned
    heads[2 * WIDTH :, :] = project[2 * WIDTH :].astype(BF16)
    length = heads.shape[1]
    for head in range(PER_GROUP):
        start = head * HEAD

        def queries_step(step, carry):
            columns = pl.ds(pl.multiple_of(step * QUERY_BLOCK, QUERY_BLOCK), QUERY_BLOCK)
            scores = nn(keys[head], heads[start : start + HEAD, columns])
            peak = jnp.max(scores, 0, keepdims=True)
            exps = jnp.exp(scores - peak)
            total = jnp.sum(exps, 0, keepdims=True)
            log_total[head : head + 1, columns] = peak + jnp.log(total)
            probs = (exps * (1.0 / total)).astype(BF16)
            values = heads[2 * WIDTH + start : 2 * WIDTH + start + HEAD, :]
            mixed_turned[start : start + HEAD, columns] = nn(values, probs).astype(BF16)
            return carry

        lax.fori_loop(0, length // QUERY_BLOCK, queries_step, 0)
    for block in range(blocks):
        mixed[block][...] = mixed_turned[:, block * count : (block + 1) * count].T


def backward_kernel(place, *refs, blocks):
    tokens, refs = refs[:blocks], refs[blocks:]
    d_mixed, refs = refs[:blocks], refs[blocks:]
    (heads, log_total, normed, weight, cosine, sines), refs = refs[:6], refs[6:]
    d_normed, refs = refs[:blocks], refs[blocks:]
    d_weight, refs = refs[:PLANES], refs[PLANES:]
    sums, d_turned, d_keys, d_values, d_project, d_whole, keys, values = refs
    plane = place[0]
    count = tokens[0].shape[0]
    length = heads.shape[1]
    for block in range(blocks):
        d_turned[:, block * count : (block + 1) * count] = d_mixed[block][...].T
    cos, sin = cosine[...], sines[...]
    half = HEAD // 2
    d_keys[...] = jnp.zeros_like(d_keys)
    d_values[...] = jnp.zeros_like(d_values)
    for head in range(PER_GROUP):
        start = head * HEAD
        keys_turned = heads.at[WIDTH + start : WIDTH + start + HEAD]
        keys[...] = keys_turned[...].T
        values[...] = heads[2 * WIDTH + start : 2 * WIDTH + start + HEAD, :].T

        def queries_step(step, carry):
            columns = pl.ds(pl.multiple_of(step * QUERY_BLOCK, QUERY_BLOCK), QUERY_BLOCK)
            queries = heads[start : start + HEAD, columns]
            incoming = d_turned[start : start + HEAD, columns]
            scores = nn(keys[...], queries)
            probs = jnp.exp(scores - log_total[head : head + 1, columns])
            d_probs = nn(values[...], incoming)
            delta = jnp.sum(probs * d_probs, 0, keepdims=True)
            d_scores = (probs * (d_probs - delta)).astype(BF16)
            d_values[start : start + HEAD, :] += nt(incoming, probs.astype(BF16))
            d_keys[start : start + HEAD, :] += nt(queries, d_scores)
            d_queries = nn(keys_turned[...], d_scores) * SCALING
            first, second = d_queries[:half], d_queries[half:]
            cos_here, sin_here = cosine[:, columns], sines[:, columns]
            d_project[start : start + half, columns] = (first * cos_here + second * sin_here).astype(BF16)
            d_project[start + half : start + HEAD, columns] = (second * cos_here - first * sin_here).astype(BF16)
            return carry

        lax.fori_loop(0, length // QUERY_BLOCK, queries_step, 0)
        first, second = d_keys[start : start + half, :], d_keys[start + half : start + HEAD, :]
        d_project[WIDTH + start : WIDTH + start + half, :] = (first * cos + second * sin).astype(BF16)
        d_project[WIDTH + start + half : WIDTH + start + HEAD, :] = (second * cos - first * sin).astype(BF16)
    d_project[2 * WIDTH :, :] = d_values[...].astype(BF16)
    d_shift = jnp.zeros((1, normed.shape[1]), F32)
    d_xhat = jnp.zeros((1, normed.shape[1]), F32)
    for block in range(blocks):
        part = nt(d_project[:, block * count : (block + 1) * count].T, weight[...])
        d_normed[block][...] = part.astype(BF16)
        xhat, _ = standardize(tokens[block][...].astype(F32))
        d_shift = d_shift + jnp.sum(part, 0, keepdims=True)
        d_xhat = d_xhat + jnp.sum(part * xhat, 0, keepdims=True)
    sums[0:1, :] = d_shift
    sums[1:2, :] = d_xhat
    sums[2:8, :] = jnp.zeros((6, normed.shape[1]), F32)
    d_whole[...] = nn(d_project[...], normed[...]).astype(BF16).T
    rows = d_weight[0].shape[0]
    for distance in range(PLANES):
        first = pl.multiple_of((plane ^ distance) * rows, 16)
        d_weight[distance][...] = d_whole[pl.ds(first, rows), :]


def attend_forward(place, tokens, weights, vectors, cosine, sines):
    blocks, (count, width) = len(tokens), tokens[0].shape
    length = blocks * count
    columns = weights[0].shape[1]
    outs = call(
        functools.partial(forward_kernel, blocks=blocks),
        "attend_forward",
        [*tokens, *weights, vectors, cosine, sines],
        [place],
        [shape_of((count, WIDTH), BF16)] * blocks
        + [
            shape_of((columns, length), BF16),
            shape_of((8, length), F32),
            shape_of((length, width), BF16),
            shape_of((width, columns), BF16),
        ],
        [pltpu.VMEM((PER_GROUP, length, HEAD), BF16), pltpu.VMEM((WIDTH, length), BF16)],
        flops=2 * length * width * columns + 8 * length * length * WIDTH,
    )
    return outs[:blocks], outs[blocks:]


def attend_backward(place, tokens, d_mixed, kept, cosine, sines):
    blocks, (count, width) = len(tokens), tokens[0].shape
    length = blocks * count
    columns = 3 * WIDTH
    rows = width // PLANES
    outs = call(
        functools.partial(backward_kernel, blocks=blocks),
        "attend_backward",
        [*tokens, *d_mixed, *kept, cosine, sines],
        [place],
        [shape_of((count, width), BF16)] * blocks
        + [shape_of((rows, columns), BF16)] * PLANES
        + [shape_of((8, width), F32)],
        [
            pltpu.VMEM((WIDTH, length), BF16),
            pltpu.VMEM((WIDTH, length), F32),
            pltpu.VMEM((WIDTH, length), F32),
            pltpu.VMEM((columns, length), BF16),
            pltpu.VMEM((width, columns), BF16),
            pltpu.VMEM((length, HEAD), BF16),
            pltpu.VMEM((length, HEAD), BF16),
        ],
        flops=4 * length * width * columns + 10 * length * length * WIDTH,
    )
    return outs[:blocks], outs[blocks : blocks + PLANES], outs[-1]


def pick(stack, index):
    return lax.dynamic_index_in_dim(stack, index, 0, keepdims=False)


def bits_of(count):
    return [1 << bit for bit in range(count.bit_length() - 1)]


def body(
    tokens,
    upstream,
    token_mask,
    time_index,
    weight_index,
    time_table,
    weight_grid,
    w_ada,
    b_ada,
    gain_one,
    gain_two,
    w_qkv,
    w_proj,
    w_up,
    b_up,
    w_down,
    b_down,
    *,
    n,
    m,
):
    side = n // PLANES
    me = lax.axis_index("seq")
    plane, spot = me // side, me % side
    place = jnp.stack([plane, spot]).astype(jnp.int32)
    shard, width = tokens.shape[2], tokens.shape[3]
    rows = w_qkv.shape[0]
    hidden_count = w_up.shape[1]
    grid_size = time_table.shape[0]
    ada_columns = w_ada.shape[1]
    count = PLANES * shard
    unit = min(width, hidden_count)
    hidden_chunks, width_chunks = hidden_count // unit, width // unit
    chunks = 2 * hidden_chunks

    def swap(value, distance):
        return lax.ppermute(value, "seq", [(i, i ^ distance) for i in range(n)])

    def swap_mlp(value, distance):
        return lax.ppermute(value, "mlp", [(i, i ^ distance) for i in range(m)])

    def between_planes(pieces):
        return [pieces[0]] + [swap(pieces[d], d * side) for d in range(1, PLANES)]

    def in_plane(pieces):
        return [pieces[0]] + [swap(pieces[e], e) for e in range(1, side)]

    def in_order(blocks, axis):
        halves = jnp.stack(blocks)
        for bit in bits_of(len(blocks)):
            here = halves.reshape((len(blocks) // (2 * bit), 2, bit) + halves.shape[1:])
            halves = jnp.where((axis & bit) != 0, here[:, ::-1], here).reshape(halves.shape)
        return halves

    def for_plane(values):
        return [pick(values, jnp.minimum(plane ^ d, MICRO - 1)) for d in range(PLANES)]

    def columns_of(value):
        return [value[:, at : at + unit] for at in range(0, value.shape[1], unit)]

    pieces = for_plane(tokens[:, 0])
    pieces, w_up, w_down, w_proj = lax.optimization_barrier((pieces, w_up, w_down, w_proj))
    own_low = jnp.concatenate(between_planes(pieces), 0)
    token_blocks = {0: own_low}
    for bit in reversed(bits_of(side)):
        for known in list(token_blocks):
            token_blocks[known | bit] = swap(token_blocks[known], bit)
    token_blocks = [token_blocks[at] for at in range(side)]

    packed = jnp.stack(columns_of(w_up) + columns_of(w_down.T) + columns_of(w_proj))
    gathered = lax.all_gather(packed, "seq", axis=0)
    if rows % 16:
        gathered = gathered.transpose(1, 0, 2, 3).reshape(1, -1, width, unit)
    full_ada = lax.all_gather(w_ada, "seq", axis=0)

    by_group = w_qkv.reshape(rows, 3, GROUPS, WIDTH).transpose(2, 0, 1, 3).reshape(GROUPS, rows, 3 * WIDTH)
    received = in_plane([pick(by_group, (spot ^ e) % GROUPS) for e in range(side)])
    received = jnp.stack(received)
    weight_blocks = {0: jnp.concatenate([pick(received, spot ^ at) for at in range(side)], 0)}
    for bit in (2, 1):
        for known in list(weight_blocks):
            weight_blocks[known | bit] = swap(weight_blocks[known], bit * side)
    weight_blocks = [weight_blocks[at] for at in range(PLANES)]

    line = [value[None] for value in (b_ada, gain_one, gain_two, b_down)]
    (small,) = call(
        modulation_kernel,
        "modulation",
        [time_table, w_ada, *line, token_mask[:, 0]],
        [time_index],
        [shape_of((8, SMALL), F32)],
    )
    small = small[None]
    for bit in bits_of(n):
        small = jnp.concatenate([small, swap(small, bit)], 0)
    vectors, scale = call(
        vectors_kernel,
        "vectors",
        [small],
        [place, weight_index, weight_grid],
        [shape_of((16, width), F32), shape_of((count, 1), F32)],
        [pltpu.VMEM((8, count), F32)],
    )

    order = ((plane ^ jnp.arange(PLANES))[None, :] * side + (spot ^ jnp.arange(side))[:, None]) * shard
    positions = (order[:, :, None] + jnp.arange(shard)).reshape(1, -1).astype(F32)
    frequency = 10000.0 ** (-jnp.arange(0, HEAD, 2).astype(F32) / HEAD)
    angles = frequency[:, None] * positions
    cosine, sines = jnp.cos(angles), jnp.sin(angles)

    mixed_blocks, kept = attend_forward(place, token_blocks, weight_blocks, vectors, cosine, sines)

    mixed_blocks = in_plane(mixed_blocks)

    own_upstream = jnp.concatenate(between_planes(for_plane(upstream[:, 0])), 0)
    d_rows = ((own_upstream.astype(F32) * scale) * vectors[GATE_TWO][None]).astype(BF16)
    d_rows = [d_rows] + [swap_mlp(d_rows, d) for d in range(1, m)]

    attended, middle, normed_two = call(
        functools.partial(project_kernel, chunks=chunks),
        "project",
        [gathered, own_low, vectors, *mixed_blocks],
        [place],
        [shape_of((count, width), F32), shape_of((count, width), F32), shape_of((count, width), BF16)],
        [pltpu.VMEM((width, width), BF16)],
        flops=2 * count * width * width,
    )
    rows_all = [normed_two] + [swap_mlp(normed_two, d) for d in range(1, m)]
    bias_up = b_up.astype(F32)[None]
    fed = [
        call(
            feed_kernel,
            "feed_forward",
            [gathered, rows_all[d], d_rows[d], bias_up],
            [],
            [shape_of((count, width), BF16 if d else F32)] * 2 + [shape_of((count, hidden_count), BF16)] * 2,
            flops=8 * count * width * hidden_count,
        )
        for d in range(m)
    ]
    d_arrived = [swap_mlp(fed[d][1], d) for d in range(1, m)]
    out_arrived = [swap_mlp(fed[d][0], d) for d in range(1, m)]
    total_chunks = chunks + width_chunks
    packed_shape = (1, total_chunks, width, unit) if rows % 16 else (n, total_chunks, rows, unit)
    grads, bias_up_sum = call(
        functools.partial(feed_grads_kernel, blocks=m),
        "feed_gradients",
        [*rows_all, *d_rows, *[f[2] for f in fed], *[f[3] for f in fed]],
        [],
        [shape_of(packed_shape, BF16), shape_of((1, hidden_count), F32)],
        flops=4 * m * count * width * hidden_count,
    )
    middle_outs = call(
        functools.partial(middle_kernel, chunks=chunks, others=m - 1),
        "middle_backward",
        [gathered, vectors, own_upstream, scale, attended, middle, fed[0][1], *d_arrived],
        [place],
        [shape_of((count, WIDTH), BF16)] * side
        + [shape_of((count, width), F32), shape_of((count, width), BF16), shape_of((8, width), F32)],
        [pltpu.VMEM((width, width), BF16)],
        flops=2 * count * width * width,
    )
    d_mixed_blocks, (d_middle, d_attended, middle_sums) = middle_outs[:side], middle_outs[side:]

    d_mixed_blocks = in_plane(d_mixed_blocks)
    if side > GROUPS:
        share = (spot < GROUPS).astype(BF16)
        d_mixed_blocks = [block * share for block in d_mixed_blocks]

    (grads,) = pl.pallas_call(
        functools.partial(project_grads_kernel, chunks=chunks),
        out_shape=[shape_of(packed_shape, BF16)],
        in_specs=[SMEM] + [VMEM] * (1 + side) + [pl.BlockSpec(memory_space=pl.ANY)],
        out_specs=[pl.BlockSpec(memory_space=pl.ANY)],
        scratch_shapes=[
            pltpu.VMEM((width, width), BF16),
            pltpu.VMEM((width_chunks, packed_shape[0]) + packed_shape[2:], BF16),
            pltpu.SemaphoreType.DMA((width_chunks,)),
        ],
        input_output_aliases={2 + side: 0},
        compiler_params=pltpu.CompilerParams(vmem_limit_bytes=56 * 1024 * 1024),
        cost_estimate=pl.CostEstimate(
            flops=2 * count * width * width, bytes_accessed=4 * count * width, transcendentals=0
        ),
        name="project_gradients",
    )(place, d_attended, *mixed_blocks, grads)
    if rows % 16:
        grads = grads.reshape(total_chunks, n, rows, unit).transpose(1, 0, 2, 3)
    grads = lax.psum_scatter(grads, "seq", scatter_dimension=0, tiled=True)[0]

    def columns_from(first, number):
        return jnp.concatenate([grads[first + at] for at in range(number)], -1).astype(F32)

    grad_up = columns_from(0, hidden_chunks)
    grad_down = columns_from(hidden_chunks, hidden_chunks).T
    grad_proj = columns_from(chunks, width_chunks)
    for bit in bits_of(m):
        grad_proj = grad_proj + swap_mlp(grad_proj.astype(BF16), bit).astype(F32)

    result, output_sums = call(
        functools.partial(output_kernel, others=m - 1),
        "output",
        [vectors, own_upstream, scale, middle, fed[0][0], *out_arrived],
        [],
        [shape_of((count, width), BF16), shape_of((8, width), F32)],
    )

    d_normed_blocks, d_weight_blocks, sums = attend_backward(
        place, token_blocks, d_mixed_blocks, kept, cosine, sines
    )

    blocks = dict(enumerate(d_normed_blocks))
    for bit in bits_of(side):
        for at in [at for at in blocks if at & bit]:
            arrived = swap(blocks.pop(at), bit)
            if len(blocks) > 1:
                blocks[at ^ bit] = (blocks[at ^ bit].astype(F32) + arrived.astype(F32)).astype(BF16)
    (d_tokens,) = call(
        tokens_kernel,
        "tokens_backward",
        [vectors, own_low, d_middle, blocks[0], arrived],
        [],
        [shape_of((count, width), BF16)],
    )

    def back_to_tokens(value):
        received = between_planes([value[d * shard : (d + 1) * shard] for d in range(PLANES)])
        received = jnp.stack(received)
        return jnp.stack([pick(received, plane ^ at) for at in range(MICRO)])[:, None]

    total = sum(piece.astype(F32) for piece in between_planes(d_weight_blocks))
    by_spot = total.astype(BF16).reshape(side, rows, 3 * WIDTH)
    received = jnp.stack(in_plane([pick(by_spot, spot ^ e) for e in range(side)]))
    grad_qkv = jnp.stack([pick(received, spot ^ group) for group in range(GROUPS)])
    grad_qkv = grad_qkv.reshape(GROUPS, rows, 3, WIDTH).transpose(1, 2, 0, 3).reshape(rows, 3 * width)
    grad_qkv = grad_qkv.astype(F32)
    for bit in bits_of(m):
        grad_qkv = grad_qkv + swap_mlp(grad_qkv.astype(BF16), bit).astype(F32)

    bias_up_rows = -(-hidden_count // width)
    bias_up_sum = jnp.pad(bias_up_sum, ((0, 0), (0, bias_up_rows * width - hidden_count)))
    small = jnp.concatenate(
        [sums[0:2], middle_sums[0:3], output_sums[0:2], bias_up_sum.reshape(-1, width)], 0
    )
    for bit in bits_of(side):
        small = small + swap(small, bit)
    small = jnp.concatenate([small, vectors[SCALE_TWO][None]], 0)[None]
    for bit in bits_of(PLANES):
        small = jnp.concatenate([small, swap(small, bit * side)], 0)
    small = in_order(list(small), plane)[:MICRO]
    grad_bias_up = jnp.sum(small[:, 7 : 7 + bias_up_rows], 0).reshape(-1)[:hidden_count]
    d_shift_one, d_xhat_one, d_gate_one, d_shift_two, d_xhat_two, d_gate_two = [small[:, at] for at in range(6)]
    index_here = time_index[:, 0]
    vector_sums = jnp.stack(
        [
            jnp.sum((1.0 + vectors[SCALES_ALL : SCALES_ALL + MICRO]) * d_xhat_one, 0),
            jnp.sum((1.0 + small[:, -1]) * d_xhat_two, 0),
            jnp.sum(small[:, 6], 0),
            jnp.pad(index_here.astype(F32), (0, width - MICRO)),
        ]
    )
    d_scale_one, d_scale_two = vectors[GAIN_ONE] * d_xhat_one, vectors[GAIN_TWO] * d_xhat_two
    small = jnp.stack([d_shift_one, d_scale_one, d_gate_one, d_shift_two, d_scale_two, d_gate_two], 1)
    small = jnp.concatenate([small.reshape(6 * MICRO, width), vector_sums], 0)[None]
    for bit in bits_of(m):
        small = jnp.concatenate([small, swap_mlp(small, bit)], 0)
    at = 6 * MICRO
    d_modulation = small[:, :at].reshape(m * MICRO, n, ada_columns)
    vector_sums = jnp.sum(small[:, at : at + 3], 0)
    index_all = small[:, at + 3, :MICRO].reshape(-1).astype(jnp.int32)
    onehot = (index_all[:, None] == jnp.arange(grid_size)[None, :]).astype(BF16)
    cond = jnp.dot(onehot, time_table, preferred_element_type=F32)
    d_modulation_own = lax.dynamic_index_in_dim(d_modulation, me, 1, keepdims=False)
    grad_ada = jnp.dot(cond.T, d_modulation_own, precision=highest)
    grad_bias_ada = jnp.sum(d_modulation_own, 0)
    d_cond = jnp.einsum("bic,idc->bd", d_modulation, full_ada.astype(F32), precision=highest)
    table_rows = grid_size // n
    onehot_own = index_all[None, :] == (me * table_rows + jnp.arange(table_rows))[:, None]
    grad_table = jnp.dot(onehot_own.astype(F32), d_cond, precision=highest)
    vector_sums = lax.dynamic_slice_in_dim(vector_sums, me * rows, rows, 1)
    return (
        back_to_tokens(result),
        back_to_tokens(d_tokens).astype(F32),
        grad_table,
        grad_ada,
        grad_bias_ada,
        vector_sums[0],
        vector_sums[1],
        grad_qkv,
        grad_proj,
        grad_up,
        grad_bias_up,
        grad_down,
        vector_sums[2],
    )


def solution(mesh):
    in_specs = (
        P(None, "mlp", "seq", None),
        P(None, "mlp", "seq", None),
        P(None, "mlp", "seq"),
        P(None, "mlp"),
        P(None, "mlp"),
        P(),
        P(),
        P(None, "seq"),
        P("seq"),
        P("seq"),
        P("seq"),
        P("seq", None),
        P("seq", None),
        P("seq", "mlp"),
        P("mlp"),
        P("mlp", "seq"),
        P("seq"),
    )
    out_specs = (
        P(None, "mlp", "seq", None),
        P(None, "mlp", "seq", None),
        P("seq", None),
        P(None, "seq"),
        P("seq"),
        P("seq"),
        P("seq"),
        P("seq", None),
        P("seq", None),
        P("seq", "mlp"),
        P("mlp"),
        P("mlp", "seq"),
        P("seq"),
    )
    run = functools.partial(body, n=mesh.shape["seq"], m=mesh.shape["mlp"])
    return jax.shard_map(run, mesh=mesh, in_specs=in_specs, out_specs=out_specs, check_vma=False)
```

```python
import functools
import math

import jax
import jax.numpy as jnp
from jax import lax
from jax.experimental import pallas as pl
from jax.experimental.pallas import tpu as pltpu
from jax.sharding import PartitionSpec as P

HEADS = 12
HEAD = 64
MICRO = 3
PLANES = 4
GROUPS = 4
PER_GROUP = HEADS // GROUPS
WIDTH = PER_GROUP * HEAD
QUERY_BLOCK = 256
SCALING = HEAD ** (-0.5)
BF16 = jnp.bfloat16
F32 = jnp.float32
highest = lax.Precision.HIGHEST
SLOPE = math.sqrt(2.0 / math.pi)
CUBIC = 0.044715
SMALL = 384

SHIFT_ONE, SCALE_ONE, GATE_ONE, SHIFT_TWO, SCALE_TWO, GATE_TWO, GAIN_ONE, GAIN_TWO, BIAS_DOWN = range(9)
SCALES_ALL, GAINS_ONE, GAINS_TWO = 9, 12, 13

VMEM = pl.BlockSpec(memory_space=pltpu.VMEM)
SMEM = pl.BlockSpec(memory_space=pltpu.SMEM)


def nn(left, right):
    return lax.dot_general(left, right, (((1,), (0,)), ((), ())), preferred_element_type=F32)


def nt(left, right):
    return lax.dot_general(left, right, (((1,), (1,)), ((), ())), preferred_element_type=F32)


def standardize(inputs):
    average = jnp.mean(inputs, -1, keepdims=True)
    centred = inputs - average
    spread = jnp.mean(centred * centred, -1, keepdims=True)
    root = lax.rsqrt(spread + 1e-06)
    return centred * root, root


def pull_norm(d_normed, gains, xhat, root):
    e = d_normed * gains
    return root * (e - jnp.mean(e, -1, keepdims=True) - xhat * jnp.mean(e * xhat, -1, keepdims=True))


def over_tokens(value):
    return jnp.sum(value, 0, keepdims=True)


def shape_of(dims, dtype):
    return jax.ShapeDtypeStruct(dims, dtype)


def call(kernel, name, operands, scalars, outs, scratch=(), us=1.0):
    moved = sum(math.prod(o.shape) * o.dtype.itemsize for o in list(operands) + list(outs))
    return pl.pallas_call(
        kernel,
        out_shape=list(outs),
        in_specs=[SMEM] * len(scalars) + [VMEM] * len(operands),
        out_specs=[VMEM] * len(outs),
        scratch_shapes=list(scratch),
        compiler_params=pltpu.CompilerParams(vmem_limit_bytes=56 * 1024 * 1024),
        cost_estimate=pl.CostEstimate(flops=int(us * 1e9), bytes_accessed=moved, transcendentals=0),
        name=name,
    )(*scalars, *operands)


def modulation_kernel(times, table, w_ada, b_ada, gain_one, gain_two, b_down, mask, small):
    columns = w_ada.shape[1]
    rows = gain_one.shape[1]
    at = lax.broadcasted_iota(jnp.int32, (8, table.shape[0]), 1)
    line = lax.broadcasted_iota(jnp.int32, (8, table.shape[0]), 0)
    wanted = jnp.where(line == 0, times[0, 0], jnp.where(line == 1, times[1, 0], times[2, 0]))
    cond = nn((at == wanted).astype(F32).astype(BF16), table[...]).astype(BF16)
    part = nn(cond, w_ada[...]) + b_ada[...].astype(F32)
    small[...] = jnp.zeros_like(small)
    small[0:MICRO, 0:columns] = part[0:MICRO]
    small[3:4, 0:rows] = gain_one[...].astype(F32)
    small[3:4, 128 : 128 + rows] = gain_two[...].astype(F32)
    small[3:4, 256 : 256 + rows] = b_down[...].astype(F32)
    small[4 : 4 + MICRO, 0 : mask.shape[1]] = mask[...].astype(F32)


def vectors_kernel(place, weight_index, weight_grid, small, vectors, scale, line):
    n = small.shape[0]
    width = vectors.shape[1]
    columns, rows, shard = 6 * width // n, width // n, scale.shape[0] // PLANES
    plane, spot = place[0], place[1]
    side = n // PLANES
    me = plane * side + spot
    last = jnp.minimum(plane, MICRO - 1)

    def one_of(three):
        return jnp.where(last == 0, three[0:1], jnp.where(last == 1, three[1:2], three[2:3]))

    def pieces(first, size):
        start = first
        while start < first + size:
            stop = min(first + size, (start // width + 1) * width)
            yield start // width, start % width, start - first, stop - start
            start = stop

    vectors[...] = jnp.zeros_like(vectors)
    for i in range(n):
        here = small.at[me ^ i]
        mine = one_of(here[0:MICRO, 0:columns])
        for part, column, offset, size in pieces(i * columns, columns):
            vectors[part : part + 1, column : column + size] = mine[:, offset : offset + size]
            if part == SCALE_ONE:
                vectors[SCALES_ALL : SCALES_ALL + MICRO, column : column + size] = here[
                    0:MICRO, offset : offset + size
                ]
        for row, offset in ((GAIN_ONE, 0), (GAIN_TWO, 128), (BIAS_DOWN, 256)):
            vectors[row : row + 1, i * rows : (i + 1) * rows] = here[3:4, offset : offset + rows]
    for to, gain, by in ((GAINS_ONE, GAIN_ONE, SCALE_ONE), (GAINS_TWO, GAIN_TWO, SCALE_TWO)):
        vectors[to : to + 1, :] = vectors[gain : gain + 1, :] * (1.0 + vectors[by : by + 1, :])
    line[...] = jnp.zeros_like(line)
    for d in range(PLANES):
        line[0:1, d * shard : (d + 1) * shard] = one_of(small[d * side, 4 : 4 + MICRO, 0:shard])
    weight = jnp.where(plane < MICRO, weight_grid[weight_index[last, 0]], 0.0)
    scale[...] = line[...].T[:, 0:1] * weight


def project_kernel(place, weight, tokens, vectors, *refs):
    side = len(refs) - 3
    mixed, (attended, middle, normed) = refs[:side], refs[side:]
    spot = place[1]
    total = jnp.zeros(attended.shape, F32)
    for e in range(side):
        other = spot ^ e
        block = mixed[e][...]
        if side > GROUPS:
            block = jnp.where(other < GROUPS, block, jnp.zeros_like(block))
        first = pl.multiple_of((other % GROUPS) * WIDTH, WIDTH)
        total = total + nn(block, weight[pl.ds(first, WIDTH), :])
    attended[...] = total
    after = tokens[...].astype(F32) + vectors[GATE_ONE : GATE_ONE + 1] * total
    middle[...] = after
    xhat, _ = standardize(after)
    normed[...] = (xhat * vectors[GAINS_TWO : GAINS_TWO + 1] + vectors[SHIFT_TWO : SHIFT_TWO + 1]).astype(BF16)


def feed_kernel(up, down, rows, d_rows, bias, output, d_normed, active, d_hidden):
    unit = min(bias.shape[1], rows.shape[1])
    out = jnp.zeros(output.shape, F32)
    back = jnp.zeros(output.shape, F32)
    for at in range(0, bias.shape[1], unit):
        columns = slice(at, at + unit)
        u = nn(rows[...], up[:, columns]) + bias[:, columns]
        square = u * u
        bent = jnp.tanh(SLOPE * u * (1.0 + CUBIC * square))
        half = 0.5 * (1.0 + bent)
        on = (u * half).astype(BF16)
        active[:, columns] = on
        slope = half + 0.5 * u * (1.0 - bent * bent) * (SLOPE * (1.0 + 3.0 * CUBIC * square))
        d_on = (nn(d_rows[...], down[:, columns]) * slope).astype(BF16)
        d_hidden[:, columns] = d_on
        out = out + nt(on, down[:, columns])
        back = back + nt(d_on, up[:, columns])
    output[...] = out.astype(output.dtype)
    d_normed[...] = back.astype(d_normed.dtype)


def scatter_store(refs, me, device, value):
    kept, sent, chunk, slot_of = refs
    distance = me ^ device
    slot = slot_of(distance)

    @pl.when(distance % 2 == 0)
    def _():
        kept[slot, chunk] = value

    @pl.when(distance % 2 == 1)
    def _():
        sent[slot, chunk] = value


def slot_z_first(distance):
    return ((distance >> 2) & 1) * 4 + ((distance >> 3) & 1) * 2 + ((distance >> 1) & 1)


def slot_y_first(distance):
    return ((distance >> 1) & 1) * 4 + ((distance >> 2) & 1) * 2 + ((distance >> 3) & 1)


def down_grads_kernel(place, *refs, blocks, scatter):
    d_rows, active = refs[:blocks], refs[blocks : 2 * blocks]
    outs = refs[2 * blocks :]
    me = place[2]
    width, count = d_rows[0].shape[1], active[0].shape[1]
    unit = min(width, count)
    turned = [ref[...].T for ref in d_rows]
    for chunk in range(count // unit):
        columns = slice(chunk * unit, (chunk + 1) * unit)
        grad = sum(nn(turned[b], active[b][:, columns]) for b in range(blocks)).astype(BF16)
        if scatter:
            rows = outs[0].shape[2]
            for i in range(width // rows):
                part = grad[i * rows : (i + 1) * rows]
                scatter_store((outs[0], outs[1], chunk, slot_z_first), me, i, part)
        else:
            outs[0][:, columns] = grad


def up_grads_kernel(place, d_attended, *refs, blocks, side, scatter):
    mixed, refs = refs[:side], refs[side:]
    rows_all, d_hidden = refs[:blocks], refs[blocks : 2 * blocks]
    outs, whole = refs[2 * blocks : -1], refs[-1]
    bias = outs[-1]
    spot, me = place[1], place[2]
    width, count = rows_all[0].shape[1], bias.shape[1]
    unit = min(width, count)
    turned = [ref[...].T for ref in rows_all]
    for chunk in range(count // unit):
        columns = slice(chunk * unit, (chunk + 1) * unit)
        grad = sum(nn(turned[b], d_hidden[b][:, columns]) for b in range(blocks)).astype(BF16)
        bias[:, columns] = sum(over_tokens(d_hidden[b][:, columns].astype(F32)) for b in range(blocks))
        if scatter:
            rows = outs[0].shape[2]
            for i in range(width // rows):
                part = grad[i * rows : (i + 1) * rows]
                scatter_store((outs[0], outs[1], chunk, slot_y_first), me, i, part)
        else:
            outs[0][:, columns] = grad
    if side > GROUPS:
        whole[...] = jnp.zeros_like(whole)
    for e in range(side):
        other = spot ^ e
        first = pl.multiple_of((other % GROUPS) * WIDTH, WIDTH)
        grad = nn(mixed[e][...].T, d_attended[...]).astype(BF16)
        if side > GROUPS:
            grad = whole[pl.ds(first, WIDTH), :] + jnp.where(other < GROUPS, grad, jnp.zeros_like(grad))
        whole[pl.ds(first, WIDTH), :] = grad
    if scatter:
        for i in range(width // rows):
            part = whole[i * rows : (i + 1) * rows, :]
            scatter_store((outs[0], outs[1], count // unit, slot_y_first), me, i, part)
    else:
        outs[1][...] = whole[...]


def add_split_kernel(own, arrived, kept, sent):
    half = own.shape[0] // 2
    kept[...] = (own[:half].astype(F32) + arrived[:half].astype(F32)).astype(BF16)
    sent[...] = (own[half:].astype(F32) + arrived[half:].astype(F32)).astype(BF16)


def add_last_kernel(own, arrived, *outs):
    for at, ref in enumerate(outs):
        ref[...] = own[0, at].astype(F32) + arrived[0, at].astype(F32)


def assemble_kernel(place, *refs, layout, outs):
    sources, targets = refs[: len(layout)], refs[len(layout) :]
    me = place[2]
    rows, unit = sources[0].shape[2:]
    for source, distances in zip(sources, layout):
        for slot, distance in enumerate(distances):
            first = pl.multiple_of((me ^ distance) * rows, 16)
            for chunk, (target, column) in enumerate(outs):
                targets[target][pl.ds(first, rows), column * unit : (column + 1) * unit] = source[slot, chunk]


def middle_kernel(place, weight, vectors, upstream, scale, attended, middle, d_own, *refs, others):
    arrived, refs = refs[:others], refs[others:]
    d_mixed, (d_middle, d_attended, sums) = refs[:-3], refs[-3:]
    spot = place[1]
    width = middle.shape[1]
    d_normed = d_own[...]
    for ref in arrived:
        d_normed = d_normed + ref[...].astype(F32)
    xhat, root = standardize(middle[...])
    d_result = upstream[...].astype(F32) * scale[...]
    d_after = d_result + pull_norm(d_normed, vectors[GAINS_TWO : GAINS_TWO + 1], xhat, root)
    d_middle[...] = d_after
    low = (vectors[GATE_ONE : GATE_ONE + 1] * d_after).astype(BF16)
    d_attended[...] = low
    for e in range(len(d_mixed)):
        first = pl.multiple_of(((spot ^ e) % GROUPS) * WIDTH, WIDTH)
        d_mixed[e][...] = nt(low, weight[pl.ds(first, WIDTH), :]).astype(BF16)
    sums[0:1, :] = over_tokens(d_after * attended[...])
    sums[1:2, :] = over_tokens(d_normed)
    sums[2:3, :] = over_tokens(d_normed * xhat)
    sums[3:8, :] = jnp.zeros((5, width), F32)


def output_kernel(vectors, upstream, scale, middle, own, *refs, others):
    arrived, (result, sums) = refs[:others], refs[others:]
    output = own[...] + vectors[BIAS_DOWN : BIAS_DOWN + 1]
    for ref in arrived:
        output = output + ref[...].astype(F32)
    gate = vectors[GATE_TWO : GATE_TWO + 1]
    result[...] = (middle[...] + gate * output).astype(BF16)
    d_result = upstream[...].astype(F32) * scale[...]
    sums[0:1, :] = over_tokens(d_result * output)
    sums[1:2, :] = over_tokens(gate * d_result)
    sums[2:8, :] = jnp.zeros((6, middle.shape[1]), F32)


def tokens_kernel(vectors, tokens, d_middle, own, arrived, d_tokens):
    xhat, root = standardize(tokens[...].astype(F32))
    d_normed = own[...].astype(F32) + arrived[...].astype(F32)
    back = pull_norm(d_normed, vectors[GAINS_ONE : GAINS_ONE + 1], xhat, root)
    d_tokens[...] = (d_middle[...] + back).astype(BF16)


def forward_kernel(place, *refs, blocks):
    tokens, refs = refs[:blocks], refs[blocks:]
    weights, refs = refs[:PLANES], refs[PLANES:]
    (vectors, cosine, sines), refs = refs[:3], refs[3:]
    gain, shift = vectors[GAINS_ONE : GAINS_ONE + 1], vectors[SHIFT_ONE : SHIFT_ONE + 1]
    mixed, refs = refs[:blocks], refs[blocks:]
    heads, log_total, normed, weight, keys, mixed_turned = refs
    plane = place[0]
    rows = weights[0].shape[0]
    count = tokens[0].shape[0]
    for distance in range(PLANES):
        first = pl.multiple_of((plane ^ distance) * rows, 16)
        weight[pl.ds(first, rows), :] = weights[distance][...]
    for block in range(blocks):
        xhat, _ = standardize(tokens[block][...].astype(F32))
        normed[block * count : (block + 1) * count, :] = (xhat * gain + shift).astype(BF16)
    project = nt(weight[...].T, normed[...])
    cos, sin = cosine[...], sines[...]
    half = HEAD // 2
    for part in range(2):
        for head in range(PER_GROUP):
            start = part * WIDTH + head * HEAD
            first, second = project[start : start + half], project[start + half : start + HEAD]
            turned = jnp.concatenate([first * cos - second * sin, second * cos + first * sin], 0).astype(BF16)
            if part == 0:
                turned = turned * jnp.asarray(SCALING, BF16)
            else:
                keys[head] = turned.T
            heads[start : start + HEAD, :] = turned
    heads[2 * WIDTH :, :] = project[2 * WIDTH :].astype(BF16)
    length = heads.shape[1]
    for head in range(PER_GROUP):
        start = head * HEAD

        def queries_step(step, carry):
            columns = pl.ds(pl.multiple_of(step * QUERY_BLOCK, QUERY_BLOCK), QUERY_BLOCK)
            scores = nn(keys[head], heads[start : start + HEAD, columns])
            peak = jnp.max(scores, 0, keepdims=True)
            exps = jnp.exp(scores - peak)
            total = jnp.sum(exps, 0, keepdims=True)
            log_total[head : head + 1, columns] = peak + jnp.log(total)
            probs = (exps * (1.0 / total)).astype(BF16)
            values = heads[2 * WIDTH + start : 2 * WIDTH + start + HEAD, :]
            mixed_turned[start : start + HEAD, columns] = nn(values, probs).astype(BF16)
            return carry

        lax.fori_loop(0, length // QUERY_BLOCK, queries_step, 0)
    for block in range(blocks):
        mixed[block][...] = mixed_turned[:, block * count : (block + 1) * count].T


def backward_kernel(place, *refs, blocks):
    tokens, refs = refs[:blocks], refs[blocks:]
    d_mixed, refs = refs[:blocks], refs[blocks:]
    (heads, log_total, normed, weight, cosine, sines), refs = refs[:6], refs[6:]
    d_normed, refs = refs[:blocks], refs[blocks:]
    d_weight, refs = refs[:PLANES], refs[PLANES:]
    sums, d_turned, d_keys, d_values, d_project, d_whole, keys, values = refs
    plane = place[0]
    count = tokens[0].shape[0]
    length = heads.shape[1]
    for block in range(blocks):
        d_turned[:, block * count : (block + 1) * count] = d_mixed[block][...].T
    cos, sin = cosine[...], sines[...]
    half = HEAD // 2
    d_keys[...] = jnp.zeros_like(d_keys)
    d_values[...] = jnp.zeros_like(d_values)
    for head in range(PER_GROUP):
        start = head * HEAD
        keys_turned = heads.at[WIDTH + start : WIDTH + start + HEAD]
        keys[...] = keys_turned[...].T
        values[...] = heads[2 * WIDTH + start : 2 * WIDTH + start + HEAD, :].T

        def queries_step(step, carry):
            columns = pl.ds(pl.multiple_of(step * QUERY_BLOCK, QUERY_BLOCK), QUERY_BLOCK)
            queries = heads[start : start + HEAD, columns]
            incoming = d_turned[start : start + HEAD, columns]
            scores = nn(keys[...], queries)
            probs = jnp.exp(scores - log_total[head : head + 1, columns])
            d_probs = nn(values[...], incoming)
            delta = jnp.sum(probs * d_probs, 0, keepdims=True)
            d_scores = (probs * (d_probs - delta)).astype(BF16)
            d_values[start : start + HEAD, :] += nt(incoming, probs.astype(BF16))
            d_keys[start : start + HEAD, :] += nt(queries, d_scores)
            d_queries = nn(keys_turned[...], d_scores) * SCALING
            first, second = d_queries[:half], d_queries[half:]
            cos_here, sin_here = cosine[:, columns], sines[:, columns]
            d_project[start : start + half, columns] = (first * cos_here + second * sin_here).astype(BF16)
            d_project[start + half : start + HEAD, columns] = (second * cos_here - first * sin_here).astype(BF16)
            return carry

        lax.fori_loop(0, length // QUERY_BLOCK, queries_step, 0)
        first, second = d_keys[start : start + half, :], d_keys[start + half : start + HEAD, :]
        d_project[WIDTH + start : WIDTH + start + half, :] = (first * cos + second * sin).astype(BF16)
        d_project[WIDTH + start + half : WIDTH + start + HEAD, :] = (second * cos - first * sin).astype(BF16)
    d_project[2 * WIDTH :, :] = d_values[...].astype(BF16)
    d_shift = jnp.zeros((1, normed.shape[1]), F32)
    d_xhat = jnp.zeros((1, normed.shape[1]), F32)
    for block in range(blocks):
        part = nt(d_project[:, block * count : (block + 1) * count].T, weight[...])
        d_normed[block][...] = part.astype(BF16)
        xhat, _ = standardize(tokens[block][...].astype(F32))
        d_shift = d_shift + jnp.sum(part, 0, keepdims=True)
        d_xhat = d_xhat + jnp.sum(part * xhat, 0, keepdims=True)
    sums[0:1, :] = d_shift
    sums[1:2, :] = d_xhat
    sums[2:8, :] = jnp.zeros((6, normed.shape[1]), F32)
    d_whole[...] = nn(d_project[...], normed[...]).astype(BF16).T
    rows = d_weight[0].shape[0]
    for distance in range(PLANES):
        first = pl.multiple_of((plane ^ distance) * rows, 16)
        d_weight[distance][...] = d_whole[pl.ds(first, rows), :]


def attend_forward(place, tokens, weights, vectors, cosine, sines):
    blocks, (count, width) = len(tokens), tokens[0].shape
    length = blocks * count
    columns = weights[0].shape[1]
    outs = call(
        functools.partial(forward_kernel, blocks=blocks),
        "attend_forward",
        [*tokens, *weights, vectors, cosine, sines],
        [place],
        [shape_of((count, WIDTH), BF16)] * blocks
        + [
            shape_of((columns, length), BF16),
            shape_of((8, length), F32),
            shape_of((length, width), BF16),
            shape_of((width, columns), BF16),
        ],
        [pltpu.VMEM((PER_GROUP, length, HEAD), BF16), pltpu.VMEM((WIDTH, length), BF16)],
        us=15.0,
    )
    return outs[:blocks], outs[blocks:]


def attend_backward(place, tokens, d_mixed, kept, cosine, sines):
    blocks, (count, width) = len(tokens), tokens[0].shape
    length = blocks * count
    columns = 3 * WIDTH
    rows = width // PLANES
    outs = call(
        functools.partial(backward_kernel, blocks=blocks),
        "attend_backward",
        [*tokens, *d_mixed, *kept, cosine, sines],
        [place],
        [shape_of((count, width), BF16)] * blocks
        + [shape_of((rows, columns), BF16)] * PLANES
        + [shape_of((8, width), F32)],
        [
            pltpu.VMEM((WIDTH, length), BF16),
            pltpu.VMEM((WIDTH, length), F32),
            pltpu.VMEM((WIDTH, length), F32),
            pltpu.VMEM((columns, length), BF16),
            pltpu.VMEM((width, columns), BF16),
            pltpu.VMEM((length, HEAD), BF16),
            pltpu.VMEM((length, HEAD), BF16),
        ],
        us=20.0,
    )
    return outs[:blocks], outs[blocks : blocks + PLANES], outs[-1]


def pick(stack, index):
    return lax.dynamic_index_in_dim(stack, index, 0, keepdims=False)


def bits_of(count):
    return [1 << bit for bit in range(count.bit_length() - 1)]


def body(
    tokens,
    upstream,
    token_mask,
    time_index,
    weight_index,
    time_table,
    weight_grid,
    w_ada,
    b_ada,
    gain_one,
    gain_two,
    w_qkv,
    w_proj,
    w_up,
    b_up,
    w_down,
    b_down,
    *,
    n,
    m,
):
    side = n // PLANES
    me = lax.axis_index("seq")
    plane, spot = me // side, me % side
    place = jnp.stack([plane, spot, me]).astype(jnp.int32)
    shard, width = tokens.shape[2], tokens.shape[3]
    rows = w_qkv.shape[0]
    hidden_count = w_up.shape[1]
    grid_size = time_table.shape[0]
    ada_columns = w_ada.shape[1]
    count = PLANES * shard
    unit = min(width, hidden_count)
    hidden_chunks, width_chunks = hidden_count // unit, width // unit

    def swap(value, distance):
        return lax.ppermute(value, "seq", [(i, i ^ distance) for i in range(n)])

    def swap_mlp(value, distance):
        return lax.ppermute(value, "mlp", [(i, i ^ distance) for i in range(m)])

    def between_planes(pieces):
        return [pieces[0]] + [swap(pieces[d], d * side) for d in range(1, PLANES)]

    def in_plane(pieces):
        return [pieces[0]] + [swap(pieces[e], e) for e in range(1, side)]

    def in_order(blocks, axis):
        halves = jnp.stack(blocks)
        for bit in bits_of(len(blocks)):
            here = halves.reshape((len(blocks) // (2 * bit), 2, bit) + halves.shape[1:])
            halves = jnp.where((axis & bit) != 0, here[:, ::-1], here).reshape(halves.shape)
        return halves

    def for_plane(values):
        return [pick(values, jnp.minimum(plane ^ d, MICRO - 1)) for d in range(PLANES)]

    def columns_of(value):
        return [value[:, at : at + unit] for at in range(0, value.shape[1], unit)]

    pieces = for_plane(tokens[:, 0])
    pieces, w_up, w_down, w_proj = lax.optimization_barrier((pieces, w_up, w_down, w_proj))
    own_low = jnp.concatenate(between_planes(pieces), 0)
    token_blocks = {0: own_low}
    for bit in reversed(bits_of(side)):
        for known in list(token_blocks):
            token_blocks[known | bit] = swap(token_blocks[known], bit)
    token_blocks = [token_blocks[at] for at in range(side)]

    full_ada = lax.all_gather(w_ada, "seq", axis=0)
    first = jnp.stack(columns_of(w_up) + columns_of(w_proj))
    second = jnp.stack(columns_of(w_down.T))
    pairwise = rows % 16 == 0 and side == 4 and unit == width
    if pairwise:
        z_bits, y_bit, core_bit = (2 * side, side), 2, 1
        blocks = {0: first}
        for bit in z_bits:
            for known in list(blocks):
                blocks[known | bit] = swap(blocks[known], bit)
        line = jnp.stack([blocks[d * side] for d in range(PLANES)])
        sources, layout = [line, swap(line, y_bit)], [[d * side + at for d in range(PLANES)] for at in (0, y_bit)]
        sources += [swap(source, core_bit) for source in sources]
        layout += [[at + core_bit for at in some] for some in layout]
        full_up, full_proj = call(
            functools.partial(
                assemble_kernel, layout=layout, outs=[(0, at) for at in range(hidden_chunks)] + [(1, 0)]
            ),
            "assemble_up",
            sources,
            [place],
            [shape_of((width, hidden_count), BF16), shape_of((width, width), BF16)],
            us=4.0,
        )
        blocks = {0: jnp.stack([second, swap(second, y_bit)])}
        for bit in z_bits:
            for known in list(blocks):
                blocks[known | bit] = swap(blocks[known], bit)
        sources = [blocks[d * side] for d in range(PLANES)]
        layout = [[d * side, d * side + y_bit] for d in range(PLANES)]
        sources += [swap(source, core_bit) for source in sources]
        layout += [[at + core_bit for at in some] for some in layout]
        (full_down,) = call(
            functools.partial(assemble_kernel, layout=layout, outs=[(0, at) for at in range(hidden_chunks)]),
            "assemble_down",
            sources,
            [place],
            [shape_of((width, hidden_count), BF16)],
            us=3.0,
        )
    else:
        gathered = lax.all_gather(jnp.concatenate([first, second]), "seq", axis=0)
        gathered = gathered.transpose(1, 0, 2, 3).reshape(-1, width, unit)

        def side_by_side(start, number):
            return jnp.concatenate([gathered[start + at] for at in range(number)], -1)

        full_up = side_by_side(0, hidden_chunks)
        full_proj = side_by_side(hidden_chunks, width_chunks)
        full_down = side_by_side(hidden_chunks + width_chunks, hidden_chunks)

    by_group = w_qkv.reshape(rows, 3, GROUPS, WIDTH).transpose(2, 0, 1, 3).reshape(GROUPS, rows, 3 * WIDTH)
    received = in_plane([pick(by_group, (spot ^ e) % GROUPS) for e in range(side)])
    received = jnp.stack(received)
    weight_blocks = {0: jnp.concatenate([pick(received, spot ^ at) for at in range(side)], 0)}
    for bit in (2, 1):
        for known in list(weight_blocks):
            weight_blocks[known | bit] = swap(weight_blocks[known], bit * side)
    weight_blocks = [weight_blocks[at] for at in range(PLANES)]

    line = [value[None] for value in (b_ada, gain_one, gain_two, b_down)]
    (small,) = call(
        modulation_kernel,
        "modulation",
        [time_table, w_ada, *line, token_mask[:, 0]],
        [time_index],
        [shape_of((8, SMALL), F32)],
    )
    small = small[None]
    for bit in bits_of(n):
        small = jnp.concatenate([small, swap(small, bit)], 0)
    vectors, scale = call(
        vectors_kernel,
        "vectors",
        [small],
        [place, weight_index, weight_grid],
        [shape_of((16, width), F32), shape_of((count, 1), F32)],
        [pltpu.VMEM((8, count), F32)],
    )

    order = ((plane ^ jnp.arange(PLANES))[None, :] * side + (spot ^ jnp.arange(side))[:, None]) * shard
    positions = (order[:, :, None] + jnp.arange(shard)).reshape(1, -1).astype(F32)
    frequency = 10000.0 ** (-jnp.arange(0, HEAD, 2).astype(F32) / HEAD)
    angles = frequency[:, None] * positions
    cosine, sines = jnp.cos(angles), jnp.sin(angles)

    mixed_blocks, kept = attend_forward(place, token_blocks, weight_blocks, vectors, cosine, sines)

    mixed_blocks = in_plane(mixed_blocks)

    own_upstream = jnp.concatenate(between_planes(for_plane(upstream[:, 0])), 0)
    d_rows = ((own_upstream.astype(F32) * scale) * vectors[GATE_TWO][None]).astype(BF16)
    d_rows = [d_rows] + [swap_mlp(d_rows, d) for d in range(1, m)]

    attended, middle, normed_two = call(
        project_kernel,
        "project",
        [full_proj, own_low, vectors, *mixed_blocks],
        [place],
        [shape_of((count, width), F32), shape_of((count, width), F32), shape_of((count, width), BF16)],
        us=3.0,
    )
    rows_all = [normed_two] + [swap_mlp(normed_two, d) for d in range(1, m)]
    bias_up = b_up.astype(F32)[None]
    fed = [
        call(
            feed_kernel,
            "feed_forward",
            [full_up, full_down, rows_all[d], d_rows[d], bias_up],
            [],
            [shape_of((count, width), BF16 if d else F32)] * 2 + [shape_of((count, hidden_count), BF16)] * 2,
            us=6.0,
        )
        for d in range(m)
    ]
    d_arrived = [swap_mlp(fed[d][1], d) for d in range(1, m)]
    out_arrived = [swap_mlp(fed[d][0], d) for d in range(1, m)]
    slots = n // 2
    if pairwise:
        down_shapes = [shape_of((slots, hidden_chunks, rows, unit), BF16)] * 2
        up_shapes = [shape_of((slots, hidden_chunks + width_chunks, rows, unit), BF16)] * 2
    else:
        down_shapes = [shape_of((width, hidden_count), BF16)]
        up_shapes = [shape_of((width, hidden_count), BF16), shape_of((width, width), BF16)]
    down_grads = call(
        functools.partial(down_grads_kernel, blocks=m, scatter=pairwise),
        "down_gradients",
        [*d_rows, *[f[2] for f in fed]],
        [place],
        down_shapes,
        us=4.0,
    )
    middle_outs = call(
        functools.partial(middle_kernel, others=m - 1),
        "middle_backward",
        [full_proj, vectors, own_upstream, scale, attended, middle, fed[0][1], *d_arrived],
        [place],
        [shape_of((count, WIDTH), BF16)] * side
        + [shape_of((count, width), F32), shape_of((count, width), BF16), shape_of((8, width), F32)],
        us=4.0,
    )
    d_mixed_blocks, (d_middle, d_attended, middle_sums) = middle_outs[:side], middle_outs[side:]

    d_mixed_blocks = in_plane(d_mixed_blocks)
    if side > GROUPS:
        share = (spot < GROUPS).astype(BF16)
        d_mixed_blocks = [block * share for block in d_mixed_blocks]

    *up_grads, bias_up_sum = call(
        functools.partial(up_grads_kernel, blocks=m, side=side, scatter=pairwise),
        "up_gradients",
        [d_attended, *mixed_blocks, *rows_all, *[f[3] for f in fed]],
        [place],
        up_shapes + [shape_of((1, hidden_count), F32)],
        [pltpu.VMEM((width, width), BF16)],
        us=5.0,
    )

    def scatter(grads, bits, name, outs):
        own, sent = grads
        arrived = swap(sent, core_bit)
        for bit in bits[:-1]:
            half = (own.shape[0] // 2,) + own.shape[1:]
            own, sent = call(add_split_kernel, name, [own, arrived], [], [shape_of(half, BF16)] * 2)
            arrived = swap(sent, bit)
        half = (own.shape[0] // 2,) + own.shape[1:]
        own, sent = call(add_split_kernel, name, [own, arrived], [], [shape_of(half, BF16)] * 2)
        return call(add_last_kernel, name, [own, swap(sent, bits[-1])], [], [shape_of((rows, unit), F32)] * outs)

    if pairwise:
        down_parts = scatter(down_grads, (side, 2 * side, y_bit), "down_sum", hidden_chunks)
        *up_parts, grad_proj = scatter(up_grads, (y_bit, side, 2 * side), "up_sum", hidden_chunks + 1)
        grad_up, grad_down = jnp.concatenate(up_parts, -1), jnp.concatenate(down_parts, -1).T
    else:
        grads = jnp.stack(columns_of(up_grads[0]) + columns_of(down_grads[0]) + columns_of(up_grads[1]))
        grads = grads.reshape(-1, n, rows, unit).transpose(1, 0, 2, 3)
        grads = lax.psum_scatter(grads, "seq", scatter_dimension=0, tiled=True)[0]

        def columns_from(start, number):
            return jnp.concatenate([grads[start + at] for at in range(number)], -1).astype(F32)

        grad_up = columns_from(0, hidden_chunks)
        grad_down = columns_from(hidden_chunks, hidden_chunks).T
        grad_proj = columns_from(2 * hidden_chunks, width_chunks)
    for bit in bits_of(m):
        grad_proj = grad_proj + swap_mlp(grad_proj.astype(BF16), bit).astype(F32)

    result, output_sums = call(
        functools.partial(output_kernel, others=m - 1),
        "output",
        [vectors, own_upstream, scale, middle, fed[0][0], *out_arrived],
        [],
        [shape_of((count, width), BF16), shape_of((8, width), F32)],
    )

    d_normed_blocks, d_weight_blocks, sums = attend_backward(
        place, token_blocks, d_mixed_blocks, kept, cosine, sines
    )

    blocks = dict(enumerate(d_normed_blocks))
    for bit in bits_of(side):
        for at in [at for at in blocks if at & bit]:
            arrived = swap(blocks.pop(at), bit)
            if len(blocks) > 1:
                blocks[at ^ bit] = (blocks[at ^ bit].astype(F32) + arrived.astype(F32)).astype(BF16)
    (d_tokens,) = call(
        tokens_kernel,
        "tokens_backward",
        [vectors, own_low, d_middle, blocks[0], arrived],
        [],
        [shape_of((count, width), BF16)],
    )

    def back_to_tokens(value):
        received = between_planes([value[d * shard : (d + 1) * shard] for d in range(PLANES)])
        received = jnp.stack(received)
        return jnp.stack([pick(received, plane ^ at) for at in range(MICRO)])[:, None]

    total = sum(piece.astype(F32) for piece in between_planes(d_weight_blocks))
    by_spot = total.astype(BF16).reshape(side, rows, 3 * WIDTH)
    received = jnp.stack(in_plane([pick(by_spot, spot ^ e) for e in range(side)]))
    grad_qkv = jnp.stack([pick(received, spot ^ group) for group in range(GROUPS)])
    grad_qkv = grad_qkv.reshape(GROUPS, rows, 3, WIDTH).transpose(1, 2, 0, 3).reshape(rows, 3 * width)
    grad_qkv = grad_qkv.astype(F32)
    for bit in bits_of(m):
        grad_qkv = grad_qkv + swap_mlp(grad_qkv.astype(BF16), bit).astype(F32)

    bias_up_rows = -(-hidden_count // width)
    bias_up_sum = jnp.pad(bias_up_sum, ((0, 0), (0, bias_up_rows * width - hidden_count)))
    small = jnp.concatenate(
        [sums[0:2], middle_sums[0:3], output_sums[0:2], bias_up_sum.reshape(-1, width)], 0
    )
    for bit in bits_of(side):
        small = small + swap(small, bit)
    small = jnp.concatenate([small, vectors[SCALE_TWO][None]], 0)[None]
    for bit in bits_of(PLANES):
        small = jnp.concatenate([small, swap(small, bit * side)], 0)
    small = in_order(list(small), plane)[:MICRO]
    grad_bias_up = jnp.sum(small[:, 7 : 7 + bias_up_rows], 0).reshape(-1)[:hidden_count]
    d_shift_one, d_xhat_one, d_gate_one, d_shift_two, d_xhat_two, d_gate_two = [small[:, at] for at in range(6)]
    index_here = time_index[:, 0]
    vector_sums = jnp.stack(
        [
            jnp.sum((1.0 + vectors[SCALES_ALL : SCALES_ALL + MICRO]) * d_xhat_one, 0),
            jnp.sum((1.0 + small[:, -1]) * d_xhat_two, 0),
            jnp.sum(small[:, 6], 0),
            jnp.pad(index_here.astype(F32), (0, width - MICRO)),
        ]
    )
    d_scale_one, d_scale_two = vectors[GAIN_ONE] * d_xhat_one, vectors[GAIN_TWO] * d_xhat_two
    small = jnp.stack([d_shift_one, d_scale_one, d_gate_one, d_shift_two, d_scale_two, d_gate_two], 1)
    small = jnp.concatenate([small.reshape(6 * MICRO, width), vector_sums], 0)[None]
    for bit in bits_of(m):
        small = jnp.concatenate([small, swap_mlp(small, bit)], 0)
    at = 6 * MICRO
    d_modulation = small[:, :at].reshape(m * MICRO, n, ada_columns)
    vector_sums = jnp.sum(small[:, at : at + 3], 0)
    index_all = small[:, at + 3, :MICRO].reshape(-1).astype(jnp.int32)
    onehot = (index_all[:, None] == jnp.arange(grid_size)[None, :]).astype(BF16)
    cond = jnp.dot(onehot, time_table, preferred_element_type=F32)
    d_modulation_own = lax.dynamic_index_in_dim(d_modulation, me, 1, keepdims=False)
    grad_ada = jnp.dot(cond.T, d_modulation_own, precision=highest)
    grad_bias_ada = jnp.sum(d_modulation_own, 0)
    d_cond = jnp.einsum("bic,idc->bd", d_modulation, full_ada.astype(F32), precision=highest)
    table_rows = grid_size // n
    onehot_own = index_all[None, :] == (me * table_rows + jnp.arange(table_rows))[:, None]
    grad_table = jnp.dot(onehot_own.astype(F32), d_cond, precision=highest)
    vector_sums = lax.dynamic_slice_in_dim(vector_sums, me * rows, rows, 1)
    return (
        back_to_tokens(result),
        back_to_tokens(d_tokens).astype(F32),
        grad_table,
        grad_ada,
        grad_bias_ada,
        vector_sums[0],
        vector_sums[1],
        grad_qkv,
        grad_proj,
        grad_up,
        grad_bias_up,
        grad_down,
        vector_sums[2],
    )


def solution(mesh):
    in_specs = (
        P(None, "mlp", "seq", None),
        P(None, "mlp", "seq", None),
        P(None, "mlp", "seq"),
        P(None, "mlp"),
        P(None, "mlp"),
        P(),
        P(),
        P(None, "seq"),
        P("seq"),
        P("seq"),
        P("seq"),
        P("seq", None),
        P("seq", None),
        P("seq", "mlp"),
        P("mlp"),
        P("mlp", "seq"),
        P("seq"),
    )
    out_specs = (
        P(None, "mlp", "seq", None),
        P(None, "mlp", "seq", None),
        P("seq", None),
        P(None, "seq"),
        P("seq"),
        P("seq"),
        P("seq"),
        P("seq", None),
        P("seq", None),
        P("seq", "mlp"),
        P("mlp"),
        P("mlp", "seq"),
        P("seq"),
    )
    run = functools.partial(body, n=mesh.shape["seq"], m=mesh.shape["mlp"])
    return jax.shard_map(run, mesh=mesh, in_specs=in_specs, out_specs=out_specs, check_vma=False)
```

```python
import functools
import math

import jax
import jax.numpy as jnp
from jax import lax
from jax.experimental import pallas as pl
from jax.experimental.pallas import tpu as pltpu
from jax.sharding import PartitionSpec as P

HEADS = 12
HEAD = 64
MICRO = 3
PLANES = 4
GROUPS = 4
PER_GROUP = HEADS // GROUPS
WIDTH = PER_GROUP * HEAD
QUERY_BLOCK = 256
SCALING = HEAD ** (-0.5)
BF16 = jnp.bfloat16
F32 = jnp.float32
highest = lax.Precision.HIGHEST
SLOPE = math.sqrt(2.0 / math.pi)
CUBIC = 0.044715
SMALL = 384

SHIFT_ONE, SCALE_ONE, GATE_ONE, SHIFT_TWO, SCALE_TWO, GATE_TWO, GAIN_ONE, GAIN_TWO, BIAS_DOWN = range(9)
SCALES_ALL, GAINS_ONE, GAINS_TWO = 9, 12, 13

VMEM = pl.BlockSpec(memory_space=pltpu.VMEM)
SMEM = pl.BlockSpec(memory_space=pltpu.SMEM)


def nn(left, right):
    return lax.dot_general(left, right, (((1,), (0,)), ((), ())), preferred_element_type=F32)


def nt(left, right):
    return lax.dot_general(left, right, (((1,), (1,)), ((), ())), preferred_element_type=F32)


def standardize(inputs):
    average = jnp.mean(inputs, -1, keepdims=True)
    centred = inputs - average
    spread = jnp.mean(centred * centred, -1, keepdims=True)
    root = lax.rsqrt(spread + 1e-06)
    return centred * root, root


def pull_norm(d_normed, gains, xhat, root):
    e = d_normed * gains
    return root * (e - jnp.mean(e, -1, keepdims=True) - xhat * jnp.mean(e * xhat, -1, keepdims=True))


def over_tokens(value):
    return jnp.sum(value, 0, keepdims=True)


def shape_of(dims, dtype):
    return jax.ShapeDtypeStruct(dims, dtype)


def call(kernel, name, operands, scalars, outs, scratch=(), us=1.0):
    moved = sum(math.prod(o.shape) * o.dtype.itemsize for o in list(operands) + list(outs))
    return pl.pallas_call(
        kernel,
        out_shape=list(outs),
        in_specs=[SMEM] * len(scalars) + [VMEM] * len(operands),
        out_specs=[VMEM] * len(outs),
        scratch_shapes=list(scratch),
        compiler_params=pltpu.CompilerParams(vmem_limit_bytes=56 * 1024 * 1024),
        cost_estimate=pl.CostEstimate(flops=int(us * 1e9), bytes_accessed=moved, transcendentals=0),
        name=name,
    )(*scalars, *operands)


def modulation_kernel(times, table, w_ada, b_ada, gain_one, gain_two, b_down, mask, small):
    columns = w_ada.shape[1]
    rows = gain_one.shape[1]
    at = lax.broadcasted_iota(jnp.int32, (8, table.shape[0]), 1)
    line = lax.broadcasted_iota(jnp.int32, (8, table.shape[0]), 0)
    wanted = jnp.where(line == 0, times[0, 0], jnp.where(line == 1, times[1, 0], times[2, 0]))
    cond = nn((at == wanted).astype(F32).astype(BF16), table[...]).astype(BF16)
    part = nn(cond, w_ada[...]) + b_ada[...].astype(F32)
    small[...] = jnp.zeros_like(small)
    small[0:MICRO, 0:columns] = part[0:MICRO]
    small[3:4, 0:rows] = gain_one[...].astype(F32)
    small[3:4, 128 : 128 + rows] = gain_two[...].astype(F32)
    small[3:4, 256 : 256 + rows] = b_down[...].astype(F32)
    small[4 : 4 + MICRO, 0 : mask.shape[1]] = mask[...].astype(F32)


def vectors_kernel(place, weight_index, weight_grid, small, vectors, scale, line):
    n = small.shape[0]
    width = vectors.shape[1]
    columns, rows, shard = 6 * width // n, width // n, scale.shape[0] // PLANES
    plane, spot = place[0], place[1]
    side = n // PLANES
    me = plane * side + spot
    last = jnp.minimum(plane, MICRO - 1)

    def one_of(three):
        return jnp.where(last == 0, three[0:1], jnp.where(last == 1, three[1:2], three[2:3]))

    def pieces(first, size):
        start = first
        while start < first + size:
            stop = min(first + size, (start // width + 1) * width)
            yield start // width, start % width, start - first, stop - start
            start = stop

    vectors[...] = jnp.zeros_like(vectors)
    for i in range(n):
        here = small.at[me ^ i]
        mine = one_of(here[0:MICRO, 0:columns])
        for part, column, offset, size in pieces(i * columns, columns):
            vectors[part : part + 1, column : column + size] = mine[:, offset : offset + size]
            if part == SCALE_ONE:
                vectors[SCALES_ALL : SCALES_ALL + MICRO, column : column + size] = here[
                    0:MICRO, offset : offset + size
                ]
        for row, offset in ((GAIN_ONE, 0), (GAIN_TWO, 128), (BIAS_DOWN, 256)):
            vectors[row : row + 1, i * rows : (i + 1) * rows] = here[3:4, offset : offset + rows]
    for to, gain, by in ((GAINS_ONE, GAIN_ONE, SCALE_ONE), (GAINS_TWO, GAIN_TWO, SCALE_TWO)):
        vectors[to : to + 1, :] = vectors[gain : gain + 1, :] * (1.0 + vectors[by : by + 1, :])
    line[...] = jnp.zeros_like(line)
    for d in range(PLANES):
        line[0:1, d * shard : (d + 1) * shard] = one_of(small[d * side, 4 : 4 + MICRO, 0:shard])
    weight = jnp.where(plane < MICRO, weight_grid[weight_index[last, 0]], 0.0)
    scale[...] = line[...].T[:, 0:1] * weight


def project_kernel(place, weight, tokens, vectors, *refs):
    side = len(refs) - 3
    mixed, (attended, middle, normed) = refs[:side], refs[side:]
    spot = place[1]
    total = jnp.zeros(attended.shape, F32)
    for e in range(side):
        other = spot ^ e
        block = mixed[e][...]
        if side > GROUPS:
            block = jnp.where(other < GROUPS, block, jnp.zeros_like(block))
        first = pl.multiple_of((other % GROUPS) * WIDTH, WIDTH)
        total = total + nn(block, weight[pl.ds(first, WIDTH), :])
    attended[...] = total
    after = tokens[...].astype(F32) + vectors[GATE_ONE : GATE_ONE + 1] * total
    middle[...] = after
    xhat, _ = standardize(after)
    normed[...] = (xhat * vectors[GAINS_TWO : GAINS_TWO + 1] + vectors[SHIFT_TWO : SHIFT_TWO + 1]).astype(BF16)


def feed_kernel(up, down, rows, d_rows, bias, output, d_normed, active, d_hidden):
    unit = min(bias.shape[1], rows.shape[1])
    out = jnp.zeros(output.shape, F32)
    back = jnp.zeros(output.shape, F32)
    for at in range(0, bias.shape[1], unit):
        columns = slice(at, at + unit)
        u = nn(rows[...], up[:, columns]) + bias[:, columns]
        square = u * u
        bent = jnp.tanh(SLOPE * u * (1.0 + CUBIC * square))
        half = 0.5 * (1.0 + bent)
        on = (u * half).astype(BF16)
        active[:, columns] = on
        slope = half + 0.5 * u * (1.0 - bent * bent) * (SLOPE * (1.0 + 3.0 * CUBIC * square))
        d_on = (nn(d_rows[...], down[:, columns]) * slope).astype(BF16)
        d_hidden[:, columns] = d_on
        out = out + nt(on, down[:, columns])
        back = back + nt(d_on, up[:, columns])
    output[...] = out.astype(output.dtype)
    d_normed[...] = back.astype(d_normed.dtype)


def scatter_store(refs, me, device, value):
    kept, sent, chunk, slot_of = refs
    distance = me ^ device
    slot = slot_of(distance)

    @pl.when(distance % 2 == 0)
    def _():
        kept[slot, chunk] = value

    @pl.when(distance % 2 == 1)
    def _():
        sent[slot, chunk] = value


def slot_z_first(distance):
    return ((distance >> 2) & 1) * 4 + ((distance >> 3) & 1) * 2 + ((distance >> 1) & 1)


def slot_y_first(distance):
    return ((distance >> 1) & 1) * 4 + ((distance >> 2) & 1) * 2 + ((distance >> 3) & 1)


def down_grads_kernel(place, *refs, blocks, scatter):
    d_rows, active = refs[:blocks], refs[blocks : 2 * blocks]
    outs = refs[2 * blocks :]
    me = place[2]
    width, count = d_rows[0].shape[1], active[0].shape[1]
    unit = min(width, count)
    turned = [ref[...].T for ref in d_rows]
    for chunk in range(count // unit):
        columns = slice(chunk * unit, (chunk + 1) * unit)
        grad = sum(nn(turned[b], active[b][:, columns]) for b in range(blocks)).astype(BF16)
        if scatter:
            rows = outs[0].shape[2]
            for i in range(width // rows):
                part = grad[i * rows : (i + 1) * rows]
                scatter_store((outs[0], outs[1], chunk, slot_z_first), me, i, part)
        else:
            outs[0][:, columns] = grad


def up_grads_kernel(place, d_attended, *refs, blocks, side, scatter):
    mixed, refs = refs[:side], refs[side:]
    rows_all, d_hidden = refs[:blocks], refs[blocks : 2 * blocks]
    outs, whole = refs[2 * blocks : -1], refs[-1]
    bias = outs[-1]
    spot, me = place[1], place[2]
    width, count = rows_all[0].shape[1], bias.shape[1]
    unit = min(width, count)
    turned = [ref[...].T for ref in rows_all]
    for chunk in range(count // unit):
        columns = slice(chunk * unit, (chunk + 1) * unit)
        grad = sum(nn(turned[b], d_hidden[b][:, columns]) for b in range(blocks)).astype(BF16)
        bias[:, columns] = sum(over_tokens(d_hidden[b][:, columns].astype(F32)) for b in range(blocks))
        if scatter:
            rows = outs[0].shape[2]
            for i in range(width // rows):
                part = grad[i * rows : (i + 1) * rows]
                scatter_store((outs[0], outs[1], chunk, slot_y_first), me, i, part)
        else:
            outs[0][:, columns] = grad
    if side > GROUPS:
        whole[...] = jnp.zeros_like(whole)
    for e in range(side):
        other = spot ^ e
        first = pl.multiple_of((other % GROUPS) * WIDTH, WIDTH)
        grad = nn(mixed[e][...].T, d_attended[...]).astype(BF16)
        if side > GROUPS:
            grad = whole[pl.ds(first, WIDTH), :] + jnp.where(other < GROUPS, grad, jnp.zeros_like(grad))
        whole[pl.ds(first, WIDTH), :] = grad
    if scatter:
        for i in range(width // rows):
            part = whole[i * rows : (i + 1) * rows, :]
            scatter_store((outs[0], outs[1], count // unit, slot_y_first), me, i, part)
    else:
        outs[1][...] = whole[...]


def qkv_grads_kernel(place, d_project, normed, *outs):
    grad = nn(d_project[...], normed[...]).astype(BF16).T
    plane = place[0]
    rows = outs[0].shape[1]
    for at in range(PLANES):
        part = grad[at * rows : (at + 1) * rows]
        distance = plane ^ at

        @pl.when(distance % 2 == 0)
        def _():
            outs[0][distance // 2] = part

        @pl.when(distance % 2 == 1)
        def _():
            outs[1][distance // 2] = part


def assemble_kernel(place, *refs, layout, outs):
    sources, targets = refs[: len(layout)], refs[len(layout) :]
    me = place[2]
    rows, unit = sources[0].shape[2:]
    for source, distances in zip(sources, layout):
        for slot, distance in enumerate(distances):
            first = pl.multiple_of((me ^ distance) * rows, 16)
            for chunk, (target, column) in enumerate(outs):
                targets[target][pl.ds(first, rows), column * unit : (column + 1) * unit] = source[slot, chunk]


def middle_kernel(place, weight, vectors, upstream, scale, attended, middle, d_own, *refs, others):
    arrived, refs = refs[:others], refs[others:]
    d_mixed, (d_middle, d_attended, sums) = refs[:-3], refs[-3:]
    spot = place[1]
    width = middle.shape[1]
    d_normed = d_own[...]
    for ref in arrived:
        d_normed = d_normed + ref[...].astype(F32)
    xhat, root = standardize(middle[...])
    d_result = upstream[...].astype(F32) * scale[...]
    d_after = d_result + pull_norm(d_normed, vectors[GAINS_TWO : GAINS_TWO + 1], xhat, root)
    d_middle[...] = d_after
    low = (vectors[GATE_ONE : GATE_ONE + 1] * d_after).astype(BF16)
    d_attended[...] = low
    for e in range(len(d_mixed)):
        first = pl.multiple_of(((spot ^ e) % GROUPS) * WIDTH, WIDTH)
        d_mixed[e][...] = nt(low, weight[pl.ds(first, WIDTH), :]).astype(BF16)
    sums[0:1, :] = over_tokens(d_after * attended[...])
    sums[1:2, :] = over_tokens(d_normed)
    sums[2:3, :] = over_tokens(d_normed * xhat)
    sums[3:8, :] = jnp.zeros((5, width), F32)


def output_kernel(vectors, upstream, scale, middle, own, *refs, others):
    arrived, (result, sums) = refs[:others], refs[others:]
    output = own[...] + vectors[BIAS_DOWN : BIAS_DOWN + 1]
    for ref in arrived:
        output = output + ref[...].astype(F32)
    gate = vectors[GATE_TWO : GATE_TWO + 1]
    result[...] = (middle[...] + gate * output).astype(BF16)
    d_result = upstream[...].astype(F32) * scale[...]
    sums[0:1, :] = over_tokens(d_result * output)
    sums[1:2, :] = over_tokens(gate * d_result)
    sums[2:8, :] = jnp.zeros((6, middle.shape[1]), F32)


def tokens_kernel(vectors, tokens, d_middle, own, arrived, d_tokens):
    xhat, root = standardize(tokens[...].astype(F32))
    d_normed = own[...].astype(F32) + arrived[...].astype(F32)
    back = pull_norm(d_normed, vectors[GAINS_ONE : GAINS_ONE + 1], xhat, root)
    d_tokens[...] = (d_middle[...] + back).astype(BF16)


def forward_kernel(place, *refs, blocks):
    tokens, refs = refs[:blocks], refs[blocks:]
    weights, refs = refs[:PLANES], refs[PLANES:]
    (vectors, cosine, sines), refs = refs[:3], refs[3:]
    gain, shift = vectors[GAINS_ONE : GAINS_ONE + 1], vectors[SHIFT_ONE : SHIFT_ONE + 1]
    mixed, refs = refs[:blocks], refs[blocks:]
    heads, log_total, normed, weight, keys, mixed_turned = refs
    plane = place[0]
    rows = weights[0].shape[0]
    count = tokens[0].shape[0]
    for distance in range(PLANES):
        first = pl.multiple_of((plane ^ distance) * rows, 16)
        weight[pl.ds(first, rows), :] = weights[distance][...]
    for block in range(blocks):
        xhat, _ = standardize(tokens[block][...].astype(F32))
        normed[block * count : (block + 1) * count, :] = (xhat * gain + shift).astype(BF16)
    project = nt(weight[...].T, normed[...])
    cos, sin = cosine[...], sines[...]
    half = HEAD // 2
    for part in range(2):
        for head in range(PER_GROUP):
            start = part * WIDTH + head * HEAD
            first, second = project[start : start + half], project[start + half : start + HEAD]
            turned = jnp.concatenate([first * cos - second * sin, second * cos + first * sin], 0).astype(BF16)
            if part == 0:
                turned = turned * jnp.asarray(SCALING, BF16)
            else:
                keys[head] = turned.T
            heads[start : start + HEAD, :] = turned
    heads[2 * WIDTH :, :] = project[2 * WIDTH :].astype(BF16)
    length = heads.shape[1]
    for head in range(PER_GROUP):
        start = head * HEAD

        def queries_step(step, carry):
            columns = pl.ds(pl.multiple_of(step * QUERY_BLOCK, QUERY_BLOCK), QUERY_BLOCK)
            scores = nn(keys[head], heads[start : start + HEAD, columns])
            peak = jnp.max(scores, 0, keepdims=True)
            exps = jnp.exp(scores - peak)
            total = jnp.sum(exps, 0, keepdims=True)
            log_total[head : head + 1, columns] = peak + jnp.log(total)
            probs = (exps * (1.0 / total)).astype(BF16)
            values = heads[2 * WIDTH + start : 2 * WIDTH + start + HEAD, :]
            mixed_turned[start : start + HEAD, columns] = nn(values, probs).astype(BF16)
            return carry

        lax.fori_loop(0, length // QUERY_BLOCK, queries_step, 0)
    for block in range(blocks):
        mixed[block][...] = mixed_turned[:, block * count : (block + 1) * count].T


def backward_kernel(*refs, blocks):
    tokens, refs = refs[:blocks], refs[blocks:]
    d_mixed, refs = refs[:blocks], refs[blocks:]
    (heads, log_total, normed, weight, cosine, sines), refs = refs[:6], refs[6:]
    (kept, sent), refs = refs[:2], refs[2:]
    sums, d_project, d_turned, d_keys, d_values, keys, values = refs
    count = tokens[0].shape[0]
    length = heads.shape[1]
    for block in range(blocks):
        d_turned[:, block * count : (block + 1) * count] = d_mixed[block][...].T
    cos, sin = cosine[...], sines[...]
    half = HEAD // 2
    d_keys[...] = jnp.zeros_like(d_keys)
    d_values[...] = jnp.zeros_like(d_values)
    for head in range(PER_GROUP):
        start = head * HEAD
        keys_turned = heads.at[WIDTH + start : WIDTH + start + HEAD]
        keys[...] = keys_turned[...].T
        values[...] = heads[2 * WIDTH + start : 2 * WIDTH + start + HEAD, :].T

        def queries_step(step, carry):
            columns = pl.ds(pl.multiple_of(step * QUERY_BLOCK, QUERY_BLOCK), QUERY_BLOCK)
            queries = heads[start : start + HEAD, columns]
            incoming = d_turned[start : start + HEAD, columns]
            scores = nn(keys[...], queries)
            probs = jnp.exp(scores - log_total[head : head + 1, columns])
            d_probs = nn(values[...], incoming)
            delta = jnp.sum(probs * d_probs, 0, keepdims=True)
            d_scores = (probs * (d_probs - delta)).astype(BF16)
            d_values[start : start + HEAD, :] += nt(incoming, probs.astype(BF16))
            d_keys[start : start + HEAD, :] += nt(queries, d_scores)
            d_queries = nn(keys_turned[...], d_scores) * SCALING
            first, second = d_queries[:half], d_queries[half:]
            cos_here, sin_here = cosine[:, columns], sines[:, columns]
            d_project[start : start + half, columns] = (first * cos_here + second * sin_here).astype(BF16)
            d_project[start + half : start + HEAD, columns] = (second * cos_here - first * sin_here).astype(BF16)
            return carry

        lax.fori_loop(0, length // QUERY_BLOCK, queries_step, 0)
        first, second = d_keys[start : start + half, :], d_keys[start + half : start + HEAD, :]
        d_project[WIDTH + start : WIDTH + start + half, :] = (first * cos + second * sin).astype(BF16)
        d_project[WIDTH + start + half : WIDTH + start + HEAD, :] = (second * cos - first * sin).astype(BF16)
    d_project[2 * WIDTH :, :] = d_values[...].astype(BF16)
    d_shift = jnp.zeros((1, normed.shape[1]), F32)
    d_xhat = jnp.zeros((1, normed.shape[1]), F32)
    for block in range(blocks):
        part = nt(d_project[:, block * count : (block + 1) * count].T, weight[...])
        (sent if block % 2 else kept)[block // 2] = part.astype(BF16)
        xhat, _ = standardize(tokens[block][...].astype(F32))
        d_shift = d_shift + jnp.sum(part, 0, keepdims=True)
        d_xhat = d_xhat + jnp.sum(part * xhat, 0, keepdims=True)
    sums[0:1, :] = d_shift
    sums[1:2, :] = d_xhat
    sums[2:8, :] = jnp.zeros((6, normed.shape[1]), F32)


def attend_forward(place, tokens, weights, vectors, cosine, sines):
    blocks, (count, width) = len(tokens), tokens[0].shape
    length = blocks * count
    columns = weights[0].shape[1]
    outs = call(
        functools.partial(forward_kernel, blocks=blocks),
        "attend_forward",
        [*tokens, *weights, vectors, cosine, sines],
        [place],
        [shape_of((count, WIDTH), BF16)] * blocks
        + [
            shape_of((columns, length), BF16),
            shape_of((8, length), F32),
            shape_of((length, width), BF16),
            shape_of((width, columns), BF16),
        ],
        [pltpu.VMEM((PER_GROUP, length, HEAD), BF16), pltpu.VMEM((WIDTH, length), BF16)],
        us=15.0,
    )
    return outs[:blocks], outs[blocks:]


def attend_backward(tokens, d_mixed, kept, cosine, sines):
    blocks, (count, width) = len(tokens), tokens[0].shape
    length = blocks * count
    columns = 3 * WIDTH
    return call(
        functools.partial(backward_kernel, blocks=blocks),
        "attend_backward",
        [*tokens, *d_mixed, *kept, cosine, sines],
        [],
        [shape_of((blocks // 2, count, width), BF16)] * 2
        + [shape_of((8, width), F32), shape_of((columns, length), BF16)],
        [
            pltpu.VMEM((WIDTH, length), BF16),
            pltpu.VMEM((WIDTH, length), F32),
            pltpu.VMEM((WIDTH, length), F32),
            pltpu.VMEM((length, HEAD), BF16),
            pltpu.VMEM((length, HEAD), BF16),
        ],
        us=20.0,
    )


def after(values, *others):
    return lax.optimization_barrier((values, others))[0]


def add(left, right):
    return (left.astype(F32) + right.astype(F32)).astype(BF16)


def pick(stack, index):
    return lax.dynamic_index_in_dim(stack, index, 0, keepdims=False)


def bits_of(count):
    return [1 << bit for bit in range(count.bit_length() - 1)]


def body(
    tokens,
    upstream,
    token_mask,
    time_index,
    weight_index,
    time_table,
    weight_grid,
    w_ada,
    b_ada,
    gain_one,
    gain_two,
    w_qkv,
    w_proj,
    w_up,
    b_up,
    w_down,
    b_down,
    *,
    n,
    m,
):
    side = n // PLANES
    me = lax.axis_index("seq")
    plane, spot = me // side, me % side
    place = jnp.stack([plane, spot, me]).astype(jnp.int32)
    shard, width = tokens.shape[2], tokens.shape[3]
    rows = w_qkv.shape[0]
    hidden_count = w_up.shape[1]
    grid_size = time_table.shape[0]
    ada_columns = w_ada.shape[1]
    count = PLANES * shard
    unit = min(width, hidden_count)
    hidden_chunks, width_chunks = hidden_count // unit, width // unit

    def swap(value, distance):
        return lax.ppermute(value, "seq", [(i, i ^ distance) for i in range(n)])

    def swap_mlp(value, distance):
        return lax.ppermute(value, "mlp", [(i, i ^ distance) for i in range(m)])

    def between_planes(pieces):
        return [pieces[0]] + [swap(pieces[d], d * side) for d in range(1, PLANES)]

    def in_plane(pieces):
        return [pieces[0]] + [swap(pieces[e], e) for e in range(1, side)]

    def in_order(blocks, axis):
        halves = jnp.stack(blocks)
        for bit in bits_of(len(blocks)):
            here = halves.reshape((len(blocks) // (2 * bit), 2, bit) + halves.shape[1:])
            halves = jnp.where((axis & bit) != 0, here[:, ::-1], here).reshape(halves.shape)
        return halves

    def for_plane(values):
        return [pick(values, jnp.minimum(plane ^ d, MICRO - 1)) for d in range(PLANES)]

    def columns_of(value):
        return [value[:, at : at + unit] for at in range(0, value.shape[1], unit)]

    pieces = for_plane(tokens[:, 0])
    own_low = jnp.concatenate(between_planes(pieces), 0)
    token_blocks = {0: own_low}
    for bit in reversed(bits_of(side)):
        for known in list(token_blocks):
            token_blocks[known | bit] = swap(token_blocks[known], bit)
    token_blocks = [token_blocks[at] for at in range(side)]

    by_group = w_qkv.reshape(rows, 3, GROUPS, WIDTH).transpose(2, 0, 1, 3).reshape(GROUPS, rows, 3 * WIDTH)
    received = in_plane([pick(by_group, (spot ^ e) % GROUPS) for e in range(side)])
    received = jnp.stack(received)
    weight_blocks = {0: jnp.concatenate([pick(received, spot ^ at) for at in range(side)], 0)}
    for bit in (2, 1):
        for known in list(weight_blocks):
            weight_blocks[known | bit] = swap(weight_blocks[known], bit * side)
    weight_blocks = [weight_blocks[at] for at in range(PLANES)]

    first = jnp.stack(columns_of(w_up) + columns_of(w_proj))
    second = jnp.stack(columns_of(w_down.T))
    first, second = after((first, second), own_low)
    pairwise = rows % 16 == 0 and side == 4 and unit == width
    if pairwise:
        z_bits, y_bit, core_bit = (2 * side, side), 2, 1
        blocks = {0: first}
        for bit in z_bits:
            for known in list(blocks):
                blocks[known | bit] = swap(blocks[known], bit)
        line = jnp.stack([blocks[d * side] for d in range(PLANES)])
        sources, layout = [line, swap(line, y_bit)], [[d * side + at for d in range(PLANES)] for at in (0, y_bit)]
        sources += [swap(source, core_bit) for source in sources]
        layout += [[at + core_bit for at in some] for some in layout]
        full_up, full_proj = call(
            functools.partial(
                assemble_kernel, layout=layout, outs=[(0, at) for at in range(hidden_chunks)] + [(1, 0)]
            ),
            "assemble_up",
            sources,
            [place],
            [shape_of((width, hidden_count), BF16), shape_of((width, width), BF16)],
            us=4.0,
        )
        blocks = {0: after(jnp.stack([second, swap(second, y_bit)]), weight_blocks)}
        for bit in z_bits:
            for known in list(blocks):
                blocks[known | bit] = swap(blocks[known], bit)
        sources = [blocks[d * side] for d in range(PLANES)]
        layout = [[d * side, d * side + y_bit] for d in range(PLANES)]
        sources += [swap(source, core_bit) for source in sources]
        layout += [[at + core_bit for at in some] for some in layout]
        (full_down,) = call(
            functools.partial(assemble_kernel, layout=layout, outs=[(0, at) for at in range(hidden_chunks)]),
            "assemble_down",
            sources,
            [place],
            [shape_of((width, hidden_count), BF16)],
            us=3.0,
        )
    else:
        gathered = lax.all_gather(jnp.concatenate([first, second]), "seq", axis=0)
        gathered = gathered.transpose(1, 0, 2, 3).reshape(-1, width, unit)

        def side_by_side(start, number):
            return jnp.concatenate([gathered[start + at] for at in range(number)], -1)

        full_up = side_by_side(0, hidden_chunks)
        full_proj = side_by_side(hidden_chunks, width_chunks)
        full_down = side_by_side(hidden_chunks + width_chunks, hidden_chunks)

    line = [value[None] for value in (b_ada, gain_one, gain_two, b_down)]
    (small,) = call(
        modulation_kernel,
        "modulation",
        [time_table, w_ada, *line, token_mask[:, 0]],
        [time_index],
        [shape_of((8, SMALL), F32)],
    )
    small = small[None]
    for bit in bits_of(n):
        small = jnp.concatenate([small, swap(small, bit)], 0)
    vectors, scale = call(
        vectors_kernel,
        "vectors",
        [small],
        [place, weight_index, weight_grid],
        [shape_of((16, width), F32), shape_of((count, 1), F32)],
        [pltpu.VMEM((8, count), F32)],
    )

    order = ((plane ^ jnp.arange(PLANES))[None, :] * side + (spot ^ jnp.arange(side))[:, None]) * shard
    positions = (order[:, :, None] + jnp.arange(shard)).reshape(1, -1).astype(F32)
    frequency = 10000.0 ** (-jnp.arange(0, HEAD, 2).astype(F32) / HEAD)
    angles = frequency[:, None] * positions
    cosine, sines = jnp.cos(angles), jnp.sin(angles)

    mixed_blocks, kept = attend_forward(place, token_blocks, weight_blocks, vectors, cosine, sines)

    full_ada = lax.all_gather(w_ada, "seq", axis=0)
    full_ada, *mixed_blocks = lax.optimization_barrier((full_ada, *mixed_blocks))

    mixed_blocks = in_plane(mixed_blocks)

    own_upstream = between_planes(after(for_plane(upstream[:, 0]), weight_blocks))
    own_upstream = jnp.concatenate(own_upstream, 0)
    d_rows = ((own_upstream.astype(F32) * scale) * vectors[GATE_TWO][None]).astype(BF16)
    d_rows = [d_rows] + [swap_mlp(d_rows, d) for d in range(1, m)]

    attended, middle, normed_two = call(
        project_kernel,
        "project",
        [full_proj, own_low, vectors, *mixed_blocks],
        [place],
        [shape_of((count, width), F32), shape_of((count, width), F32), shape_of((count, width), BF16)],
        us=3.0,
    )
    rows_all = [normed_two] + [swap_mlp(normed_two, d) for d in range(1, m)]
    bias_up = b_up.astype(F32)[None]
    fed = [
        call(
            feed_kernel,
            "feed_forward",
            [full_up, full_down, rows_all[d], d_rows[d], bias_up],
            [],
            [shape_of((count, width), BF16 if d else F32)] * 2 + [shape_of((count, hidden_count), BF16)] * 2,
            us=6.0,
        )
        for d in range(m)
    ]
    d_arrived = [swap_mlp(fed[d][1], d) for d in range(1, m)]
    out_arrived = [swap_mlp(fed[d][0], d) for d in range(1, m)]
    slots = n // 2
    if pairwise:
        down_shapes = [shape_of((slots, hidden_chunks, rows, unit), BF16)] * 2
        up_shapes = [shape_of((slots, hidden_chunks + width_chunks, rows, unit), BF16)] * 2
    else:
        down_shapes = [shape_of((width, hidden_count), BF16)]
        up_shapes = [shape_of((width, hidden_count), BF16), shape_of((width, width), BF16)]
    down_grads = call(
        functools.partial(down_grads_kernel, blocks=m, scatter=pairwise),
        "down_gradients",
        [*d_rows, *[f[2] for f in fed]],
        [place],
        down_shapes,
        us=4.0,
    )
    d_arrived, *down_grads = lax.optimization_barrier((d_arrived, *down_grads))
    middle_outs = call(
        functools.partial(middle_kernel, others=m - 1),
        "middle_backward",
        [full_proj, vectors, own_upstream, scale, attended, middle, fed[0][1], *d_arrived],
        [place],
        [shape_of((count, WIDTH), BF16)] * side
        + [shape_of((count, width), F32), shape_of((count, width), BF16), shape_of((8, width), F32)],
        us=4.0,
    )
    d_mixed_blocks, (d_middle, d_attended, middle_sums) = middle_outs[:side], middle_outs[side:]

    d_mixed_blocks = in_plane(d_mixed_blocks)
    if side > GROUPS:
        share = (spot < GROUPS).astype(BF16)
        d_mixed_blocks = [block * share for block in d_mixed_blocks]

    *up_grads, bias_up_sum = call(
        functools.partial(up_grads_kernel, blocks=m, side=side, scatter=pairwise),
        "up_gradients",
        [d_attended, *mixed_blocks, *rows_all, *[f[3] for f in fed]],
        [place],
        up_shapes + [shape_of((1, hidden_count), F32)],
        [pltpu.VMEM((width, width), BF16)],
        us=5.0,
    )

    def add_halves(own, arrived):
        half = own.shape[0] // 2
        return add(own[:half], arrived[:half]), add(own[half:], arrived[half:])

    def back_to_tokens(value):
        received = between_planes([value[d * shard : (d + 1) * shard] for d in range(PLANES)])
        received = jnp.stack(received)
        return jnp.stack([pick(received, plane ^ at) for at in range(MICRO)])[:, None]

    if pairwise:
        down_arrived = swap(down_grads[1], core_bit)
        up_own, up_sent, down_arrived, out_arrived, *d_mixed_blocks = lax.optimization_barrier(
            (*up_grads, down_arrived, out_arrived, *d_mixed_blocks)
        )
        up_arrived = swap(up_sent, core_bit)
        down_own, down_sent = add_halves(down_grads[0], down_arrived)

    result, output_sums = call(
        functools.partial(output_kernel, others=m - 1),
        "output",
        [vectors, own_upstream, scale, middle, fed[0][0], *out_arrived],
        [],
        [shape_of((count, width), BF16), shape_of((8, width), F32)],
    )
    if pairwise:
        up_own, up_sent = add_halves(up_own, after(up_arrived, result, down_sent))
        down_sent, up_sent, result, *d_mixed_blocks = lax.optimization_barrier(
            (down_sent, up_sent, result, *d_mixed_blocks)
        )
    result = back_to_tokens(result)

    d_kept, d_sent, sums, d_project = attend_backward(token_blocks, d_mixed_blocks, kept, cosine, sines)
    if pairwise:
        down_arrived, up_arrived = swap(down_sent, side), swap(up_sent, y_bit)
        d_sent, sums, result, down_arrived, up_arrived = lax.optimization_barrier(
            (d_sent, sums, result, down_arrived, up_arrived)
        )
        arrived = swap(d_sent, core_bit)
        down_own, down_sent = add_halves(down_own, down_arrived)
        up_own, up_sent = add_halves(up_own, up_arrived)
        d_project, down_sent, up_sent = lax.optimization_barrier((d_project, down_sent, up_sent))
    else:
        arrived = swap(d_sent, 1)
    (grad_own, grad_sent) = call(
        qkv_grads_kernel,
        "qkv_gradients",
        [d_project, kept[2]],
        [place],
        [shape_of((2, width // PLANES, 3 * WIDTH), BF16)] * 2,
        us=2.0,
    )
    blocks = {2 * at: d_kept[at] for at in range(side // 2)}
    steps = [arrived]
    for at in range(side // 2):
        blocks[2 * at] = add(blocks[2 * at], arrived[at])
    for bit in bits_of(side)[1:]:
        for at in [at for at in blocks if at & bit]:
            arrived = swap(blocks.pop(at), bit)
            steps.append(arrived)
            if len(blocks) > 1:
                blocks[at ^ bit] = add(blocks[at ^ bit], arrived)
    (d_tokens,) = call(
        tokens_kernel,
        "tokens_backward",
        [vectors, own_low, d_middle, blocks[0], arrived],
        [],
        [shape_of((count, width), BF16)],
    )

    if pairwise:
        arrived = after((swap(down_sent, 2 * side), swap(up_sent, side)), steps[0])
        down_own, down_sent = add_halves(down_own, arrived[0])
        up_own, up_sent = add_halves(up_own, arrived[1])
        down_parts = down_own[0].astype(F32) + swap(down_sent, y_bit)[0].astype(F32)
        up_parts = up_own[0].astype(F32) + swap(up_sent, 2 * side)[0].astype(F32)
        grad_up = jnp.concatenate([up_parts[at] for at in range(hidden_chunks)], -1)
        grad_down = jnp.concatenate([down_parts[at] for at in range(hidden_chunks)], -1).T
        grad_proj = up_parts[hidden_chunks]
    else:
        grads = jnp.stack(columns_of(up_grads[0]) + columns_of(down_grads[0]) + columns_of(up_grads[1]))
        grads = grads.reshape(-1, n, rows, unit).transpose(1, 0, 2, 3)
        grads = lax.psum_scatter(grads, "seq", scatter_dimension=0, tiled=True)[0]

        def columns_from(start, number):
            return jnp.concatenate([grads[start + at] for at in range(number)], -1).astype(F32)

        grad_up = columns_from(0, hidden_chunks)
        grad_down = columns_from(hidden_chunks, hidden_chunks).T
        grad_proj = columns_from(2 * hidden_chunks, width_chunks)
    for bit in bits_of(m):
        grad_proj = grad_proj + swap_mlp(grad_proj.astype(BF16), bit).astype(F32)

    arrived = after(swap(grad_sent, side), steps[0])
    arrived = swap(add(grad_own[1], arrived[1]), 2 * side).astype(F32) + arrived[0].astype(F32)
    total = grad_own[0].astype(F32) + arrived
    by_spot = after(total.astype(BF16), steps[-1]).reshape(side, rows, 3 * WIDTH)
    received = jnp.stack(in_plane([pick(by_spot, spot ^ e) for e in range(side)]))
    grad_qkv = jnp.stack([pick(received, spot ^ group) for group in range(GROUPS)])
    grad_qkv = grad_qkv.reshape(GROUPS, rows, 3, WIDTH).transpose(1, 2, 0, 3).reshape(rows, 3 * width)
    grad_qkv = grad_qkv.astype(F32)
    for bit in bits_of(m):
        grad_qkv = grad_qkv + swap_mlp(grad_qkv.astype(BF16), bit).astype(F32)

    bias_up_rows = -(-hidden_count // width)
    bias_up_sum = jnp.pad(bias_up_sum, ((0, 0), (0, bias_up_rows * width - hidden_count)))
    small = jnp.concatenate(
        [sums[0:2], middle_sums[0:3], output_sums[0:2], bias_up_sum.reshape(-1, width)], 0
    )
    small = small + swap(small, 1)
    small = after(small, steps[0])
    for bit in bits_of(side)[1:]:
        small = small + swap(small, bit)
    small = jnp.concatenate([small, vectors[SCALE_TWO][None]], 0)[None]
    small = after(small, steps[-1])
    for bit in bits_of(PLANES):
        small = jnp.concatenate([small, swap(small, bit * side)], 0)
    small = in_order(list(small), plane)[:MICRO]
    grad_bias_up = jnp.sum(small[:, 7 : 7 + bias_up_rows], 0).reshape(-1)[:hidden_count]
    d_shift_one, d_xhat_one, d_gate_one, d_shift_two, d_xhat_two, d_gate_two = [small[:, at] for at in range(6)]
    index_here = time_index[:, 0]
    vector_sums = jnp.stack(
        [
            jnp.sum((1.0 + vectors[SCALES_ALL : SCALES_ALL + MICRO]) * d_xhat_one, 0),
            jnp.sum((1.0 + small[:, -1]) * d_xhat_two, 0),
            jnp.sum(small[:, 6], 0),
            jnp.pad(index_here.astype(F32), (0, width - MICRO)),
        ]
    )
    d_scale_one, d_scale_two = vectors[GAIN_ONE] * d_xhat_one, vectors[GAIN_TWO] * d_xhat_two
    small = jnp.stack([d_shift_one, d_scale_one, d_gate_one, d_shift_two, d_scale_two, d_gate_two], 1)
    small = jnp.concatenate([small.reshape(6 * MICRO, width), vector_sums], 0)[None]
    for bit in bits_of(m):
        small = jnp.concatenate([small, swap_mlp(small, bit)], 0)
    at = 6 * MICRO
    d_modulation = small[:, :at].reshape(m * MICRO, n, ada_columns)
    vector_sums = jnp.sum(small[:, at : at + 3], 0)
    index_all = small[:, at + 3, :MICRO].reshape(-1).astype(jnp.int32)
    onehot = (index_all[:, None] == jnp.arange(grid_size)[None, :]).astype(BF16)
    cond = jnp.dot(onehot, time_table, preferred_element_type=F32)
    d_modulation_own = lax.dynamic_index_in_dim(d_modulation, me, 1, keepdims=False)
    grad_ada = jnp.dot(cond.T, d_modulation_own, precision=highest)
    grad_bias_ada = jnp.sum(d_modulation_own, 0)
    d_cond = jnp.einsum("bic,idc->bd", d_modulation, full_ada.astype(F32), precision=highest)
    table_rows = grid_size // n
    onehot_own = index_all[None, :] == (me * table_rows + jnp.arange(table_rows))[:, None]
    grad_table = jnp.dot(onehot_own.astype(F32), d_cond, precision=highest)
    vector_sums = lax.dynamic_slice_in_dim(vector_sums, me * rows, rows, 1)
    return (
        result,
        back_to_tokens(d_tokens).astype(F32),
        grad_table,
        grad_ada,
        grad_bias_ada,
        vector_sums[0],
        vector_sums[1],
        grad_qkv,
        grad_proj,
        grad_up,
        grad_bias_up,
        grad_down,
        vector_sums[2],
    )


def solution(mesh):
    in_specs = (
        P(None, "mlp", "seq", None),
        P(None, "mlp", "seq", None),
        P(None, "mlp", "seq"),
        P(None, "mlp"),
        P(None, "mlp"),
        P(),
        P(),
        P(None, "seq"),
        P("seq"),
        P("seq"),
        P("seq"),
        P("seq", None),
        P("seq", None),
        P("seq", "mlp"),
        P("mlp"),
        P("mlp", "seq"),
        P("seq"),
    )
    out_specs = (
        P(None, "mlp", "seq", None),
        P(None, "mlp", "seq", None),
        P("seq", None),
        P(None, "seq"),
        P("seq"),
        P("seq"),
        P("seq"),
        P("seq", None),
        P("seq", None),
        P("seq", "mlp"),
        P("mlp"),
        P("mlp", "seq"),
        P("seq"),
    )
    run = functools.partial(body, n=mesh.shape["seq"], m=mesh.shape["mlp"])
    return jax.shard_map(run, mesh=mesh, in_specs=in_specs, out_specs=out_specs, check_vma=False)
```

```python
import functools
import math

import jax
import jax.numpy as jnp
from jax import lax
from jax.experimental import pallas as pl
from jax.experimental.pallas import tpu as pltpu
from jax.sharding import PartitionSpec as P

HEADS = 12
HEAD = 64
MICRO = 3
PLANES = 4
GROUPS = 4
PER_GROUP = HEADS // GROUPS
WIDTH = PER_GROUP * HEAD
QUERY_BLOCK = 256
SCALING = HEAD ** (-0.5)
BF16 = jnp.bfloat16
F32 = jnp.float32
highest = lax.Precision.HIGHEST
SLOPE = math.sqrt(2.0 / math.pi)
CUBIC = 0.044715

SHIFT_ONE, SCALE_ONE, GATE_ONE, SHIFT_TWO, SCALE_TWO, GATE_TWO, GAIN_ONE, GAIN_TWO, BIAS_DOWN = range(9)
SCALES_ALL, GAINS_ONE, GAINS_TWO = 9, 12, 13

VMEM = pl.BlockSpec(memory_space=pltpu.VMEM)
SMEM = pl.BlockSpec(memory_space=pltpu.SMEM)


def nn(left, right):
    return lax.dot_general(left, right, (((1,), (0,)), ((), ())), preferred_element_type=F32)


def nt(left, right):
    return lax.dot_general(left, right, (((1,), (1,)), ((), ())), preferred_element_type=F32)


def standardize(inputs):
    average = jnp.mean(inputs, -1, keepdims=True)
    centred = inputs - average
    spread = jnp.mean(centred * centred, -1, keepdims=True)
    root = lax.rsqrt(spread + 1e-06)
    return centred * root, root


def pull_norm(d_normed, gains, xhat, root):
    e = d_normed * gains
    return root * (e - jnp.mean(e, -1, keepdims=True) - xhat * jnp.mean(e * xhat, -1, keepdims=True))


def over_tokens(value):
    return jnp.sum(value, 0, keepdims=True)


def shape_of(dims, dtype):
    return jax.ShapeDtypeStruct(dims, dtype)


def call(kernel, name, operands, scalars, outs, scratch=(), us=1.0, far=()):
    moved = sum(math.prod(o.shape) * o.dtype.itemsize for o in list(operands) + list(outs))
    return pl.pallas_call(
        kernel,
        out_shape=list(outs),
        in_specs=[SMEM] * len(scalars) + [pl.BlockSpec(memory_space=pl.ANY)] * len(far) + [VMEM] * len(operands),
        out_specs=[VMEM] * len(outs),
        scratch_shapes=list(scratch),
        compiler_params=pltpu.CompilerParams(vmem_limit_bytes=56 * 1024 * 1024),
        cost_estimate=pl.CostEstimate(flops=int(us * 1e9), bytes_accessed=moved, transcendentals=0),
        name=name,
    )(*scalars, *far, *operands)


def fetch(gathered, chunks, weights, arrived):
    copies = [
        pltpu.make_async_copy(gathered.at[:, chunk], weights.at[at], arrived.at[at])
        for at, chunk in enumerate(chunks)
    ]
    for copy in copies:
        copy.start()
    return copies


def whole(weights, at):
    return weights[at].reshape(weights.shape[1] * weights.shape[2], weights.shape[3])


def group_rows(weights, group):
    blocks = WIDTH // weights.shape[2]
    parts = [
        weights[at, pl.ds(group * blocks, blocks)].reshape(WIDTH, weights.shape[3])
        for at in range(weights.shape[0])
    ]
    return parts[0] if len(parts) == 1 else jnp.concatenate(parts, -1)


def modulation_kernel(times, table, w_ada, b_ada, gain_one, gain_two, b_down, mask, small):
    columns = w_ada.shape[1]
    rows = gain_one.shape[1]
    at = lax.broadcasted_iota(jnp.int32, (8, table.shape[0]), 1)
    line = lax.broadcasted_iota(jnp.int32, (8, table.shape[0]), 0)
    wanted = jnp.where(line == 0, times[0, 0], jnp.where(line == 1, times[1, 0], times[2, 0]))
    cond = nn((at == wanted).astype(F32).astype(BF16), table[...]).astype(BF16)
    part = nn(cond, w_ada[...]) + b_ada[...].astype(F32)
    small[...] = jnp.zeros_like(small)
    at = 0
    for s in range(MICRO):
        small[0:1, at : at + columns] = part[s : s + 1]
        at += columns
    for ref in (gain_one, gain_two, b_down):
        small[0:1, at : at + rows] = ref[...].astype(F32)
        at += rows
    for s in range(MICRO):
        small[0:1, at : at + mask.shape[1]] = mask[s : s + 1, :].astype(F32)
        at += mask.shape[1]


def vectors_kernel(place, weight_index, weight_grid, small, vectors, scale, line):
    n = small.shape[0]
    width = vectors.shape[1]
    columns, rows, shard = 6 * width // n, width // n, scale.shape[0] // PLANES
    plane, spot = place[0], place[1]
    side = n // PLANES
    me = plane * side + spot
    last = jnp.minimum(plane, MICRO - 1)

    def one_of(three):
        return jnp.where(last == 0, three[0], jnp.where(last == 1, three[1], three[2]))

    def pieces(first, size):
        start = first
        while start < first + size:
            stop = min(first + size, (start // width + 1) * width)
            yield start // width, start % width, start - first, stop - start
            start = stop

    vectors[...] = jnp.zeros_like(vectors)
    for i in range(n):
        here = small[pl.ds(me ^ i, 1), :]
        each = [here[:, s * columns : (s + 1) * columns] for s in range(MICRO)]
        mine = one_of(each)
        for part, column, offset, size in pieces(i * columns, columns):
            vectors[part : part + 1, column : column + size] = mine[:, offset : offset + size]
            if part == SCALE_ONE:
                for s in range(MICRO):
                    vectors[SCALES_ALL + s : SCALES_ALL + s + 1, column : column + size] = each[s][
                        :, offset : offset + size
                    ]
        for row in (GAIN_ONE, GAIN_TWO, BIAS_DOWN):
            start = MICRO * columns + (row - GAIN_ONE) * rows
            vectors[row : row + 1, i * rows : (i + 1) * rows] = here[:, start : start + rows]
    for to, gain, by in ((GAINS_ONE, GAIN_ONE, SCALE_ONE), (GAINS_TWO, GAIN_TWO, SCALE_TWO)):
        vectors[to : to + 1, :] = vectors[gain : gain + 1, :] * (1.0 + vectors[by : by + 1, :])
    line[...] = jnp.zeros_like(line)
    for d in range(PLANES):
        here = small[d * side : d * side + 1, :]
        start = MICRO * (columns + rows)
        three = [here[:, start + s * shard : start + (s + 1) * shard] for s in range(MICRO)]
        line[0:1, d * shard : (d + 1) * shard] = one_of(three)
    weight = jnp.where(plane < MICRO, weight_grid[weight_index[last, 0]], 0.0)
    scale[...] = line[...].T[:, 0:1] * weight


def project_kernel(place, gathered, tokens, vectors, *refs, chunks):
    side = len(refs) - 5
    mixed, (attended, middle, normed, weights, arrived) = refs[:side], refs[side:]
    spot = place[1]
    copies = fetch(gathered, chunks, weights, arrived)
    for copy in copies:
        copy.wait()
    total = jnp.zeros(attended.shape, F32)
    for e in range(side):
        other = spot ^ e
        block = mixed[e][...]
        if side > GROUPS:
            block = jnp.where(other < GROUPS, block, jnp.zeros_like(block))
        total = total + nn(block, group_rows(weights, other % GROUPS))
    attended[...] = total
    after = tokens[...].astype(F32) + vectors[GATE_ONE : GATE_ONE + 1] * total
    middle[...] = after
    xhat, _ = standardize(after)
    normed[...] = (xhat * vectors[GAINS_TWO : GAINS_TWO + 1] + vectors[SHIFT_TWO : SHIFT_TWO + 1]).astype(BF16)


def feed_kernel(gathered, rows, d_rows, bias, output, d_normed, active, d_hidden, weights, arrived):
    parts = weights.shape[0] // 2
    unit = weights.shape[3]
    order = [at for part in range(parts) for at in (part, parts + part)]
    copies = fetch(gathered, order, weights, arrived)
    out = jnp.zeros(output.shape, F32)
    back = jnp.zeros(output.shape, F32)
    for part in range(parts):
        columns = slice(part * unit, (part + 1) * unit)
        copies[2 * part].wait()
        up = whole(weights, 2 * part)
        u = nn(rows[...], up) + bias[:, columns]
        square = u * u
        bent = jnp.tanh(SLOPE * u * (1.0 + CUBIC * square))
        half = 0.5 * (1.0 + bent)
        on = (u * half).astype(BF16)
        active[:, columns] = on
        slope = half + 0.5 * u * (1.0 - bent * bent) * (SLOPE * (1.0 + 3.0 * CUBIC * square))
        copies[2 * part + 1].wait()
        down = whole(weights, 2 * part + 1)
        d_on = (nn(d_rows[...], down) * slope).astype(BF16)
        d_hidden[:, columns] = d_on
        out = out + nt(on, down)
        back = back + nt(d_on, up)
    output[...] = out.astype(output.dtype)
    d_normed[...] = back.astype(d_normed.dtype)


def scatter_store(refs, me, device, value):
    kept, sent, chunk, slot_of = refs
    distance = me ^ device
    slot = slot_of(distance)

    @pl.when(distance % 2 == 0)
    def _():
        kept[slot, chunk] = value

    @pl.when(distance % 2 == 1)
    def _():
        sent[slot, chunk] = value


def slot_y_first(distance):
    return ((distance >> 1) & 1) * 4 + ((distance >> 2) & 1) * 2 + ((distance >> 3) & 1)


def down_grads_kernel(*refs, blocks):
    d_rows, active, out = refs[:blocks], refs[blocks:-1], refs[-1]
    unit = out.shape[3]
    turned = [ref[...].T for ref in d_rows]
    for chunk in range(out.shape[1]):
        columns = slice(chunk * unit, (chunk + 1) * unit)
        grad = sum(nn(turned[b], active[b][:, columns]) for b in range(blocks)).astype(BF16)
        out[:, chunk] = grad.reshape(out.shape[0], out.shape[2], unit)


def up_grads_kernel(place, d_attended, *refs, blocks, side, scatter):
    mixed, refs = refs[:side], refs[side:]
    rows_all, d_hidden = refs[:blocks], refs[blocks : 2 * blocks]
    outs, whole = refs[2 * blocks : -1], refs[-1]
    bias = outs[-1]
    spot, me = place[1], place[2]
    width, count = rows_all[0].shape[1], bias.shape[1]
    unit = min(width, count)
    turned = [ref[...].T for ref in rows_all]
    for chunk in range(count // unit):
        columns = slice(chunk * unit, (chunk + 1) * unit)
        grad = sum(nn(turned[b], d_hidden[b][:, columns]) for b in range(blocks)).astype(BF16)
        bias[:, columns] = sum(over_tokens(d_hidden[b][:, columns].astype(F32)) for b in range(blocks))
        if scatter:
            rows = outs[0].shape[2]
            for i in range(width // rows):
                part = grad[i * rows : (i + 1) * rows]
                scatter_store((outs[0], outs[1], chunk, slot_y_first), me, i, part)
        else:
            outs[0][:, columns] = grad
    if side > GROUPS:
        whole[...] = jnp.zeros_like(whole)
    for e in range(side):
        other = spot ^ e
        first = pl.multiple_of((other % GROUPS) * WIDTH, WIDTH)
        grad = nn(mixed[e][...].T, d_attended[...]).astype(BF16)
        if side > GROUPS:
            grad = whole[pl.ds(first, WIDTH), :] + jnp.where(other < GROUPS, grad, jnp.zeros_like(grad))
        whole[pl.ds(first, WIDTH), :] = grad
    if scatter:
        for i in range(width // rows):
            part = whole[i * rows : (i + 1) * rows, :]
            scatter_store((outs[0], outs[1], count // unit, slot_y_first), me, i, part)
    else:
        outs[1][...] = whole[...]


def qkv_grads_kernel(place, d_project, normed, *outs):
    grad = nn(d_project[...], normed[...]).astype(BF16).T
    plane = place[0]
    rows = outs[0].shape[1]
    for at in range(PLANES):
        part = grad[at * rows : (at + 1) * rows]
        distance = plane ^ at

        @pl.when(distance % 2 == 0)
        def _():
            outs[0][distance // 2] = part

        @pl.when(distance % 2 == 1)
        def _():
            outs[1][distance // 2] = part


def normed_backward_kernel(d_project, weight, *refs, blocks):
    tokens, (kept, sent, sums) = refs[:blocks], refs[blocks:]
    count = tokens[0].shape[0]
    d_shift = jnp.zeros((1, weight.shape[0]), F32)
    d_xhat = jnp.zeros((1, weight.shape[0]), F32)
    for block in range(blocks):
        part = nt(d_project[:, block * count : (block + 1) * count].T, weight[...])
        (sent if block % 2 else kept)[block // 2] = part.astype(BF16)
        xhat, _ = standardize(tokens[block][...].astype(F32))
        d_shift = d_shift + over_tokens(part)
        d_xhat = d_xhat + over_tokens(part * xhat)
    sums[0:1, :] = d_shift
    sums[1:2, :] = d_xhat
    sums[2:8, :] = jnp.zeros((6, weight.shape[0]), F32)


def middle_kernel(place, gathered, vectors, upstream, scale, attended, middle, d_own, *refs, others, chunks):
    arrived, refs = refs[:others], refs[others:]
    d_mixed, (d_middle, d_attended, sums, weights, copied) = refs[:-5], refs[-5:]
    spot = place[1]
    copies = fetch(gathered, chunks, weights, copied)
    width = middle.shape[1]
    d_normed = d_own[...]
    for ref in arrived:
        d_normed = d_normed + ref[...].astype(F32)
    xhat, root = standardize(middle[...])
    d_result = upstream[...].astype(F32) * scale[...]
    d_after = d_result + pull_norm(d_normed, vectors[GAINS_TWO : GAINS_TWO + 1], xhat, root)
    d_middle[...] = d_after
    low = (vectors[GATE_ONE : GATE_ONE + 1] * d_after).astype(BF16)
    d_attended[...] = low
    for copy in copies:
        copy.wait()
    for e in range(len(d_mixed)):
        d_mixed[e][...] = nt(low, group_rows(weights, (spot ^ e) % GROUPS)).astype(BF16)
    sums[0:1, :] = over_tokens(d_after * attended[...])
    sums[1:2, :] = over_tokens(d_normed)
    sums[2:3, :] = over_tokens(d_normed * xhat)
    sums[3:8, :] = jnp.zeros((5, width), F32)


def output_kernel(vectors, upstream, scale, middle, own, *refs, others):
    arrived, (result, sums) = refs[:others], refs[others:]
    output = own[...] + vectors[BIAS_DOWN : BIAS_DOWN + 1]
    for ref in arrived:
        output = output + ref[...].astype(F32)
    gate = vectors[GATE_TWO : GATE_TWO + 1]
    result[...] = (middle[...] + gate * output).astype(BF16)
    d_result = upstream[...].astype(F32) * scale[...]
    sums[0:1, :] = over_tokens(d_result * output)
    sums[1:2, :] = over_tokens(gate * d_result)
    sums[2:8, :] = jnp.zeros((6, middle.shape[1]), F32)


def tokens_kernel(vectors, tokens, d_middle, own, arrived, d_tokens):
    xhat, root = standardize(tokens[...].astype(F32))
    d_normed = own[...].astype(F32) + arrived[...].astype(F32)
    back = pull_norm(d_normed, vectors[GAINS_ONE : GAINS_ONE + 1], xhat, root)
    d_tokens[...] = (d_middle[...] + back).astype(BF16)


def forward_kernel(place, *refs, blocks, halves):
    tokens, refs = refs[:blocks], refs[blocks:]
    count = 2 if halves else PLANES
    weights, refs = refs[:count], refs[count:]
    (vectors, cosine, sines), refs = refs[:3], refs[3:]
    gain, shift = vectors[GAINS_ONE : GAINS_ONE + 1], vectors[SHIFT_ONE : SHIFT_ONE + 1]
    mixed, refs = refs[:blocks], refs[blocks:]
    heads, log_total, normed, weight, keys, mixed_turned = refs
    plane = place[0]
    rows = weights[0].shape[-2]
    count = tokens[0].shape[0]
    if halves:
        for half in range(2):
            for distance in range(PLANES):
                first = pl.multiple_of((plane ^ distance) * 2 * rows + (place[3] ^ half) * rows, 16)
                weight[pl.ds(first, rows), :] = weights[half][distance]
    else:
        for distance in range(PLANES):
            first = pl.multiple_of((plane ^ distance) * rows, 8)
            weight[pl.ds(first, rows), :] = weights[distance][...]
    for block in range(blocks):
        xhat, _ = standardize(tokens[block][...].astype(F32))
        normed[block * count : (block + 1) * count, :] = (xhat * gain + shift).astype(BF16)
    project = nt(weight[...].T, normed[...])
    cos, sin = cosine[...], sines[...]
    half = HEAD // 2
    for part in range(2):
        for head in range(PER_GROUP):
            start = part * WIDTH + head * HEAD
            first, second = project[start : start + half], project[start + half : start + HEAD]
            turned = jnp.concatenate([first * cos - second * sin, second * cos + first * sin], 0).astype(BF16)
            if part == 0:
                turned = turned * jnp.asarray(SCALING, BF16)
            else:
                keys[head] = turned.T
            heads[start : start + HEAD, :] = turned
    heads[2 * WIDTH :, :] = project[2 * WIDTH :].astype(BF16)
    length = heads.shape[1]
    for head in range(PER_GROUP):
        start = head * HEAD

        def queries_step(step, carry):
            columns = pl.ds(pl.multiple_of(step * QUERY_BLOCK, QUERY_BLOCK), QUERY_BLOCK)
            scores = nn(keys[head], heads[start : start + HEAD, columns])
            peak = jnp.max(scores, 0, keepdims=True)
            exps = jnp.exp(scores - peak)
            total = jnp.sum(exps, 0, keepdims=True)
            log_total[head : head + 1, columns] = peak + jnp.log(total)
            probs = (exps * (1.0 / total)).astype(BF16)
            values = heads[2 * WIDTH + start : 2 * WIDTH + start + HEAD, :]
            mixed_turned[start : start + HEAD, columns] = nn(values, probs).astype(BF16)
            return carry

        lax.fori_loop(0, length // QUERY_BLOCK, queries_step, 0)
    for block in range(blocks):
        mixed[block][...] = mixed_turned[:, block * count : (block + 1) * count].T


def backward_kernel(*refs, blocks):
    d_mixed, refs = refs[:blocks], refs[blocks:]
    (heads, log_total, cosine, sines), refs = refs[:4], refs[4:]
    d_project, d_turned, d_keys, d_values, keys, values = refs
    count = d_mixed[0].shape[0]
    length = heads.shape[1]
    for block in range(blocks):
        d_turned[:, block * count : (block + 1) * count] = d_mixed[block][...].T
    cos, sin = cosine[...], sines[...]
    half = HEAD // 2
    d_keys[...] = jnp.zeros_like(d_keys)
    d_values[...] = jnp.zeros_like(d_values)
    for head in range(PER_GROUP):
        start = head * HEAD
        keys_turned = heads.at[WIDTH + start : WIDTH + start + HEAD]
        keys[...] = keys_turned[...].T
        values[...] = heads[2 * WIDTH + start : 2 * WIDTH + start + HEAD, :].T

        def queries_step(step, carry):
            columns = pl.ds(pl.multiple_of(step * QUERY_BLOCK, QUERY_BLOCK), QUERY_BLOCK)
            queries = heads[start : start + HEAD, columns]
            incoming = d_turned[start : start + HEAD, columns]
            scores = nn(keys[...], queries)
            probs = jnp.exp(scores - log_total[head : head + 1, columns])
            d_probs = nn(values[...], incoming)
            delta = jnp.sum(probs * d_probs, 0, keepdims=True)
            d_scores = (probs * (d_probs - delta)).astype(BF16)
            d_values[start : start + HEAD, :] += nt(incoming, probs.astype(BF16))
            d_keys[start : start + HEAD, :] += nt(queries, d_scores)
            d_queries = nn(keys_turned[...], d_scores) * SCALING
            first, second = d_queries[:half], d_queries[half:]
            cos_here, sin_here = cosine[:, columns], sines[:, columns]
            d_project[start : start + half, columns] = (first * cos_here + second * sin_here).astype(BF16)
            d_project[start + half : start + HEAD, columns] = (second * cos_here - first * sin_here).astype(BF16)
            return carry

        lax.fori_loop(0, length // QUERY_BLOCK, queries_step, 0)
        first, second = d_keys[start : start + half, :], d_keys[start + half : start + HEAD, :]
        d_project[WIDTH + start : WIDTH + start + half, :] = (first * cos + second * sin).astype(BF16)
        d_project[WIDTH + start + half : WIDTH + start + HEAD, :] = (second * cos - first * sin).astype(BF16)
    d_project[2 * WIDTH :, :] = d_values[...].astype(BF16)


def attend_forward(place, tokens, weights, vectors, cosine, sines, halves):
    blocks, (count, width) = len(tokens), tokens[0].shape
    length = blocks * count
    columns = weights[0].shape[-1]
    outs = call(
        functools.partial(forward_kernel, blocks=blocks, halves=halves),
        "attend_forward",
        [*tokens, *weights, vectors, cosine, sines],
        [place],
        [shape_of((count, WIDTH), BF16)] * blocks
        + [
            shape_of((columns, length), BF16),
            shape_of((8, length), F32),
            shape_of((length, width), BF16),
            shape_of((width, columns), BF16),
        ],
        [pltpu.VMEM((PER_GROUP, length, HEAD), BF16), pltpu.VMEM((WIDTH, length), BF16)],
        us=15.0,
    )
    return outs[:blocks], outs[blocks:]


def attend_backward(d_mixed, heads, log_total, cosine, sines):
    blocks, length = len(d_mixed), heads.shape[1]
    (d_project,) = call(
        functools.partial(backward_kernel, blocks=blocks),
        "attend_backward",
        [*d_mixed, heads, log_total, cosine, sines],
        [],
        [shape_of((3 * WIDTH, length), BF16)],
        [
            pltpu.VMEM((WIDTH, length), BF16),
            pltpu.VMEM((WIDTH, length), F32),
            pltpu.VMEM((WIDTH, length), F32),
            pltpu.VMEM((length, HEAD), BF16),
            pltpu.VMEM((length, HEAD), BF16),
        ],
        us=18.0,
    )
    return d_project


def after(values, *others):
    return lax.optimization_barrier((values, others))[0]


def add(left, right):
    return (left.astype(F32) + right.astype(F32)).astype(BF16)


def pick(stack, index):
    return lax.dynamic_index_in_dim(stack, index, 0, keepdims=False)


def bits_of(count):
    return [1 << bit for bit in range(count.bit_length() - 1)]


def body(
    tokens,
    upstream,
    token_mask,
    time_index,
    weight_index,
    time_table,
    weight_grid,
    w_ada,
    b_ada,
    gain_one,
    gain_two,
    w_qkv,
    w_proj,
    w_up,
    b_up,
    w_down,
    b_down,
    *,
    n,
    m,
):
    side = n // PLANES
    me = lax.axis_index("seq")
    plane, spot = me // side, me % side
    slice_of = lax.axis_index("mlp")
    place = jnp.stack([plane, spot, me, slice_of]).astype(jnp.int32)
    shard, width = tokens.shape[2], tokens.shape[3]
    rows = w_qkv.shape[0]
    hidden_count = w_up.shape[1]
    grid_size = time_table.shape[0]
    ada_columns = w_ada.shape[1]
    count = PLANES * shard
    unit = min(width, hidden_count)
    hidden_chunks, width_chunks = hidden_count // unit, width // unit
    pairwise = rows % 16 == 0 and side == GROUPS and unit == width and m == 2
    z_bits, y_bit, core_bit = (2 * side, side), 2, 1

    def swap(value, distance):
        return lax.ppermute(value, "seq", [(i, i ^ distance) for i in range(n)])

    def swap_mlp(value, distance):
        return lax.ppermute(value, "mlp", [(i, i ^ distance) for i in range(m)])

    def between_planes(pieces):
        return [pieces[0]] + [swap(pieces[d], d * side) for d in range(1, PLANES)]

    def in_plane(pieces):
        return [pieces[0]] + [swap(pieces[e], e) for e in range(1, side)]

    def in_order(blocks, axis):
        halves = jnp.stack(blocks)
        for bit in bits_of(len(blocks)):
            here = halves.reshape((len(blocks) // (2 * bit), 2, bit) + halves.shape[1:])
            halves = jnp.where((axis & bit) != 0, here[:, ::-1], here).reshape(halves.shape)
        return halves

    def for_plane(values):
        return [pick(values, jnp.minimum(plane ^ d, MICRO - 1)) for d in range(PLANES)]

    def columns_of(value):
        return [value[:, at : at + unit] for at in range(0, value.shape[1], unit)]

    packed = jnp.stack(columns_of(w_up) + columns_of(w_down.T) + columns_of(w_proj))
    gathered = lax.all_gather(packed, "seq", axis=0)
    if not pairwise:
        gathered = gathered.transpose(1, 0, 2, 3).reshape(-1, GROUPS, WIDTH, unit).transpose(1, 0, 2, 3)
    blocks_shape = (gathered.shape[0],) + gathered.shape[2:]
    proj_chunks = list(range(2 * hidden_chunks, 2 * hidden_chunks + width_chunks))

    def weight_scratch(number):
        return [pltpu.VMEM((number,) + blocks_shape, BF16), pltpu.SemaphoreType.DMA((number,))]

    pieces = for_plane(tokens[:, 0])
    own_low = jnp.concatenate(between_planes(pieces), 0)
    token_blocks = {0: own_low}
    for bit in reversed(bits_of(side)):
        for known in list(token_blocks):
            token_blocks[known | bit] = swap(token_blocks[known], bit)
    token_blocks = [token_blocks[at] for at in range(side)]

    by_group = w_qkv.reshape(rows, 3, GROUPS, WIDTH).transpose(2, 0, 1, 3).reshape(GROUPS, rows, 3 * WIDTH)
    received = in_plane([pick(by_group, (spot ^ e) % GROUPS) for e in range(side)])
    received = jnp.stack(received)
    weight_block = jnp.concatenate([pick(received, spot ^ at) for at in range(side)], 0)
    if pairwise:
        weight_block = pick(weight_block.reshape(2, width // 8, 3 * WIDTH), slice_of)
    weight_blocks = {0: weight_block}
    for bit in (2, 1):
        for known in list(weight_blocks):
            weight_blocks[known | bit] = swap(weight_blocks[known], bit * side)
    weight_blocks = [weight_blocks[at] for at in range(PLANES)]
    if pairwise:
        weight_blocks = jnp.stack(weight_blocks)
        weight_blocks = [weight_blocks, swap_mlp(weight_blocks, 1)]

    line = [value[None] for value in (b_ada, gain_one, gain_two, b_down)]
    (small,) = call(
        modulation_kernel,
        "modulation",
        [time_table, w_ada, *line, token_mask[:, 0]],
        [time_index],
        [shape_of((1, -(-MICRO * (ada_columns + rows + shard) // 128) * 128), F32)],
    )
    for bit in bits_of(n):
        small = jnp.concatenate([small, swap(small, bit)], 0)
    vectors, scale = call(
        vectors_kernel,
        "vectors",
        [small],
        [place, weight_index, weight_grid],
        [shape_of((16, width), F32), shape_of((count, 1), F32)],
        [pltpu.VMEM((8, count), F32)],
    )

    order = ((plane ^ jnp.arange(PLANES))[None, :] * side + (spot ^ jnp.arange(side))[:, None]) * shard
    positions = (order[:, :, None] + jnp.arange(shard)).reshape(1, -1).astype(F32)
    frequency = 10000.0 ** (-jnp.arange(0, HEAD, 2).astype(F32) / HEAD)
    angles = frequency[:, None] * positions
    cosine, sines = jnp.cos(angles), jnp.sin(angles)

    mixed_blocks, kept = attend_forward(
        place, token_blocks, weight_blocks, vectors, cosine, sines, pairwise
    )

    full_ada = lax.all_gather(after(w_ada, token_blocks[0]), "seq", axis=0)

    mixed_blocks = in_plane(mixed_blocks)

    own_upstream = between_planes(after(for_plane(upstream[:, 0]), weight_blocks))
    own_upstream = jnp.concatenate(own_upstream, 0)
    d_rows = ((own_upstream.astype(F32) * scale) * vectors[GATE_TWO][None]).astype(BF16)
    d_rows = [d_rows] + [swap_mlp(d_rows, d) for d in range(1, m)]

    attended, middle, normed_two = call(
        functools.partial(project_kernel, chunks=proj_chunks),
        "project",
        [own_low, vectors, *mixed_blocks],
        [place],
        [shape_of((count, width), F32), shape_of((count, width), F32), shape_of((count, width), BF16)],
        weight_scratch(width_chunks),
        us=3.0,
        far=[gathered],
    )
    rows_all = [normed_two] + [swap_mlp(normed_two, d) for d in range(1, m)]
    bias_up = b_up.astype(F32)[None]
    fed = [
        call(
            feed_kernel,
            "feed_forward",
            [rows_all[d], d_rows[d], bias_up],
            [],
            [shape_of((count, width), BF16 if d else F32)] * 2 + [shape_of((count, hidden_count), BF16)] * 2,
            weight_scratch(2 * hidden_chunks),
            us=6.0,
            far=[gathered],
        )
        for d in range(m)
    ]
    d_arrived = [swap_mlp(fed[d][1], d) for d in range(1, m)]
    out_arrived = [swap_mlp(fed[d][0], d) for d in range(1, m)]
    slots = n // 2
    down_shape = (n, hidden_chunks, rows, unit) if pairwise else (GROUPS, hidden_chunks, WIDTH, unit)
    if pairwise:
        up_shapes = [shape_of((slots, hidden_chunks + width_chunks, rows, unit), BF16)] * 2
    else:
        up_shapes = [shape_of((width, hidden_count), BF16), shape_of((width, width), BF16)]
    (down_grads,) = call(
        functools.partial(down_grads_kernel, blocks=m),
        "down_gradients",
        [*d_rows, *[f[2] for f in fed]],
        [],
        [shape_of(down_shape, BF16)],
        us=6.0,
    )
    d_arrived, down_grads = lax.optimization_barrier((d_arrived, down_grads))
    if not pairwise:
        down_grads = down_grads.transpose(1, 0, 2, 3).reshape(hidden_chunks, n, rows, unit).transpose(1, 0, 2, 3)
    down_grads = lax.psum_scatter(down_grads, "seq", scatter_dimension=0, tiled=True)
    middle_outs = call(
        functools.partial(middle_kernel, others=m - 1, chunks=proj_chunks),
        "middle_backward",
        [vectors, own_upstream, scale, attended, middle, fed[0][1], *d_arrived],
        [place],
        [shape_of((count, WIDTH), BF16)] * side
        + [shape_of((count, width), F32), shape_of((count, width), BF16), shape_of((8, width), F32)],
        weight_scratch(width_chunks),
        us=4.0,
        far=[gathered],
    )
    d_mixed_blocks, (d_middle, d_attended, middle_sums) = middle_outs[:side], middle_outs[side:]

    d_mixed_blocks = in_plane(d_mixed_blocks)
    if side > GROUPS:
        share = (spot < GROUPS).astype(BF16)
        d_mixed_blocks = [block * share for block in d_mixed_blocks]

    *up_grads, bias_up_sum = call(
        functools.partial(up_grads_kernel, blocks=m, side=side, scatter=pairwise),
        "up_gradients",
        [d_attended, *mixed_blocks, *rows_all, *[f[3] for f in fed]],
        [place],
        up_shapes + [shape_of((1, hidden_count), F32)],
        [pltpu.VMEM((width, width), BF16)],
        us=7.0,
    )

    def add_halves(own, arrived):
        half = own.shape[0] // 2
        return add(own[:half], arrived[:half]), add(own[half:], arrived[half:])

    def back_to_tokens(value):
        received = between_planes([value[d * shard : (d + 1) * shard] for d in range(PLANES)])
        received = jnp.stack(received)
        return jnp.stack([pick(received, plane ^ at) for at in range(MICRO)])[:, None]

    if pairwise:
        up_own, up_sent, out_arrived, *d_mixed_blocks = lax.optimization_barrier(
            (*up_grads, out_arrived, *d_mixed_blocks)
        )
        up_arrived = swap(up_sent, core_bit)

    result, output_sums = call(
        functools.partial(output_kernel, others=m - 1),
        "output",
        [vectors, own_upstream, scale, middle, fed[0][0], *out_arrived],
        [],
        [shape_of((count, width), BF16), shape_of((8, width), F32)],
    )
    if pairwise:
        up_own, up_sent = add_halves(up_own, after(up_arrived, result))
        up_sent, result, *d_mixed_blocks = lax.optimization_barrier((up_sent, result, *d_mixed_blocks))
    result = back_to_tokens(result)

    d_project = attend_backward(d_mixed_blocks, kept[0], kept[1], cosine, sines)
    if pairwise:
        up_arrived = swap(up_sent, y_bit)
        d_project, result, up_arrived = lax.optimization_barrier((d_project, result, up_arrived))
    grad_own, grad_sent = call(
        qkv_grads_kernel,
        "qkv_gradients",
        [d_project, kept[2]],
        [place],
        [shape_of((2, width // PLANES, 3 * WIDTH), BF16)] * 2,
        us=4.0,
    )
    d_project = after(d_project, grad_sent)
    d_kept, d_sent, sums = call(
        functools.partial(normed_backward_kernel, blocks=side),
        "normed_backward",
        [d_project, kept[3], *token_blocks],
        [],
        [shape_of((side // 2, count, width), BF16)] * 2 + [shape_of((8, width), F32)],
        us=4.0,
    )
    if pairwise:
        up_own, up_sent = add_halves(up_own, after(up_arrived, d_sent))
    arrived = swap(d_sent, 1)

    blocks = {2 * at: d_kept[at] for at in range(side // 2)}
    steps = [arrived]
    for at in range(side // 2):
        blocks[2 * at] = add(blocks[2 * at], arrived[at])
    for bit in bits_of(side)[1:]:
        for at in [at for at in blocks if at & bit]:
            arrived = swap(blocks.pop(at), bit)
            steps.append(arrived)
            if len(blocks) > 1:
                blocks[at ^ bit] = add(blocks[at ^ bit], arrived)
    (d_tokens,) = call(
        tokens_kernel,
        "tokens_backward",
        [vectors, own_low, d_middle, blocks[0], arrived],
        [],
        [shape_of((count, width), BF16)],
    )

    if pairwise:
        up_own, up_sent = add_halves(up_own, after(swap(up_sent, side), steps[0]))
        up_parts = up_own[0].astype(F32) + swap(up_sent, 2 * side)[0].astype(F32)
        grad_up = jnp.concatenate([up_parts[at] for at in range(hidden_chunks)], -1)
        grad_proj = up_parts[hidden_chunks]
    else:
        grads = jnp.stack(columns_of(up_grads[0]) + columns_of(up_grads[1]))
        grads = grads.reshape(-1, n, rows, unit).transpose(1, 0, 2, 3)
        grads = lax.psum_scatter(grads, "seq", scatter_dimension=0, tiled=True)[0]

        def columns_from(start, number):
            return jnp.concatenate([grads[start + at] for at in range(number)], -1).astype(F32)

        grad_up = columns_from(0, hidden_chunks)
        grad_proj = columns_from(hidden_chunks, width_chunks)
    for bit in bits_of(m):
        grad_proj = grad_proj + swap_mlp(grad_proj.astype(BF16), bit).astype(F32)

    arrived = after(swap(grad_sent, side), steps[0])
    arrived = swap(add(grad_own[1], arrived[1]), 2 * side).astype(F32) + arrived[0].astype(F32)
    total = grad_own[0].astype(F32) + arrived
    by_spot = after(total.astype(BF16), steps[-1]).reshape(side, rows, 3 * WIDTH)
    received = jnp.stack(in_plane([pick(by_spot, spot ^ e) for e in range(side)]))
    grad_qkv = jnp.stack([pick(received, spot ^ group) for group in range(GROUPS)])
    grad_qkv = grad_qkv.reshape(GROUPS, rows, 3, WIDTH).transpose(1, 2, 0, 3).reshape(rows, 3 * width)
    grad_qkv = grad_qkv.astype(F32)
    for bit in bits_of(m):
        grad_qkv = grad_qkv + swap_mlp(grad_qkv.astype(BF16), bit).astype(F32)

    down_grads = after(down_grads[0], steps[-1]).astype(F32)
    grad_down = jnp.concatenate([down_grads[at] for at in range(hidden_chunks)], -1).T

    bias_up_rows = -(-hidden_count // width)
    bias_up_sum = jnp.pad(bias_up_sum, ((0, 0), (0, bias_up_rows * width - hidden_count)))
    small = jnp.concatenate(
        [sums[0:2], middle_sums[0:3], output_sums[0:2], bias_up_sum.reshape(-1, width)], 0
    )
    small = small + swap(small, 1)
    small = after(small, steps[0])
    for bit in bits_of(side)[1:]:
        small = small + swap(small, bit)
    small = jnp.concatenate([small, vectors[SCALE_TWO][None]], 0)[None]
    small = after(small, steps[-1])
    for bit in bits_of(PLANES):
        small = jnp.concatenate([small, swap(small, bit * side)], 0)
    small = in_order(list(small), plane)[:MICRO]
    grad_bias_up = jnp.sum(small[:, 7 : 7 + bias_up_rows], 0).reshape(-1)[:hidden_count]
    d_shift_one, d_xhat_one, d_gate_one, d_shift_two, d_xhat_two, d_gate_two = [small[:, at] for at in range(6)]
    index_here = time_index[:, 0]
    vector_sums = jnp.stack(
        [
            jnp.sum((1.0 + vectors[SCALES_ALL : SCALES_ALL + MICRO]) * d_xhat_one, 0),
            jnp.sum((1.0 + small[:, -1]) * d_xhat_two, 0),
            jnp.sum(small[:, 6], 0),
            jnp.pad(index_here.astype(F32), (0, width - MICRO)),
        ]
    )
    d_scale_one, d_scale_two = vectors[GAIN_ONE] * d_xhat_one, vectors[GAIN_TWO] * d_xhat_two
    small = jnp.stack([d_shift_one, d_scale_one, d_gate_one, d_shift_two, d_scale_two, d_gate_two], 1)
    small = jnp.concatenate([small.reshape(6 * MICRO, width), vector_sums], 0)[None]
    for bit in bits_of(m):
        small = jnp.concatenate([small, swap_mlp(small, bit)], 0)
    at = 6 * MICRO
    d_modulation = small[:, :at].reshape(m * MICRO, n, ada_columns)
    vector_sums = jnp.sum(small[:, at : at + 3], 0)
    index_all = small[:, at + 3, :MICRO].reshape(-1).astype(jnp.int32)
    onehot = (index_all[:, None] == jnp.arange(grid_size)[None, :]).astype(BF16)
    cond = jnp.dot(onehot, time_table, preferred_element_type=F32)
    d_modulation_own = lax.dynamic_index_in_dim(d_modulation, me, 1, keepdims=False)
    grad_ada = jnp.dot(cond.T, d_modulation_own, precision=highest)
    grad_bias_ada = jnp.sum(d_modulation_own, 0)
    d_cond = jnp.einsum("bic,idc->bd", d_modulation, full_ada.astype(F32), precision=highest)
    table_rows = grid_size // n
    onehot_own = index_all[None, :] == (me * table_rows + jnp.arange(table_rows))[:, None]
    grad_table = jnp.dot(onehot_own.astype(F32), d_cond, precision=highest)
    vector_sums = lax.dynamic_slice_in_dim(vector_sums, me * rows, rows, 1)
    return (
        result,
        back_to_tokens(d_tokens).astype(F32),
        grad_table,
        grad_ada,
        grad_bias_ada,
        vector_sums[0],
        vector_sums[1],
        grad_qkv,
        grad_proj,
        grad_up,
        grad_bias_up,
        grad_down,
        vector_sums[2],
    )


def solution(mesh):
    in_specs = (
        P(None, "mlp", "seq", None),
        P(None, "mlp", "seq", None),
        P(None, "mlp", "seq"),
        P(None, "mlp"),
        P(None, "mlp"),
        P(),
        P(),
        P(None, "seq"),
        P("seq"),
        P("seq"),
        P("seq"),
        P("seq", None),
        P("seq", None),
        P("seq", "mlp"),
        P("mlp"),
        P("mlp", "seq"),
        P("seq"),
    )
    out_specs = (
        P(None, "mlp", "seq", None),
        P(None, "mlp", "seq", None),
        P("seq", None),
        P(None, "seq"),
        P("seq"),
        P("seq"),
        P("seq"),
        P("seq", None),
        P("seq", None),
        P("seq", "mlp"),
        P("mlp"),
        P("mlp", "seq"),
        P("seq"),
    )
    run = functools.partial(body, n=mesh.shape["seq"], m=mesh.shape["mlp"])
    return jax.shard_map(run, mesh=mesh, in_specs=in_specs, out_specs=out_specs, check_vma=False)
```

```python
import functools
import math

import jax
import jax.numpy as jnp
from jax import lax
from jax.experimental import pallas as pl
from jax.experimental.pallas import tpu as pltpu
from jax.sharding import PartitionSpec as P

HEADS = 12
HEAD = 64
MICRO = 3
PLANES = 4
GROUPS = 4
PER_GROUP = HEADS // GROUPS
WIDTH = PER_GROUP * HEAD
QUERY_BLOCK = 256
SCALING = HEAD ** (-0.5)
BF16 = jnp.bfloat16
F32 = jnp.float32
highest = lax.Precision.HIGHEST
SLOPE = math.sqrt(2.0 / math.pi)
CUBIC = 0.044715

SHIFT_ONE, SCALE_ONE, GATE_ONE, SHIFT_TWO, SCALE_TWO, GATE_TWO, GAIN_ONE, GAIN_TWO, BIAS_DOWN = range(9)
SCALES_ALL, GAINS_ONE, GAINS_TWO = 9, 12, 13

VMEM = pl.BlockSpec(memory_space=pltpu.VMEM)
SMEM = pl.BlockSpec(memory_space=pltpu.SMEM)


def nn(left, right):
    return lax.dot_general(left, right, (((1,), (0,)), ((), ())), preferred_element_type=F32)


def nt(left, right):
    return lax.dot_general(left, right, (((1,), (1,)), ((), ())), preferred_element_type=F32)


def standardize(inputs):
    average = jnp.mean(inputs, -1, keepdims=True)
    centred = inputs - average
    spread = jnp.mean(centred * centred, -1, keepdims=True)
    root = lax.rsqrt(spread + 1e-06)
    return centred * root, root


def pull_norm(d_normed, gains, xhat, root):
    e = d_normed * gains
    return root * (e - jnp.mean(e, -1, keepdims=True) - xhat * jnp.mean(e * xhat, -1, keepdims=True))


def over_tokens(value):
    return jnp.sum(value, 0, keepdims=True)


def shape_of(dims, dtype):
    return jax.ShapeDtypeStruct(dims, dtype)


def call(kernel, name, operands, scalars, outs, scratch=(), us=1.0, far=()):
    moved = sum(math.prod(o.shape) * o.dtype.itemsize for o in list(operands) + list(outs))
    return pl.pallas_call(
        kernel,
        out_shape=list(outs),
        in_specs=[SMEM] * len(scalars) + [pl.BlockSpec(memory_space=pl.ANY)] * len(far) + [VMEM] * len(operands),
        out_specs=[VMEM] * len(outs),
        scratch_shapes=list(scratch),
        compiler_params=pltpu.CompilerParams(vmem_limit_bytes=56 * 1024 * 1024),
        cost_estimate=pl.CostEstimate(flops=int(us * 1e9), bytes_accessed=moved, transcendentals=0),
        name=name,
    )(*scalars, *far, *operands)


def fetch(gathered, chunks, weights, arrived):
    copies = [
        pltpu.make_async_copy(gathered.at[:, chunk], weights.at[at], arrived.at[at])
        for at, chunk in enumerate(chunks)
    ]
    for copy in copies:
        copy.start()
    return copies


def whole(weights, at):
    return weights[at].reshape(weights.shape[1] * weights.shape[2], weights.shape[3])


def group_rows(weights, group):
    blocks = WIDTH // weights.shape[2]
    parts = [
        weights[at, pl.ds(group * blocks, blocks)].reshape(WIDTH, weights.shape[3])
        for at in range(weights.shape[0])
    ]
    return parts[0] if len(parts) == 1 else jnp.concatenate(parts, -1)


def modulation(times, table, w_ada, b_ada, gain_one, gain_two, b_down, mask, small):
    columns = w_ada.shape[1]
    rows = gain_one.shape[1]
    at = lax.broadcasted_iota(jnp.int32, (8, table.shape[0]), 1)
    line = lax.broadcasted_iota(jnp.int32, (8, table.shape[0]), 0)
    wanted = jnp.where(line == 0, times[0, 0], jnp.where(line == 1, times[1, 0], times[2, 0]))
    cond = nn((at == wanted).astype(F32).astype(BF16), table[...]).astype(BF16)
    part = nn(cond, w_ada[...]) + b_ada[...].astype(F32)
    small[...] = jnp.zeros_like(small)
    at = 0
    for s in range(MICRO):
        small[0:1, at : at + columns] = part[s : s + 1]
        at += columns
    for ref in (gain_one, gain_two, b_down):
        small[0:1, at : at + rows] = ref[...].astype(F32)
        at += rows
    for s in range(MICRO):
        small[0:1, at : at + mask.shape[1]] = mask[s : s + 1, :].astype(F32)
        at += mask.shape[1]


def prepare_kernel(
    place, times, tokens, w_qkv, w_up, w_down, w_proj, table, w_ada, b_ada, gain_one, gain_two, b_down, mask, *outs
):
    packed, small, outs = outs[0], outs[1], outs[2:]
    columns_out, token_out = outs[:-PLANES], outs[-PLANES:]
    plane, spot = place[0], place[1]
    for d, out in enumerate(token_out):
        out[...] = tokens[jnp.minimum(plane ^ d, MICRO - 1)]
    width = w_proj.shape[1]
    by_group = [
        jnp.concatenate([w_qkv[:, p * width + g * WIDTH : p * width + (g + 1) * WIDTH] for p in range(3)], -1)
        for g in range(GROUPS)
    ]
    for e, out in enumerate(columns_out):
        group = (spot ^ e) % GROUPS
        here = by_group[0]
        for g in range(1, GROUPS):
            here = jnp.where(group == g, by_group[g], here)
        out[...] = here
    unit = packed.shape[2]
    chunk = 0
    for value in (w_up[...], w_down[...].T, w_proj[...]):
        for at in range(0, value.shape[1], unit):
            packed[chunk] = value[:, at : at + unit]
            chunk += 1
    modulation(times, table, w_ada, b_ada, gain_one, gain_two, b_down, mask, small)


def vectors_kernel(place, weight_index, weight_grid, small, vectors, scale, line):
    n = small.shape[0]
    width = vectors.shape[1]
    columns, rows, shard = 6 * width // n, width // n, scale.shape[0] // PLANES
    plane, spot = place[0], place[1]
    side = n // PLANES
    me = plane * side + spot
    last = jnp.minimum(plane, MICRO - 1)

    def one_of(three):
        return jnp.where(last == 0, three[0], jnp.where(last == 1, three[1], three[2]))

    def pieces(first, size):
        start = first
        while start < first + size:
            stop = min(first + size, (start // width + 1) * width)
            yield start // width, start % width, start - first, stop - start
            start = stop

    vectors[...] = jnp.zeros_like(vectors)
    for i in range(n):
        here = small[pl.ds(me ^ i, 1), :]
        each = [here[:, s * columns : (s + 1) * columns] for s in range(MICRO)]
        mine = one_of(each)
        for part, column, offset, size in pieces(i * columns, columns):
            vectors[part : part + 1, column : column + size] = mine[:, offset : offset + size]
            if part == SCALE_ONE:
                for s in range(MICRO):
                    vectors[SCALES_ALL + s : SCALES_ALL + s + 1, column : column + size] = each[s][
                        :, offset : offset + size
                    ]
        for row in (GAIN_ONE, GAIN_TWO, BIAS_DOWN):
            start = MICRO * columns + (row - GAIN_ONE) * rows
            vectors[row : row + 1, i * rows : (i + 1) * rows] = here[:, start : start + rows]
    for to, gain, by in ((GAINS_ONE, GAIN_ONE, SCALE_ONE), (GAINS_TWO, GAIN_TWO, SCALE_TWO)):
        vectors[to : to + 1, :] = vectors[gain : gain + 1, :] * (1.0 + vectors[by : by + 1, :])
    line[...] = jnp.zeros_like(line)
    for d in range(PLANES):
        here = small[d * side : d * side + 1, :]
        start = MICRO * (columns + rows)
        three = [here[:, start + s * shard : start + (s + 1) * shard] for s in range(MICRO)]
        line[0:1, d * shard : (d + 1) * shard] = one_of(three)
    weight = jnp.where(plane < MICRO, weight_grid[weight_index[last, 0]], 0.0)
    scale[...] = line[...].T[:, 0:1] * weight


def project_kernel(place, gathered, tokens, vectors, *refs, chunks):
    side = len(refs) - 5
    mixed, (attended, middle, normed, weights, arrived) = refs[:side], refs[side:]
    spot = place[1]
    copies = fetch(gathered, chunks, weights, arrived)
    for copy in copies:
        copy.wait()
    total = jnp.zeros(attended.shape, F32)
    for e in range(side):
        other = spot ^ e
        block = mixed[e][...]
        if side > GROUPS:
            block = jnp.where(other < GROUPS, block, jnp.zeros_like(block))
        total = total + nn(block, group_rows(weights, other % GROUPS))
    attended[...] = total
    after = tokens[...].astype(F32) + vectors[GATE_ONE : GATE_ONE + 1] * total
    middle[...] = after
    xhat, _ = standardize(after)
    normed[...] = (xhat * vectors[GAINS_TWO : GAINS_TWO + 1] + vectors[SHIFT_TWO : SHIFT_TWO + 1]).astype(BF16)


def feed_kernel(gathered, rows, d_rows, bias, output, d_normed, active, d_hidden, weights, arrived):
    parts = weights.shape[0] // 2
    unit = weights.shape[3]
    order = [at for part in range(parts) for at in (part, parts + part)]
    copies = fetch(gathered, order, weights, arrived)
    out = jnp.zeros(output.shape, F32)
    back = jnp.zeros(output.shape, F32)
    for part in range(parts):
        columns = slice(part * unit, (part + 1) * unit)
        copies[2 * part].wait()
        up = whole(weights, 2 * part)
        u = nn(rows[...], up) + bias[:, columns]
        square = u * u
        bent = jnp.tanh(SLOPE * u * (1.0 + CUBIC * square))
        half = 0.5 * (1.0 + bent)
        on = (u * half).astype(BF16)
        active[:, columns] = on
        slope = half + 0.5 * u * (1.0 - bent * bent) * (SLOPE * (1.0 + 3.0 * CUBIC * square))
        copies[2 * part + 1].wait()
        down = whole(weights, 2 * part + 1)
        d_on = (nn(d_rows[...], down) * slope).astype(BF16)
        d_hidden[:, columns] = d_on
        out = out + nt(on, down)
        back = back + nt(d_on, up)
    output[...] = out.astype(output.dtype)
    d_normed[...] = back.astype(d_normed.dtype)


def scatter_store(refs, me, device, value):
    kept, sent, chunk, slot_of = refs
    distance = me ^ device
    slot = slot_of(distance)

    @pl.when(distance % 2 == 0)
    def _():
        kept[slot, chunk] = value

    @pl.when(distance % 2 == 1)
    def _():
        sent[slot, chunk] = value


def slot_y_first(distance):
    return ((distance >> 1) & 1) * 4 + ((distance >> 2) & 1) * 2 + ((distance >> 3) & 1)


def down_grads_kernel(*refs, blocks):
    d_rows, active, out = refs[:blocks], refs[blocks:-1], refs[-1]
    unit = out.shape[3]
    turned = [ref[...].T for ref in d_rows]
    for chunk in range(out.shape[1]):
        columns = slice(chunk * unit, (chunk + 1) * unit)
        grad = sum(nn(turned[b], active[b][:, columns]) for b in range(blocks)).astype(BF16)
        out[:, chunk] = grad.reshape(out.shape[0], out.shape[2], unit)


def up_grads_kernel(place, *refs, blocks, scatter):
    rows_all, d_hidden, outs = refs[:blocks], refs[blocks : 2 * blocks], refs[2 * blocks :]
    bias = outs[-1]
    me = place[2]
    width, count = rows_all[0].shape[1], bias.shape[1]
    unit = min(width, count)
    turned = [ref[...].T for ref in rows_all]
    for chunk in range(count // unit):
        columns = slice(chunk * unit, (chunk + 1) * unit)
        grad = sum(nn(turned[b], d_hidden[b][:, columns]) for b in range(blocks)).astype(BF16)
        bias[:, columns] = sum(over_tokens(d_hidden[b][:, columns].astype(F32)) for b in range(blocks))
        if scatter:
            rows = outs[0].shape[2]
            for i in range(width // rows):
                part = grad[i * rows : (i + 1) * rows]
                scatter_store((outs[0], outs[1], chunk, slot_y_first), me, i, part)
        else:
            outs[0][:, columns] = grad


def proj_grads_kernel(place, d_attended, *refs, side, scatter):
    mixed, outs, whole_grad = refs[:side], refs[side:-1], refs[-1]
    spot, me = place[1], place[2]
    width = d_attended.shape[1]
    if side > GROUPS:
        whole_grad[...] = jnp.zeros_like(whole_grad)
    for e in range(side):
        other = spot ^ e
        first = pl.multiple_of((other % GROUPS) * WIDTH, WIDTH)
        grad = nn(mixed[e][...].T, d_attended[...]).astype(BF16)
        if side > GROUPS:
            grad = whole_grad[pl.ds(first, WIDTH), :] + jnp.where(other < GROUPS, grad, jnp.zeros_like(grad))
        whole_grad[pl.ds(first, WIDTH), :] = grad
    if scatter:
        rows = outs[0].shape[2]
        for i in range(width // rows):
            part = whole_grad[i * rows : (i + 1) * rows, :]
            scatter_store((outs[0], outs[1], 0, slot_y_first), me, i, part)
    else:
        outs[0][...] = whole_grad[...]


def qkv_grads_kernel(place, d_project, normed, *outs):
    grad = nn(d_project[...], normed[...]).astype(BF16).T
    plane, slice_of = place[0], place[3]
    rows = outs[0].shape[1]
    if len(outs[0].shape) == 3 and outs[0].shape[0] == PLANES:
        for at in range(PLANES):
            distance = plane ^ at
            slot = (distance % 2) * 2 + distance // 2
            halves = [grad[(2 * at + half) * rows : (2 * at + half + 1) * rows] for half in range(2)]
            outs[0][slot] = jnp.where(slice_of == 0, halves[0], halves[1])
            outs[1][slot] = jnp.where(slice_of == 0, halves[1], halves[0])
    else:
        for at in range(PLANES):
            part = grad[at * rows : (at + 1) * rows]
            distance = plane ^ at

            @pl.when(distance % 2 == 0)
            def _():
                outs[0][distance // 2] = part

            @pl.when(distance % 2 == 1)
            def _():
                outs[1][distance // 2] = part


def normed_backward_kernel(d_project, weight, *refs, blocks):
    tokens, (kept, sent, sums) = refs[:blocks], refs[blocks:]
    count = tokens[0].shape[0]
    d_shift = jnp.zeros((1, weight.shape[0]), F32)
    d_xhat = jnp.zeros((1, weight.shape[0]), F32)
    for block in range(blocks):
        part = nt(d_project[:, block * count : (block + 1) * count].T, weight[...])
        (sent if block % 2 else kept)[block // 2] = part.astype(BF16)
        xhat, _ = standardize(tokens[block][...].astype(F32))
        d_shift = d_shift + over_tokens(part)
        d_xhat = d_xhat + over_tokens(part * xhat)
    sums[0:1, :] = d_shift
    sums[1:2, :] = d_xhat
    sums[2:8, :] = jnp.zeros((6, weight.shape[0]), F32)


def middle_kernel(place, gathered, vectors, upstream, scale, attended, middle, d_own, *refs, others, chunks):
    arrived, refs = refs[:others], refs[others:]
    d_mixed, (d_middle, d_attended, sums, weights, copied) = refs[:-5], refs[-5:]
    spot = place[1]
    copies = fetch(gathered, chunks, weights, copied)
    width = middle.shape[1]
    d_normed = d_own[...]
    for ref in arrived:
        d_normed = d_normed + ref[...].astype(F32)
    xhat, root = standardize(middle[...])
    d_result = upstream[...].astype(F32) * scale[...]
    d_after = d_result + pull_norm(d_normed, vectors[GAINS_TWO : GAINS_TWO + 1], xhat, root)
    d_middle[...] = d_after
    low = (vectors[GATE_ONE : GATE_ONE + 1] * d_after).astype(BF16)
    d_attended[...] = low
    for copy in copies:
        copy.wait()
    for e in range(len(d_mixed)):
        d_mixed[e][...] = nt(low, group_rows(weights, (spot ^ e) % GROUPS)).astype(BF16)
    sums[0:1, :] = over_tokens(d_after * attended[...])
    sums[1:2, :] = over_tokens(d_normed)
    sums[2:3, :] = over_tokens(d_normed * xhat)
    sums[3:8, :] = jnp.zeros((5, width), F32)


def output_kernel(vectors, upstream, scale, middle, own, *refs, others):
    arrived, (result, sums) = refs[:others], refs[others:]
    output = own[...] + vectors[BIAS_DOWN : BIAS_DOWN + 1]
    for ref in arrived:
        output = output + ref[...].astype(F32)
    gate = vectors[GATE_TWO : GATE_TWO + 1]
    result[...] = (middle[...] + gate * output).astype(BF16)
    d_result = upstream[...].astype(F32) * scale[...]
    sums[0:1, :] = over_tokens(d_result * output)
    sums[1:2, :] = over_tokens(gate * d_result)
    sums[2:8, :] = jnp.zeros((6, middle.shape[1]), F32)


def tokens_kernel(vectors, tokens, d_middle, own, arrived, d_tokens):
    xhat, root = standardize(tokens[...].astype(F32))
    d_normed = own[...].astype(F32) + arrived[...].astype(F32)
    back = pull_norm(d_normed, vectors[GAINS_ONE : GAINS_ONE + 1], xhat, root)
    d_tokens[...] = (d_middle[...] + back).astype(BF16)


def forward_kernel(place, *refs, blocks, halves):
    tokens, refs = refs[:blocks], refs[blocks:]
    count = 2 if halves else PLANES
    weights, refs = refs[:count], refs[count:]
    (vectors, cosine, sines), refs = refs[:3], refs[3:]
    gain, shift = vectors[GAINS_ONE : GAINS_ONE + 1], vectors[SHIFT_ONE : SHIFT_ONE + 1]
    mixed, refs = refs[:blocks], refs[blocks:]
    heads, log_total, normed, weight, keys, mixed_turned = refs
    plane = place[0]
    rows = weights[0].shape[-2]
    count = tokens[0].shape[0]
    if halves:
        for half in range(2):
            for distance in range(PLANES):
                first = pl.multiple_of((plane ^ distance) * 2 * rows + (place[3] ^ half) * rows, 16)
                weight[pl.ds(first, rows), :] = weights[half][distance]
    else:
        for distance in range(PLANES):
            first = pl.multiple_of((plane ^ distance) * rows, 8)
            weight[pl.ds(first, rows), :] = weights[distance][...]
    for block in range(blocks):
        xhat, _ = standardize(tokens[block][...].astype(F32))
        normed[block * count : (block + 1) * count, :] = (xhat * gain + shift).astype(BF16)
    project = nt(weight[...].T, normed[...])
    cos, sin = cosine[...], sines[...]
    half = HEAD // 2
    for part in range(2):
        for head in range(PER_GROUP):
            start = part * WIDTH + head * HEAD
            first, second = project[start : start + half], project[start + half : start + HEAD]
            turned = jnp.concatenate([first * cos - second * sin, second * cos + first * sin], 0).astype(BF16)
            if part == 0:
                turned = turned * jnp.asarray(SCALING, BF16)
            else:
                keys[head] = turned.T
            heads[start : start + HEAD, :] = turned
    heads[2 * WIDTH :, :] = project[2 * WIDTH :].astype(BF16)
    length = heads.shape[1]
    for head in range(PER_GROUP):
        start = head * HEAD

        def queries_step(step, carry):
            columns = pl.ds(pl.multiple_of(step * QUERY_BLOCK, QUERY_BLOCK), QUERY_BLOCK)
            scores = nn(keys[head], heads[start : start + HEAD, columns])
            peak = jnp.max(scores, 0, keepdims=True)
            exps = jnp.exp(scores - peak)
            total = jnp.sum(exps, 0, keepdims=True)
            log_total[head : head + 1, columns] = peak + jnp.log(total)
            probs = (exps * (1.0 / total)).astype(BF16)
            values = heads[2 * WIDTH + start : 2 * WIDTH + start + HEAD, :]
            mixed_turned[start : start + HEAD, columns] = nn(values, probs).astype(BF16)
            return carry

        lax.fori_loop(0, length // QUERY_BLOCK, queries_step, 0)
    for block in range(blocks):
        mixed[block][...] = mixed_turned[:, block * count : (block + 1) * count].T


def backward_kernel(*refs, blocks):
    d_mixed, refs = refs[:blocks], refs[blocks:]
    (heads, log_total, cosine, sines), refs = refs[:4], refs[4:]
    d_project, d_turned, d_keys, d_values, keys, values = refs
    count = d_mixed[0].shape[0]
    length = heads.shape[1]
    for block in range(blocks):
        d_turned[:, block * count : (block + 1) * count] = d_mixed[block][...].T
    cos, sin = cosine[...], sines[...]
    half = HEAD // 2
    d_keys[...] = jnp.zeros_like(d_keys)
    d_values[...] = jnp.zeros_like(d_values)
    for head in range(PER_GROUP):
        start = head * HEAD
        keys_turned = heads.at[WIDTH + start : WIDTH + start + HEAD]
        keys[...] = keys_turned[...].T
        values[...] = heads[2 * WIDTH + start : 2 * WIDTH + start + HEAD, :].T

        def queries_step(step, carry):
            columns = pl.ds(pl.multiple_of(step * QUERY_BLOCK, QUERY_BLOCK), QUERY_BLOCK)
            queries = heads[start : start + HEAD, columns]
            incoming = d_turned[start : start + HEAD, columns]
            scores = nn(keys[...], queries)
            probs = jnp.exp(scores - log_total[head : head + 1, columns])
            d_probs = nn(values[...], incoming)
            delta = jnp.sum(probs * d_probs, 0, keepdims=True)
            d_scores = (probs * (d_probs - delta)).astype(BF16)
            d_values[start : start + HEAD, :] += nt(incoming, probs.astype(BF16))
            d_keys[start : start + HEAD, :] += nt(queries, d_scores)
            d_queries = nn(keys_turned[...], d_scores) * SCALING
            first, second = d_queries[:half], d_queries[half:]
            cos_here, sin_here = cosine[:, columns], sines[:, columns]
            d_project[start : start + half, columns] = (first * cos_here + second * sin_here).astype(BF16)
            d_project[start + half : start + HEAD, columns] = (second * cos_here - first * sin_here).astype(BF16)
            return carry

        lax.fori_loop(0, length // QUERY_BLOCK, queries_step, 0)
        first, second = d_keys[start : start + half, :], d_keys[start + half : start + HEAD, :]
        d_project[WIDTH + start : WIDTH + start + half, :] = (first * cos + second * sin).astype(BF16)
        d_project[WIDTH + start + half : WIDTH + start + HEAD, :] = (second * cos - first * sin).astype(BF16)
    d_project[2 * WIDTH :, :] = d_values[...].astype(BF16)


def attend_forward(place, tokens, weights, vectors, cosine, sines, halves):
    blocks, (count, width) = len(tokens), tokens[0].shape
    length = blocks * count
    columns = weights[0].shape[-1]
    outs = call(
        functools.partial(forward_kernel, blocks=blocks, halves=halves),
        "attend_forward",
        [*tokens, *weights, vectors, cosine, sines],
        [place],
        [shape_of((count, WIDTH), BF16)] * blocks
        + [
            shape_of((columns, length), BF16),
            shape_of((8, length), F32),
            shape_of((length, width), BF16),
            shape_of((width, columns), BF16),
        ],
        [pltpu.VMEM((PER_GROUP, length, HEAD), BF16), pltpu.VMEM((WIDTH, length), BF16)],
        us=15.0,
    )
    return outs[:blocks], outs[blocks:]


def attend_backward(d_mixed, heads, log_total, cosine, sines):
    blocks, length = len(d_mixed), heads.shape[1]
    (d_project,) = call(
        functools.partial(backward_kernel, blocks=blocks),
        "attend_backward",
        [*d_mixed, heads, log_total, cosine, sines],
        [],
        [shape_of((3 * WIDTH, length), BF16)],
        [
            pltpu.VMEM((WIDTH, length), BF16),
            pltpu.VMEM((WIDTH, length), F32),
            pltpu.VMEM((WIDTH, length), F32),
            pltpu.VMEM((length, HEAD), BF16),
            pltpu.VMEM((length, HEAD), BF16),
        ],
        us=18.0,
    )
    return d_project


def after(values, *others):
    return lax.optimization_barrier((values, others))[0]


def add(left, right):
    return (left.astype(F32) + right.astype(F32)).astype(BF16)


def pick(stack, index):
    return lax.dynamic_index_in_dim(stack, index, 0, keepdims=False)


def bits_of(count):
    return [1 << bit for bit in range(count.bit_length() - 1)]


def body(
    tokens,
    upstream,
    token_mask,
    time_index,
    weight_index,
    time_table,
    weight_grid,
    w_ada,
    b_ada,
    gain_one,
    gain_two,
    w_qkv,
    w_proj,
    w_up,
    b_up,
    w_down,
    b_down,
    *,
    n,
    m,
):
    side = n // PLANES
    me = lax.axis_index("seq")
    plane, spot = me // side, me % side
    slice_of = lax.axis_index("mlp")
    place = jnp.stack([plane, spot, me, slice_of]).astype(jnp.int32)
    shard, width = tokens.shape[2], tokens.shape[3]
    rows = w_qkv.shape[0]
    hidden_count = w_up.shape[1]
    grid_size = time_table.shape[0]
    ada_columns = w_ada.shape[1]
    count = PLANES * shard
    unit = min(width, hidden_count)
    hidden_chunks, width_chunks = hidden_count // unit, width // unit
    pairwise = rows % 16 == 0 and side == GROUPS and unit == width and m == 2
    z_bits, y_bit, core_bit = (2 * side, side), 2, 1

    def swap(value, distance):
        return lax.ppermute(value, "seq", [(i, i ^ distance) for i in range(n)])

    def swap_mlp(value, distance):
        return lax.ppermute(value, "mlp", [(i, i ^ distance) for i in range(m)])

    def between_planes(pieces):
        return [pieces[0]] + [swap(pieces[d], d * side) for d in range(1, PLANES)]

    def in_plane(pieces):
        return [pieces[0]] + [swap(pieces[e], e) for e in range(1, side)]

    def in_order(blocks, axis):
        halves = jnp.stack(blocks)
        for bit in bits_of(len(blocks)):
            here = halves.reshape((len(blocks) // (2 * bit), 2, bit) + halves.shape[1:])
            halves = jnp.where((axis & bit) != 0, here[:, ::-1], here).reshape(halves.shape)
        return halves

    def for_plane(values):
        return [pick(values, jnp.minimum(plane ^ d, MICRO - 1)) for d in range(PLANES)]

    def columns_of(value):
        return [value[:, at : at + unit] for at in range(0, value.shape[1], unit)]

    line = [value[None] for value in (b_ada, gain_one, gain_two, b_down)]
    small_count = -(-MICRO * (ada_columns + rows + shard) // 128) * 128
    first_shapes = [shape_of((2 * hidden_chunks + width_chunks, rows, unit), BF16), shape_of((1, small_count), F32)]
    first_shapes += [shape_of((rows, 3 * WIDTH), BF16)] * side + [shape_of((shard, width), BF16)] * PLANES
    packed, small, *pieces = call(
        prepare_kernel,
        "prepare",
        [tokens[:, 0], w_qkv, w_up, w_down, w_proj, time_table, w_ada, *line, token_mask[:, 0]],
        [place, time_index],
        first_shapes,
        us=4.0,
    )
    group_columns, token_pieces = pieces[:side], pieces[side:]

    gathered = lax.all_gather(packed, "seq", axis=0)
    if not pairwise:
        gathered = gathered.transpose(1, 0, 2, 3).reshape(-1, GROUPS, WIDTH, unit).transpose(1, 0, 2, 3)
    blocks_shape = (gathered.shape[0],) + gathered.shape[2:]
    proj_chunks = list(range(2 * hidden_chunks, 2 * hidden_chunks + width_chunks))

    def weight_scratch(number):
        return [pltpu.VMEM((number,) + blocks_shape, BF16), pltpu.SemaphoreType.DMA((number,))]

    own_low = jnp.concatenate(between_planes(token_pieces), 0)
    token_blocks = {0: own_low}
    for bit in reversed(bits_of(side)):
        for known in list(token_blocks):
            token_blocks[known | bit] = swap(token_blocks[known], bit)
    token_blocks = [token_blocks[at] for at in range(side)]

    received = jnp.stack(in_plane(group_columns))
    weight_block = jnp.concatenate([pick(received, spot ^ at) for at in range(side)], 0)
    if pairwise:
        weight_block = pick(weight_block.reshape(2, width // 8, 3 * WIDTH), slice_of)
    weight_blocks = {0: weight_block}
    for bit in (2, 1):
        for known in list(weight_blocks):
            weight_blocks[known | bit] = swap(weight_blocks[known], bit * side)
    weight_blocks = [weight_blocks[at] for at in range(PLANES)]
    if pairwise:
        weight_blocks = jnp.stack(weight_blocks)
        weight_blocks = [weight_blocks, swap_mlp(weight_blocks, 1)]

    for bit in bits_of(n):
        small = jnp.concatenate([small, swap(small, bit)], 0)
    vectors, scale = call(
        vectors_kernel,
        "vectors",
        [small],
        [place, weight_index, weight_grid],
        [shape_of((16, width), F32), shape_of((count, 1), F32)],
        [pltpu.VMEM((8, count), F32)],
    )

    order = ((plane ^ jnp.arange(PLANES))[None, :] * side + (spot ^ jnp.arange(side))[:, None]) * shard
    positions = (order[:, :, None] + jnp.arange(shard)).reshape(1, -1).astype(F32)
    frequency = 10000.0 ** (-jnp.arange(0, HEAD, 2).astype(F32) / HEAD)
    angles = frequency[:, None] * positions
    cosine, sines = jnp.cos(angles), jnp.sin(angles)

    mixed_blocks, kept = attend_forward(
        place, token_blocks, weight_blocks, vectors, cosine, sines, pairwise
    )

    full_ada = lax.all_gather(after(w_ada, token_blocks[0]), "seq", axis=0)

    mixed_blocks = in_plane(mixed_blocks)

    own_upstream = between_planes(after(for_plane(upstream[:, 0]), weight_blocks))
    own_upstream = after(own_upstream, kept[1])
    own_upstream = jnp.concatenate(own_upstream, 0)
    d_rows = ((own_upstream.astype(F32) * scale) * vectors[GATE_TWO][None]).astype(BF16)
    d_rows = [d_rows] + [swap_mlp(d_rows, d) for d in range(1, m)]

    attended, middle, normed_two = call(
        functools.partial(project_kernel, chunks=proj_chunks),
        "project",
        [own_low, vectors, *mixed_blocks],
        [place],
        [shape_of((count, width), F32), shape_of((count, width), F32), shape_of((count, width), BF16)],
        weight_scratch(width_chunks),
        us=3.0,
        far=[gathered],
    )
    rows_all = [normed_two] + [swap_mlp(normed_two, d) for d in range(1, m)]
    bias_up = b_up.astype(F32)[None]
    fed = [
        call(
            feed_kernel,
            "feed_forward",
            [rows_all[d], d_rows[d], bias_up],
            [],
            [shape_of((count, width), BF16 if d else F32)] * 2 + [shape_of((count, hidden_count), BF16)] * 2,
            weight_scratch(2 * hidden_chunks),
            us=6.0,
            far=[gathered],
        )
        for d in range(m)
    ]
    d_arrived = [swap_mlp(fed[d][1], d) for d in range(1, m)]
    out_arrived = [swap_mlp(fed[d][0], d) for d in range(1, m)]
    slots = n // 2
    down_shape = (n, hidden_chunks, rows, unit) if pairwise else (GROUPS, hidden_chunks, WIDTH, unit)
    if pairwise:
        up_shapes = [shape_of((slots, hidden_chunks, rows, unit), BF16)] * 2
        proj_shapes = [shape_of((slots, width_chunks, rows, unit), BF16)] * 2
    else:
        up_shapes = [shape_of((width, hidden_count), BF16)]
        proj_shapes = [shape_of((width, width), BF16)]
    (down_grads,) = call(
        functools.partial(down_grads_kernel, blocks=m),
        "down_gradients",
        [*d_rows, *[f[2] for f in fed]],
        [],
        [shape_of(down_shape, BF16)],
        us=6.0,
    )
    *up_grads, bias_up_sum = call(
        functools.partial(up_grads_kernel, blocks=m, scatter=pairwise),
        "up_gradients",
        [*rows_all, *[f[3] for f in fed]],
        [place],
        up_shapes + [shape_of((1, hidden_count), F32)],
        us=5.0,
    )
    d_arrived, down_grads, full_ada, *up_grads = lax.optimization_barrier(
        (d_arrived, down_grads, full_ada, *up_grads)
    )
    if not pairwise:
        down_grads = down_grads.transpose(1, 0, 2, 3).reshape(hidden_chunks, n, rows, unit).transpose(1, 0, 2, 3)
    down_grads = lax.psum_scatter(down_grads, "seq", scatter_dimension=0, tiled=True)
    middle_outs = call(
        functools.partial(middle_kernel, others=m - 1, chunks=proj_chunks),
        "middle_backward",
        [vectors, own_upstream, scale, attended, middle, fed[0][1], *d_arrived],
        [place],
        [shape_of((count, WIDTH), BF16)] * side
        + [shape_of((count, width), F32), shape_of((count, width), BF16), shape_of((8, width), F32)],
        weight_scratch(width_chunks),
        us=4.0,
        far=[gathered],
    )
    d_mixed_blocks, (d_middle, d_attended, middle_sums) = middle_outs[:side], middle_outs[side:]

    d_mixed_blocks = in_plane(d_mixed_blocks)
    if side > GROUPS:
        share = (spot < GROUPS).astype(BF16)
        d_mixed_blocks = [block * share for block in d_mixed_blocks]

    proj_grads = call(
        functools.partial(proj_grads_kernel, side=side, scatter=pairwise),
        "proj_gradients",
        [d_attended, *mixed_blocks],
        [place],
        proj_shapes,
        [pltpu.VMEM((width, width), BF16)],
        us=2.0,
    )

    def add_halves(own, arrived):
        half = own.shape[0] // 2
        return add(own[:half], arrived[:half]), add(own[half:], arrived[half:])

    def back_to_tokens(value):
        received = between_planes([value[d * shard : (d + 1) * shard] for d in range(PLANES)])
        received = jnp.stack(received)
        return jnp.stack([pick(received, plane ^ at) for at in range(MICRO)])[:, None]

    if pairwise:
        up_own, up_sent = add_halves(up_grads[0], swap(up_grads[1], core_bit))

    result, output_sums = call(
        functools.partial(output_kernel, others=m - 1),
        "output",
        [vectors, own_upstream, scale, middle, fed[0][0], *out_arrived],
        [],
        [shape_of((count, width), BF16), shape_of((8, width), F32)],
    )
    if pairwise:
        proj_own, proj_sent, up_sent, result, *d_mixed_blocks = lax.optimization_barrier(
            (*proj_grads, up_sent, result, *d_mixed_blocks)
        )
    result = back_to_tokens(result)

    d_project = attend_backward(d_mixed_blocks, kept[0], kept[1], cosine, sines)
    if pairwise:
        up_arrived, proj_arrived = swap(up_sent, y_bit), swap(proj_sent, core_bit)
        d_project, result, up_arrived, proj_arrived = lax.optimization_barrier(
            (d_project, result, up_arrived, proj_arrived)
        )
    qkv_shape = (PLANES, width // 8, 3 * WIDTH) if pairwise else (2, width // PLANES, 3 * WIDTH)
    grad_own, grad_sent = call(
        qkv_grads_kernel,
        "qkv_gradients",
        [d_project, kept[2]],
        [place],
        [shape_of(qkv_shape, BF16)] * 2,
        us=4.0,
    )
    d_project = after(d_project, grad_sent)
    d_kept, d_sent, sums = call(
        functools.partial(normed_backward_kernel, blocks=side),
        "normed_backward",
        [d_project, kept[3], *token_blocks],
        [],
        [shape_of((side // 2, count, width), BF16)] * 2 + [shape_of((8, width), F32)],
        us=4.0,
    )
    if pairwise:
        up_own, up_sent = add_halves(up_own, after(up_arrived, grad_sent))
        proj_own, proj_sent = add_halves(proj_own, after(proj_arrived, grad_sent))
        grad_arrived = after(swap_mlp(grad_sent, 1), d_sent)
        grad_own, grad_sent = add_halves(grad_own, grad_arrived)
    arrived = swap(d_sent, 1)

    blocks = {2 * at: d_kept[at] for at in range(side // 2)}
    steps = [arrived]
    for at in range(side // 2):
        blocks[2 * at] = add(blocks[2 * at], arrived[at])
    for bit in bits_of(side)[1:]:
        for at in [at for at in blocks if at & bit]:
            arrived = swap(blocks.pop(at), bit)
            steps.append(arrived)
            if len(blocks) > 1:
                blocks[at ^ bit] = add(blocks[at ^ bit], arrived)
    (d_tokens,) = call(
        tokens_kernel,
        "tokens_backward",
        [vectors, own_low, d_middle, blocks[0], arrived],
        [],
        [shape_of((count, width), BF16)],
    )

    if pairwise:
        up_own, up_sent = add_halves(up_own, after(swap(up_sent, side), steps[0]))
        proj_own, proj_sent = add_halves(proj_own, after(swap(proj_sent, y_bit), steps[0]))
        proj_own, proj_sent = add_halves(proj_own, swap(proj_sent, side))
        up_parts = up_own[0].astype(F32) + after(swap(up_sent, 2 * side), d_tokens)[0].astype(F32)
        grad_up = jnp.concatenate([up_parts[at] for at in range(hidden_chunks)], -1)
        grad_proj = proj_own[0, 0].astype(F32) + after(swap(proj_sent, 2 * side), d_tokens)[0, 0].astype(F32)
    else:
        grads = jnp.stack(columns_of(up_grads[0]) + columns_of(proj_grads[0]))
        grads = grads.reshape(-1, n, rows, unit).transpose(1, 0, 2, 3)
        grads = lax.psum_scatter(grads, "seq", scatter_dimension=0, tiled=True)[0]

        def columns_from(start, number):
            return jnp.concatenate([grads[start + at] for at in range(number)], -1).astype(F32)

        grad_up = columns_from(0, hidden_chunks)
        grad_proj = columns_from(hidden_chunks, width_chunks)
    for bit in bits_of(m):
        grad_proj = grad_proj + swap_mlp(grad_proj.astype(BF16), bit).astype(F32)

    arrived = after(swap(grad_sent, side), steps[0])
    if pairwise:
        grad_own, grad_sent = add_halves(grad_own, arrived)
        arrived = after(swap(grad_sent, 2 * side), d_tokens)
        total = grad_own[0].astype(F32) + arrived[0].astype(F32)
        by_spot = total.astype(BF16).reshape(2, rows, 3 * WIDTH)
        slices = [pick(by_spot, (spot ^ e) % 2) for e in range(side)]
    else:
        arrived = swap(add(grad_own[1], arrived[1]), 2 * side).astype(F32) + arrived[0].astype(F32)
        total = grad_own[0].astype(F32) + arrived
        by_spot = total.astype(BF16).reshape(side, rows, 3 * WIDTH)
        slices = [pick(by_spot, spot ^ e) for e in range(side)]
    received = jnp.stack(in_plane(slices))
    grad_qkv = jnp.stack([pick(received, spot ^ group) for group in range(GROUPS)])
    grad_qkv = grad_qkv.reshape(GROUPS, rows, 3, WIDTH).transpose(1, 2, 0, 3).reshape(rows, 3 * width)
    if pairwise:
        grad_qkv = jnp.where(spot // 2 == slice_of, grad_qkv, swap_mlp(grad_qkv, 1)).astype(F32)
    else:
        grad_qkv = grad_qkv.astype(F32)
        for bit in bits_of(m):
            grad_qkv = grad_qkv + swap_mlp(grad_qkv.astype(BF16), bit).astype(F32)

    down_grads = after(down_grads[0], steps[-1]).astype(F32)
    grad_down = jnp.concatenate([down_grads[at] for at in range(hidden_chunks)], -1).T

    bias_up_rows = -(-hidden_count // width)
    bias_up_sum = jnp.pad(bias_up_sum, ((0, 0), (0, bias_up_rows * width - hidden_count)))
    small = jnp.concatenate(
        [sums[0:2], middle_sums[0:3], output_sums[0:2], bias_up_sum.reshape(-1, width)], 0
    )
    small = small + swap(small, 1)
    small = after(small, steps[0])
    for bit in bits_of(side)[1:]:
        small = small + swap(small, bit)
    small = jnp.concatenate([small, vectors[SCALE_TWO][None]], 0)[None]
    small = after(small, steps[-1])
    for bit in bits_of(PLANES):
        small = jnp.concatenate([small, swap(small, bit * side)], 0)
    small = in_order(list(small), plane)[:MICRO]
    grad_bias_up = jnp.sum(small[:, 7 : 7 + bias_up_rows], 0).reshape(-1)[:hidden_count]
    d_shift_one, d_xhat_one, d_gate_one, d_shift_two, d_xhat_two, d_gate_two = [small[:, at] for at in range(6)]
    index_here = time_index[:, 0]
    vector_sums = jnp.stack(
        [
            jnp.sum((1.0 + vectors[SCALES_ALL : SCALES_ALL + MICRO]) * d_xhat_one, 0),
            jnp.sum((1.0 + small[:, -1]) * d_xhat_two, 0),
            jnp.sum(small[:, 6], 0),
            jnp.pad(index_here.astype(F32), (0, width - MICRO)),
        ]
    )
    d_scale_one, d_scale_two = vectors[GAIN_ONE] * d_xhat_one, vectors[GAIN_TWO] * d_xhat_two
    small = jnp.stack([d_shift_one, d_scale_one, d_gate_one, d_shift_two, d_scale_two, d_gate_two], 1)
    small = jnp.concatenate([small.reshape(6 * MICRO, width), vector_sums], 0)[None]
    for bit in bits_of(m):
        small = jnp.concatenate([small, swap_mlp(small, bit)], 0)
    at = 6 * MICRO
    d_modulation = small[:, :at].reshape(m * MICRO, n, ada_columns)
    vector_sums = jnp.sum(small[:, at : at + 3], 0)
    index_all = small[:, at + 3, :MICRO].reshape(-1).astype(jnp.int32)
    onehot = (index_all[:, None] == jnp.arange(grid_size)[None, :]).astype(BF16)
    cond = jnp.dot(onehot, time_table, preferred_element_type=F32)
    d_modulation_own = lax.dynamic_index_in_dim(d_modulation, me, 1, keepdims=False)
    grad_ada = jnp.dot(cond.T, d_modulation_own, precision=highest)
    grad_bias_ada = jnp.sum(d_modulation_own, 0)
    d_cond = jnp.einsum("bic,idc->bd", d_modulation, full_ada.astype(F32), precision=highest)
    table_rows = grid_size // n
    onehot_own = index_all[None, :] == (me * table_rows + jnp.arange(table_rows))[:, None]
    grad_table = jnp.dot(onehot_own.astype(F32), d_cond, precision=highest)
    vector_sums = lax.dynamic_slice_in_dim(vector_sums, me * rows, rows, 1)
    return (
        result,
        back_to_tokens(d_tokens).astype(F32),
        grad_table,
        grad_ada,
        grad_bias_ada,
        vector_sums[0],
        vector_sums[1],
        grad_qkv,
        grad_proj,
        grad_up,
        grad_bias_up,
        grad_down,
        vector_sums[2],
    )


def solution(mesh):
    in_specs = (
        P(None, "mlp", "seq", None),
        P(None, "mlp", "seq", None),
        P(None, "mlp", "seq"),
        P(None, "mlp"),
        P(None, "mlp"),
        P(),
        P(),
        P(None, "seq"),
        P("seq"),
        P("seq"),
        P("seq"),
        P("seq", None),
        P("seq", None),
        P("seq", "mlp"),
        P("mlp"),
        P("mlp", "seq"),
        P("seq"),
    )
    out_specs = (
        P(None, "mlp", "seq", None),
        P(None, "mlp", "seq", None),
        P("seq", None),
        P(None, "seq"),
        P("seq"),
        P("seq"),
        P("seq"),
        P("seq", None),
        P("seq", None),
        P("seq", "mlp"),
        P("mlp"),
        P("mlp", "seq"),
        P("seq"),
    )
    run = functools.partial(body, n=mesh.shape["seq"], m=mesh.shape["mlp"])
    return jax.shard_map(run, mesh=mesh, in_specs=in_specs, out_specs=out_specs, check_vma=False)
```

```python
import functools
import math

import jax
import jax.numpy as jnp
from jax import lax
from jax.experimental import pallas as pl
from jax.experimental.pallas import tpu as pltpu
from jax.sharding import PartitionSpec as P

HEADS = 12
HEAD = 64
MICRO = 3
PLANES = 4
GROUPS = 4
PER_GROUP = HEADS // GROUPS
WIDTH = PER_GROUP * HEAD
QUERY_BLOCK = 256
SCALING = HEAD ** (-0.5)
BF16 = jnp.bfloat16
F32 = jnp.float32
highest = lax.Precision.HIGHEST
SLOPE = math.sqrt(2.0 / math.pi)
CUBIC = 0.044715

SHIFT_ONE, SCALE_ONE, GATE_ONE, SHIFT_TWO, SCALE_TWO, GATE_TWO, GAIN_ONE, GAIN_TWO, BIAS_DOWN = range(9)
SCALES_ALL, GAINS_ONE, GAINS_TWO = 9, 12, 13

VMEM = pl.BlockSpec(memory_space=pltpu.VMEM)
SMEM = pl.BlockSpec(memory_space=pltpu.SMEM)


def nn(left, right):
    return lax.dot_general(left, right, (((1,), (0,)), ((), ())), preferred_element_type=F32)


def nt(left, right):
    return lax.dot_general(left, right, (((1,), (1,)), ((), ())), preferred_element_type=F32)


def standardize(inputs):
    average = jnp.mean(inputs, -1, keepdims=True)
    centred = inputs - average
    spread = jnp.mean(centred * centred, -1, keepdims=True)
    root = lax.rsqrt(spread + 1e-06)
    return centred * root, root


def pull_norm(d_normed, gains, xhat, root):
    e = d_normed * gains
    return root * (e - jnp.mean(e, -1, keepdims=True) - xhat * jnp.mean(e * xhat, -1, keepdims=True))


def over_tokens(value):
    return jnp.sum(value, 0, keepdims=True)


def shape_of(dims, dtype):
    return jax.ShapeDtypeStruct(dims, dtype)


def call(kernel, name, operands, scalars, outs, scratch=(), us=1.0, far=()):
    moved = sum(math.prod(o.shape) * o.dtype.itemsize for o in list(operands) + list(outs))
    return pl.pallas_call(
        kernel,
        out_shape=list(outs),
        in_specs=[SMEM] * len(scalars) + [pl.BlockSpec(memory_space=pl.ANY)] * len(far) + [VMEM] * len(operands),
        out_specs=[VMEM] * len(outs),
        scratch_shapes=list(scratch),
        compiler_params=pltpu.CompilerParams(vmem_limit_bytes=56 * 1024 * 1024),
        cost_estimate=pl.CostEstimate(flops=int(us * 1e9), bytes_accessed=moved, transcendentals=0),
        name=name,
    )(*scalars, *far, *operands)


def fetch(gathered, chunks, weights, arrived):
    copies = [
        pltpu.make_async_copy(gathered.at[:, chunk], weights.at[at], arrived.at[at])
        for at, chunk in enumerate(chunks)
    ]
    for copy in copies:
        copy.start()
    return copies


def whole(weights, at):
    return weights[at].reshape(weights.shape[1] * weights.shape[2], weights.shape[3])


def group_rows(weights, group):
    blocks = WIDTH // weights.shape[2]
    parts = [
        weights[at, pl.ds(group * blocks, blocks)].reshape(WIDTH, weights.shape[3])
        for at in range(weights.shape[0])
    ]
    return parts[0] if len(parts) == 1 else jnp.concatenate(parts, -1)


def modulation(times, table, ada, b_ada, gain_one, gain_two, b_down, mask, small):
    columns = ada.shape[0]
    rows = gain_one.shape[1]
    at = lax.broadcasted_iota(jnp.int32, (8, table.shape[0]), 1)
    line = lax.broadcasted_iota(jnp.int32, (8, table.shape[0]), 0)
    wanted = jnp.where(line == 0, times[0], jnp.where(line == 1, times[1], times[2]))
    cond = nn((at == wanted).astype(F32).astype(BF16), table[...]).astype(BF16)
    part = nt(cond, ada[...]) + b_ada[...].astype(F32)
    small[...] = jnp.zeros_like(small)
    at = 0
    for s in range(MICRO):
        small[0:1, at : at + columns] = part[s : s + 1]
        at += columns
    for ref in (gain_one, gain_two, b_down):
        small[0:1, at : at + rows] = ref[...].astype(F32)
        at += rows
    for s in range(MICRO):
        small[0:1, at : at + mask.shape[1]] = mask[s : s + 1, :].astype(F32)
        at += mask.shape[1]


def prepare_kernel(
    place, times, tokens, upstream, w_qkv, w_up, down, w_proj, table, ada, b_ada, gain_one, gain_two, b_down, mask, *outs
):
    packed, small, outs = outs[0], outs[1], outs[2:]
    columns_out, token_out = outs[:-PLANES], outs[-PLANES:]
    plane, spot = place[0], place[1]
    shard = tokens.shape[1]
    for d, out in enumerate(token_out):
        out[0:shard, :] = tokens[jnp.minimum(plane ^ d, MICRO - 1)]
        out[shard:, :] = upstream[jnp.minimum(plane ^ d, MICRO - 1)]
    width = w_proj.shape[1]
    by_group = [
        jnp.concatenate([w_qkv[:, p * width + g * WIDTH : p * width + (g + 1) * WIDTH] for p in range(3)], -1)
        for g in range(GROUPS)
    ]
    for e, out in enumerate(columns_out):
        group = (spot ^ e) % GROUPS
        here = by_group[0]
        for g in range(1, GROUPS):
            here = jnp.where(group == g, by_group[g], here)
        out[...] = here
    unit = packed.shape[2]
    chunk = 0
    for value in (w_up[...], down[...], w_proj[...]):
        for at in range(0, value.shape[1], unit):
            packed[chunk] = value[:, at : at + unit]
            chunk += 1
    modulation(times, table, ada, b_ada, gain_one, gain_two, b_down, mask, small)


def vectors_kernel(place, weight_index, weight_grid, small, vectors, scale, line):
    n = small.shape[0]
    width = vectors.shape[1]
    columns, rows, shard = 6 * width // n, width // n, scale.shape[0] // PLANES
    plane, spot = place[0], place[1]
    side = n // PLANES
    me = plane * side + spot
    last = jnp.minimum(plane, MICRO - 1)

    def one_of(three):
        return jnp.where(last == 0, three[0], jnp.where(last == 1, three[1], three[2]))

    def pieces(first, size):
        start = first
        while start < first + size:
            stop = min(first + size, (start // width + 1) * width)
            yield start // width, start % width, start - first, stop - start
            start = stop

    vectors[...] = jnp.zeros_like(vectors)
    for i in range(n):
        here = small[pl.ds(me ^ i, 1), :]
        each = [here[:, s * columns : (s + 1) * columns] for s in range(MICRO)]
        mine = one_of(each)
        for part, column, offset, size in pieces(i * columns, columns):
            vectors[part : part + 1, column : column + size] = mine[:, offset : offset + size]
            if part == SCALE_ONE:
                for s in range(MICRO):
                    vectors[SCALES_ALL + s : SCALES_ALL + s + 1, column : column + size] = each[s][
                        :, offset : offset + size
                    ]
        for row in (GAIN_ONE, GAIN_TWO, BIAS_DOWN):
            start = MICRO * columns + (row - GAIN_ONE) * rows
            vectors[row : row + 1, i * rows : (i + 1) * rows] = here[:, start : start + rows]
    for to, gain, by in ((GAINS_ONE, GAIN_ONE, SCALE_ONE), (GAINS_TWO, GAIN_TWO, SCALE_TWO)):
        vectors[to : to + 1, :] = vectors[gain : gain + 1, :] * (1.0 + vectors[by : by + 1, :])
    line[...] = jnp.zeros_like(line)
    for d in range(PLANES):
        here = small[d * side : d * side + 1, :]
        start = MICRO * (columns + rows)
        three = [here[:, start + s * shard : start + (s + 1) * shard] for s in range(MICRO)]
        line[0:1, d * shard : (d + 1) * shard] = one_of(three)
    weight = jnp.where(plane < MICRO, weight_grid[weight_index[last]], 0.0)
    scale[...] = line[...].T[:, 0:1] * weight


def project_kernel(place, gathered, tokens, vectors, *refs, chunks):
    side = len(refs) - 5
    mixed, (attended, middle, normed, weights, arrived) = refs[:side], refs[side:]
    spot = place[1]
    copies = fetch(gathered, chunks, weights, arrived)
    for copy in copies:
        copy.wait()
    total = jnp.zeros(attended.shape, F32)
    for e in range(side):
        other = spot ^ e
        block = mixed[e][...]
        if side > GROUPS:
            block = jnp.where(other < GROUPS, block, jnp.zeros_like(block))
        total = total + nn(block, group_rows(weights, other % GROUPS))
    attended[...] = total
    after = tokens[...].astype(F32) + vectors[GATE_ONE : GATE_ONE + 1] * total
    middle[...] = after
    xhat, _ = standardize(after)
    normed[...] = (xhat * vectors[GAINS_TWO : GAINS_TWO + 1] + vectors[SHIFT_TWO : SHIFT_TWO + 1]).astype(BF16)


def feed_kernel(gathered, rows, d_rows, bias, output, d_normed, active, d_hidden, weights, arrived):
    parts = weights.shape[0] // 2
    unit = weights.shape[3]
    order = [at for part in range(parts) for at in (part, parts + part)]
    copies = fetch(gathered, order, weights, arrived)
    out = jnp.zeros(output.shape, F32)
    back = jnp.zeros(output.shape, F32)
    for part in range(parts):
        columns = slice(part * unit, (part + 1) * unit)
        copies[2 * part].wait()
        up = whole(weights, 2 * part)
        u = nn(rows[...], up) + bias[:, columns]
        square = u * u
        bent = jnp.tanh(SLOPE * u * (1.0 + CUBIC * square))
        half = 0.5 * (1.0 + bent)
        on = (u * half).astype(BF16)
        active[:, columns] = on
        slope = half + 0.5 * u * (1.0 - bent * bent) * (SLOPE * (1.0 + 3.0 * CUBIC * square))
        copies[2 * part + 1].wait()
        down = whole(weights, 2 * part + 1)
        d_on = (nn(d_rows[...], down) * slope).astype(BF16)
        d_hidden[:, columns] = d_on
        out = out + nt(on, down)
        back = back + nt(d_on, up)
    output[...] = out.astype(output.dtype)
    d_normed[...] = back.astype(d_normed.dtype)


def scatter_store(refs, me, device, value):
    kept, sent, chunk, slot_of = refs
    distance = me ^ device
    slot = slot_of(distance)

    @pl.when(distance % 2 == 0)
    def _():
        kept[slot, chunk] = value

    @pl.when(distance % 2 == 1)
    def _():
        sent[slot, chunk] = value


def slot_y_first(distance):
    return ((distance >> 1) & 1) * 4 + ((distance >> 2) & 1) * 2 + ((distance >> 3) & 1)


def down_grads_kernel(*refs, blocks):
    d_rows, active, out = refs[:blocks], refs[blocks:-1], refs[-1]
    unit = out.shape[3]
    turned = [ref[...].T for ref in d_rows]
    for chunk in range(out.shape[1]):
        columns = slice(chunk * unit, (chunk + 1) * unit)
        grad = sum(nn(turned[b], active[b][:, columns]) for b in range(blocks)).astype(BF16)
        out[:, chunk] = grad.reshape(out.shape[0], out.shape[2], unit)


def up_grads_kernel(place, *refs, blocks, scatter):
    rows_all, d_hidden, outs = refs[:blocks], refs[blocks : 2 * blocks], refs[2 * blocks :]
    bias = outs[-1]
    me = place[2]
    width, count = rows_all[0].shape[1], bias.shape[1]
    unit = min(width, count)
    turned = [ref[...].T for ref in rows_all]
    for chunk in range(count // unit):
        columns = slice(chunk * unit, (chunk + 1) * unit)
        grad = sum(nn(turned[b], d_hidden[b][:, columns]) for b in range(blocks)).astype(BF16)
        bias[:, columns] = sum(over_tokens(d_hidden[b][:, columns].astype(F32)) for b in range(blocks))
        if scatter:
            rows = outs[0].shape[2]
            for i in range(width // rows):
                part = grad[i * rows : (i + 1) * rows]
                scatter_store((outs[0], outs[1], chunk, slot_y_first), me, i, part)
        else:
            outs[0][:, columns] = grad


def proj_grads_kernel(place, d_attended, *refs, side, scatter):
    mixed, refs = refs[:side], refs[side:]
    spot, me = place[1], place[2]
    width = d_attended.shape[1]
    whole_grad = refs[-1]
    if side > GROUPS:
        whole_grad[...] = jnp.zeros_like(whole_grad)
    for e in range(side):
        other = spot ^ e
        first = pl.multiple_of((other % GROUPS) * WIDTH, WIDTH)
        grad = nn(mixed[e][...].T, d_attended[...]).astype(BF16)
        if side > GROUPS:
            grad = whole_grad[pl.ds(first, WIDTH), :] + jnp.where(other < GROUPS, grad, jnp.zeros_like(grad))
        whole_grad[pl.ds(first, WIDTH), :] = grad
    if not scatter:
        refs[0][...] = whole_grad[...]
        return
    _, _, own, sent, ready, done, _ = refs
    rows, chunk = own.shape[2], own.shape[1] - 1
    for i in range(width // rows):
        part = whole_grad[i * rows : (i + 1) * rows, :]
        scatter_store((ready.at[0], ready.at[1], 0, slot_y_first), me, i, part)
    copies = [
        pltpu.make_async_copy(ready.at[at, :, 0], out.at[:, chunk], done.at[at])
        for at, out in enumerate((own, sent))
    ]
    for copy in copies:
        copy.start()
    for copy in copies:
        copy.wait()


def qkv_grads_kernel(place, d_project, normed, *outs):
    grad = nn(d_project[...], normed[...]).astype(BF16).T
    plane, slice_of = place[0], place[3]
    rows = outs[0].shape[1]
    if len(outs[0].shape) == 3 and outs[0].shape[0] == PLANES:
        for at in range(PLANES):
            distance = plane ^ at
            slot = (distance % 2) * 2 + distance // 2
            halves = [grad[(2 * at + half) * rows : (2 * at + half + 1) * rows] for half in range(2)]
            outs[0][slot] = jnp.where(slice_of == 0, halves[0], halves[1])
            outs[1][slot] = jnp.where(slice_of == 0, halves[1], halves[0])
    else:
        for at in range(PLANES):
            part = grad[at * rows : (at + 1) * rows]
            distance = plane ^ at

            @pl.when(distance % 2 == 0)
            def _():
                outs[0][distance // 2] = part

            @pl.when(distance % 2 == 1)
            def _():
                outs[1][distance // 2] = part


def normed_backward_kernel(d_project, weight, *refs, blocks):
    tokens, (kept, sent, sums) = refs[:blocks], refs[blocks:]
    count = tokens[0].shape[0]
    d_shift = jnp.zeros((1, weight.shape[0]), F32)
    d_xhat = jnp.zeros((1, weight.shape[0]), F32)
    for block in range(blocks):
        part = nt(d_project[:, block * count : (block + 1) * count].T, weight[...])
        (sent if block % 2 else kept)[block // 2] = part.astype(BF16)
        xhat, _ = standardize(tokens[block][...].astype(F32))
        d_shift = d_shift + over_tokens(part)
        d_xhat = d_xhat + over_tokens(part * xhat)
    sums[0:1, :] = d_shift
    sums[1:2, :] = d_xhat
    sums[2:8, :] = jnp.zeros((6, weight.shape[0]), F32)


def middle_kernel(place, gathered, vectors, upstream, scale, attended, middle, d_own, *refs, others, chunks):
    arrived, refs = refs[:others], refs[others:]
    d_mixed, (d_middle, d_attended, sums, weights, copied) = refs[:-5], refs[-5:]
    spot = place[1]
    copies = fetch(gathered, chunks, weights, copied)
    width = middle.shape[1]
    d_normed = d_own[...]
    for ref in arrived:
        d_normed = d_normed + ref[...].astype(F32)
    xhat, root = standardize(middle[...])
    d_result = upstream[...].astype(F32) * scale[...]
    d_after = d_result + pull_norm(d_normed, vectors[GAINS_TWO : GAINS_TWO + 1], xhat, root)
    d_middle[...] = d_after
    low = (vectors[GATE_ONE : GATE_ONE + 1] * d_after).astype(BF16)
    d_attended[...] = low
    for copy in copies:
        copy.wait()
    for e in range(len(d_mixed)):
        d_mixed[e][...] = nt(low, group_rows(weights, (spot ^ e) % GROUPS)).astype(BF16)
    sums[0:1, :] = over_tokens(d_after * attended[...])
    sums[1:2, :] = over_tokens(d_normed)
    sums[2:3, :] = over_tokens(d_normed * xhat)
    sums[3:8, :] = jnp.zeros((5, width), F32)


def output_kernel(vectors, upstream, scale, middle, own, *refs, others):
    arrived, (result, sums) = refs[:others], refs[others:]
    output = own[...] + vectors[BIAS_DOWN : BIAS_DOWN + 1]
    for ref in arrived:
        output = output + ref[...].astype(F32)
    gate = vectors[GATE_TWO : GATE_TWO + 1]
    result[...] = (middle[...] + gate * output).astype(BF16)
    d_result = upstream[...].astype(F32) * scale[...]
    sums[0:1, :] = over_tokens(d_result * output)
    sums[1:2, :] = over_tokens(gate * d_result)
    sums[2:8, :] = jnp.zeros((6, middle.shape[1]), F32)


def tokens_kernel(vectors, tokens, d_middle, own, arrived, d_tokens):
    xhat, root = standardize(tokens[...].astype(F32))
    d_normed = own[...].astype(F32) + arrived[...].astype(F32)
    back = pull_norm(d_normed, vectors[GAINS_ONE : GAINS_ONE + 1], xhat, root)
    d_tokens[...] = (d_middle[...] + back).astype(BF16)


def forward_kernel(place, *refs, blocks, halves):
    tokens, refs = refs[:blocks], refs[blocks:]
    count = 2 if halves else PLANES
    weights, refs = refs[:count], refs[count:]
    (vectors, cosine, sines), refs = refs[:3], refs[3:]
    gain, shift = vectors[GAINS_ONE : GAINS_ONE + 1], vectors[SHIFT_ONE : SHIFT_ONE + 1]
    mixed, refs = refs[:blocks], refs[blocks:]
    heads, log_total, normed, weight, keys, mixed_turned = refs
    plane = place[0]
    rows = weights[0].shape[-2]
    count = tokens[0].shape[0]
    if halves:
        for half in range(2):
            for distance in range(PLANES):
                first = pl.multiple_of((plane ^ distance) * 2 * rows + (place[3] ^ half) * rows, 16)
                weight[pl.ds(first, rows), :] = weights[half][distance]
    else:
        for distance in range(PLANES):
            first = pl.multiple_of((plane ^ distance) * rows, 8)
            weight[pl.ds(first, rows), :] = weights[distance][...]
    for block in range(blocks):
        xhat, _ = standardize(tokens[block][...].astype(F32))
        normed[block * count : (block + 1) * count, :] = (xhat * gain + shift).astype(BF16)
    project = nt(weight[...].T, normed[...])
    cos, sin = cosine[...], sines[...]
    half = HEAD // 2
    for part in range(2):
        for head in range(PER_GROUP):
            start = part * WIDTH + head * HEAD
            first, second = project[start : start + half], project[start + half : start + HEAD]
            turned = jnp.concatenate([first * cos - second * sin, second * cos + first * sin], 0).astype(BF16)
            if part == 0:
                turned = turned * jnp.asarray(SCALING, BF16)
            else:
                keys[head] = turned.T
            heads[start : start + HEAD, :] = turned
    heads[2 * WIDTH :, :] = project[2 * WIDTH :].astype(BF16)
    length = heads.shape[1]
    for head in range(PER_GROUP):
        start = head * HEAD

        def queries_step(step, carry):
            columns = pl.ds(pl.multiple_of(step * QUERY_BLOCK, QUERY_BLOCK), QUERY_BLOCK)
            scores = nn(keys[head], heads[start : start + HEAD, columns])
            peak = jnp.max(scores, 0, keepdims=True)
            exps = jnp.exp(scores - peak)
            total = jnp.sum(exps, 0, keepdims=True)
            log_total[head : head + 1, columns] = peak + jnp.log(total)
            probs = (exps * (1.0 / total)).astype(BF16)
            values = heads[2 * WIDTH + start : 2 * WIDTH + start + HEAD, :]
            mixed_turned[start : start + HEAD, columns] = nn(values, probs).astype(BF16)
            return carry

        lax.fori_loop(0, length // QUERY_BLOCK, queries_step, 0)
    for block in range(blocks):
        mixed[block][...] = mixed_turned[:, block * count : (block + 1) * count].T


def backward_kernel(*refs, blocks):
    d_mixed, refs = refs[:blocks], refs[blocks:]
    (heads, log_total, cosine, sines), refs = refs[:4], refs[4:]
    d_project, d_turned, d_keys, d_values, keys, values = refs
    count = d_mixed[0].shape[0]
    length = heads.shape[1]
    for block in range(blocks):
        d_turned[:, block * count : (block + 1) * count] = d_mixed[block][...].T
    cos, sin = cosine[...], sines[...]
    half = HEAD // 2
    d_keys[...] = jnp.zeros_like(d_keys)
    d_values[...] = jnp.zeros_like(d_values)
    for head in range(PER_GROUP):
        start = head * HEAD
        keys_turned = heads.at[WIDTH + start : WIDTH + start + HEAD]
        keys[...] = keys_turned[...].T
        values[...] = heads[2 * WIDTH + start : 2 * WIDTH + start + HEAD, :].T

        def queries_step(step, carry):
            columns = pl.ds(pl.multiple_of(step * QUERY_BLOCK, QUERY_BLOCK), QUERY_BLOCK)
            queries = heads[start : start + HEAD, columns]
            incoming = d_turned[start : start + HEAD, columns]
            scores = nn(keys[...], queries)
            probs = jnp.exp(scores - log_total[head : head + 1, columns])
            d_probs = nn(values[...], incoming)
            delta = jnp.sum(probs * d_probs, 0, keepdims=True)
            d_scores = (probs * (d_probs - delta)).astype(BF16)
            d_values[start : start + HEAD, :] += nt(incoming, probs.astype(BF16))
            d_keys[start : start + HEAD, :] += nt(queries, d_scores)
            d_queries = nn(keys_turned[...], d_scores) * SCALING
            first, second = d_queries[:half], d_queries[half:]
            cos_here, sin_here = cosine[:, columns], sines[:, columns]
            d_project[start : start + half, columns] = (first * cos_here + second * sin_here).astype(BF16)
            d_project[start + half : start + HEAD, columns] = (second * cos_here - first * sin_here).astype(BF16)
            return carry

        lax.fori_loop(0, length // QUERY_BLOCK, queries_step, 0)
        first, second = d_keys[start : start + half, :], d_keys[start + half : start + HEAD, :]
        d_project[WIDTH + start : WIDTH + start + half, :] = (first * cos + second * sin).astype(BF16)
        d_project[WIDTH + start + half : WIDTH + start + HEAD, :] = (second * cos - first * sin).astype(BF16)
    d_project[2 * WIDTH :, :] = d_values[...].astype(BF16)


def attend_forward(place, tokens, weights, vectors, cosine, sines, halves):
    blocks, (count, width) = len(tokens), tokens[0].shape
    length = blocks * count
    columns = weights[0].shape[-1]
    outs = call(
        functools.partial(forward_kernel, blocks=blocks, halves=halves),
        "attend_forward",
        [*tokens, *weights, vectors, cosine, sines],
        [place],
        [shape_of((count, WIDTH), BF16)] * blocks
        + [
            shape_of((columns, length), BF16),
            shape_of((8, length), F32),
            shape_of((length, width), BF16),
            shape_of((width, columns), BF16),
        ],
        [pltpu.VMEM((PER_GROUP, length, HEAD), BF16), pltpu.VMEM((WIDTH, length), BF16)],
        us=15.0,
    )
    return outs[:blocks], outs[blocks:]


def attend_backward(d_mixed, heads, log_total, cosine, sines):
    blocks, length = len(d_mixed), heads.shape[1]
    (d_project,) = call(
        functools.partial(backward_kernel, blocks=blocks),
        "attend_backward",
        [*d_mixed, heads, log_total, cosine, sines],
        [],
        [shape_of((3 * WIDTH, length), BF16)],
        [
            pltpu.VMEM((WIDTH, length), BF16),
            pltpu.VMEM((WIDTH, length), F32),
            pltpu.VMEM((WIDTH, length), F32),
            pltpu.VMEM((length, HEAD), BF16),
            pltpu.VMEM((length, HEAD), BF16),
        ],
        us=18.0,
    )
    return d_project


def after(values, *others):
    return lax.optimization_barrier((values, others))[0]


def add(left, right):
    return (left.astype(F32) + right.astype(F32)).astype(BF16)


def pick(stack, index):
    return lax.dynamic_index_in_dim(stack, index, 0, keepdims=False)


def bits_of(count):
    return [1 << bit for bit in range(count.bit_length() - 1)]


def body(
    tokens,
    upstream,
    token_mask,
    time_index,
    weight_index,
    time_table,
    weight_grid,
    w_ada,
    b_ada,
    gain_one,
    gain_two,
    w_qkv,
    w_proj,
    w_up,
    b_up,
    w_down,
    b_down,
    *,
    n,
    m,
):
    side = n // PLANES
    me = lax.axis_index("seq")
    plane, spot = me // side, me % side
    slice_of = lax.axis_index("mlp")
    place = jnp.stack([plane, spot, me, slice_of]).astype(jnp.int32)
    shard, width = tokens.shape[2], tokens.shape[3]
    rows = w_qkv.shape[0]
    hidden_count = w_up.shape[1]
    grid_size = time_table.shape[0]
    ada_columns = w_ada.shape[1]
    count = PLANES * shard
    unit = min(width, hidden_count)
    hidden_chunks, width_chunks = hidden_count // unit, width // unit
    pairwise = rows % 16 == 0 and side == GROUPS and unit == width and m == 2
    z_bits, y_bit, core_bit = (2 * side, side), 2, 1

    def swap(value, distance):
        return lax.ppermute(value, "seq", [(i, i ^ distance) for i in range(n)])

    def swap_mlp(value, distance):
        return lax.ppermute(value, "mlp", [(i, i ^ distance) for i in range(m)])

    def between_planes(pieces):
        return [pieces[0]] + [swap(pieces[d], d * side) for d in range(1, PLANES)]

    def in_plane(pieces):
        return [pieces[0]] + [swap(pieces[e], e) for e in range(1, side)]

    def in_order(blocks, axis):
        halves = jnp.stack(blocks)
        for bit in bits_of(len(blocks)):
            here = halves.reshape((len(blocks) // (2 * bit), 2, bit) + halves.shape[1:])
            halves = jnp.where((axis & bit) != 0, here[:, ::-1], here).reshape(halves.shape)
        return halves

    def for_plane(values):
        return [pick(values, jnp.minimum(plane ^ d, MICRO - 1)) for d in range(PLANES)]

    def columns_of(value):
        return [value[:, at : at + unit] for at in range(0, value.shape[1], unit)]

    line = [value[None] for value in (b_ada, gain_one, gain_two, b_down)]
    small_count = -(-MICRO * (ada_columns + rows + shard) // 128) * 128
    first_shapes = [shape_of((2 * hidden_chunks + width_chunks, rows, unit), BF16), shape_of((1, small_count), F32)]
    first_shapes += [shape_of((rows, 3 * WIDTH), BF16)] * side + [shape_of((2 * shard, width), BF16)] * PLANES
    packed, small, *pieces = call(
        prepare_kernel,
        "prepare",
        [tokens[:, 0], upstream[:, 0], w_qkv, w_up, w_down.T, w_proj, time_table, w_ada.T, *line, token_mask[:, 0]],
        [place, time_index[:, 0]],
        first_shapes,
        us=4.0,
    )
    group_columns, token_pieces = pieces[:side], pieces[side:]

    gathered = lax.all_gather(packed, "seq", axis=0)
    if not pairwise:
        gathered = gathered.transpose(1, 0, 2, 3).reshape(-1, GROUPS, WIDTH, unit).transpose(1, 0, 2, 3)
    blocks_shape = (gathered.shape[0],) + gathered.shape[2:]
    proj_chunks = list(range(2 * hidden_chunks, 2 * hidden_chunks + width_chunks))

    def weight_scratch(number):
        return [pltpu.VMEM((number,) + blocks_shape, BF16), pltpu.SemaphoreType.DMA((number,))]

    received = jnp.stack(in_plane(group_columns))
    arrived = after(between_planes(token_pieces), received)
    own_low = jnp.concatenate([piece[:shard] for piece in arrived], 0)
    own_upstream = jnp.concatenate([piece[shard:] for piece in arrived], 0)
    token_blocks = {0: own_low}
    for bit in reversed(bits_of(side)):
        for known in list(token_blocks):
            token_blocks[known | bit] = swap(token_blocks[known], bit)
    token_blocks = [token_blocks[at] for at in range(side)]

    weight_block = jnp.concatenate([pick(received, spot ^ at) for at in range(side)], 0)
    if pairwise:
        weight_block = pick(weight_block.reshape(2, width // 8, 3 * WIDTH), slice_of)
    weight_blocks = {0: weight_block}
    for bit in (2, 1):
        for known in list(weight_blocks):
            weight_blocks[known | bit] = swap(weight_blocks[known], bit * side)
    weight_blocks = [weight_blocks[at] for at in range(PLANES)]
    if pairwise:
        weight_blocks = jnp.stack(weight_blocks)
        weight_blocks = [weight_blocks, swap_mlp(weight_blocks, 1)]

    for bit in bits_of(n):
        small = jnp.concatenate([small, swap(small, bit)], 0)
    vectors, scale = call(
        vectors_kernel,
        "vectors",
        [small],
        [place, weight_index[:, 0], weight_grid],
        [shape_of((16, width), F32), shape_of((count, 1), F32)],
        [pltpu.VMEM((8, count), F32)],
    )

    order = ((plane ^ jnp.arange(PLANES))[None, :] * side + (spot ^ jnp.arange(side))[:, None]) * shard
    positions = (order[:, :, None] + jnp.arange(shard)).reshape(1, -1).astype(F32)
    frequency = 10000.0 ** (-jnp.arange(0, HEAD, 2).astype(F32) / HEAD)
    angles = frequency[:, None] * positions
    cosine, sines = jnp.cos(angles), jnp.sin(angles)

    mixed_blocks, kept = attend_forward(
        place, token_blocks, weight_blocks, vectors, cosine, sines, pairwise
    )

    full_ada = lax.all_gather(after(w_ada, gathered), "seq", axis=0)

    mixed_blocks = in_plane(mixed_blocks)

    d_rows = ((own_upstream.astype(F32) * scale) * vectors[GATE_TWO][None]).astype(BF16)
    d_rows = [d_rows] + [swap_mlp(d_rows, d) for d in range(1, m)]

    attended, middle, normed_two = call(
        functools.partial(project_kernel, chunks=proj_chunks),
        "project",
        [own_low, vectors, *mixed_blocks],
        [place],
        [shape_of((count, width), F32), shape_of((count, width), F32), shape_of((count, width), BF16)],
        weight_scratch(width_chunks),
        us=3.0,
        far=[gathered],
    )
    rows_all = [normed_two] + [swap_mlp(normed_two, d) for d in range(1, m)]
    bias_up = b_up.astype(F32)[None]
    fed = [
        call(
            feed_kernel,
            "feed_forward",
            [rows_all[d], d_rows[d], bias_up],
            [],
            [shape_of((count, width), BF16 if d else F32)] * 2 + [shape_of((count, hidden_count), BF16)] * 2,
            weight_scratch(2 * hidden_chunks),
            us=6.0,
            far=[gathered],
        )
        for d in range(m)
    ]
    d_arrived = [swap_mlp(fed[d][1], d) for d in range(1, m)]
    out_arrived = [swap_mlp(fed[d][0], d) for d in range(1, m)]
    slots = n // 2
    down_shape = (n, hidden_chunks, rows, unit) if pairwise else (GROUPS, hidden_chunks, WIDTH, unit)
    if pairwise:
        up_shapes = [shape_of((slots, hidden_chunks + width_chunks, rows, unit), BF16)] * 2
    else:
        up_shapes = [shape_of((width, hidden_count), BF16)]
    (down_grads,) = call(
        functools.partial(down_grads_kernel, blocks=m),
        "down_gradients",
        [*d_rows, *[f[2] for f in fed]],
        [],
        [shape_of(down_shape, BF16)],
        us=6.0,
    )
    *up_grads, bias_up_sum = call(
        functools.partial(up_grads_kernel, blocks=m, scatter=pairwise),
        "up_gradients",
        [*rows_all, *[f[3] for f in fed]],
        [place],
        up_shapes + [shape_of((1, hidden_count), F32)],
        us=5.0,
    )
    d_arrived, down_grads, full_ada, *up_grads = lax.optimization_barrier(
        (d_arrived, down_grads, full_ada, *up_grads)
    )
    if not pairwise:
        down_grads = down_grads.transpose(1, 0, 2, 3).reshape(hidden_chunks, n, rows, unit).transpose(1, 0, 2, 3)
    down_grads = lax.psum_scatter(down_grads, "seq", scatter_dimension=0, tiled=True)
    middle_outs = call(
        functools.partial(middle_kernel, others=m - 1, chunks=proj_chunks),
        "middle_backward",
        [vectors, own_upstream, scale, attended, middle, fed[0][1], *d_arrived],
        [place],
        [shape_of((count, WIDTH), BF16)] * side
        + [shape_of((count, width), F32), shape_of((count, width), BF16), shape_of((8, width), F32)],
        weight_scratch(width_chunks),
        us=4.0,
        far=[gathered],
    )
    d_mixed_blocks, (d_middle, d_attended, middle_sums) = middle_outs[:side], middle_outs[side:]

    d_mixed_blocks = in_plane(d_mixed_blocks)
    if side > GROUPS:
        share = (spot < GROUPS).astype(BF16)
        d_mixed_blocks = [block * share for block in d_mixed_blocks]

    anywhere = pl.BlockSpec(memory_space=pl.ANY)
    proj_grads = pl.pallas_call(
        functools.partial(proj_grads_kernel, side=side, scatter=pairwise),
        out_shape=up_shapes if pairwise else [shape_of((width, width), BF16)],
        in_specs=[SMEM] + [VMEM] * (1 + side) + ([anywhere] * 2 if pairwise else []),
        out_specs=[anywhere] * 2 if pairwise else [VMEM],
        scratch_shapes=(
            [pltpu.VMEM((2, slots, 1, rows, unit), BF16), pltpu.SemaphoreType.DMA((2,))] if pairwise else []
        )
        + [pltpu.VMEM((width, width), BF16)],
        input_output_aliases={2 + side: 0, 3 + side: 1} if pairwise else {},
        compiler_params=pltpu.CompilerParams(vmem_limit_bytes=56 * 1024 * 1024),
        cost_estimate=pl.CostEstimate(flops=2 * 10**9, bytes_accessed=4 * 10**6, transcendentals=0),
        name="proj_gradients",
    )(place, d_attended, *mixed_blocks, *(up_grads if pairwise else []))

    def add_halves(own, arrived):
        half = own.shape[0] // 2
        return add(own[:half], arrived[:half]), add(own[half:], arrived[half:])

    def back_to_tokens(value):
        received = between_planes([value[d * shard : (d + 1) * shard] for d in range(PLANES)])
        received = jnp.stack(received)
        return jnp.stack([pick(received, plane ^ at) for at in range(MICRO)])[:, None]

    if pairwise:
        up_arrived = swap(proj_grads[1], core_bit)
        out_arrived = after(out_arrived, proj_grads[0])

    result, output_sums = call(
        functools.partial(output_kernel, others=m - 1),
        "output",
        [vectors, own_upstream, scale, middle, fed[0][0], *out_arrived],
        [],
        [shape_of((count, width), BF16), shape_of((8, width), F32)],
    )
    if pairwise:
        up_own, up_sent = add_halves(proj_grads[0], after(up_arrived, result, *d_mixed_blocks))
        up_sent, result, *d_mixed_blocks = lax.optimization_barrier((up_sent, result, *d_mixed_blocks))
    result = back_to_tokens(result)

    d_project = attend_backward(d_mixed_blocks, kept[0], kept[1], cosine, sines)
    if pairwise:
        up_arrived = swap(up_sent, y_bit)
        d_project, result, up_arrived = lax.optimization_barrier((d_project, result, up_arrived))
    qkv_shape = (PLANES, width // 8, 3 * WIDTH) if pairwise else (2, width // PLANES, 3 * WIDTH)
    grad_own, grad_sent = call(
        qkv_grads_kernel,
        "qkv_gradients",
        [d_project, kept[2]],
        [place],
        [shape_of(qkv_shape, BF16)] * 2,
        us=4.0,
    )
    d_project = after(d_project, grad_sent)
    d_kept, d_sent, sums = call(
        functools.partial(normed_backward_kernel, blocks=side),
        "normed_backward",
        [d_project, kept[3], *token_blocks],
        [],
        [shape_of((side // 2, count, width), BF16)] * 2 + [shape_of((8, width), F32)],
        us=4.0,
    )
    if pairwise:
        up_own, up_sent = add_halves(up_own, after(up_arrived, grad_sent))
        grad_arrived = after(swap_mlp(grad_sent, 1), d_sent)
        grad_own, grad_sent = add_halves(grad_own, grad_arrived)
    arrived = swap(d_sent, 1)

    blocks = {2 * at: d_kept[at] for at in range(side // 2)}
    steps = [arrived]
    for at in range(side // 2):
        blocks[2 * at] = add(blocks[2 * at], arrived[at])
    for bit in bits_of(side)[1:]:
        for at in [at for at in blocks if at & bit]:
            arrived = swap(blocks.pop(at), bit)
            steps.append(arrived)
            if len(blocks) > 1:
                blocks[at ^ bit] = add(blocks[at ^ bit], arrived)
    (d_tokens,) = call(
        tokens_kernel,
        "tokens_backward",
        [vectors, own_low, d_middle, blocks[0], arrived],
        [],
        [shape_of((count, width), BF16)],
    )

    if pairwise:
        up_own, up_sent = add_halves(up_own, after(swap(up_sent, side), steps[0]))
        up_parts = up_own[0].astype(F32) + after(swap(up_sent, 2 * side), d_tokens)[0].astype(F32)
        grad_up = jnp.concatenate([up_parts[at] for at in range(hidden_chunks)], -1)
        grad_proj = up_parts[hidden_chunks]
    else:
        grads = jnp.stack(columns_of(up_grads[0]) + columns_of(proj_grads[0]))
        grads = grads.reshape(-1, n, rows, unit).transpose(1, 0, 2, 3)
        grads = lax.psum_scatter(grads, "seq", scatter_dimension=0, tiled=True)[0]

        def columns_from(start, number):
            return jnp.concatenate([grads[start + at] for at in range(number)], -1).astype(F32)

        grad_up = columns_from(0, hidden_chunks)
        grad_proj = columns_from(hidden_chunks, width_chunks)
    for bit in bits_of(m):
        grad_proj = grad_proj + swap_mlp(grad_proj.astype(BF16), bit).astype(F32)

    arrived = after(swap(grad_sent, side), steps[0])
    if pairwise:
        grad_own, grad_sent = add_halves(grad_own, arrived)
        arrived = after(swap(grad_sent, 2 * side), d_tokens)
        total = grad_own[0].astype(F32) + arrived[0].astype(F32)
        by_spot = total.astype(BF16).reshape(2, rows, 3 * WIDTH)
        slices = [pick(by_spot, (spot ^ e) % 2) for e in range(side)]
    else:
        arrived = swap(add(grad_own[1], arrived[1]), 2 * side).astype(F32) + arrived[0].astype(F32)
        total = grad_own[0].astype(F32) + arrived
        by_spot = total.astype(BF16).reshape(side, rows, 3 * WIDTH)
        slices = [pick(by_spot, spot ^ e) for e in range(side)]
    received = jnp.stack(in_plane(slices))
    grad_qkv = jnp.stack([pick(received, spot ^ group) for group in range(GROUPS)])
    grad_qkv = grad_qkv.reshape(GROUPS, rows, 3, WIDTH).transpose(1, 2, 0, 3).reshape(rows, 3 * width)
    if pairwise:
        grad_qkv = jnp.where(spot // 2 == slice_of, grad_qkv, swap_mlp(grad_qkv, 1)).astype(F32)
    else:
        grad_qkv = grad_qkv.astype(F32)
        for bit in bits_of(m):
            grad_qkv = grad_qkv + swap_mlp(grad_qkv.astype(BF16), bit).astype(F32)

    down_grads = after(down_grads[0], steps[-1]).astype(F32)
    grad_down = jnp.concatenate([down_grads[at] for at in range(hidden_chunks)], -1).T

    bias_up_rows = -(-hidden_count // width)
    bias_up_sum = jnp.pad(bias_up_sum, ((0, 0), (0, bias_up_rows * width - hidden_count)))
    small = jnp.concatenate(
        [sums[0:2], middle_sums[0:3], output_sums[0:2], bias_up_sum.reshape(-1, width)], 0
    )
    small = small + swap(small, 1)
    small = after(small, steps[0])
    for bit in bits_of(side)[1:]:
        small = small + swap(small, bit)
    small = jnp.concatenate([small, vectors[SCALE_TWO][None]], 0)[None]
    small = after(small, steps[-1])
    for bit in bits_of(PLANES):
        small = jnp.concatenate([small, swap(small, bit * side)], 0)
    small = in_order(list(small), plane)[:MICRO]
    grad_bias_up = jnp.sum(small[:, 7 : 7 + bias_up_rows], 0).reshape(-1)[:hidden_count]
    d_shift_one, d_xhat_one, d_gate_one, d_shift_two, d_xhat_two, d_gate_two = [small[:, at] for at in range(6)]
    index_here = time_index[:, 0]
    vector_sums = jnp.stack(
        [
            jnp.sum((1.0 + vectors[SCALES_ALL : SCALES_ALL + MICRO]) * d_xhat_one, 0),
            jnp.sum((1.0 + small[:, -1]) * d_xhat_two, 0),
            jnp.sum(small[:, 6], 0),
            jnp.pad(index_here.astype(F32), (0, width - MICRO)),
        ]
    )
    d_scale_one, d_scale_two = vectors[GAIN_ONE] * d_xhat_one, vectors[GAIN_TWO] * d_xhat_two
    small = jnp.stack([d_shift_one, d_scale_one, d_gate_one, d_shift_two, d_scale_two, d_gate_two], 1)
    small = jnp.concatenate([small.reshape(6 * MICRO, width), vector_sums], 0)[None]
    for bit in bits_of(m):
        small = jnp.concatenate([small, swap_mlp(small, bit)], 0)
    at = 6 * MICRO
    d_modulation = small[:, :at].reshape(m * MICRO, n, ada_columns)
    vector_sums = jnp.sum(small[:, at : at + 3], 0)
    index_all = small[:, at + 3, :MICRO].reshape(-1).astype(jnp.int32)
    onehot = (index_all[:, None] == jnp.arange(grid_size)[None, :]).astype(BF16)
    cond = jnp.dot(onehot, time_table, preferred_element_type=F32)
    d_modulation_own = lax.dynamic_index_in_dim(d_modulation, me, 1, keepdims=False)
    grad_ada = jnp.dot(cond.T, d_modulation_own, precision=highest)
    grad_bias_ada = jnp.sum(d_modulation_own, 0)
    d_cond = jnp.einsum("bic,idc->bd", d_modulation, full_ada.astype(F32), precision=highest)
    table_rows = grid_size // n
    onehot_own = index_all[None, :] == (me * table_rows + jnp.arange(table_rows))[:, None]
    grad_table = jnp.dot(onehot_own.astype(F32), d_cond, precision=highest)
    vector_sums = lax.dynamic_slice_in_dim(vector_sums, me * rows, rows, 1)
    return (
        result,
        back_to_tokens(d_tokens).astype(F32),
        grad_table,
        grad_ada,
        grad_bias_ada,
        vector_sums[0],
        vector_sums[1],
        grad_qkv,
        grad_proj,
        grad_up,
        grad_bias_up,
        grad_down,
        vector_sums[2],
    )


def solution(mesh):
    in_specs = (
        P(None, "mlp", "seq", None),
        P(None, "mlp", "seq", None),
        P(None, "mlp", "seq"),
        P(None, "mlp"),
        P(None, "mlp"),
        P(),
        P(),
        P(None, "seq"),
        P("seq"),
        P("seq"),
        P("seq"),
        P("seq", None),
        P("seq", None),
        P("seq", "mlp"),
        P("mlp"),
        P("mlp", "seq"),
        P("seq"),
    )
    out_specs = (
        P(None, "mlp", "seq", None),
        P(None, "mlp", "seq", None),
        P("seq", None),
        P(None, "seq"),
        P("seq"),
        P("seq"),
        P("seq"),
        P("seq", None),
        P("seq", None),
        P("seq", "mlp"),
        P("mlp"),
        P("mlp", "seq"),
        P("seq"),
    )
    run = functools.partial(body, n=mesh.shape["seq"], m=mesh.shape["mlp"])
    return jax.shard_map(run, mesh=mesh, in_specs=in_specs, out_specs=out_specs, check_vma=False)
```

```python
import functools
import math

import jax
import jax.numpy as jnp
from jax import lax
from jax.experimental import pallas as pl
from jax.experimental.pallas import tpu as pltpu
from jax.sharding import PartitionSpec as P

HEADS = 12
HEAD = 64
MICRO = 3
PLANES = 4
GROUPS = 4
PER_GROUP = HEADS // GROUPS
WIDTH = PER_GROUP * HEAD
QUERY_BLOCK = 256
SCALING = HEAD ** (-0.5)
BF16 = jnp.bfloat16
F32 = jnp.float32
highest = lax.Precision.HIGHEST
SLOPE = math.sqrt(2.0 / math.pi)
CUBIC = 0.044715

SHIFT_ONE, SCALE_ONE, GATE_ONE, SHIFT_TWO, SCALE_TWO, GATE_TWO, GAIN_ONE, GAIN_TWO, BIAS_DOWN = range(9)
SCALES_ALL, GAINS_ONE, GAINS_TWO = 9, 12, 13

VMEM = pl.BlockSpec(memory_space=pltpu.VMEM)
SMEM = pl.BlockSpec(memory_space=pltpu.SMEM)


def nn(left, right):
    return lax.dot_general(left, right, (((1,), (0,)), ((), ())), preferred_element_type=F32)


def nt(left, right):
    return lax.dot_general(left, right, (((1,), (1,)), ((), ())), preferred_element_type=F32)


def standardize(inputs):
    average = jnp.mean(inputs, -1, keepdims=True)
    centred = inputs - average
    spread = jnp.mean(centred * centred, -1, keepdims=True)
    root = lax.rsqrt(spread + 1e-06)
    return centred * root, root


def pull_norm(d_normed, gains, xhat, root):
    e = d_normed * gains
    return root * (e - jnp.mean(e, -1, keepdims=True) - xhat * jnp.mean(e * xhat, -1, keepdims=True))


def over_tokens(value):
    return jnp.sum(value, 0, keepdims=True)


def shape_of(dims, dtype):
    return jax.ShapeDtypeStruct(dims, dtype)


def call(kernel, name, operands, scalars, outs, scratch=(), us=1.0, far=()):
    moved = sum(math.prod(o.shape) * o.dtype.itemsize for o in list(operands) + list(outs))
    return pl.pallas_call(
        kernel,
        out_shape=list(outs),
        in_specs=[SMEM] * len(scalars) + [pl.BlockSpec(memory_space=pl.ANY)] * len(far) + [VMEM] * len(operands),
        out_specs=[VMEM] * len(outs),
        scratch_shapes=list(scratch),
        compiler_params=pltpu.CompilerParams(vmem_limit_bytes=56 * 1024 * 1024),
        cost_estimate=pl.CostEstimate(flops=int(us * 1e9), bytes_accessed=moved, transcendentals=0),
        name=name,
    )(*scalars, *far, *operands)


def fetch(gathered, chunks, weights, arrived):
    copies = [
        pltpu.make_async_copy(gathered.at[:, chunk], weights.at[at], arrived.at[at])
        for at, chunk in enumerate(chunks)
    ]
    for copy in copies:
        copy.start()
    return copies


def whole(weights, at):
    return weights[at].reshape(weights.shape[1] * weights.shape[2], weights.shape[3])


def group_rows(weights, group):
    blocks = WIDTH // weights.shape[2]
    parts = [
        weights[at, pl.ds(group * blocks, blocks)].reshape(WIDTH, weights.shape[3])
        for at in range(weights.shape[0])
    ]
    return parts[0] if len(parts) == 1 else jnp.concatenate(parts, -1)


def modulation(times, table, ada, b_ada, gain_one, gain_two, b_down, mask, small):
    columns = ada.shape[0]
    rows = gain_one.shape[1]
    at = lax.broadcasted_iota(jnp.int32, (8, table.shape[0]), 1)
    line = lax.broadcasted_iota(jnp.int32, (8, table.shape[0]), 0)
    wanted = jnp.where(line == 0, times[0], jnp.where(line == 1, times[1], times[2]))
    cond = nn((at == wanted).astype(F32).astype(BF16), table[...]).astype(BF16)
    part = nt(cond, ada[...]) + b_ada[...].astype(F32)
    small[...] = jnp.zeros_like(small)
    at = 0
    for s in range(MICRO):
        small[0:1, at : at + columns] = part[s : s + 1]
        at += columns
    for ref in (gain_one, gain_two, b_down):
        small[0:1, at : at + rows] = ref[...].astype(F32)
        at += rows
    for s in range(MICRO):
        small[0:1, at : at + mask.shape[1]] = mask[s : s + 1, :].astype(F32)
        at += mask.shape[1]


def prepare_kernel(
    place, times, tokens, upstream, w_qkv, w_up, down, w_proj, table, ada, b_ada, gain_one, gain_two, b_down, mask, *outs
):
    packed, small, outs = outs[0], outs[1], outs[2:]
    columns_out, token_out = outs[:-PLANES], outs[-PLANES:]
    plane, spot = place[0], place[1]
    shard = tokens.shape[1]
    for d, out in enumerate(token_out):
        out[0:shard, :] = tokens[jnp.minimum(plane ^ d, MICRO - 1)]
        out[shard:, :] = upstream[jnp.minimum(plane ^ d, MICRO - 1)]
    width = w_proj.shape[1]
    by_group = [
        jnp.concatenate([w_qkv[:, p * width + g * WIDTH : p * width + (g + 1) * WIDTH] for p in range(3)], -1)
        for g in range(GROUPS)
    ]
    for e, out in enumerate(columns_out):
        group = (spot ^ e) % GROUPS
        here = by_group[0]
        for g in range(1, GROUPS):
            here = jnp.where(group == g, by_group[g], here)
        out[...] = here
    unit = packed.shape[2]
    chunk = 0
    for value in (w_up[...], down[...], w_proj[...]):
        for at in range(0, value.shape[1], unit):
            packed[chunk] = value[:, at : at + unit]
            chunk += 1
    modulation(times, table, ada, b_ada, gain_one, gain_two, b_down, mask, small)


def vectors_kernel(place, weight_index, weight_grid, small, vectors, scale, line):
    n = small.shape[0]
    width = vectors.shape[1]
    columns, rows, shard = 6 * width // n, width // n, scale.shape[0] // PLANES
    plane, spot = place[0], place[1]
    side = n // PLANES
    me = plane * side + spot
    last = jnp.minimum(plane, MICRO - 1)

    def one_of(three):
        return jnp.where(last == 0, three[0], jnp.where(last == 1, three[1], three[2]))

    def pieces(first, size):
        start = first
        while start < first + size:
            stop = min(first + size, (start // width + 1) * width)
            yield start // width, start % width, start - first, stop - start
            start = stop

    vectors[...] = jnp.zeros_like(vectors)
    for i in range(n):
        here = small[pl.ds(me ^ i, 1), :]
        each = [here[:, s * columns : (s + 1) * columns] for s in range(MICRO)]
        mine = one_of(each)
        for part, column, offset, size in pieces(i * columns, columns):
            vectors[part : part + 1, column : column + size] = mine[:, offset : offset + size]
            if part == SCALE_ONE:
                for s in range(MICRO):
                    vectors[SCALES_ALL + s : SCALES_ALL + s + 1, column : column + size] = each[s][
                        :, offset : offset + size
                    ]
        for row in (GAIN_ONE, GAIN_TWO, BIAS_DOWN):
            start = MICRO * columns + (row - GAIN_ONE) * rows
            vectors[row : row + 1, i * rows : (i + 1) * rows] = here[:, start : start + rows]
    for to, gain, by in ((GAINS_ONE, GAIN_ONE, SCALE_ONE), (GAINS_TWO, GAIN_TWO, SCALE_TWO)):
        vectors[to : to + 1, :] = vectors[gain : gain + 1, :] * (1.0 + vectors[by : by + 1, :])
    line[...] = jnp.zeros_like(line)
    for d in range(PLANES):
        here = small[d * side : d * side + 1, :]
        start = MICRO * (columns + rows)
        three = [here[:, start + s * shard : start + (s + 1) * shard] for s in range(MICRO)]
        line[0:1, d * shard : (d + 1) * shard] = one_of(three)
    weight = jnp.where(plane < MICRO, weight_grid[weight_index[last]], 0.0)
    scale[...] = line[...].T[:, 0:1] * weight


def project_kernel(place, gathered, tokens, vectors, *refs, chunks):
    side = len(refs) - 5
    mixed, (attended, middle, normed, weights, arrived) = refs[:side], refs[side:]
    spot = place[1]
    copies = fetch(gathered, chunks, weights, arrived)
    for copy in copies:
        copy.wait()
    total = jnp.zeros(attended.shape, F32)
    for e in range(side):
        other = spot ^ e
        block = mixed[e][...]
        if side > GROUPS:
            block = jnp.where(other < GROUPS, block, jnp.zeros_like(block))
        total = total + nn(block, group_rows(weights, other % GROUPS))
    attended[...] = total
    after = tokens[...].astype(F32) + vectors[GATE_ONE : GATE_ONE + 1] * total
    middle[...] = after
    xhat, _ = standardize(after)
    normed[...] = (xhat * vectors[GAINS_TWO : GAINS_TWO + 1] + vectors[SHIFT_TWO : SHIFT_TWO + 1]).astype(BF16)


def feed_kernel(gathered, rows, d_rows, bias, output, d_normed, active, d_hidden, weights, arrived):
    parts = weights.shape[0] // 2
    unit = weights.shape[3]
    order = [at for part in range(parts) for at in (part, parts + part)]
    copies = fetch(gathered, order, weights, arrived)
    out = jnp.zeros(output.shape, F32)
    back = jnp.zeros(output.shape, F32)
    for part in range(parts):
        columns = slice(part * unit, (part + 1) * unit)
        copies[2 * part].wait()
        up = whole(weights, 2 * part)
        u = nn(rows[...], up) + bias[:, columns]
        square = u * u
        bent = jnp.tanh(SLOPE * u * (1.0 + CUBIC * square))
        half = 0.5 * (1.0 + bent)
        on = (u * half).astype(BF16)
        active[:, columns] = on
        slope = half + 0.5 * u * (1.0 - bent * bent) * (SLOPE * (1.0 + 3.0 * CUBIC * square))
        copies[2 * part + 1].wait()
        down = whole(weights, 2 * part + 1)
        d_on = (nn(d_rows[...], down) * slope).astype(BF16)
        d_hidden[:, columns] = d_on
        out = out + nt(on, down)
        back = back + nt(d_on, up)
    output[...] = out.astype(output.dtype)
    d_normed[...] = back.astype(d_normed.dtype)


def scatter_store(refs, me, device, value):
    kept, sent, chunk, slot_of = refs
    distance = me ^ device
    slot = slot_of(distance)

    @pl.when(distance % 2 == 0)
    def _():
        kept[slot, chunk] = value

    @pl.when(distance % 2 == 1)
    def _():
        sent[slot, chunk] = value


def slot_y_first(distance):
    return ((distance >> 1) & 1) * 4 + ((distance >> 2) & 1) * 2 + ((distance >> 3) & 1)


def down_grads_kernel(*refs, blocks):
    d_rows, active, out = refs[:blocks], refs[blocks:-1], refs[-1]
    unit = out.shape[3]
    turned = [ref[...].T for ref in d_rows]
    for chunk in range(out.shape[1]):
        columns = slice(chunk * unit, (chunk + 1) * unit)
        grad = sum(nn(turned[b], active[b][:, columns]) for b in range(blocks)).astype(BF16)
        out[:, chunk] = grad.reshape(out.shape[0], out.shape[2], unit)


def up_grads_kernel(place, *refs, blocks, scatter):
    rows_all, d_hidden, outs = refs[:blocks], refs[blocks : 2 * blocks], refs[2 * blocks :]
    bias = outs[-1]
    me = place[2]
    width, count = rows_all[0].shape[1], bias.shape[1]
    unit = min(width, count)
    turned = [ref[...].T for ref in rows_all]
    for chunk in range(count // unit):
        columns = slice(chunk * unit, (chunk + 1) * unit)
        grad = sum(nn(turned[b], d_hidden[b][:, columns]) for b in range(blocks)).astype(BF16)
        bias[:, columns] = sum(over_tokens(d_hidden[b][:, columns].astype(F32)) for b in range(blocks))
        if scatter:
            rows = outs[0].shape[2]
            for i in range(width // rows):
                part = grad[i * rows : (i + 1) * rows]
                scatter_store((outs[0], outs[1], chunk, slot_y_first), me, i, part)
        else:
            outs[0][:, columns] = grad


def proj_grads_kernel(place, d_attended, *refs, side, scatter):
    mixed, refs = refs[:side], refs[side:]
    spot, me = place[1], place[2]
    width = d_attended.shape[1]
    whole_grad = refs[-1]
    if side > GROUPS:
        whole_grad[...] = jnp.zeros_like(whole_grad)
    for e in range(side):
        other = spot ^ e
        first = pl.multiple_of((other % GROUPS) * WIDTH, WIDTH)
        grad = nn(mixed[e][...].T, d_attended[...]).astype(BF16)
        if side > GROUPS:
            grad = whole_grad[pl.ds(first, WIDTH), :] + jnp.where(other < GROUPS, grad, jnp.zeros_like(grad))
        whole_grad[pl.ds(first, WIDTH), :] = grad
    if not scatter:
        refs[0][...] = whole_grad[...]
        return
    _, _, own, sent, ready, done, _ = refs
    rows, chunk = own.shape[2], own.shape[1] - 1
    for i in range(width // rows):
        part = whole_grad[i * rows : (i + 1) * rows, :]
        scatter_store((ready.at[0], ready.at[1], 0, slot_y_first), me, i, part)
    copies = [
        pltpu.make_async_copy(ready.at[at, :, 0], out.at[:, chunk], done.at[at])
        for at, out in enumerate((own, sent))
    ]
    for copy in copies:
        copy.start()
    for copy in copies:
        copy.wait()


def qkv_grads_kernel(place, d_project, normed, *outs):
    grad = nn(d_project[...], normed[...]).astype(BF16).T
    plane, slice_of = place[0], place[3]
    rows = outs[0].shape[1]
    if len(outs[0].shape) == 3 and outs[0].shape[0] == PLANES:
        for at in range(PLANES):
            distance = plane ^ at
            slot = (distance % 2) * 2 + distance // 2
            halves = [grad[(2 * at + half) * rows : (2 * at + half + 1) * rows] for half in range(2)]
            outs[0][slot] = jnp.where(slice_of == 0, halves[0], halves[1])
            outs[1][slot] = jnp.where(slice_of == 0, halves[1], halves[0])
    else:
        for at in range(PLANES):
            part = grad[at * rows : (at + 1) * rows]
            distance = plane ^ at

            @pl.when(distance % 2 == 0)
            def _():
                outs[0][distance // 2] = part

            @pl.when(distance % 2 == 1)
            def _():
                outs[1][distance // 2] = part


def normed_backward_kernel(d_project, weight, *refs, blocks):
    tokens, (kept, sent, sums) = refs[:blocks], refs[blocks:]
    count = tokens[0].shape[0]
    d_shift = jnp.zeros((1, weight.shape[0]), F32)
    d_xhat = jnp.zeros((1, weight.shape[0]), F32)
    for block in range(blocks):
        part = nt(d_project[:, block * count : (block + 1) * count].T, weight[...])
        (sent if block % 2 else kept)[block // 2] = part.astype(BF16)
        xhat, _ = standardize(tokens[block][...].astype(F32))
        d_shift = d_shift + over_tokens(part)
        d_xhat = d_xhat + over_tokens(part * xhat)
    sums[0:1, :] = d_shift
    sums[1:2, :] = d_xhat
    sums[2:8, :] = jnp.zeros((6, weight.shape[0]), F32)


def middle_kernel(place, gathered, vectors, upstream, scale, attended, middle, d_own, *refs, others, chunks):
    arrived, refs = refs[:others], refs[others:]
    d_mixed, (d_middle, d_attended, sums, weights, copied) = refs[:-5], refs[-5:]
    spot = place[1]
    copies = fetch(gathered, chunks, weights, copied)
    width = middle.shape[1]
    d_normed = d_own[...]
    for ref in arrived:
        d_normed = d_normed + ref[...].astype(F32)
    xhat, root = standardize(middle[...])
    d_result = upstream[...].astype(F32) * scale[...]
    d_after = d_result + pull_norm(d_normed, vectors[GAINS_TWO : GAINS_TWO + 1], xhat, root)
    d_middle[...] = d_after
    low = (vectors[GATE_ONE : GATE_ONE + 1] * d_after).astype(BF16)
    d_attended[...] = low
    for copy in copies:
        copy.wait()
    for e in range(len(d_mixed)):
        d_mixed[e][...] = nt(low, group_rows(weights, (spot ^ e) % GROUPS)).astype(BF16)
    sums[0:1, :] = over_tokens(d_after * attended[...])
    sums[1:2, :] = over_tokens(d_normed)
    sums[2:3, :] = over_tokens(d_normed * xhat)
    sums[3:8, :] = jnp.zeros((5, width), F32)


def output_kernel(vectors, upstream, scale, middle, own, *refs, others):
    arrived, (result, sums) = refs[:others], refs[others:]
    output = own[...] + vectors[BIAS_DOWN : BIAS_DOWN + 1]
    for ref in arrived:
        output = output + ref[...].astype(F32)
    gate = vectors[GATE_TWO : GATE_TWO + 1]
    result[...] = (middle[...] + gate * output).astype(BF16)
    d_result = upstream[...].astype(F32) * scale[...]
    sums[0:1, :] = over_tokens(d_result * output)
    sums[1:2, :] = over_tokens(gate * d_result)
    sums[2:8, :] = jnp.zeros((6, middle.shape[1]), F32)


def tokens_kernel(vectors, tokens, d_middle, own, arrived, d_tokens):
    xhat, root = standardize(tokens[...].astype(F32))
    d_normed = own[...].astype(F32) + arrived[...].astype(F32)
    back = pull_norm(d_normed, vectors[GAINS_ONE : GAINS_ONE + 1], xhat, root)
    d_tokens[...] = (d_middle[...] + back).astype(BF16)


def forward_kernel(place, *refs, blocks, halves):
    tokens, refs = refs[:blocks], refs[blocks:]
    count = 2 if halves else PLANES
    weights, refs = refs[:count], refs[count:]
    (vectors, cosine, sines), refs = refs[:3], refs[3:]
    gain, shift = vectors[GAINS_ONE : GAINS_ONE + 1], vectors[SHIFT_ONE : SHIFT_ONE + 1]
    mixed, refs = refs[:blocks], refs[blocks:]
    heads, log_total, normed, weight, keys, mixed_turned = refs
    plane = place[0]
    rows = weights[0].shape[-2]
    count = tokens[0].shape[0]
    if halves:
        for half in range(2):
            for distance in range(PLANES):
                first = pl.multiple_of((plane ^ distance) * 2 * rows + (place[3] ^ half) * rows, 16)
                weight[pl.ds(first, rows), :] = weights[half][distance]
    else:
        for distance in range(PLANES):
            first = pl.multiple_of((plane ^ distance) * rows, 8)
            weight[pl.ds(first, rows), :] = weights[distance][...]
    for block in range(blocks):
        xhat, _ = standardize(tokens[block][...].astype(F32))
        normed[block * count : (block + 1) * count, :] = (xhat * gain + shift).astype(BF16)
    project = nt(weight[...].T, normed[...])
    cos, sin = cosine[...], sines[...]
    half = HEAD // 2
    for part in range(2):
        for head in range(PER_GROUP):
            start = part * WIDTH + head * HEAD
            first, second = project[start : start + half], project[start + half : start + HEAD]
            turned = jnp.concatenate([first * cos - second * sin, second * cos + first * sin], 0).astype(BF16)
            if part == 0:
                turned = turned * jnp.asarray(SCALING, BF16)
            else:
                keys[head] = turned.T
            heads[start : start + HEAD, :] = turned
    heads[2 * WIDTH :, :] = project[2 * WIDTH :].astype(BF16)
    length = heads.shape[1]
    for head in range(PER_GROUP):
        start = head * HEAD

        def queries_step(step, carry):
            columns = pl.ds(pl.multiple_of(step * QUERY_BLOCK, QUERY_BLOCK), QUERY_BLOCK)
            scores = nn(keys[head], heads[start : start + HEAD, columns])
            peak = jnp.max(scores, 0, keepdims=True)
            exps = jnp.exp(scores - peak)
            total = jnp.sum(exps, 0, keepdims=True)
            log_total[head : head + 1, columns] = peak + jnp.log(total)
            probs = (exps * (1.0 / total)).astype(BF16)
            values = heads[2 * WIDTH + start : 2 * WIDTH + start + HEAD, :]
            mixed_turned[start : start + HEAD, columns] = nn(values, probs).astype(BF16)
            return carry

        lax.fori_loop(0, length // QUERY_BLOCK, queries_step, 0)
    for block in range(blocks):
        mixed[block][...] = mixed_turned[:, block * count : (block + 1) * count].T


def backward_kernel(*refs, blocks):
    d_mixed, refs = refs[:blocks], refs[blocks:]
    (heads, log_total, cosine, sines), refs = refs[:4], refs[4:]
    d_project, d_turned, d_keys, d_values, keys, values = refs
    count = d_mixed[0].shape[0]
    length = heads.shape[1]
    for block in range(blocks):
        d_turned[:, block * count : (block + 1) * count] = d_mixed[block][...].T
    cos, sin = cosine[...], sines[...]
    half = HEAD // 2
    d_keys[...] = jnp.zeros_like(d_keys)
    d_values[...] = jnp.zeros_like(d_values)
    for head in range(PER_GROUP):
        start = head * HEAD
        keys_turned = heads.at[WIDTH + start : WIDTH + start + HEAD]
        keys[...] = keys_turned[...].T
        values[...] = heads[2 * WIDTH + start : 2 * WIDTH + start + HEAD, :].T

        def queries_step(step, carry):
            columns = pl.ds(pl.multiple_of(step * QUERY_BLOCK, QUERY_BLOCK), QUERY_BLOCK)
            queries = heads[start : start + HEAD, columns]
            incoming = d_turned[start : start + HEAD, columns]
            scores = nn(keys[...], queries)
            probs = jnp.exp(scores - log_total[head : head + 1, columns])
            d_probs = nn(values[...], incoming)
            delta = jnp.sum(probs * d_probs, 0, keepdims=True)
            d_scores = (probs * (d_probs - delta)).astype(BF16)
            d_values[start : start + HEAD, :] += nt(incoming, probs.astype(BF16))
            d_keys[start : start + HEAD, :] += nt(queries, d_scores)
            d_queries = nn(keys_turned[...], d_scores) * SCALING
            first, second = d_queries[:half], d_queries[half:]
            cos_here, sin_here = cosine[:, columns], sines[:, columns]
            d_project[start : start + half, columns] = (first * cos_here + second * sin_here).astype(BF16)
            d_project[start + half : start + HEAD, columns] = (second * cos_here - first * sin_here).astype(BF16)
            return carry

        lax.fori_loop(0, length // QUERY_BLOCK, queries_step, 0)
        first, second = d_keys[start : start + half, :], d_keys[start + half : start + HEAD, :]
        d_project[WIDTH + start : WIDTH + start + half, :] = (first * cos + second * sin).astype(BF16)
        d_project[WIDTH + start + half : WIDTH + start + HEAD, :] = (second * cos - first * sin).astype(BF16)
    d_project[2 * WIDTH :, :] = d_values[...].astype(BF16)


def attend_forward(place, tokens, weights, vectors, cosine, sines, halves):
    blocks, (count, width) = len(tokens), tokens[0].shape
    length = blocks * count
    columns = weights[0].shape[-1]
    outs = call(
        functools.partial(forward_kernel, blocks=blocks, halves=halves),
        "attend_forward",
        [*tokens, *weights, vectors, cosine, sines],
        [place],
        [shape_of((count, WIDTH), BF16)] * blocks
        + [
            shape_of((columns, length), BF16),
            shape_of((8, length), F32),
            shape_of((length, width), BF16),
            shape_of((width, columns), BF16),
        ],
        [pltpu.VMEM((PER_GROUP, length, HEAD), BF16), pltpu.VMEM((WIDTH, length), BF16)],
        us=15.0,
    )
    return outs[:blocks], outs[blocks:]


def attend_backward(d_mixed, heads, log_total, cosine, sines):
    blocks, length = len(d_mixed), heads.shape[1]
    (d_project,) = call(
        functools.partial(backward_kernel, blocks=blocks),
        "attend_backward",
        [*d_mixed, heads, log_total, cosine, sines],
        [],
        [shape_of((3 * WIDTH, length), BF16)],
        [
            pltpu.VMEM((WIDTH, length), BF16),
            pltpu.VMEM((WIDTH, length), F32),
            pltpu.VMEM((WIDTH, length), F32),
            pltpu.VMEM((length, HEAD), BF16),
            pltpu.VMEM((length, HEAD), BF16),
        ],
        us=18.0,
    )
    return d_project


def after(values, *others):
    return lax.optimization_barrier((values, others))[0]


def add(left, right):
    return (left.astype(F32) + right.astype(F32)).astype(BF16)


def pick(stack, index):
    return lax.dynamic_index_in_dim(stack, index, 0, keepdims=False)


def bits_of(count):
    return [1 << bit for bit in range(count.bit_length() - 1)]


def body(
    tokens,
    upstream,
    token_mask,
    time_index,
    weight_index,
    time_table,
    weight_grid,
    w_ada,
    b_ada,
    gain_one,
    gain_two,
    w_qkv,
    w_proj,
    w_up,
    b_up,
    w_down,
    b_down,
    *,
    n,
    m,
):
    side = n // PLANES
    me = lax.axis_index("seq")
    plane, spot = me // side, me % side
    slice_of = lax.axis_index("mlp")
    place = jnp.stack([plane, spot, me, slice_of]).astype(jnp.int32)
    shard, width = tokens.shape[2], tokens.shape[3]
    rows = w_qkv.shape[0]
    hidden_count = w_up.shape[1]
    grid_size = time_table.shape[0]
    ada_columns = w_ada.shape[1]
    count = PLANES * shard
    unit = min(width, hidden_count)
    hidden_chunks, width_chunks = hidden_count // unit, width // unit
    pairwise = rows % 16 == 0 and side == GROUPS and unit == width and m == 2
    z_bits, y_bit, core_bit = (2 * side, side), 2, 1

    def swap(value, distance):
        return lax.ppermute(value, "seq", [(i, i ^ distance) for i in range(n)])

    def swap_mlp(value, distance):
        return lax.ppermute(value, "mlp", [(i, i ^ distance) for i in range(m)])

    def between_planes(pieces):
        return [pieces[0]] + [swap(pieces[d], d * side) for d in range(1, PLANES)]

    def in_plane(pieces):
        return [pieces[0]] + [swap(pieces[e], e) for e in range(1, side)]

    def in_order(blocks, axis):
        halves = jnp.stack(blocks)
        for bit in bits_of(len(blocks)):
            here = halves.reshape((len(blocks) // (2 * bit), 2, bit) + halves.shape[1:])
            halves = jnp.where((axis & bit) != 0, here[:, ::-1], here).reshape(halves.shape)
        return halves

    def for_plane(values):
        return [pick(values, jnp.minimum(plane ^ d, MICRO - 1)) for d in range(PLANES)]

    def columns_of(value):
        return [value[:, at : at + unit] for at in range(0, value.shape[1], unit)]

    line = [value[None] for value in (b_ada, gain_one, gain_two, b_down)]
    small_count = -(-MICRO * (ada_columns + rows + shard) // 128) * 128
    first_shapes = [shape_of((2 * hidden_chunks + width_chunks, rows, unit), BF16), shape_of((1, small_count), F32)]
    first_shapes += [shape_of((rows, 3 * WIDTH), BF16)] * side + [shape_of((2 * shard, width), BF16)] * PLANES
    packed, small, *pieces = call(
        prepare_kernel,
        "prepare",
        [tokens[:, 0], upstream[:, 0], w_qkv, w_up, w_down.T, w_proj, time_table, w_ada.T, *line, token_mask[:, 0]],
        [place, time_index[:, 0]],
        first_shapes,
        us=4.0,
    )
    group_columns, token_pieces = pieces[:side], pieces[side:]

    received = jnp.stack(in_plane(group_columns))
    arrived = after(between_planes(token_pieces), received)
    own_low = jnp.concatenate([piece[:shard] for piece in arrived], 0)
    own_upstream = jnp.concatenate([piece[shard:] for piece in arrived], 0)
    token_blocks = {0: own_low}
    for bit in reversed(bits_of(side)):
        for known in list(token_blocks):
            token_blocks[known | bit] = swap(token_blocks[known], bit)
    token_blocks = [token_blocks[at] for at in range(side)]

    gathered = lax.all_gather(after(packed, arrived), "seq", axis=0)
    if not pairwise:
        gathered = gathered.transpose(1, 0, 2, 3).reshape(-1, GROUPS, WIDTH, unit).transpose(1, 0, 2, 3)
    blocks_shape = (gathered.shape[0],) + gathered.shape[2:]
    proj_chunks = list(range(2 * hidden_chunks, 2 * hidden_chunks + width_chunks))

    def weight_scratch(number):
        return [pltpu.VMEM((number,) + blocks_shape, BF16), pltpu.SemaphoreType.DMA((number,))]

    weight_block = jnp.concatenate([pick(received, spot ^ at) for at in range(side)], 0)
    if pairwise:
        weight_block = pick(weight_block.reshape(2, width // 8, 3 * WIDTH), slice_of)
    weight_blocks = {0: weight_block}
    for bit in (2, 1):
        for known in list(weight_blocks):
            weight_blocks[known | bit] = swap(weight_blocks[known], bit * side)
    weight_blocks = [weight_blocks[at] for at in range(PLANES)]
    if pairwise:
        weight_blocks = jnp.stack(weight_blocks)
        weight_blocks = [weight_blocks, swap_mlp(weight_blocks, 1)]

    for bit in bits_of(n):
        small = jnp.concatenate([small, swap(small, bit)], 0)
    vectors, scale = call(
        vectors_kernel,
        "vectors",
        [small],
        [place, weight_index[:, 0], weight_grid],
        [shape_of((16, width), F32), shape_of((count, 1), F32)],
        [pltpu.VMEM((8, count), F32)],
    )

    order = ((plane ^ jnp.arange(PLANES))[None, :] * side + (spot ^ jnp.arange(side))[:, None]) * shard
    positions = (order[:, :, None] + jnp.arange(shard)).reshape(1, -1).astype(F32)
    frequency = 10000.0 ** (-jnp.arange(0, HEAD, 2).astype(F32) / HEAD)
    angles = frequency[:, None] * positions
    cosine, sines = jnp.cos(angles), jnp.sin(angles)

    mixed_blocks, kept = attend_forward(
        place, token_blocks, weight_blocks, vectors, cosine, sines, pairwise
    )

    full_ada = lax.all_gather(after(w_ada, gathered), "seq", axis=0)

    mixed_blocks = in_plane(mixed_blocks)

    d_rows = ((own_upstream.astype(F32) * scale) * vectors[GATE_TWO][None]).astype(BF16)
    d_rows = [d_rows] + [swap_mlp(d_rows, d) for d in range(1, m)]

    attended, middle, normed_two = call(
        functools.partial(project_kernel, chunks=proj_chunks),
        "project",
        [own_low, vectors, *mixed_blocks],
        [place],
        [shape_of((count, width), F32), shape_of((count, width), F32), shape_of((count, width), BF16)],
        weight_scratch(width_chunks),
        us=3.0,
        far=[gathered],
    )
    rows_all = [normed_two] + [swap_mlp(normed_two, d) for d in range(1, m)]
    bias_up = b_up.astype(F32)[None]
    fed = [
        call(
            feed_kernel,
            "feed_forward",
            [rows_all[d], d_rows[d], bias_up],
            [],
            [shape_of((count, width), BF16 if d else F32)] * 2 + [shape_of((count, hidden_count), BF16)] * 2,
            weight_scratch(2 * hidden_chunks),
            us=6.0,
            far=[gathered],
        )
        for d in range(m)
    ]
    d_arrived = [swap_mlp(fed[d][1], d) for d in range(1, m)]
    out_arrived = [swap_mlp(fed[d][0], d) for d in range(1, m)]
    slots = n // 2
    down_shape = (n, hidden_chunks, rows, unit) if pairwise else (GROUPS, hidden_chunks, WIDTH, unit)
    if pairwise:
        up_shapes = [shape_of((slots, hidden_chunks + width_chunks, rows, unit), BF16)] * 2
    else:
        up_shapes = [shape_of((width, hidden_count), BF16)]
    (down_grads,) = call(
        functools.partial(down_grads_kernel, blocks=m),
        "down_gradients",
        [*d_rows, *[f[2] for f in fed]],
        [],
        [shape_of(down_shape, BF16)],
        us=6.0,
    )
    *up_grads, bias_up_sum = call(
        functools.partial(up_grads_kernel, blocks=m, scatter=pairwise),
        "up_gradients",
        [*rows_all, *[f[3] for f in fed]],
        [place],
        up_shapes + [shape_of((1, hidden_count), F32)],
        us=5.0,
    )
    d_arrived, down_grads, full_ada, *up_grads = lax.optimization_barrier(
        (d_arrived, down_grads, full_ada, *up_grads)
    )
    if not pairwise:
        down_grads = down_grads.transpose(1, 0, 2, 3).reshape(hidden_chunks, n, rows, unit).transpose(1, 0, 2, 3)
    down_grads = lax.psum_scatter(down_grads, "seq", scatter_dimension=0, tiled=True)
    middle_outs = call(
        functools.partial(middle_kernel, others=m - 1, chunks=proj_chunks),
        "middle_backward",
        [vectors, own_upstream, scale, attended, middle, fed[0][1], *d_arrived],
        [place],
        [shape_of((count, WIDTH), BF16)] * side
        + [shape_of((count, width), F32), shape_of((count, width), BF16), shape_of((8, width), F32)],
        weight_scratch(width_chunks),
        us=4.0,
        far=[gathered],
    )
    d_mixed_blocks, (d_middle, d_attended, middle_sums) = middle_outs[:side], middle_outs[side:]

    d_mixed_blocks = in_plane(d_mixed_blocks)
    if side > GROUPS:
        share = (spot < GROUPS).astype(BF16)
        d_mixed_blocks = [block * share for block in d_mixed_blocks]

    anywhere = pl.BlockSpec(memory_space=pl.ANY)
    proj_grads = pl.pallas_call(
        functools.partial(proj_grads_kernel, side=side, scatter=pairwise),
        out_shape=up_shapes if pairwise else [shape_of((width, width), BF16)],
        in_specs=[SMEM] + [VMEM] * (1 + side) + ([anywhere] * 2 if pairwise else []),
        out_specs=[anywhere] * 2 if pairwise else [VMEM],
        scratch_shapes=(
            [pltpu.VMEM((2, slots, 1, rows, unit), BF16), pltpu.SemaphoreType.DMA((2,))] if pairwise else []
        )
        + [pltpu.VMEM((width, width), BF16)],
        input_output_aliases={2 + side: 0, 3 + side: 1} if pairwise else {},
        compiler_params=pltpu.CompilerParams(vmem_limit_bytes=56 * 1024 * 1024),
        cost_estimate=pl.CostEstimate(flops=2 * 10**9, bytes_accessed=4 * 10**6, transcendentals=0),
        name="proj_gradients",
    )(place, d_attended, *mixed_blocks, *(up_grads if pairwise else []))

    def add_halves(own, arrived):
        half = own.shape[0] // 2
        return add(own[:half], arrived[:half]), add(own[half:], arrived[half:])

    def back_to_tokens(value):
        received = between_planes([value[d * shard : (d + 1) * shard] for d in range(PLANES)])
        received = jnp.stack(received)
        return jnp.stack([pick(received, plane ^ at) for at in range(MICRO)])[:, None]

    if pairwise:
        proj_sent, out_arrived = lax.optimization_barrier((proj_grads[1], out_arrived))
        up_arrived = swap(proj_sent, core_bit)

    result, output_sums = call(
        functools.partial(output_kernel, others=m - 1),
        "output",
        [vectors, own_upstream, scale, middle, fed[0][0], *out_arrived],
        [],
        [shape_of((count, width), BF16), shape_of((8, width), F32)],
    )
    if pairwise:
        up_own, up_sent = add_halves(proj_grads[0], after(up_arrived, result, *d_mixed_blocks))
        up_sent, result, *d_mixed_blocks = lax.optimization_barrier((up_sent, result, *d_mixed_blocks))
    result = back_to_tokens(result)

    d_project = attend_backward(d_mixed_blocks, kept[0], kept[1], cosine, sines)
    if pairwise:
        up_arrived = swap(up_sent, y_bit)
        d_project, result = lax.optimization_barrier((d_project, result))
    qkv_shape = (PLANES, width // 8, 3 * WIDTH) if pairwise else (2, width // PLANES, 3 * WIDTH)
    grad_own, grad_sent = call(
        qkv_grads_kernel,
        "qkv_gradients",
        [d_project, kept[2]],
        [place],
        [shape_of(qkv_shape, BF16)] * 2,
        us=4.0,
    )
    d_project = after(d_project, grad_sent, up_arrived) if pairwise else d_project
    d_kept, d_sent, sums = call(
        functools.partial(normed_backward_kernel, blocks=side),
        "normed_backward",
        [d_project, kept[3], *token_blocks],
        [],
        [shape_of((side // 2, count, width), BF16)] * 2 + [shape_of((8, width), F32)],
        us=4.0,
    )
    if pairwise:
        up_own, up_sent = add_halves(up_own, up_arrived)
        grad_arrived = after(swap_mlp(grad_sent, 1), d_sent)
        grad_own, grad_sent = add_halves(grad_own, grad_arrived)
    arrived = swap(d_sent, 1)

    blocks = {2 * at: d_kept[at] for at in range(side // 2)}
    steps = [arrived]
    for at in range(side // 2):
        blocks[2 * at] = add(blocks[2 * at], arrived[at])
    for bit in bits_of(side)[1:]:
        for at in [at for at in blocks if at & bit]:
            arrived = swap(blocks.pop(at), bit)
            steps.append(arrived)
            if len(blocks) > 1:
                blocks[at ^ bit] = add(blocks[at ^ bit], arrived)
    bias_up_rows = -(-hidden_count // width)
    bias_up_sum = jnp.pad(bias_up_sum, ((0, 0), (0, bias_up_rows * width - hidden_count)))
    small = jnp.concatenate(
        [sums[0:2], middle_sums[0:3], output_sums[0:2], bias_up_sum.reshape(-1, width)], 0
    )
    small = small + swap(small, 1)
    small = after(small, steps[0])
    for bit in bits_of(side)[1:]:
        small = small + swap(small, bit)
    small = jnp.concatenate([small, vectors[SCALE_TWO][None]], 0)[None]
    for bit in bits_of(PLANES):
        small = jnp.concatenate([small, swap(small, bit * side)], 0)
    arrived, small = lax.optimization_barrier((arrived, small))
    (d_tokens,) = call(
        tokens_kernel,
        "tokens_backward",
        [vectors, own_low, d_middle, blocks[0], arrived],
        [],
        [shape_of((count, width), BF16)],
    )
    returned = back_to_tokens(d_tokens)

    if pairwise:
        up_own, up_sent = add_halves(up_own, after(swap(up_sent, side), d_tokens))
        up_parts = up_own[0].astype(F32) + after(swap(up_sent, 2 * side), returned)[0].astype(F32)
        grad_up = jnp.concatenate([up_parts[at] for at in range(hidden_chunks)], -1)
        grad_proj = up_parts[hidden_chunks]
    else:
        grads = jnp.stack(columns_of(up_grads[0]) + columns_of(proj_grads[0]))
        grads = grads.reshape(-1, n, rows, unit).transpose(1, 0, 2, 3)
        grads = lax.psum_scatter(grads, "seq", scatter_dimension=0, tiled=True)[0]

        def columns_from(start, number):
            return jnp.concatenate([grads[start + at] for at in range(number)], -1).astype(F32)

        grad_up = columns_from(0, hidden_chunks)
        grad_proj = columns_from(hidden_chunks, width_chunks)
    for bit in bits_of(m):
        grad_proj = grad_proj + swap_mlp(grad_proj.astype(BF16), bit).astype(F32)

    arrived = after(swap(grad_sent, side), d_tokens)
    if pairwise:
        grad_own, grad_sent = add_halves(grad_own, arrived)
        arrived = after(swap(grad_sent, 2 * side), returned)
        total = grad_own[0].astype(F32) + arrived[0].astype(F32)
        by_spot = total.astype(BF16).reshape(2, rows, 3 * WIDTH)
        slices = [pick(by_spot, (spot ^ e) % 2) for e in range(side)]
    else:
        arrived = swap(add(grad_own[1], arrived[1]), 2 * side).astype(F32) + arrived[0].astype(F32)
        total = grad_own[0].astype(F32) + arrived
        by_spot = total.astype(BF16).reshape(side, rows, 3 * WIDTH)
        slices = [pick(by_spot, spot ^ e) for e in range(side)]
    received = jnp.stack(in_plane(slices))
    grad_qkv = jnp.stack([pick(received, spot ^ group) for group in range(GROUPS)])
    grad_qkv = grad_qkv.reshape(GROUPS, rows, 3, WIDTH).transpose(1, 2, 0, 3).reshape(rows, 3 * width)
    if pairwise:
        grad_qkv = jnp.where(spot // 2 == slice_of, grad_qkv, swap_mlp(grad_qkv, 1)).astype(F32)
    else:
        grad_qkv = grad_qkv.astype(F32)
        for bit in bits_of(m):
            grad_qkv = grad_qkv + swap_mlp(grad_qkv.astype(BF16), bit).astype(F32)

    down_grads = after(down_grads[0], d_sent).astype(F32)
    grad_down = jnp.concatenate([down_grads[at] for at in range(hidden_chunks)], -1).T

    small = in_order(list(small), plane)[:MICRO]
    grad_bias_up = jnp.sum(small[:, 7 : 7 + bias_up_rows], 0).reshape(-1)[:hidden_count]
    d_shift_one, d_xhat_one, d_gate_one, d_shift_two, d_xhat_two, d_gate_two = [small[:, at] for at in range(6)]
    index_here = time_index[:, 0]
    vector_sums = jnp.stack(
        [
            jnp.sum((1.0 + vectors[SCALES_ALL : SCALES_ALL + MICRO]) * d_xhat_one, 0),
            jnp.sum((1.0 + small[:, -1]) * d_xhat_two, 0),
            jnp.sum(small[:, 6], 0),
            jnp.pad(index_here.astype(F32), (0, width - MICRO)),
        ]
    )
    d_scale_one, d_scale_two = vectors[GAIN_ONE] * d_xhat_one, vectors[GAIN_TWO] * d_xhat_two
    small = jnp.stack([d_shift_one, d_scale_one, d_gate_one, d_shift_two, d_scale_two, d_gate_two], 1)
    small = jnp.concatenate([small.reshape(6 * MICRO, width), vector_sums], 0)[None]
    for bit in bits_of(m):
        small = jnp.concatenate([small, swap_mlp(small, bit)], 0)
    at = 6 * MICRO
    d_modulation = small[:, :at].reshape(m * MICRO, n, ada_columns)
    vector_sums = jnp.sum(small[:, at : at + 3], 0)
    index_all = small[:, at + 3, :MICRO].reshape(-1).astype(jnp.int32)
    onehot = (index_all[:, None] == jnp.arange(grid_size)[None, :]).astype(BF16)
    cond = jnp.dot(onehot, time_table, preferred_element_type=F32)
    d_modulation_own = lax.dynamic_index_in_dim(d_modulation, me, 1, keepdims=False)
    grad_ada = jnp.dot(cond.T, d_modulation_own, precision=highest)
    grad_bias_ada = jnp.sum(d_modulation_own, 0)
    d_cond = jnp.einsum("bic,idc->bd", d_modulation, full_ada.astype(F32), precision=highest)
    table_rows = grid_size // n
    onehot_own = index_all[None, :] == (me * table_rows + jnp.arange(table_rows))[:, None]
    grad_table = jnp.dot(onehot_own.astype(F32), d_cond, precision=highest)
    vector_sums = lax.dynamic_slice_in_dim(vector_sums, me * rows, rows, 1)
    return (
        result,
        returned.astype(F32),
        grad_table,
        grad_ada,
        grad_bias_ada,
        vector_sums[0],
        vector_sums[1],
        grad_qkv,
        grad_proj,
        grad_up,
        grad_bias_up,
        grad_down,
        vector_sums[2],
    )


def solution(mesh):
    in_specs = (
        P(None, "mlp", "seq", None),
        P(None, "mlp", "seq", None),
        P(None, "mlp", "seq"),
        P(None, "mlp"),
        P(None, "mlp"),
        P(),
        P(),
        P(None, "seq"),
        P("seq"),
        P("seq"),
        P("seq"),
        P("seq", None),
        P("seq", None),
        P("seq", "mlp"),
        P("mlp"),
        P("mlp", "seq"),
        P("seq"),
    )
    out_specs = (
        P(None, "mlp", "seq", None),
        P(None, "mlp", "seq", None),
        P("seq", None),
        P(None, "seq"),
        P("seq"),
        P("seq"),
        P("seq"),
        P("seq", None),
        P("seq", None),
        P("seq", "mlp"),
        P("mlp"),
        P("mlp", "seq"),
        P("seq"),
    )
    run = functools.partial(body, n=mesh.shape["seq"], m=mesh.shape["mlp"])
    return jax.shard_map(run, mesh=mesh, in_specs=in_specs, out_specs=out_specs, check_vma=False)
```

```python
import functools
import math

import jax
import jax.numpy as jnp
from jax import lax
from jax.experimental import pallas as pl
from jax.experimental.pallas import tpu as pltpu
from jax.sharding import PartitionSpec as P

HEADS = 12
HEAD = 64
MICRO = 3
PLANES = 4
GROUPS = 4
PER_GROUP = HEADS // GROUPS
WIDTH = PER_GROUP * HEAD
QUERY_BLOCK = 256
SCALING = HEAD ** (-0.5)
BF16 = jnp.bfloat16
F32 = jnp.float32
highest = lax.Precision.HIGHEST
SLOPE = math.sqrt(2.0 / math.pi)
CUBIC = 0.044715

SHIFT_ONE, SCALE_ONE, GATE_ONE, SHIFT_TWO, SCALE_TWO, GATE_TWO, GAIN_ONE, GAIN_TWO, BIAS_DOWN = range(9)
SCALES_ALL, GAINS_ONE, GAINS_TWO = 9, 12, 13

VMEM = pl.BlockSpec(memory_space=pltpu.VMEM)
SMEM = pl.BlockSpec(memory_space=pltpu.SMEM)


def nn(left, right):
    return lax.dot_general(left, right, (((1,), (0,)), ((), ())), preferred_element_type=F32)


def nt(left, right):
    return lax.dot_general(left, right, (((1,), (1,)), ((), ())), preferred_element_type=F32)


def standardize(inputs):
    average = jnp.mean(inputs, -1, keepdims=True)
    centred = inputs - average
    spread = jnp.mean(centred * centred, -1, keepdims=True)
    root = lax.rsqrt(spread + 1e-06)
    return centred * root, root


def pull_norm(d_normed, gains, xhat, root):
    e = d_normed * gains
    return root * (e - jnp.mean(e, -1, keepdims=True) - xhat * jnp.mean(e * xhat, -1, keepdims=True))


def over_tokens(value):
    return jnp.sum(value, 0, keepdims=True)


def shape_of(dims, dtype):
    return jax.ShapeDtypeStruct(dims, dtype)


def call(kernel, name, operands, scalars, outs, scratch=(), us=1.0, far=()):
    moved = sum(math.prod(o.shape) * o.dtype.itemsize for o in list(operands) + list(outs))
    return pl.pallas_call(
        kernel,
        out_shape=list(outs),
        in_specs=[SMEM] * len(scalars) + [pl.BlockSpec(memory_space=pl.ANY)] * len(far) + [VMEM] * len(operands),
        out_specs=[VMEM] * len(outs),
        scratch_shapes=list(scratch),
        compiler_params=pltpu.CompilerParams(vmem_limit_bytes=56 * 1024 * 1024),
        cost_estimate=pl.CostEstimate(flops=int(us * 1e9), bytes_accessed=moved, transcendentals=0),
        name=name,
    )(*scalars, *far, *operands)


def fetch(gathered, chunks, weights, arrived):
    copies = [
        pltpu.make_async_copy(gathered.at[:, chunk], weights.at[at], arrived.at[at])
        for at, chunk in enumerate(chunks)
    ]
    for copy in copies:
        copy.start()
    return copies


def whole(weights, at):
    return weights[at].reshape(weights.shape[1] * weights.shape[2], weights.shape[3])


def group_rows(weights, group, me=None):
    blocks = WIDTH // weights.shape[2]
    if me is not None:
        return jnp.concatenate([weights[0, me ^ (group * blocks + at)] for at in range(blocks)], 0)
    parts = [
        weights[at, pl.ds(group * blocks, blocks)].reshape(WIDTH, weights.shape[3])
        for at in range(weights.shape[0])
    ]
    return parts[0] if len(parts) == 1 else jnp.concatenate(parts, -1)


def modulation(times, table, ada, b_ada, gain_one, gain_two, b_down, mask, small):
    columns = ada.shape[0]
    rows = gain_one.shape[1]
    at = lax.broadcasted_iota(jnp.int32, (8, table.shape[0]), 1)
    line = lax.broadcasted_iota(jnp.int32, (8, table.shape[0]), 0)
    wanted = jnp.where(line == 0, times[0], jnp.where(line == 1, times[1], times[2]))
    cond = nn((at == wanted).astype(F32).astype(BF16), table[...]).astype(BF16)
    part = nt(cond, ada[...]) + b_ada[...].astype(F32)
    small[...] = jnp.zeros_like(small)
    at = 0
    for s in range(MICRO):
        small[0:1, at : at + columns] = part[s : s + 1]
        at += columns
    for ref in (gain_one, gain_two, b_down):
        small[0:1, at : at + rows] = ref[...].astype(F32)
        at += rows
    for s in range(MICRO):
        small[0:1, at : at + mask.shape[1]] = mask[s : s + 1, :].astype(F32)
        at += mask.shape[1]


def prepare_kernel(
    place, times, tokens, upstream, w_qkv, w_up, down, w_proj, table, ada, b_ada, gain_one, gain_two, b_down, mask, *outs
):
    packed, small, outs = outs[0], outs[1], outs[2:]
    columns_out, token_out = outs[:-PLANES], outs[-PLANES:]
    plane, spot = place[0], place[1]
    shard = tokens.shape[1]
    for d, out in enumerate(token_out):
        out[0:shard, :] = tokens[jnp.minimum(plane ^ d, MICRO - 1)]
        out[shard:, :] = upstream[jnp.minimum(plane ^ d, MICRO - 1)]
    width = w_proj.shape[1]
    by_group = [
        jnp.concatenate([w_qkv[:, p * width + g * WIDTH : p * width + (g + 1) * WIDTH] for p in range(3)], -1)
        for g in range(GROUPS)
    ]
    for e, out in enumerate(columns_out):
        group = (spot ^ e) % GROUPS
        here = by_group[0]
        for g in range(1, GROUPS):
            here = jnp.where(group == g, by_group[g], here)
        out[...] = here
    unit = packed.shape[2]
    chunk = 0
    for value in (w_up[...], down[...], w_proj[...]):
        for at in range(0, value.shape[1], unit):
            packed[chunk] = value[:, at : at + unit]
            chunk += 1
    modulation(times, table, ada, b_ada, gain_one, gain_two, b_down, mask, small)


def vectors_kernel(place, weight_index, weight_grid, small, vectors, scale, line):
    n = small.shape[0]
    width = vectors.shape[1]
    columns, rows, shard = 6 * width // n, width // n, scale.shape[0] // PLANES
    plane, spot = place[0], place[1]
    side = n // PLANES
    me = plane * side + spot
    last = jnp.minimum(plane, MICRO - 1)

    def one_of(three):
        return jnp.where(last == 0, three[0], jnp.where(last == 1, three[1], three[2]))

    def pieces(first, size):
        start = first
        while start < first + size:
            stop = min(first + size, (start // width + 1) * width)
            yield start // width, start % width, start - first, stop - start
            start = stop

    vectors[...] = jnp.zeros_like(vectors)
    for i in range(n):
        here = small[pl.ds(me ^ i, 1), :]
        each = [here[:, s * columns : (s + 1) * columns] for s in range(MICRO)]
        mine = one_of(each)
        for part, column, offset, size in pieces(i * columns, columns):
            vectors[part : part + 1, column : column + size] = mine[:, offset : offset + size]
            if part == SCALE_ONE:
                for s in range(MICRO):
                    vectors[SCALES_ALL + s : SCALES_ALL + s + 1, column : column + size] = each[s][
                        :, offset : offset + size
                    ]
        for row in (GAIN_ONE, GAIN_TWO, BIAS_DOWN):
            start = MICRO * columns + (row - GAIN_ONE) * rows
            vectors[row : row + 1, i * rows : (i + 1) * rows] = here[:, start : start + rows]
    for to, gain, by in ((GAINS_ONE, GAIN_ONE, SCALE_ONE), (GAINS_TWO, GAIN_TWO, SCALE_TWO)):
        vectors[to : to + 1, :] = vectors[gain : gain + 1, :] * (1.0 + vectors[by : by + 1, :])
    line[...] = jnp.zeros_like(line)
    for d in range(PLANES):
        here = small[d * side : d * side + 1, :]
        start = MICRO * (columns + rows)
        three = [here[:, start + s * shard : start + (s + 1) * shard] for s in range(MICRO)]
        line[0:1, d * shard : (d + 1) * shard] = one_of(three)
    weight = jnp.where(plane < MICRO, weight_grid[weight_index[last]], 0.0)
    scale[...] = line[...].T[:, 0:1] * weight


def project_kernel(place, gathered, tokens, vectors, *refs, chunks, slots):
    side = len(refs) - 5
    mixed, (attended, middle, normed, weights, arrived) = refs[:side], refs[side:]
    spot = place[1]
    copies = fetch(gathered, chunks, weights, arrived)
    for copy in copies:
        copy.wait()
    total = jnp.zeros(attended.shape, F32)
    for e in range(side):
        other = spot ^ e
        block = mixed[e][...]
        if side > GROUPS:
            block = jnp.where(other < GROUPS, block, jnp.zeros_like(block))
        total = total + nn(block, group_rows(weights, other % GROUPS, place[2] if slots else None))
    attended[...] = total
    after = tokens[...].astype(F32) + vectors[GATE_ONE : GATE_ONE + 1] * total
    middle[...] = after
    xhat, _ = standardize(after)
    normed[...] = (xhat * vectors[GAINS_TWO : GAINS_TWO + 1] + vectors[SHIFT_TWO : SHIFT_TWO + 1]).astype(BF16)


def feed_kernel(gathered, rows, d_rows, bias, output, d_normed, active, d_hidden, weights, arrived):
    parts = weights.shape[0] // 2
    unit = weights.shape[3]
    order = [at for part in range(parts) for at in (part, parts + part)]
    copies = fetch(gathered, order, weights, arrived)
    out = jnp.zeros(output.shape, F32)
    back = jnp.zeros(output.shape, F32)
    for part in range(parts):
        columns = slice(part * unit, (part + 1) * unit)
        copies[2 * part].wait()
        up = whole(weights, 2 * part)
        u = nn(rows[...], up) + bias[:, columns]
        square = u * u
        bent = jnp.tanh(SLOPE * u * (1.0 + CUBIC * square))
        half = 0.5 * (1.0 + bent)
        on = (u * half).astype(BF16)
        active[:, columns] = on
        slope = half + 0.5 * u * (1.0 - bent * bent) * (SLOPE * (1.0 + 3.0 * CUBIC * square))
        copies[2 * part + 1].wait()
        down = whole(weights, 2 * part + 1)
        d_on = (nn(d_rows[...], down) * slope).astype(BF16)
        d_hidden[:, columns] = d_on
        out = out + nt(on, down)
        back = back + nt(d_on, up)
    output[...] = out.astype(output.dtype)
    d_normed[...] = back.astype(d_normed.dtype)


def scatter_store(refs, me, device, value):
    kept, sent, chunk, slot_of = refs
    distance = me ^ device
    slot = slot_of(distance)

    @pl.when(distance % 2 == 0)
    def _():
        kept[slot, chunk] = value

    @pl.when(distance % 2 == 1)
    def _():
        sent[slot, chunk] = value


def slot_y_first(distance):
    return ((distance >> 1) & 1) * 4 + ((distance >> 2) & 1) * 2 + ((distance >> 3) & 1)


def down_grads_kernel(*refs, blocks):
    d_rows, active, out = refs[:blocks], refs[blocks:-1], refs[-1]
    unit = out.shape[3]
    turned = [ref[...].T for ref in d_rows]
    for chunk in range(out.shape[1]):
        columns = slice(chunk * unit, (chunk + 1) * unit)
        grad = sum(nn(turned[b], active[b][:, columns]) for b in range(blocks)).astype(BF16)
        out[:, chunk] = grad.reshape(out.shape[0], out.shape[2], unit)


def up_grads_kernel(place, *refs, blocks, scatter):
    rows_all, d_hidden, outs = refs[:blocks], refs[blocks : 2 * blocks], refs[2 * blocks :]
    bias = outs[-1]
    me = place[2]
    width, count = rows_all[0].shape[1], bias.shape[1]
    unit = min(width, count)
    turned = [ref[...].T for ref in rows_all]
    for chunk in range(count // unit):
        columns = slice(chunk * unit, (chunk + 1) * unit)
        grad = sum(nn(turned[b], d_hidden[b][:, columns]) for b in range(blocks)).astype(BF16)
        bias[:, columns] = sum(over_tokens(d_hidden[b][:, columns].astype(F32)) for b in range(blocks))
        if scatter:
            rows = outs[0].shape[2]
            for i in range(width // rows):
                part = grad[i * rows : (i + 1) * rows]
                scatter_store((outs[0], outs[1], chunk, slot_y_first), me, i, part)
        else:
            outs[0][:, columns] = grad


def proj_grads_kernel(place, d_attended, *refs, side, scatter):
    mixed, refs = refs[:side], refs[side:]
    spot, me = place[1], place[2]
    width = d_attended.shape[1]
    whole_grad = refs[-1]
    if side > GROUPS:
        whole_grad[...] = jnp.zeros_like(whole_grad)
    for e in range(side):
        other = spot ^ e
        first = pl.multiple_of((other % GROUPS) * WIDTH, WIDTH)
        grad = nn(mixed[e][...].T, d_attended[...]).astype(BF16)
        if side > GROUPS:
            grad = whole_grad[pl.ds(first, WIDTH), :] + jnp.where(other < GROUPS, grad, jnp.zeros_like(grad))
        whole_grad[pl.ds(first, WIDTH), :] = grad
    if not scatter:
        refs[0][...] = whole_grad[...]
        return
    _, _, own, sent, ready, done, _ = refs
    rows, chunk = own.shape[2], own.shape[1] - 1
    for i in range(width // rows):
        part = whole_grad[i * rows : (i + 1) * rows, :]
        scatter_store((ready.at[0], ready.at[1], 0, slot_y_first), me, i, part)
    copies = [
        pltpu.make_async_copy(ready.at[at, :, 0], out.at[:, chunk], done.at[at])
        for at, out in enumerate((own, sent))
    ]
    for copy in copies:
        copy.start()
    for copy in copies:
        copy.wait()


def qkv_grads_kernel(place, d_project, normed, *outs):
    grad = nn(d_project[...], normed[...]).astype(BF16).T
    plane, slice_of = place[0], place[3]
    rows = outs[0].shape[1]
    if len(outs[0].shape) == 3 and outs[0].shape[0] == PLANES:
        for at in range(PLANES):
            distance = plane ^ at
            slot = (distance % 2) * 2 + distance // 2
            halves = [grad[(2 * at + half) * rows : (2 * at + half + 1) * rows] for half in range(2)]
            outs[0][slot] = jnp.where(slice_of == 0, halves[0], halves[1])
            outs[1][slot] = jnp.where(slice_of == 0, halves[1], halves[0])
    else:
        for at in range(PLANES):
            part = grad[at * rows : (at + 1) * rows]
            distance = plane ^ at

            @pl.when(distance % 2 == 0)
            def _():
                outs[0][distance // 2] = part

            @pl.when(distance % 2 == 1)
            def _():
                outs[1][distance // 2] = part


def normed_backward_kernel(d_project, weight, *refs, blocks):
    tokens, (kept, sent, sums) = refs[:blocks], refs[blocks:]
    count = tokens[0].shape[0]
    d_shift = jnp.zeros((1, weight.shape[0]), F32)
    d_xhat = jnp.zeros((1, weight.shape[0]), F32)
    for block in range(blocks):
        part = nt(d_project[:, block * count : (block + 1) * count].T, weight[...])
        (sent if block % 2 else kept)[block // 2] = part.astype(BF16)
        xhat, _ = standardize(tokens[block][...].astype(F32))
        d_shift = d_shift + over_tokens(part)
        d_xhat = d_xhat + over_tokens(part * xhat)
    sums[0:1, :] = d_shift
    sums[1:2, :] = d_xhat
    sums[2:8, :] = jnp.zeros((6, weight.shape[0]), F32)


def middle_kernel(place, gathered, vectors, upstream, scale, attended, middle, d_own, *refs, others, chunks, slots):
    arrived, refs = refs[:others], refs[others:]
    d_mixed, (d_middle, d_attended, sums, weights, copied) = refs[:-5], refs[-5:]
    spot = place[1]
    copies = fetch(gathered, chunks, weights, copied)
    width = middle.shape[1]
    d_normed = d_own[...]
    for ref in arrived:
        d_normed = d_normed + ref[...].astype(F32)
    xhat, root = standardize(middle[...])
    d_result = upstream[...].astype(F32) * scale[...]
    d_after = d_result + pull_norm(d_normed, vectors[GAINS_TWO : GAINS_TWO + 1], xhat, root)
    d_middle[...] = d_after
    low = (vectors[GATE_ONE : GATE_ONE + 1] * d_after).astype(BF16)
    d_attended[...] = low
    for copy in copies:
        copy.wait()
    for e in range(len(d_mixed)):
        rows_here = group_rows(weights, (spot ^ e) % GROUPS, place[2] if slots else None)
        d_mixed[e][...] = nt(low, rows_here).astype(BF16)
    sums[0:1, :] = over_tokens(d_after * attended[...])
    sums[1:2, :] = over_tokens(d_normed)
    sums[2:3, :] = over_tokens(d_normed * xhat)
    sums[3:8, :] = jnp.zeros((5, width), F32)


def output_kernel(vectors, upstream, scale, middle, own, *refs, others):
    arrived, (result, sums) = refs[:others], refs[others:]
    output = own[...] + vectors[BIAS_DOWN : BIAS_DOWN + 1]
    for ref in arrived:
        output = output + ref[...].astype(F32)
    gate = vectors[GATE_TWO : GATE_TWO + 1]
    result[...] = (middle[...] + gate * output).astype(BF16)
    d_result = upstream[...].astype(F32) * scale[...]
    sums[0:1, :] = over_tokens(d_result * output)
    sums[1:2, :] = over_tokens(gate * d_result)
    sums[2:8, :] = jnp.zeros((6, middle.shape[1]), F32)


def tokens_kernel(vectors, tokens, d_middle, own, arrived, d_tokens):
    xhat, root = standardize(tokens[...].astype(F32))
    d_normed = own[...].astype(F32) + arrived[...].astype(F32)
    back = pull_norm(d_normed, vectors[GAINS_ONE : GAINS_ONE + 1], xhat, root)
    d_tokens[...] = (d_middle[...] + back).astype(BF16)


def forward_kernel(place, *refs, blocks, halves):
    tokens, refs = refs[:blocks], refs[blocks:]
    count = 2 if halves else PLANES
    weights, refs = refs[:count], refs[count:]
    (vectors, cosine, sines), refs = refs[:3], refs[3:]
    gain, shift = vectors[GAINS_ONE : GAINS_ONE + 1], vectors[SHIFT_ONE : SHIFT_ONE + 1]
    mixed, refs = refs[:blocks], refs[blocks:]
    heads, log_total, normed, weight, keys, mixed_turned = refs
    plane = place[0]
    rows = weights[0].shape[-2]
    count = tokens[0].shape[0]
    if halves:
        for half in range(2):
            for distance in range(PLANES):
                first = pl.multiple_of((plane ^ distance) * 2 * rows + (place[3] ^ half) * rows, 16)
                weight[pl.ds(first, rows), :] = weights[half][distance]
    else:
        for distance in range(PLANES):
            first = pl.multiple_of((plane ^ distance) * rows, 8)
            weight[pl.ds(first, rows), :] = weights[distance][...]
    for block in range(blocks):
        xhat, _ = standardize(tokens[block][...].astype(F32))
        normed[block * count : (block + 1) * count, :] = (xhat * gain + shift).astype(BF16)
    project = nt(weight[...].T, normed[...])
    cos, sin = cosine[...], sines[...]
    half = HEAD // 2
    for part in range(2):
        for head in range(PER_GROUP):
            start = part * WIDTH + head * HEAD
            first, second = project[start : start + half], project[start + half : start + HEAD]
            turned = jnp.concatenate([first * cos - second * sin, second * cos + first * sin], 0).astype(BF16)
            if part == 0:
                turned = turned * jnp.asarray(SCALING, BF16)
            else:
                keys[head] = turned.T
            heads[start : start + HEAD, :] = turned
    heads[2 * WIDTH :, :] = project[2 * WIDTH :].astype(BF16)
    length = heads.shape[1]
    for head in range(PER_GROUP):
        start = head * HEAD

        def queries_step(step, carry):
            columns = pl.ds(pl.multiple_of(step * QUERY_BLOCK, QUERY_BLOCK), QUERY_BLOCK)
            scores = nn(keys[head], heads[start : start + HEAD, columns])
            peak = jnp.max(scores, 0, keepdims=True)
            exps = jnp.exp(scores - peak)
            total = jnp.sum(exps, 0, keepdims=True)
            log_total[head : head + 1, columns] = peak + jnp.log(total)
            probs = (exps * (1.0 / total)).astype(BF16)
            values = heads[2 * WIDTH + start : 2 * WIDTH + start + HEAD, :]
            mixed_turned[start : start + HEAD, columns] = nn(values, probs).astype(BF16)
            return carry

        lax.fori_loop(0, length // QUERY_BLOCK, queries_step, 0)
    for block in range(blocks):
        mixed[block][...] = mixed_turned[:, block * count : (block + 1) * count].T


def backward_kernel(*refs, blocks):
    d_mixed, refs = refs[:blocks], refs[blocks:]
    (heads, log_total, cosine, sines), refs = refs[:4], refs[4:]
    d_project, d_turned, d_keys, d_values, keys, values = refs
    count = d_mixed[0].shape[0]
    length = heads.shape[1]
    for block in range(blocks):
        d_turned[:, block * count : (block + 1) * count] = d_mixed[block][...].T
    cos, sin = cosine[...], sines[...]
    half = HEAD // 2
    d_keys[...] = jnp.zeros_like(d_keys)
    d_values[...] = jnp.zeros_like(d_values)
    for head in range(PER_GROUP):
        start = head * HEAD
        keys_turned = heads.at[WIDTH + start : WIDTH + start + HEAD]
        keys[...] = keys_turned[...].T
        values[...] = heads[2 * WIDTH + start : 2 * WIDTH + start + HEAD, :].T

        def queries_step(step, carry):
            columns = pl.ds(pl.multiple_of(step * QUERY_BLOCK, QUERY_BLOCK), QUERY_BLOCK)
            queries = heads[start : start + HEAD, columns]
            incoming = d_turned[start : start + HEAD, columns]
            scores = nn(keys[...], queries)
            probs = jnp.exp(scores - log_total[head : head + 1, columns])
            d_probs = nn(values[...], incoming)
            delta = jnp.sum(probs * d_probs, 0, keepdims=True)
            d_scores = (probs * (d_probs - delta)).astype(BF16)
            d_values[start : start + HEAD, :] += nt(incoming, probs.astype(BF16))
            d_keys[start : start + HEAD, :] += nt(queries, d_scores)
            d_queries = nn(keys_turned[...], d_scores) * SCALING
            first, second = d_queries[:half], d_queries[half:]
            cos_here, sin_here = cosine[:, columns], sines[:, columns]
            d_project[start : start + half, columns] = (first * cos_here + second * sin_here).astype(BF16)
            d_project[start + half : start + HEAD, columns] = (second * cos_here - first * sin_here).astype(BF16)
            return carry

        lax.fori_loop(0, length // QUERY_BLOCK, queries_step, 0)
        first, second = d_keys[start : start + half, :], d_keys[start + half : start + HEAD, :]
        d_project[WIDTH + start : WIDTH + start + half, :] = (first * cos + second * sin).astype(BF16)
        d_project[WIDTH + start + half : WIDTH + start + HEAD, :] = (second * cos - first * sin).astype(BF16)
    d_project[2 * WIDTH :, :] = d_values[...].astype(BF16)


def attend_forward(place, tokens, weights, vectors, cosine, sines, halves):
    blocks, (count, width) = len(tokens), tokens[0].shape
    length = blocks * count
    columns = weights[0].shape[-1]
    outs = call(
        functools.partial(forward_kernel, blocks=blocks, halves=halves),
        "attend_forward",
        [*tokens, *weights, vectors, cosine, sines],
        [place],
        [shape_of((count, WIDTH), BF16)] * blocks
        + [
            shape_of((columns, length), BF16),
            shape_of((8, length), F32),
            shape_of((length, width), BF16),
            shape_of((width, columns), BF16),
        ],
        [pltpu.VMEM((PER_GROUP, length, HEAD), BF16), pltpu.VMEM((WIDTH, length), BF16)],
        us=15.0,
    )
    return outs[:blocks], outs[blocks:]


def attend_backward(d_mixed, heads, log_total, cosine, sines):
    blocks, length = len(d_mixed), heads.shape[1]
    (d_project,) = call(
        functools.partial(backward_kernel, blocks=blocks),
        "attend_backward",
        [*d_mixed, heads, log_total, cosine, sines],
        [],
        [shape_of((3 * WIDTH, length), BF16)],
        [
            pltpu.VMEM((WIDTH, length), BF16),
            pltpu.VMEM((WIDTH, length), F32),
            pltpu.VMEM((WIDTH, length), F32),
            pltpu.VMEM((length, HEAD), BF16),
            pltpu.VMEM((length, HEAD), BF16),
        ],
        us=30.0,
    )
    return d_project


def after(values, *others):
    return lax.optimization_barrier((values, others))[0]


def add(left, right):
    return (left.astype(F32) + right.astype(F32)).astype(BF16)


def pick(stack, index):
    return lax.dynamic_index_in_dim(stack, index, 0, keepdims=False)


def bits_of(count):
    return [1 << bit for bit in range(count.bit_length() - 1)]


def body(
    tokens,
    upstream,
    token_mask,
    time_index,
    weight_index,
    time_table,
    weight_grid,
    w_ada,
    b_ada,
    gain_one,
    gain_two,
    w_qkv,
    w_proj,
    w_up,
    b_up,
    w_down,
    b_down,
    *,
    n,
    m,
):
    side = n // PLANES
    me = lax.axis_index("seq")
    plane, spot = me // side, me % side
    slice_of = lax.axis_index("mlp")
    place = jnp.stack([plane, spot, me, slice_of]).astype(jnp.int32)
    shard, width = tokens.shape[2], tokens.shape[3]
    rows = w_qkv.shape[0]
    hidden_count = w_up.shape[1]
    grid_size = time_table.shape[0]
    ada_columns = w_ada.shape[1]
    count = PLANES * shard
    unit = min(width, hidden_count)
    hidden_chunks, width_chunks = hidden_count // unit, width // unit
    pairwise = rows % 16 == 0 and side == GROUPS and unit == width and m == 2
    z_bits, y_bit, core_bit = (2 * side, side), 2, 1

    def swap(value, distance):
        return lax.ppermute(value, "seq", [(i, i ^ distance) for i in range(n)])

    def swap_mlp(value, distance):
        return lax.ppermute(value, "mlp", [(i, i ^ distance) for i in range(m)])

    def between_planes(pieces):
        return [pieces[0]] + [swap(pieces[d], d * side) for d in range(1, PLANES)]

    def in_plane(pieces):
        return [pieces[0]] + [swap(pieces[e], e) for e in range(1, side)]

    def in_order(blocks, axis):
        halves = jnp.stack(blocks)
        for bit in bits_of(len(blocks)):
            here = halves.reshape((len(blocks) // (2 * bit), 2, bit) + halves.shape[1:])
            halves = jnp.where((axis & bit) != 0, here[:, ::-1], here).reshape(halves.shape)
        return halves

    def for_plane(values):
        return [pick(values, jnp.minimum(plane ^ d, MICRO - 1)) for d in range(PLANES)]

    def columns_of(value):
        return [value[:, at : at + unit] for at in range(0, value.shape[1], unit)]

    line = [value[None] for value in (b_ada, gain_one, gain_two, b_down)]
    small_count = -(-MICRO * (ada_columns + rows + shard) // 128) * 128
    first_shapes = [shape_of((2 * hidden_chunks + width_chunks, rows, unit), BF16), shape_of((1, small_count), F32)]
    first_shapes += [shape_of((rows, 3 * WIDTH), BF16)] * side + [shape_of((2 * shard, width), BF16)] * PLANES
    ring_chunks = 2 * hidden_chunks + (0 if pairwise else width_chunks)
    packed, small, *pieces = call(
        prepare_kernel,
        "prepare",
        [tokens[:, 0], upstream[:, 0], w_qkv, w_up, w_down.T, w_proj, time_table, w_ada.T, *line, token_mask[:, 0]],
        [place, time_index[:, 0]],
        first_shapes,
        us=4.0,
    )
    group_columns, token_pieces = pieces[:side], pieces[side:]

    token_arrived = between_planes(token_pieces)

    received = jnp.stack(in_plane(group_columns))
    weight_block = jnp.concatenate([pick(received, spot ^ at) for at in range(side)], 0)
    if pairwise:
        weight_block = pick(weight_block.reshape(2, width // 8, 3 * WIDTH), slice_of)
    weight_blocks = {0: weight_block}
    for bit in (2, 1):
        for known in list(weight_blocks):
            weight_blocks[known | bit] = swap(weight_blocks[known], bit * side)
    weight_blocks = [weight_blocks[at] for at in range(PLANES)]
    far_block = weight_blocks[2]
    if pairwise:
        weight_blocks = jnp.stack(weight_blocks)
        weight_blocks = [weight_blocks, swap_mlp(weight_blocks, 1)]

    for bit in bits_of(n)[:-1]:
        small = jnp.concatenate([small, swap(small, bit)], 0)
    arrived, small = lax.optimization_barrier((token_arrived, after(small, far_block)))
    own_low = jnp.concatenate([piece[:shard] for piece in arrived], 0)
    own_upstream = jnp.concatenate([piece[shard:] for piece in arrived], 0)
    token_blocks = {0: own_low}
    for bit in reversed(bits_of(side)):
        for known in list(token_blocks):
            token_blocks[known | bit] = swap(token_blocks[known], bit)
    token_blocks = [token_blocks[at] for at in range(side)]

    gathered = lax.all_gather(after(packed[:ring_chunks], token_arrived, far_block), "seq", axis=0)
    if pairwise:
        line = packed[2 * hidden_chunks][None]
        for bit in (2 * side, side, y_bit, core_bit):
            line = jnp.concatenate([line, swap(line, bit)], 0)
        bits = (2 * side, side, y_bit, core_bit)
        slot_bits = [sum(bit for at, bit in enumerate(bits) if (slot >> at) & 1) for slot in range(n)]
        order_back = [slot_bits.index(distance) for distance in range(n)]
        gathered_proj = jnp.stack([line[slot] for slot in order_back])[:, None]
    else:
        gathered_proj = None
        gathered = gathered.transpose(1, 0, 2, 3).reshape(-1, GROUPS, WIDTH, unit).transpose(1, 0, 2, 3)
    blocks_shape = (gathered.shape[0],) + gathered.shape[2:]
    proj_chunks = [0] if pairwise else list(range(2 * hidden_chunks, 2 * hidden_chunks + width_chunks))
    gathered_proj = gathered_proj if pairwise else gathered

    def weight_scratch(number):
        return [pltpu.VMEM((number,) + blocks_shape, BF16), pltpu.SemaphoreType.DMA((number,))]

    for bit in bits_of(n)[-1:]:
        small = jnp.concatenate([small, swap(small, bit)], 0)
    vectors, scale = call(
        vectors_kernel,
        "vectors",
        [small],
        [place, weight_index[:, 0], weight_grid],
        [shape_of((16, width), F32), shape_of((count, 1), F32)],
        [pltpu.VMEM((8, count), F32)],
    )

    order = ((plane ^ jnp.arange(PLANES))[None, :] * side + (spot ^ jnp.arange(side))[:, None]) * shard
    positions = (order[:, :, None] + jnp.arange(shard)).reshape(1, -1).astype(F32)
    frequency = 10000.0 ** (-jnp.arange(0, HEAD, 2).astype(F32) / HEAD)
    angles = frequency[:, None] * positions
    cosine, sines = jnp.cos(angles), jnp.sin(angles)

    mixed_blocks, kept = attend_forward(
        place, token_blocks, weight_blocks, vectors, cosine, sines, pairwise
    )

    full_ada = lax.all_gather(after(w_ada, gathered), "seq", axis=0)

    mixed_blocks = in_plane(mixed_blocks)

    d_rows = ((own_upstream.astype(F32) * scale) * vectors[GATE_TWO][None]).astype(BF16)
    d_rows = [d_rows] + [swap_mlp(d_rows, d) for d in range(1, m)]

    attended, middle, normed_two = call(
        functools.partial(project_kernel, chunks=proj_chunks, slots=pairwise),
        "project",
        [own_low, vectors, *mixed_blocks],
        [place],
        [shape_of((count, width), F32), shape_of((count, width), F32), shape_of((count, width), BF16)],
        weight_scratch(width_chunks),
        us=3.0,
        far=[gathered_proj],
    )
    rows_all = [normed_two] + [swap_mlp(normed_two, d) for d in range(1, m)]
    bias_up = b_up.astype(F32)[None]
    fed = [
        call(
            feed_kernel,
            "feed_forward",
            [rows_all[d], d_rows[d], bias_up],
            [],
            [shape_of((count, width), BF16 if d else F32)] * 2 + [shape_of((count, hidden_count), BF16)] * 2,
            weight_scratch(2 * hidden_chunks),
            us=6.0,
            far=[gathered],
        )
        for d in range(m)
    ]
    d_arrived = [swap_mlp(fed[d][1], d) for d in range(1, m)]
    out_arrived = [swap_mlp(fed[d][0], d) for d in range(1, m)]
    slots = n // 2
    down_shape = (n, hidden_chunks, rows, unit) if pairwise else (GROUPS, hidden_chunks, WIDTH, unit)
    if pairwise:
        up_shapes = [shape_of((slots, hidden_chunks + width_chunks, rows, unit), BF16)] * 2
    else:
        up_shapes = [shape_of((width, hidden_count), BF16)]
    (down_grads,) = call(
        functools.partial(down_grads_kernel, blocks=m),
        "down_gradients",
        [*d_rows, *[f[2] for f in fed]],
        [],
        [shape_of(down_shape, BF16)],
        us=6.0,
    )
    *up_grads, bias_up_sum = call(
        functools.partial(up_grads_kernel, blocks=m, scatter=pairwise),
        "up_gradients",
        [*rows_all, *[f[3] for f in fed]],
        [place],
        up_shapes + [shape_of((1, hidden_count), F32)],
        us=5.0,
    )
    d_arrived, down_grads, full_ada, *up_grads = lax.optimization_barrier(
        (d_arrived, down_grads, full_ada, *up_grads)
    )
    if not pairwise:
        down_grads = down_grads.transpose(1, 0, 2, 3).reshape(hidden_chunks, n, rows, unit).transpose(1, 0, 2, 3)
    down_grads = lax.psum_scatter(down_grads, "seq", scatter_dimension=0, tiled=True)
    middle_outs = call(
        functools.partial(middle_kernel, others=m - 1, chunks=proj_chunks, slots=pairwise),
        "middle_backward",
        [vectors, own_upstream, scale, attended, middle, fed[0][1], *d_arrived],
        [place],
        [shape_of((count, WIDTH), BF16)] * side
        + [shape_of((count, width), F32), shape_of((count, width), BF16), shape_of((8, width), F32)],
        weight_scratch(width_chunks),
        us=4.0,
        far=[gathered_proj],
    )
    d_mixed_blocks, (d_middle, d_attended, middle_sums) = middle_outs[:side], middle_outs[side:]

    d_mixed_blocks = in_plane(d_mixed_blocks)
    if side > GROUPS:
        share = (spot < GROUPS).astype(BF16)
        d_mixed_blocks = [block * share for block in d_mixed_blocks]

    anywhere = pl.BlockSpec(memory_space=pl.ANY)
    proj_grads = pl.pallas_call(
        functools.partial(proj_grads_kernel, side=side, scatter=pairwise),
        out_shape=up_shapes if pairwise else [shape_of((width, width), BF16)],
        in_specs=[SMEM] + [VMEM] * (1 + side) + ([anywhere] * 2 if pairwise else []),
        out_specs=[anywhere] * 2 if pairwise else [VMEM],
        scratch_shapes=(
            [pltpu.VMEM((2, slots, 1, rows, unit), BF16), pltpu.SemaphoreType.DMA((2,))] if pairwise else []
        )
        + [pltpu.VMEM((width, width), BF16)],
        input_output_aliases={2 + side: 0, 3 + side: 1} if pairwise else {},
        compiler_params=pltpu.CompilerParams(vmem_limit_bytes=56 * 1024 * 1024),
        cost_estimate=pl.CostEstimate(flops=2 * 10**9, bytes_accessed=4 * 10**6, transcendentals=0),
        name="proj_gradients",
    )(place, d_attended, *mixed_blocks, *(up_grads if pairwise else []))

    def add_halves(own, arrived):
        half = own.shape[0] // 2
        return add(own[:half], arrived[:half]), add(own[half:], arrived[half:])

    def back_to_tokens(value):
        received = between_planes([value[d * shard : (d + 1) * shard] for d in range(PLANES)])
        received = jnp.stack(received)
        return jnp.stack([pick(received, plane ^ at) for at in range(MICRO)])[:, None]

    if pairwise:
        proj_sent, out_arrived = lax.optimization_barrier((proj_grads[1], out_arrived))
        up_arrived = swap(proj_sent, core_bit)

    result, output_sums = call(
        functools.partial(output_kernel, others=m - 1),
        "output",
        [vectors, own_upstream, scale, middle, fed[0][0], *out_arrived],
        [],
        [shape_of((count, width), BF16), shape_of((8, width), F32)],
    )
    if pairwise:
        up_own, up_sent = add_halves(proj_grads[0], after(up_arrived, result, *d_mixed_blocks))
        up_sent, result, *d_mixed_blocks = lax.optimization_barrier((up_sent, result, *d_mixed_blocks))
    result = back_to_tokens(result)

    d_project = attend_backward(d_mixed_blocks, kept[0], kept[1], cosine, sines)
    if pairwise:
        up_arrived = swap(up_sent, y_bit)
        d_project, result = lax.optimization_barrier((d_project, result))
    qkv_shape = (PLANES, width // 8, 3 * WIDTH) if pairwise else (2, width // PLANES, 3 * WIDTH)
    d_kept, d_sent, sums = call(
        functools.partial(normed_backward_kernel, blocks=side),
        "normed_backward",
        [d_project, kept[3], *token_blocks],
        [],
        [shape_of((side // 2, count, width), BF16)] * 2 + [shape_of((8, width), F32)],
        us=2.0,
    )
    d_project = after(d_project, d_sent, up_arrived) if pairwise else d_project
    grad_own, grad_sent = call(
        qkv_grads_kernel,
        "qkv_gradients",
        [d_project, kept[2]],
        [place],
        [shape_of(qkv_shape, BF16)] * 2,
        us=4.0,
    )

    arrived = after(swap(d_sent, 1), grad_sent)
    blocks = {2 * at: add(d_kept[at], arrived[at]) for at in range(side // 2)}
    if pairwise:
        up_arrived = after(up_arrived, blocks[y_bit])
        up_own, up_sent = add_halves(up_own, up_arrived)
        grad_arrived = swap_mlp(grad_sent, 1)
        grad_own, grad_sent = add_halves(grad_own, grad_arrived)
    bias_up_rows = -(-hidden_count // width)
    bias_up_sum = jnp.pad(bias_up_sum, ((0, 0), (0, bias_up_rows * width - hidden_count)))
    small = jnp.concatenate(
        [sums[0:2], middle_sums[0:3], output_sums[0:2], bias_up_sum.reshape(-1, width)], 0
    )
    small = small + swap(small, 1)
    for bit in bits_of(side)[1:]:
        for at in [at for at in blocks if at & bit]:
            arrived = swap(blocks.pop(at), bit)
            if len(blocks) > 1:
                blocks[at ^ bit] = add(blocks[at ^ bit], arrived)
    small = after(small, arrived)
    for bit in bits_of(side)[1:]:
        small = small + swap(small, bit)
    near_arrived = swap(grad_sent, side)
    small = jnp.concatenate([after(small, near_arrived), vectors[SCALE_TWO][None]], 0)[None]
    for bit in bits_of(PLANES):
        small = jnp.concatenate([small, swap(small, bit * side)], 0)
    (d_tokens,) = call(
        tokens_kernel,
        "tokens_backward",
        [vectors, own_low, d_middle, blocks[0], after(arrived, grad_arrived) if pairwise else arrived],
        [],
        [shape_of((count, width), BF16)],
    )
    returned = back_to_tokens(after(d_tokens, near_arrived) if pairwise else d_tokens)

    if pairwise:
        up_own, up_sent = add_halves(up_own, after(swap(up_sent, side), d_tokens))
        up_parts = up_own[0].astype(F32) + after(swap(up_sent, 2 * side), returned)[0].astype(F32)
        grad_up = jnp.concatenate([up_parts[at] for at in range(hidden_chunks)], -1)
        grad_proj = up_parts[hidden_chunks]
    else:
        grads = jnp.stack(columns_of(up_grads[0]) + columns_of(proj_grads[0]))
        grads = grads.reshape(-1, n, rows, unit).transpose(1, 0, 2, 3)
        grads = lax.psum_scatter(grads, "seq", scatter_dimension=0, tiled=True)[0]

        def columns_from(start, number):
            return jnp.concatenate([grads[start + at] for at in range(number)], -1).astype(F32)

        grad_up = columns_from(0, hidden_chunks)
        grad_proj = columns_from(hidden_chunks, width_chunks)
    for bit in bits_of(m):
        grad_proj = grad_proj + swap_mlp(grad_proj.astype(BF16), bit).astype(F32)

    arrived = near_arrived
    if pairwise:
        grad_own, grad_sent = add_halves(grad_own, arrived)
        arrived = after(swap(grad_sent, 2 * side), returned)
        total = grad_own[0].astype(F32) + arrived[0].astype(F32)
        by_spot = total.astype(BF16).reshape(2, rows, 3 * WIDTH)
        slices = [pick(by_spot, (spot ^ e) % 2) for e in range(side)]
    else:
        arrived = swap(add(grad_own[1], arrived[1]), 2 * side).astype(F32) + arrived[0].astype(F32)
        total = grad_own[0].astype(F32) + arrived
        by_spot = total.astype(BF16).reshape(side, rows, 3 * WIDTH)
        slices = [pick(by_spot, spot ^ e) for e in range(side)]
    received = jnp.stack(in_plane(slices))
    grad_qkv = jnp.stack([pick(received, spot ^ group) for group in range(GROUPS)])
    grad_qkv = grad_qkv.reshape(GROUPS, rows, 3, WIDTH).transpose(1, 2, 0, 3).reshape(rows, 3 * width)
    if pairwise:
        grad_qkv = jnp.where(spot // 2 == slice_of, grad_qkv, swap_mlp(grad_qkv, 1)).astype(F32)
    else:
        grad_qkv = grad_qkv.astype(F32)
        for bit in bits_of(m):
            grad_qkv = grad_qkv + swap_mlp(grad_qkv.astype(BF16), bit).astype(F32)

    down_grads = after(down_grads[0], d_sent).astype(F32)
    grad_down = jnp.concatenate([down_grads[at] for at in range(hidden_chunks)], -1).T

    small = in_order(list(small), plane)[:MICRO]
    grad_bias_up = jnp.sum(small[:, 7 : 7 + bias_up_rows], 0).reshape(-1)[:hidden_count]
    d_shift_one, d_xhat_one, d_gate_one, d_shift_two, d_xhat_two, d_gate_two = [small[:, at] for at in range(6)]
    index_here = time_index[:, 0]
    vector_sums = jnp.stack(
        [
            jnp.sum((1.0 + vectors[SCALES_ALL : SCALES_ALL + MICRO]) * d_xhat_one, 0),
            jnp.sum((1.0 + small[:, -1]) * d_xhat_two, 0),
            jnp.sum(small[:, 6], 0),
            jnp.pad(index_here.astype(F32), (0, width - MICRO)),
        ]
    )
    d_scale_one, d_scale_two = vectors[GAIN_ONE] * d_xhat_one, vectors[GAIN_TWO] * d_xhat_two
    small = jnp.stack([d_shift_one, d_scale_one, d_gate_one, d_shift_two, d_scale_two, d_gate_two], 1)
    small = jnp.concatenate([small.reshape(6 * MICRO, width), vector_sums], 0)[None]
    for bit in bits_of(m):
        small = jnp.concatenate([small, swap_mlp(small, bit)], 0)
    at = 6 * MICRO
    d_modulation = small[:, :at].reshape(m * MICRO, n, ada_columns)
    vector_sums = jnp.sum(small[:, at : at + 3], 0)
    index_all = small[:, at + 3, :MICRO].reshape(-1).astype(jnp.int32)
    onehot = (index_all[:, None] == jnp.arange(grid_size)[None, :]).astype(BF16)
    cond = jnp.dot(onehot, time_table, preferred_element_type=F32)
    d_modulation_own = lax.dynamic_index_in_dim(d_modulation, me, 1, keepdims=False)
    grad_ada = jnp.dot(cond.T, d_modulation_own, precision=highest)
    grad_bias_ada = jnp.sum(d_modulation_own, 0)
    d_cond = jnp.einsum("bic,idc->bd", d_modulation, full_ada.astype(F32), precision=highest)
    table_rows = grid_size // n
    onehot_own = index_all[None, :] == (me * table_rows + jnp.arange(table_rows))[:, None]
    grad_table = jnp.dot(onehot_own.astype(F32), d_cond, precision=highest)
    vector_sums = lax.dynamic_slice_in_dim(vector_sums, me * rows, rows, 1)
    return (
        result,
        returned.astype(F32),
        grad_table,
        grad_ada,
        grad_bias_ada,
        vector_sums[0],
        vector_sums[1],
        grad_qkv,
        grad_proj,
        grad_up,
        grad_bias_up,
        grad_down,
        vector_sums[2],
    )


def solution(mesh):
    in_specs = (
        P(None, "mlp", "seq", None),
        P(None, "mlp", "seq", None),
        P(None, "mlp", "seq"),
        P(None, "mlp"),
        P(None, "mlp"),
        P(),
        P(),
        P(None, "seq"),
        P("seq"),
        P("seq"),
        P("seq"),
        P("seq", None),
        P("seq", None),
        P("seq", "mlp"),
        P("mlp"),
        P("mlp", "seq"),
        P("seq"),
    )
    out_specs = (
        P(None, "mlp", "seq", None),
        P(None, "mlp", "seq", None),
        P("seq", None),
        P(None, "seq"),
        P("seq"),
        P("seq"),
        P("seq"),
        P("seq", None),
        P("seq", None),
        P("seq", "mlp"),
        P("mlp"),
        P("mlp", "seq"),
        P("seq"),
    )
    run = functools.partial(body, n=mesh.shape["seq"], m=mesh.shape["mlp"])
    return jax.shard_map(run, mesh=mesh, in_specs=in_specs, out_specs=out_specs, check_vma=False)
```

```python
import functools
import math

import jax
import jax.numpy as jnp
from jax import lax
from jax.experimental import pallas as pl
from jax.experimental.pallas import tpu as pltpu
from jax.sharding import PartitionSpec as P

HEADS = 12
HEAD = 64
MICRO = 3
PLANES = 4
GROUPS = 4
PER_GROUP = HEADS // GROUPS
WIDTH = PER_GROUP * HEAD
QUERY_BLOCK = 256
SCALING = HEAD ** (-0.5)
BF16 = jnp.bfloat16
F32 = jnp.float32
highest = lax.Precision.HIGHEST
SLOPE = math.sqrt(2.0 / math.pi)
CUBIC = 0.044715

SHIFT_ONE, SCALE_ONE, GATE_ONE, SHIFT_TWO, SCALE_TWO, GATE_TWO, GAIN_ONE, GAIN_TWO, BIAS_DOWN = range(9)
SCALES_ALL, GAINS_ONE, GAINS_TWO = 9, 12, 13

VMEM = pl.BlockSpec(memory_space=pltpu.VMEM)
SMEM = pl.BlockSpec(memory_space=pltpu.SMEM)


def nn(left, right):
    return lax.dot_general(left, right, (((1,), (0,)), ((), ())), preferred_element_type=F32)


def nt(left, right):
    return lax.dot_general(left, right, (((1,), (1,)), ((), ())), preferred_element_type=F32)


def standardize(inputs):
    average = jnp.mean(inputs, -1, keepdims=True)
    centred = inputs - average
    spread = jnp.mean(centred * centred, -1, keepdims=True)
    root = lax.rsqrt(spread + 1e-06)
    return centred * root, root


def pull_norm(d_normed, gains, xhat, root):
    e = d_normed * gains
    return root * (e - jnp.mean(e, -1, keepdims=True) - xhat * jnp.mean(e * xhat, -1, keepdims=True))


def over_tokens(value):
    return jnp.sum(value, 0, keepdims=True)


def shape_of(dims, dtype):
    return jax.ShapeDtypeStruct(dims, dtype)


def call(kernel, name, operands, scalars, outs, scratch=(), us=1.0, far=()):
    moved = sum(math.prod(o.shape) * o.dtype.itemsize for o in list(operands) + list(outs))
    return pl.pallas_call(
        kernel,
        out_shape=list(outs),
        in_specs=[SMEM] * len(scalars) + [pl.BlockSpec(memory_space=pl.ANY)] * len(far) + [VMEM] * len(operands),
        out_specs=[VMEM] * len(outs),
        scratch_shapes=list(scratch),
        compiler_params=pltpu.CompilerParams(vmem_limit_bytes=56 * 1024 * 1024),
        cost_estimate=pl.CostEstimate(flops=int(us * 1e9), bytes_accessed=moved, transcendentals=0),
        name=name,
    )(*scalars, *far, *operands)


def fetch(gathered, chunks, weights, arrived):
    copies = [
        pltpu.make_async_copy(gathered.at[:, chunk], weights.at[at], arrived.at[at])
        for at, chunk in enumerate(chunks)
    ]
    for copy in copies:
        copy.start()
    return copies


def whole(weights, at):
    return weights[at].reshape(weights.shape[1] * weights.shape[2], weights.shape[3])


def group_rows(weights, group, me=None):
    blocks = WIDTH // weights.shape[2]
    if me is not None:
        return jnp.concatenate([weights[0, me ^ (group * blocks + at)] for at in range(blocks)], 0)
    parts = [
        weights[at, pl.ds(group * blocks, blocks)].reshape(WIDTH, weights.shape[3])
        for at in range(weights.shape[0])
    ]
    return parts[0] if len(parts) == 1 else jnp.concatenate(parts, -1)


def modulation(times, table, ada, b_ada, gain_one, gain_two, b_down, mask, small):
    columns = ada.shape[0]
    rows = gain_one.shape[1]
    at = lax.broadcasted_iota(jnp.int32, (8, table.shape[0]), 1)
    line = lax.broadcasted_iota(jnp.int32, (8, table.shape[0]), 0)
    wanted = jnp.where(line == 0, times[0], jnp.where(line == 1, times[1], times[2]))
    cond = nn((at == wanted).astype(F32).astype(BF16), table[...]).astype(BF16)
    part = nt(cond, ada[...]) + b_ada[...].astype(F32)
    small[...] = jnp.zeros_like(small)
    at = 0
    for s in range(MICRO):
        small[0:1, at : at + columns] = part[s : s + 1]
        at += columns
    for ref in (gain_one, gain_two, b_down):
        small[0:1, at : at + rows] = ref[...].astype(F32)
        at += rows
    for s in range(MICRO):
        small[0:1, at : at + mask.shape[1]] = mask[s : s + 1, :].astype(F32)
        at += mask.shape[1]


def prepare_kernel(
    place, times, tokens, upstream, w_qkv, w_up, down, w_proj, table, ada, b_ada, gain_one, gain_two, b_down, mask, *outs
):
    packed, small, outs = outs[0], outs[1], outs[2:]
    columns_out, token_out, upstream_out = outs[: -2 * PLANES], outs[-2 * PLANES : -PLANES], outs[-PLANES:]
    plane, spot = place[0], place[1]
    for d in range(PLANES):
        token_out[d][...] = tokens[jnp.minimum(plane ^ d, MICRO - 1)]
        upstream_out[d][...] = upstream[jnp.minimum(plane ^ d, MICRO - 1)]
    width = w_proj.shape[1]
    by_group = [
        jnp.concatenate([w_qkv[:, p * width + g * WIDTH : p * width + (g + 1) * WIDTH] for p in range(3)], -1)
        for g in range(GROUPS)
    ]
    for e, out in enumerate(columns_out):
        group = (spot ^ e) % GROUPS
        here = by_group[0]
        for g in range(1, GROUPS):
            here = jnp.where(group == g, by_group[g], here)
        out[...] = here
    unit = packed.shape[2]
    chunk = 0
    for value in (w_up[...], down[...], w_proj[...]):
        for at in range(0, value.shape[1], unit):
            packed[chunk] = value[:, at : at + unit]
            chunk += 1
    modulation(times, table, ada, b_ada, gain_one, gain_two, b_down, mask, small)


def vectors_kernel(place, weight_index, weight_grid, small, vectors, scale, line):
    n = small.shape[0]
    width = vectors.shape[1]
    columns, rows, shard = 6 * width // n, width // n, scale.shape[0] // PLANES
    plane, spot = place[0], place[1]
    side = n // PLANES
    me = plane * side + spot
    last = jnp.minimum(plane, MICRO - 1)

    def one_of(three):
        return jnp.where(last == 0, three[0], jnp.where(last == 1, three[1], three[2]))

    def pieces(first, size):
        start = first
        while start < first + size:
            stop = min(first + size, (start // width + 1) * width)
            yield start // width, start % width, start - first, stop - start
            start = stop

    vectors[...] = jnp.zeros_like(vectors)
    for i in range(n):
        here = small[pl.ds(me ^ i, 1), :]
        each = [here[:, s * columns : (s + 1) * columns] for s in range(MICRO)]
        mine = one_of(each)
        for part, column, offset, size in pieces(i * columns, columns):
            vectors[part : part + 1, column : column + size] = mine[:, offset : offset + size]
            if part == SCALE_ONE:
                for s in range(MICRO):
                    vectors[SCALES_ALL + s : SCALES_ALL + s + 1, column : column + size] = each[s][
                        :, offset : offset + size
                    ]
        for row in (GAIN_ONE, GAIN_TWO, BIAS_DOWN):
            start = MICRO * columns + (row - GAIN_ONE) * rows
            vectors[row : row + 1, i * rows : (i + 1) * rows] = here[:, start : start + rows]
    for to, gain, by in ((GAINS_ONE, GAIN_ONE, SCALE_ONE), (GAINS_TWO, GAIN_TWO, SCALE_TWO)):
        vectors[to : to + 1, :] = vectors[gain : gain + 1, :] * (1.0 + vectors[by : by + 1, :])
    line[...] = jnp.zeros_like(line)
    for d in range(PLANES):
        here = small[d * side : d * side + 1, :]
        start = MICRO * (columns + rows)
        three = [here[:, start + s * shard : start + (s + 1) * shard] for s in range(MICRO)]
        line[0:1, d * shard : (d + 1) * shard] = one_of(three)
    weight = jnp.where(plane < MICRO, weight_grid[weight_index[last]], 0.0)
    scale[...] = line[...].T[:, 0:1] * weight


def project_kernel(place, gathered, tokens, vectors, *refs, chunks, slots):
    side = len(refs) - 5
    mixed, (attended, middle, normed, weights, arrived) = refs[:side], refs[side:]
    spot = place[1]
    copies = fetch(gathered, chunks, weights, arrived)
    for copy in copies:
        copy.wait()
    total = jnp.zeros(attended.shape, F32)
    for e in range(side):
        other = spot ^ e
        block = mixed[e][...]
        if side > GROUPS:
            block = jnp.where(other < GROUPS, block, jnp.zeros_like(block))
        total = total + nn(block, group_rows(weights, other % GROUPS, place[2] if slots else None))
    attended[...] = total
    after = tokens[...].astype(F32) + vectors[GATE_ONE : GATE_ONE + 1] * total
    middle[...] = after
    xhat, _ = standardize(after)
    normed[...] = (xhat * vectors[GAINS_TWO : GAINS_TWO + 1] + vectors[SHIFT_TWO : SHIFT_TWO + 1]).astype(BF16)


def feed_kernel(gathered, rows, d_rows, bias, output, d_normed, active, d_hidden, weights, arrived):
    parts = weights.shape[0] // 2
    unit = weights.shape[3]
    order = [at for part in range(parts) for at in (part, parts + part)]
    copies = fetch(gathered, order, weights, arrived)
    out = jnp.zeros(output.shape, F32)
    back = jnp.zeros(output.shape, F32)
    for part in range(parts):
        columns = slice(part * unit, (part + 1) * unit)
        copies[2 * part].wait()
        up = whole(weights, 2 * part)
        u = nn(rows[...], up) + bias[:, columns]
        square = u * u
        bent = jnp.tanh(SLOPE * u * (1.0 + CUBIC * square))
        half = 0.5 * (1.0 + bent)
        on = (u * half).astype(BF16)
        active[:, columns] = on
        slope = half + 0.5 * u * (1.0 - bent * bent) * (SLOPE * (1.0 + 3.0 * CUBIC * square))
        copies[2 * part + 1].wait()
        down = whole(weights, 2 * part + 1)
        d_on = (nn(d_rows[...], down) * slope).astype(BF16)
        d_hidden[:, columns] = d_on
        out = out + nt(on, down)
        back = back + nt(d_on, up)
    output[...] = out.astype(output.dtype)
    d_normed[...] = back.astype(d_normed.dtype)


def scatter_store(refs, me, device, value):
    kept, sent, chunk, slot_of = refs
    distance = me ^ device
    slot = slot_of(distance)

    @pl.when(distance % 2 == 0)
    def _():
        kept[slot, chunk] = value

    @pl.when(distance % 2 == 1)
    def _():
        sent[slot, chunk] = value


def slot_y_first(distance):
    return ((distance >> 1) & 1) * 4 + ((distance >> 2) & 1) * 2 + ((distance >> 3) & 1)


def down_grads_kernel(*refs, blocks):
    d_rows, active, out = refs[:blocks], refs[blocks:-1], refs[-1]
    unit = out.shape[3]
    turned = [ref[...].T for ref in d_rows]
    for chunk in range(out.shape[1]):
        columns = slice(chunk * unit, (chunk + 1) * unit)
        grad = sum(nn(turned[b], active[b][:, columns]) for b in range(blocks)).astype(BF16)
        out[:, chunk] = grad.reshape(out.shape[0], out.shape[2], unit)


def up_grads_kernel(place, *refs, blocks, scatter):
    rows_all, d_hidden, outs = refs[:blocks], refs[blocks : 2 * blocks], refs[2 * blocks :]
    bias = outs[-1]
    me = place[2]
    width, count = rows_all[0].shape[1], bias.shape[1]
    unit = min(width, count)
    turned = [ref[...].T for ref in rows_all]
    for chunk in range(count // unit):
        columns = slice(chunk * unit, (chunk + 1) * unit)
        grad = sum(nn(turned[b], d_hidden[b][:, columns]) for b in range(blocks)).astype(BF16)
        bias[:, columns] = sum(over_tokens(d_hidden[b][:, columns].astype(F32)) for b in range(blocks))
        if scatter:
            rows = outs[0].shape[2]
            for i in range(width // rows):
                part = grad[i * rows : (i + 1) * rows]
                scatter_store((outs[0], outs[1], chunk, slot_y_first), me, i, part)
        else:
            outs[0][:, columns] = grad


def proj_grads_kernel(place, d_attended, *refs, side, scatter):
    mixed, refs = refs[:side], refs[side:]
    spot, me = place[1], place[2]
    width = d_attended.shape[1]
    whole_grad = refs[-1]
    if side > GROUPS:
        whole_grad[...] = jnp.zeros_like(whole_grad)
    for e in range(side):
        other = spot ^ e
        first = pl.multiple_of((other % GROUPS) * WIDTH, WIDTH)
        grad = nn(mixed[e][...].T, d_attended[...]).astype(BF16)
        if side > GROUPS:
            grad = whole_grad[pl.ds(first, WIDTH), :] + jnp.where(other < GROUPS, grad, jnp.zeros_like(grad))
        whole_grad[pl.ds(first, WIDTH), :] = grad
    if not scatter:
        refs[0][...] = whole_grad[...]
        return
    _, _, own, sent, ready, done, _ = refs
    rows, chunk = own.shape[2], own.shape[1] - 1
    for i in range(width // rows):
        part = whole_grad[i * rows : (i + 1) * rows, :]
        scatter_store((ready.at[0], ready.at[1], 0, slot_y_first), me, i, part)
    copies = [
        pltpu.make_async_copy(ready.at[at, :, 0], out.at[:, chunk], done.at[at])
        for at, out in enumerate((own, sent))
    ]
    for copy in copies:
        copy.start()
    for copy in copies:
        copy.wait()


def qkv_grads_kernel(place, d_project, normed, *outs):
    grad = nn(d_project[...], normed[...]).astype(BF16).T
    plane, slice_of = place[0], place[3]
    rows = outs[0].shape[1]
    if len(outs[0].shape) == 3 and outs[0].shape[0] == PLANES:
        for at in range(PLANES):
            distance = plane ^ at
            slot = (distance % 2) * 2 + distance // 2
            halves = [grad[(2 * at + half) * rows : (2 * at + half + 1) * rows] for half in range(2)]
            outs[0][slot] = jnp.where(slice_of == 0, halves[0], halves[1])
            outs[1][slot] = jnp.where(slice_of == 0, halves[1], halves[0])
    else:
        for at in range(PLANES):
            part = grad[at * rows : (at + 1) * rows]
            distance = plane ^ at

            @pl.when(distance % 2 == 0)
            def _():
                outs[0][distance // 2] = part

            @pl.when(distance % 2 == 1)
            def _():
                outs[1][distance // 2] = part


def normed_backward_kernel(d_project, weight, *refs, blocks):
    tokens, (kept, sent, sums) = refs[:blocks], refs[blocks:]
    count = tokens[0].shape[0]
    d_shift = jnp.zeros((1, weight.shape[0]), F32)
    d_xhat = jnp.zeros((1, weight.shape[0]), F32)
    for block in range(blocks):
        part = nt(d_project[:, block * count : (block + 1) * count].T, weight[...])
        (sent if block % 2 else kept)[block // 2] = part.astype(BF16)
        xhat, _ = standardize(tokens[block][...].astype(F32))
        d_shift = d_shift + over_tokens(part)
        d_xhat = d_xhat + over_tokens(part * xhat)
    sums[0:1, :] = d_shift
    sums[1:2, :] = d_xhat
    sums[2:8, :] = jnp.zeros((6, weight.shape[0]), F32)


def middle_kernel(place, gathered, vectors, upstream, scale, attended, middle, d_own, *refs, others, chunks, slots):
    arrived, refs = refs[:others], refs[others:]
    d_mixed, (d_middle, d_attended, sums, weights, copied) = refs[:-5], refs[-5:]
    spot = place[1]
    copies = fetch(gathered, chunks, weights, copied)
    width = middle.shape[1]
    d_normed = d_own[...]
    for ref in arrived:
        d_normed = d_normed + ref[...].astype(F32)
    xhat, root = standardize(middle[...])
    d_result = upstream[...].astype(F32) * scale[...]
    d_after = d_result + pull_norm(d_normed, vectors[GAINS_TWO : GAINS_TWO + 1], xhat, root)
    d_middle[...] = d_after
    low = (vectors[GATE_ONE : GATE_ONE + 1] * d_after).astype(BF16)
    d_attended[...] = low
    for copy in copies:
        copy.wait()
    for e in range(len(d_mixed)):
        rows_here = group_rows(weights, (spot ^ e) % GROUPS, place[2] if slots else None)
        d_mixed[e][...] = nt(low, rows_here).astype(BF16)
    sums[0:1, :] = over_tokens(d_after * attended[...])
    sums[1:2, :] = over_tokens(d_normed)
    sums[2:3, :] = over_tokens(d_normed * xhat)
    sums[3:8, :] = jnp.zeros((5, width), F32)


def output_kernel(vectors, upstream, scale, middle, own, *refs, others):
    arrived, (result, sums) = refs[:others], refs[others:]
    output = own[...] + vectors[BIAS_DOWN : BIAS_DOWN + 1]
    for ref in arrived:
        output = output + ref[...].astype(F32)
    gate = vectors[GATE_TWO : GATE_TWO + 1]
    result[...] = (middle[...] + gate * output).astype(BF16)
    d_result = upstream[...].astype(F32) * scale[...]
    sums[0:1, :] = over_tokens(d_result * output)
    sums[1:2, :] = over_tokens(gate * d_result)
    sums[2:8, :] = jnp.zeros((6, middle.shape[1]), F32)


def tokens_kernel(vectors, tokens, d_middle, own, arrived, d_tokens):
    xhat, root = standardize(tokens[...].astype(F32))
    d_normed = own[...].astype(F32) + arrived[...].astype(F32)
    back = pull_norm(d_normed, vectors[GAINS_ONE : GAINS_ONE + 1], xhat, root)
    d_tokens[...] = (d_middle[...] + back).astype(BF16)


def forward_kernel(place, *refs, blocks, halves):
    tokens, refs = refs[:blocks], refs[blocks:]
    count = 2 if halves else PLANES
    weights, refs = refs[:count], refs[count:]
    (vectors, cosine, sines), refs = refs[:3], refs[3:]
    gain, shift = vectors[GAINS_ONE : GAINS_ONE + 1], vectors[SHIFT_ONE : SHIFT_ONE + 1]
    mixed, refs = refs[:blocks], refs[blocks:]
    heads, log_total, normed, weight, keys, mixed_turned = refs
    plane = place[0]
    rows = weights[0].shape[-2]
    count = tokens[0].shape[0]
    if halves:
        for half in range(2):
            for distance in range(PLANES):
                first = pl.multiple_of((plane ^ distance) * 2 * rows + (place[3] ^ half) * rows, 16)
                weight[pl.ds(first, rows), :] = weights[half][distance]
    else:
        for distance in range(PLANES):
            first = pl.multiple_of((plane ^ distance) * rows, 8)
            weight[pl.ds(first, rows), :] = weights[distance][...]
    for block in range(blocks):
        xhat, _ = standardize(tokens[block][...].astype(F32))
        normed[block * count : (block + 1) * count, :] = (xhat * gain + shift).astype(BF16)
    project = nt(weight[...].T, normed[...])
    cos, sin = cosine[...], sines[...]
    half = HEAD // 2
    for part in range(2):
        for head in range(PER_GROUP):
            start = part * WIDTH + head * HEAD
            first, second = project[start : start + half], project[start + half : start + HEAD]
            turned = jnp.concatenate([first * cos - second * sin, second * cos + first * sin], 0).astype(BF16)
            if part == 0:
                turned = turned * jnp.asarray(SCALING, BF16)
            else:
                keys[head] = turned.T
            heads[start : start + HEAD, :] = turned
    heads[2 * WIDTH :, :] = project[2 * WIDTH :].astype(BF16)
    length = heads.shape[1]
    for head in range(PER_GROUP):
        start = head * HEAD

        def queries_step(step, carry):
            columns = pl.ds(pl.multiple_of(step * QUERY_BLOCK, QUERY_BLOCK), QUERY_BLOCK)
            scores = nn(keys[head], heads[start : start + HEAD, columns])
            peak = jnp.max(scores, 0, keepdims=True)
            exps = jnp.exp(scores - peak)
            total = jnp.sum(exps, 0, keepdims=True)
            log_total[head : head + 1, columns] = peak + jnp.log(total)
            probs = (exps * (1.0 / total)).astype(BF16)
            values = heads[2 * WIDTH + start : 2 * WIDTH + start + HEAD, :]
            mixed_turned[start : start + HEAD, columns] = nn(values, probs).astype(BF16)
            return carry

        lax.fori_loop(0, length // QUERY_BLOCK, queries_step, 0, unroll=True)
    for block in range(blocks):
        mixed[block][...] = mixed_turned[:, block * count : (block + 1) * count].T


def backward_kernel(*refs, blocks):
    d_mixed, refs = refs[:blocks], refs[blocks:]
    (heads, log_total, cosine, sines), refs = refs[:4], refs[4:]
    d_project, d_turned, d_keys, d_values, keys, values = refs
    count = d_mixed[0].shape[0]
    length = heads.shape[1]
    for block in range(blocks):
        d_turned[:, block * count : (block + 1) * count] = d_mixed[block][...].T
    cos, sin = cosine[...], sines[...]
    half = HEAD // 2
    d_keys[...] = jnp.zeros_like(d_keys)
    d_values[...] = jnp.zeros_like(d_values)
    for head in range(PER_GROUP):
        start = head * HEAD
        keys_turned = heads.at[WIDTH + start : WIDTH + start + HEAD]
        keys[...] = keys_turned[...].T
        values[...] = heads[2 * WIDTH + start : 2 * WIDTH + start + HEAD, :].T

        def queries_step(step, carry):
            columns = pl.ds(pl.multiple_of(step * QUERY_BLOCK, QUERY_BLOCK), QUERY_BLOCK)
            queries = heads[start : start + HEAD, columns]
            incoming = d_turned[start : start + HEAD, columns]
            scores = nn(keys[...], queries)
            probs = jnp.exp(scores - log_total[head : head + 1, columns])
            d_probs = nn(values[...], incoming)
            delta = jnp.sum(probs * d_probs, 0, keepdims=True)
            d_scores = (probs * (d_probs - delta)).astype(BF16)
            d_values[start : start + HEAD, :] += nt(incoming, probs.astype(BF16))
            d_keys[start : start + HEAD, :] += nt(queries, d_scores)
            d_queries = nn(keys_turned[...], d_scores) * SCALING
            first, second = d_queries[:half], d_queries[half:]
            cos_here, sin_here = cosine[:, columns], sines[:, columns]
            d_project[start : start + half, columns] = (first * cos_here + second * sin_here).astype(BF16)
            d_project[start + half : start + HEAD, columns] = (second * cos_here - first * sin_here).astype(BF16)
            return carry

        lax.fori_loop(0, length // QUERY_BLOCK, queries_step, 0, unroll=True)
        first, second = d_keys[start : start + half, :], d_keys[start + half : start + HEAD, :]
        d_project[WIDTH + start : WIDTH + start + half, :] = (first * cos + second * sin).astype(BF16)
        d_project[WIDTH + start + half : WIDTH + start + HEAD, :] = (second * cos - first * sin).astype(BF16)
    d_project[2 * WIDTH :, :] = d_values[...].astype(BF16)


def attend_forward(place, tokens, weights, vectors, cosine, sines, halves):
    blocks, (count, width) = len(tokens), tokens[0].shape
    length = blocks * count
    columns = weights[0].shape[-1]
    outs = call(
        functools.partial(forward_kernel, blocks=blocks, halves=halves),
        "attend_forward",
        [*tokens, *weights, vectors, cosine, sines],
        [place],
        [shape_of((count, WIDTH), BF16)] * blocks
        + [
            shape_of((columns, length), BF16),
            shape_of((8, length), F32),
            shape_of((length, width), BF16),
            shape_of((width, columns), BF16),
        ],
        [pltpu.VMEM((PER_GROUP, length, HEAD), BF16), pltpu.VMEM((WIDTH, length), BF16)],
        us=15.0,
    )
    return outs[:blocks], outs[blocks:]


def attend_backward(d_mixed, heads, log_total, cosine, sines):
    blocks, length = len(d_mixed), heads.shape[1]
    (d_project,) = call(
        functools.partial(backward_kernel, blocks=blocks),
        "attend_backward",
        [*d_mixed, heads, log_total, cosine, sines],
        [],
        [shape_of((3 * WIDTH, length), BF16)],
        [
            pltpu.VMEM((WIDTH, length), BF16),
            pltpu.VMEM((WIDTH, length), F32),
            pltpu.VMEM((WIDTH, length), F32),
            pltpu.VMEM((length, HEAD), BF16),
            pltpu.VMEM((length, HEAD), BF16),
        ],
        us=18.0,
    )
    return d_project


def after(values, *others):
    return lax.optimization_barrier((values, others))[0]


def add(left, right):
    return (left.astype(F32) + right.astype(F32)).astype(BF16)


def pick(stack, index):
    return lax.dynamic_index_in_dim(stack, index, 0, keepdims=False)


def bits_of(count):
    return [1 << bit for bit in range(count.bit_length() - 1)]


def body(
    tokens,
    upstream,
    token_mask,
    time_index,
    weight_index,
    time_table,
    weight_grid,
    w_ada,
    b_ada,
    gain_one,
    gain_two,
    w_qkv,
    w_proj,
    w_up,
    b_up,
    w_down,
    b_down,
    *,
    n,
    m,
):
    side = n // PLANES
    me = lax.axis_index("seq")
    plane, spot = me // side, me % side
    slice_of = lax.axis_index("mlp")
    place = jnp.stack([plane, spot, me, slice_of]).astype(jnp.int32)
    shard, width = tokens.shape[2], tokens.shape[3]
    rows = w_qkv.shape[0]
    hidden_count = w_up.shape[1]
    grid_size = time_table.shape[0]
    ada_columns = w_ada.shape[1]
    count = PLANES * shard
    unit = min(width, hidden_count)
    hidden_chunks, width_chunks = hidden_count // unit, width // unit
    pairwise = rows % 16 == 0 and side == GROUPS and unit == width and m == 2
    z_bits, y_bit, core_bit = (2 * side, side), 2, 1

    def swap(value, distance):
        return lax.ppermute(value, "seq", [(i, i ^ distance) for i in range(n)])

    def swap_mlp(value, distance):
        return lax.ppermute(value, "mlp", [(i, i ^ distance) for i in range(m)])

    def between_planes(pieces):
        return [pieces[0]] + [swap(pieces[d], d * side) for d in range(1, PLANES)]

    def in_plane(pieces):
        return [pieces[0]] + [swap(pieces[e], e) for e in range(1, side)]

    def in_order(blocks, axis):
        halves = jnp.stack(blocks)
        for bit in bits_of(len(blocks)):
            here = halves.reshape((len(blocks) // (2 * bit), 2, bit) + halves.shape[1:])
            halves = jnp.where((axis & bit) != 0, here[:, ::-1], here).reshape(halves.shape)
        return halves

    def for_plane(values):
        return [pick(values, jnp.minimum(plane ^ d, MICRO - 1)) for d in range(PLANES)]

    def columns_of(value):
        return [value[:, at : at + unit] for at in range(0, value.shape[1], unit)]

    line = [value[None] for value in (b_ada, gain_one, gain_two, b_down)]
    small_count = -(-MICRO * (ada_columns + rows + shard) // 128) * 128
    first_shapes = [shape_of((2 * hidden_chunks + width_chunks, rows, unit), BF16), shape_of((1, small_count), F32)]
    first_shapes += [shape_of((rows, 3 * WIDTH), BF16)] * side + [shape_of((shard, width), BF16)] * (2 * PLANES)
    packed, small, *pieces = call(
        prepare_kernel,
        "prepare",
        [tokens[:, 0], upstream[:, 0], w_qkv, w_up, w_down.T, w_proj, time_table, w_ada.T, *line, token_mask[:, 0]],
        [place, time_index[:, 0]],
        first_shapes,
        us=4.0,
    )
    group_columns, token_pieces, upstream_pieces = pieces[:side], pieces[side : side + PLANES], pieces[side + PLANES :]

    token_arrived = between_planes(token_pieces)

    received = jnp.stack(in_plane(group_columns))
    weight_block = jnp.concatenate([pick(received, spot ^ at) for at in range(side)], 0)
    if pairwise:
        weight_block = pick(weight_block.reshape(2, width // 8, 3 * WIDTH), slice_of)
    weight_blocks = {0: weight_block}
    for bit in (2, 1):
        for known in list(weight_blocks):
            weight_blocks[known | bit] = swap(weight_blocks[known], bit * side)
    weight_blocks = [weight_blocks[at] for at in range(PLANES)]
    far_block = weight_blocks[2]
    if pairwise:
        weight_blocks = jnp.stack(weight_blocks)
        weight_blocks = [weight_blocks, swap_mlp(weight_blocks, 1)]

    for bit in bits_of(n)[:-1]:
        small = jnp.concatenate([small, swap(small, bit)], 0)
    arrived, small = lax.optimization_barrier((token_arrived, after(small, far_block)))
    own_low = jnp.concatenate(arrived, 0)
    token_blocks = {0: own_low}
    for bit in reversed(bits_of(side)):
        for known in list(token_blocks):
            token_blocks[known | bit] = swap(token_blocks[known], bit)
    token_blocks = [token_blocks[at] for at in range(side)]

    gathered = lax.all_gather(after(packed, token_arrived, far_block), "seq", axis=0)
    if not pairwise:
        gathered = gathered.transpose(1, 0, 2, 3).reshape(-1, GROUPS, WIDTH, unit).transpose(1, 0, 2, 3)
    blocks_shape = (gathered.shape[0],) + gathered.shape[2:]
    proj_chunks = list(range(2 * hidden_chunks, 2 * hidden_chunks + width_chunks))

    def weight_scratch(number):
        return [pltpu.VMEM((number,) + blocks_shape, BF16), pltpu.SemaphoreType.DMA((number,))]

    for bit in bits_of(n)[-1:]:
        small = jnp.concatenate([small, swap(small, bit)], 0)
    vectors, scale = call(
        vectors_kernel,
        "vectors",
        [small],
        [place, weight_index[:, 0], weight_grid],
        [shape_of((16, width), F32), shape_of((count, 1), F32)],
        [pltpu.VMEM((8, count), F32)],
    )

    order = ((plane ^ jnp.arange(PLANES))[None, :] * side + (spot ^ jnp.arange(side))[:, None]) * shard
    positions = (order[:, :, None] + jnp.arange(shard)).reshape(1, -1).astype(F32)
    frequency = 10000.0 ** (-jnp.arange(0, HEAD, 2).astype(F32) / HEAD)
    angles = frequency[:, None] * positions
    cosine, sines = jnp.cos(angles), jnp.sin(angles)

    mixed_blocks, kept = attend_forward(
        place, token_blocks, weight_blocks, vectors, cosine, sines, pairwise
    )

    full_ada = lax.all_gather(after(w_ada, gathered), "seq", axis=0)

    mixed_blocks = in_plane(mixed_blocks)

    own_upstream = between_planes(after(upstream_pieces, weight_blocks))
    own_upstream = jnp.concatenate(after(own_upstream, kept[1]), 0)
    d_rows = ((own_upstream.astype(F32) * scale) * vectors[GATE_TWO][None]).astype(BF16)
    d_rows = [d_rows] + [swap_mlp(d_rows, d) for d in range(1, m)]

    attended, middle, normed_two = call(
        functools.partial(project_kernel, chunks=proj_chunks, slots=False),
        "project",
        [own_low, vectors, *mixed_blocks],
        [place],
        [shape_of((count, width), F32), shape_of((count, width), F32), shape_of((count, width), BF16)],
        weight_scratch(width_chunks),
        us=3.0,
        far=[gathered],
    )
    rows_all = [normed_two] + [swap_mlp(normed_two, d) for d in range(1, m)]
    bias_up = b_up.astype(F32)[None]
    fed = [
        call(
            feed_kernel,
            "feed_forward",
            [rows_all[d], d_rows[d], bias_up],
            [],
            [shape_of((count, width), BF16 if d else F32)] * 2 + [shape_of((count, hidden_count), BF16)] * 2,
            weight_scratch(2 * hidden_chunks),
            us=6.0,
            far=[gathered],
        )
        for d in range(m)
    ]
    d_arrived = [swap_mlp(fed[d][1], d) for d in range(1, m)]
    out_arrived = [swap_mlp(fed[d][0], d) for d in range(1, m)]
    slots = n // 2
    down_shape = (n, hidden_chunks, rows, unit) if pairwise else (GROUPS, hidden_chunks, WIDTH, unit)
    if pairwise:
        up_shapes = [shape_of((slots, hidden_chunks + width_chunks, rows, unit), BF16)] * 2
    else:
        up_shapes = [shape_of((width, hidden_count), BF16)]
    (down_grads,) = call(
        functools.partial(down_grads_kernel, blocks=m),
        "down_gradients",
        [*d_rows, *[f[2] for f in fed]],
        [],
        [shape_of(down_shape, BF16)],
        us=6.0,
    )
    *up_grads, bias_up_sum = call(
        functools.partial(up_grads_kernel, blocks=m, scatter=pairwise),
        "up_gradients",
        [*rows_all, *[f[3] for f in fed]],
        [place],
        up_shapes + [shape_of((1, hidden_count), F32)],
        us=5.0,
    )
    d_arrived, down_grads, full_ada, *up_grads = lax.optimization_barrier(
        (d_arrived, down_grads, full_ada, *up_grads)
    )
    if not pairwise:
        down_grads = down_grads.transpose(1, 0, 2, 3).reshape(hidden_chunks, n, rows, unit).transpose(1, 0, 2, 3)
    down_grads = lax.psum_scatter(down_grads, "seq", scatter_dimension=0, tiled=True)
    middle_outs = call(
        functools.partial(middle_kernel, others=m - 1, chunks=proj_chunks, slots=False),
        "middle_backward",
        [vectors, own_upstream, scale, attended, middle, fed[0][1], *d_arrived],
        [place],
        [shape_of((count, WIDTH), BF16)] * side
        + [shape_of((count, width), F32), shape_of((count, width), BF16), shape_of((8, width), F32)],
        weight_scratch(width_chunks),
        us=4.0,
        far=[gathered],
    )
    d_mixed_blocks, (d_middle, d_attended, middle_sums) = middle_outs[:side], middle_outs[side:]

    d_mixed_blocks = in_plane(d_mixed_blocks)
    if side > GROUPS:
        share = (spot < GROUPS).astype(BF16)
        d_mixed_blocks = [block * share for block in d_mixed_blocks]

    anywhere = pl.BlockSpec(memory_space=pl.ANY)
    proj_grads = pl.pallas_call(
        functools.partial(proj_grads_kernel, side=side, scatter=pairwise),
        out_shape=up_shapes if pairwise else [shape_of((width, width), BF16)],
        in_specs=[SMEM] + [VMEM] * (1 + side) + ([anywhere] * 2 if pairwise else []),
        out_specs=[anywhere] * 2 if pairwise else [VMEM],
        scratch_shapes=(
            [pltpu.VMEM((2, slots, 1, rows, unit), BF16), pltpu.SemaphoreType.DMA((2,))] if pairwise else []
        )
        + [pltpu.VMEM((width, width), BF16)],
        input_output_aliases={2 + side: 0, 3 + side: 1} if pairwise else {},
        compiler_params=pltpu.CompilerParams(vmem_limit_bytes=56 * 1024 * 1024),
        cost_estimate=pl.CostEstimate(flops=2 * 10**9, bytes_accessed=4 * 10**6, transcendentals=0),
        name="proj_gradients",
    )(place, d_attended, *mixed_blocks, *(up_grads if pairwise else []))

    def add_halves(own, arrived):
        half = own.shape[0] // 2
        return add(own[:half], arrived[:half]), add(own[half:], arrived[half:])

    def back_to_tokens(value):
        received = between_planes([value[d * shard : (d + 1) * shard] for d in range(PLANES)])
        received = jnp.stack(received)
        return jnp.stack([pick(received, plane ^ at) for at in range(MICRO)])[:, None]

    if pairwise:
        proj_sent, out_arrived = lax.optimization_barrier((proj_grads[1], out_arrived))
        up_arrived = swap(proj_sent, core_bit)

    result, output_sums = call(
        functools.partial(output_kernel, others=m - 1),
        "output",
        [vectors, own_upstream, scale, middle, fed[0][0], *out_arrived],
        [],
        [shape_of((count, width), BF16), shape_of((8, width), F32)],
    )
    if pairwise:
        up_own, up_sent = add_halves(proj_grads[0], after(up_arrived, result, *d_mixed_blocks))
        up_sent, result, *d_mixed_blocks = lax.optimization_barrier((up_sent, result, *d_mixed_blocks))
    result = back_to_tokens(result)

    d_project = attend_backward(d_mixed_blocks, kept[0], kept[1], cosine, sines)
    if pairwise:
        up_arrived = swap(up_sent, y_bit)
        d_project, result = lax.optimization_barrier((d_project, result))
    qkv_shape = (PLANES, width // 8, 3 * WIDTH) if pairwise else (2, width // PLANES, 3 * WIDTH)
    d_kept, d_sent, sums = call(
        functools.partial(normed_backward_kernel, blocks=side),
        "normed_backward",
        [d_project, kept[3], *token_blocks],
        [],
        [shape_of((side // 2, count, width), BF16)] * 2 + [shape_of((8, width), F32)],
        us=2.0,
    )
    d_project = after(d_project, d_sent, up_arrived) if pairwise else d_project
    grad_own, grad_sent = call(
        qkv_grads_kernel,
        "qkv_gradients",
        [d_project, kept[2]],
        [place],
        [shape_of(qkv_shape, BF16)] * 2,
        us=4.0,
    )

    arrived = after(swap(d_sent, 1), grad_sent)
    blocks = {2 * at: add(d_kept[at], arrived[at]) for at in range(side // 2)}
    if pairwise:
        up_arrived = after(up_arrived, blocks[y_bit])
        up_own, up_sent = add_halves(up_own, up_arrived)
        grad_arrived = swap_mlp(grad_sent, 1)
        grad_own, grad_sent = add_halves(grad_own, grad_arrived)
    bias_up_rows = -(-hidden_count // width)
    bias_up_sum = jnp.pad(bias_up_sum, ((0, 0), (0, bias_up_rows * width - hidden_count)))
    small = jnp.concatenate(
        [sums[0:2], middle_sums[0:3], output_sums[0:2], bias_up_sum.reshape(-1, width)], 0
    )
    small = small + swap(small, 1)
    for bit in bits_of(side)[1:]:
        for at in [at for at in blocks if at & bit]:
            arrived = swap(blocks.pop(at), bit)
            if len(blocks) > 1:
                blocks[at ^ bit] = add(blocks[at ^ bit], arrived)
    small = after(small, arrived)
    for bit in bits_of(side)[1:]:
        small = small + swap(small, bit)
    near_arrived = swap(grad_sent, side)
    small = jnp.concatenate([after(small, near_arrived), vectors[SCALE_TWO][None]], 0)[None]
    for bit in bits_of(PLANES):
        small = jnp.concatenate([small, swap(small, bit * side)], 0)
    (d_tokens,) = call(
        tokens_kernel,
        "tokens_backward",
        [vectors, own_low, d_middle, blocks[0], after(arrived, grad_arrived) if pairwise else arrived],
        [],
        [shape_of((count, width), BF16)],
    )
    if pairwise:
        grad_own, grad_sent = add_halves(grad_own, after(near_arrived, d_tokens))
        far_arrived = swap(grad_sent, 2 * side)
        d_tokens = after(d_tokens, far_arrived)
    returned = back_to_tokens(d_tokens)

    if pairwise:
        up_own, up_sent = add_halves(up_own, after(swap(up_sent, side), d_tokens))
        up_parts = up_own[0].astype(F32) + after(swap(up_sent, 2 * side), returned)[0].astype(F32)
        grad_up = jnp.concatenate([up_parts[at] for at in range(hidden_chunks)], -1)
        grad_proj = up_parts[hidden_chunks]
    else:
        grads = jnp.stack(columns_of(up_grads[0]) + columns_of(proj_grads[0]))
        grads = grads.reshape(-1, n, rows, unit).transpose(1, 0, 2, 3)
        grads = lax.psum_scatter(grads, "seq", scatter_dimension=0, tiled=True)[0]

        def columns_from(start, number):
            return jnp.concatenate([grads[start + at] for at in range(number)], -1).astype(F32)

        grad_up = columns_from(0, hidden_chunks)
        grad_proj = columns_from(hidden_chunks, width_chunks)
    for bit in bits_of(m):
        grad_proj = grad_proj + swap_mlp(grad_proj.astype(BF16), bit).astype(F32)

    arrived = near_arrived
    if pairwise:
        arrived = far_arrived
        total = grad_own[0].astype(F32) + arrived[0].astype(F32)
        by_spot = total.astype(BF16).reshape(2, rows, 3 * WIDTH)
        slices = [pick(by_spot, (spot ^ e) % 2) for e in range(side)]
    else:
        arrived = swap(add(grad_own[1], arrived[1]), 2 * side).astype(F32) + arrived[0].astype(F32)
        total = grad_own[0].astype(F32) + arrived
        by_spot = total.astype(BF16).reshape(side, rows, 3 * WIDTH)
        slices = [pick(by_spot, spot ^ e) for e in range(side)]
    received = jnp.stack(in_plane(slices))
    grad_qkv = jnp.stack([pick(received, spot ^ group) for group in range(GROUPS)])
    grad_qkv = grad_qkv.reshape(GROUPS, rows, 3, WIDTH).transpose(1, 2, 0, 3).reshape(rows, 3 * width)
    if pairwise:
        grad_qkv = jnp.where(spot // 2 == slice_of, grad_qkv, swap_mlp(grad_qkv, 1)).astype(F32)
    else:
        grad_qkv = grad_qkv.astype(F32)
        for bit in bits_of(m):
            grad_qkv = grad_qkv + swap_mlp(grad_qkv.astype(BF16), bit).astype(F32)

    down_grads = after(down_grads[0], d_sent).astype(F32)
    grad_down = jnp.concatenate([down_grads[at] for at in range(hidden_chunks)], -1).T

    small = in_order(list(small), plane)[:MICRO]
    grad_bias_up = jnp.sum(small[:, 7 : 7 + bias_up_rows], 0).reshape(-1)[:hidden_count]
    d_shift_one, d_xhat_one, d_gate_one, d_shift_two, d_xhat_two, d_gate_two = [small[:, at] for at in range(6)]
    index_here = time_index[:, 0]
    vector_sums = jnp.stack(
        [
            jnp.sum((1.0 + vectors[SCALES_ALL : SCALES_ALL + MICRO]) * d_xhat_one, 0),
            jnp.sum((1.0 + small[:, -1]) * d_xhat_two, 0),
            jnp.sum(small[:, 6], 0),
            jnp.pad(index_here.astype(F32), (0, width - MICRO)),
        ]
    )
    d_scale_one, d_scale_two = vectors[GAIN_ONE] * d_xhat_one, vectors[GAIN_TWO] * d_xhat_two
    small = jnp.stack([d_shift_one, d_scale_one, d_gate_one, d_shift_two, d_scale_two, d_gate_two], 1)
    small = jnp.concatenate([small.reshape(6 * MICRO, width), vector_sums], 0)[None]
    for bit in bits_of(m):
        small = jnp.concatenate([small, swap_mlp(small, bit)], 0)
    at = 6 * MICRO
    d_modulation = small[:, :at].reshape(m * MICRO, n, ada_columns)
    vector_sums = jnp.sum(small[:, at : at + 3], 0)
    index_all = small[:, at + 3, :MICRO].reshape(-1).astype(jnp.int32)
    onehot = (index_all[:, None] == jnp.arange(grid_size)[None, :]).astype(BF16)
    cond = jnp.dot(onehot, time_table, preferred_element_type=F32)
    d_modulation_own = lax.dynamic_index_in_dim(d_modulation, me, 1, keepdims=False)
    grad_ada = jnp.dot(cond.T, d_modulation_own, precision=highest)
    grad_bias_ada = jnp.sum(d_modulation_own, 0)
    d_cond = jnp.einsum("bic,idc->bd", d_modulation, full_ada.astype(F32), precision=highest)
    table_rows = grid_size // n
    onehot_own = index_all[None, :] == (me * table_rows + jnp.arange(table_rows))[:, None]
    grad_table = jnp.dot(onehot_own.astype(F32), d_cond, precision=highest)
    vector_sums = lax.dynamic_slice_in_dim(vector_sums, me * rows, rows, 1)
    return (
        result,
        returned.astype(F32),
        grad_table,
        grad_ada,
        grad_bias_ada,
        vector_sums[0],
        vector_sums[1],
        grad_qkv,
        grad_proj,
        grad_up,
        grad_bias_up,
        grad_down,
        vector_sums[2],
    )


def solution(mesh):
    in_specs = (
        P(None, "mlp", "seq", None),
        P(None, "mlp", "seq", None),
        P(None, "mlp", "seq"),
        P(None, "mlp"),
        P(None, "mlp"),
        P(),
        P(),
        P(None, "seq"),
        P("seq"),
        P("seq"),
        P("seq"),
        P("seq", None),
        P("seq", None),
        P("seq", "mlp"),
        P("mlp"),
        P("mlp", "seq"),
        P("seq"),
    )
    out_specs = (
        P(None, "mlp", "seq", None),
        P(None, "mlp", "seq", None),
        P("seq", None),
        P(None, "seq"),
        P("seq"),
        P("seq"),
        P("seq"),
        P("seq", None),
        P("seq", None),
        P("seq", "mlp"),
        P("mlp"),
        P("mlp", "seq"),
        P("seq"),
    )
    run = functools.partial(body, n=mesh.shape["seq"], m=mesh.shape["mlp"])
    return jax.shard_map(run, mesh=mesh, in_specs=in_specs, out_specs=out_specs, check_vma=False)
```

```python
import functools
import math

import jax
import jax.numpy as jnp
from jax import lax
from jax.experimental import pallas as pl
from jax.experimental.pallas import tpu as pltpu
from jax.sharding import PartitionSpec as P

HEADS = 12
HEAD = 64
MICRO = 3
PLANES = 4
GROUPS = 4
PER_GROUP = HEADS // GROUPS
WIDTH = PER_GROUP * HEAD
QUERY_BLOCK = 256
SCALING = HEAD ** (-0.5)
BF16 = jnp.bfloat16
F32 = jnp.float32
highest = lax.Precision.HIGHEST
SLOPE = math.sqrt(2.0 / math.pi)
CUBIC = 0.044715

SHIFT_ONE, SCALE_ONE, GATE_ONE, SHIFT_TWO, SCALE_TWO, GATE_TWO, GAIN_ONE, GAIN_TWO, BIAS_DOWN = range(9)
SCALES_ALL, GAINS_ONE, GAINS_TWO = 9, 12, 13

VMEM = pl.BlockSpec(memory_space=pltpu.VMEM)
SMEM = pl.BlockSpec(memory_space=pltpu.SMEM)


def nn(left, right):
    return lax.dot_general(left, right, (((1,), (0,)), ((), ())), preferred_element_type=F32)


def nt(left, right):
    return lax.dot_general(left, right, (((1,), (1,)), ((), ())), preferred_element_type=F32)


def standardize(inputs):
    average = jnp.mean(inputs, -1, keepdims=True)
    centred = inputs - average
    spread = jnp.mean(centred * centred, -1, keepdims=True)
    root = lax.rsqrt(spread + 1e-06)
    return centred * root, root


def pull_norm(d_normed, gains, xhat, root):
    e = d_normed * gains
    return root * (e - jnp.mean(e, -1, keepdims=True) - xhat * jnp.mean(e * xhat, -1, keepdims=True))


def over_tokens(value):
    return jnp.sum(value, 0, keepdims=True)


def shape_of(dims, dtype):
    return jax.ShapeDtypeStruct(dims, dtype)


def call(kernel, name, operands, scalars, outs, scratch=(), us=1.0, far=()):
    moved = sum(math.prod(o.shape) * o.dtype.itemsize for o in list(operands) + list(outs))
    return pl.pallas_call(
        kernel,
        out_shape=list(outs),
        in_specs=[SMEM] * len(scalars) + [pl.BlockSpec(memory_space=pl.ANY)] * len(far) + [VMEM] * len(operands),
        out_specs=[VMEM] * len(outs),
        scratch_shapes=list(scratch),
        compiler_params=pltpu.CompilerParams(vmem_limit_bytes=56 * 1024 * 1024),
        cost_estimate=pl.CostEstimate(flops=int(us * 1e9), bytes_accessed=moved, transcendentals=0),
        name=name,
    )(*scalars, *far, *operands)


def fetch(gathered, chunks, weights, arrived):
    copies = [
        pltpu.make_async_copy(gathered.at[:, chunk], weights.at[at], arrived.at[at])
        for at, chunk in enumerate(chunks)
    ]
    for copy in copies:
        copy.start()
    return copies


def whole(weights, at):
    return weights[at].reshape(weights.shape[1] * weights.shape[2], weights.shape[3])


def group_rows(weights, group, me=None):
    blocks = WIDTH // weights.shape[2]
    if me is not None:
        return jnp.concatenate([weights[0, me ^ (group * blocks + at)] for at in range(blocks)], 0)
    parts = [
        weights[at, pl.ds(group * blocks, blocks)].reshape(WIDTH, weights.shape[3])
        for at in range(weights.shape[0])
    ]
    return parts[0] if len(parts) == 1 else jnp.concatenate(parts, -1)


def modulation(times, table, ada, b_ada, gain_one, gain_two, b_down, mask, small):
    columns = ada.shape[0]
    rows = gain_one.shape[1]
    at = lax.broadcasted_iota(jnp.int32, (8, table.shape[0]), 1)
    line = lax.broadcasted_iota(jnp.int32, (8, table.shape[0]), 0)
    wanted = jnp.where(line == 0, times[0], jnp.where(line == 1, times[1], times[2]))
    cond = nn((at == wanted).astype(F32).astype(BF16), table[...]).astype(BF16)
    part = nt(cond, ada[...]) + b_ada[...].astype(F32)
    small[...] = jnp.zeros_like(small)
    at = 0
    for s in range(MICRO):
        small[0:1, at : at + columns] = part[s : s + 1]
        at += columns
    for ref in (gain_one, gain_two, b_down):
        small[0:1, at : at + rows] = ref[...].astype(F32)
        at += rows
    for s in range(MICRO):
        small[0:1, at : at + mask.shape[1]] = mask[s : s + 1, :].astype(F32)
        at += mask.shape[1]


def prepare_kernel(
    place, times, tokens, upstream, w_qkv, w_up, down, w_proj, table, ada, b_ada, gain_one, gain_two, b_down, mask, *outs
):
    packed, small, outs = outs[0], outs[1], outs[2:]
    columns_out, token_out, upstream_out = outs[: -2 * PLANES], outs[-2 * PLANES : -PLANES], outs[-PLANES:]
    plane, spot = place[0], place[1]
    for d in range(PLANES):
        token_out[d][...] = tokens[jnp.minimum(plane ^ d, MICRO - 1)]
        upstream_out[d][...] = upstream[jnp.minimum(plane ^ d, MICRO - 1)]
    width = w_proj.shape[1]
    by_group = [
        jnp.concatenate([w_qkv[:, p * width + g * WIDTH : p * width + (g + 1) * WIDTH] for p in range(3)], -1)
        for g in range(GROUPS)
    ]
    for e, out in enumerate(columns_out):
        group = (spot ^ e) % GROUPS
        here = by_group[0]
        for g in range(1, GROUPS):
            here = jnp.where(group == g, by_group[g], here)
        out[...] = here
    unit = packed.shape[2]
    chunk = 0
    for value in (w_up[...], down[...], w_proj[...]):
        for at in range(0, value.shape[1], unit):
            packed[chunk] = value[:, at : at + unit]
            chunk += 1
    modulation(times, table, ada, b_ada, gain_one, gain_two, b_down, mask, small)


def vectors_kernel(place, weight_index, weight_grid, small, vectors, scale, line):
    n = small.shape[0]
    width = vectors.shape[1]
    columns, rows, shard = 6 * width // n, width // n, scale.shape[0] // PLANES
    plane, spot = place[0], place[1]
    side = n // PLANES
    me = plane * side + spot
    last = jnp.minimum(plane, MICRO - 1)

    def one_of(three):
        return jnp.where(last == 0, three[0], jnp.where(last == 1, three[1], three[2]))

    def pieces(first, size):
        start = first
        while start < first + size:
            stop = min(first + size, (start // width + 1) * width)
            yield start // width, start % width, start - first, stop - start
            start = stop

    vectors[...] = jnp.zeros_like(vectors)
    for i in range(n):
        here = small[pl.ds(me ^ i, 1), :]
        each = [here[:, s * columns : (s + 1) * columns] for s in range(MICRO)]
        mine = one_of(each)
        for part, column, offset, size in pieces(i * columns, columns):
            vectors[part : part + 1, column : column + size] = mine[:, offset : offset + size]
            if part == SCALE_ONE:
                for s in range(MICRO):
                    vectors[SCALES_ALL + s : SCALES_ALL + s + 1, column : column + size] = each[s][
                        :, offset : offset + size
                    ]
        for row in (GAIN_ONE, GAIN_TWO, BIAS_DOWN):
            start = MICRO * columns + (row - GAIN_ONE) * rows
            vectors[row : row + 1, i * rows : (i + 1) * rows] = here[:, start : start + rows]
    for to, gain, by in ((GAINS_ONE, GAIN_ONE, SCALE_ONE), (GAINS_TWO, GAIN_TWO, SCALE_TWO)):
        vectors[to : to + 1, :] = vectors[gain : gain + 1, :] * (1.0 + vectors[by : by + 1, :])
    line[...] = jnp.zeros_like(line)
    for d in range(PLANES):
        here = small[d * side : d * side + 1, :]
        start = MICRO * (columns + rows)
        three = [here[:, start + s * shard : start + (s + 1) * shard] for s in range(MICRO)]
        line[0:1, d * shard : (d + 1) * shard] = one_of(three)
    weight = jnp.where(plane < MICRO, weight_grid[weight_index[last]], 0.0)
    scale[...] = line[...].T[:, 0:1] * weight


def project_kernel(place, gathered, tokens, vectors, *refs, chunks, slots):
    side = len(refs) - 5
    mixed, (attended, middle, normed, weights, arrived) = refs[:side], refs[side:]
    spot = place[1]
    copies = fetch(gathered, chunks, weights, arrived)
    for copy in copies:
        copy.wait()
    total = jnp.zeros(attended.shape, F32)
    for e in range(side):
        other = spot ^ e
        block = mixed[e][...]
        if side > GROUPS:
            block = jnp.where(other < GROUPS, block, jnp.zeros_like(block))
        total = total + nn(block, group_rows(weights, other % GROUPS, place[2] if slots else None))
    attended[...] = total
    after = tokens[...].astype(F32) + vectors[GATE_ONE : GATE_ONE + 1] * total
    middle[...] = after
    xhat, _ = standardize(after)
    normed[...] = (xhat * vectors[GAINS_TWO : GAINS_TWO + 1] + vectors[SHIFT_TWO : SHIFT_TWO + 1]).astype(BF16)


def feed_kernel(gathered, rows, d_rows, bias, output, d_normed, active, d_hidden, weights, arrived):
    parts = weights.shape[0] // 2
    unit = weights.shape[3]
    order = [at for part in range(parts) for at in (part, parts + part)]
    copies = fetch(gathered, order, weights, arrived)
    out = jnp.zeros(output.shape, F32)
    back = jnp.zeros(output.shape, F32)
    for part in range(parts):
        columns = slice(part * unit, (part + 1) * unit)
        copies[2 * part].wait()
        up = whole(weights, 2 * part)
        u = nn(rows[...], up) + bias[:, columns]
        square = u * u
        bent = jnp.tanh(SLOPE * u * (1.0 + CUBIC * square))
        half = 0.5 * (1.0 + bent)
        on = (u * half).astype(BF16)
        active[:, columns] = on
        slope = half + 0.5 * u * (1.0 - bent * bent) * (SLOPE * (1.0 + 3.0 * CUBIC * square))
        copies[2 * part + 1].wait()
        down = whole(weights, 2 * part + 1)
        d_on = (nn(d_rows[...], down) * slope).astype(BF16)
        d_hidden[:, columns] = d_on
        out = out + nt(on, down)
        back = back + nt(d_on, up)
    output[...] = out.astype(output.dtype)
    d_normed[...] = back.astype(d_normed.dtype)


def scatter_store(refs, me, device, value):
    kept, sent, chunk, slot_of = refs
    distance = me ^ device
    slot = slot_of(distance)

    @pl.when(distance % 2 == 0)
    def _():
        kept[slot, chunk] = value

    @pl.when(distance % 2 == 1)
    def _():
        sent[slot, chunk] = value


def slot_y_first(distance):
    return ((distance >> 1) & 1) * 4 + ((distance >> 2) & 1) * 2 + ((distance >> 3) & 1)


def down_grads_kernel(place, *refs, blocks, scatter):
    d_rows, active, outs = refs[:blocks], refs[blocks : 2 * blocks], refs[2 * blocks :]
    me = place[2]
    width, count = d_rows[0].shape[1], active[0].shape[1]
    unit = min(width, count)
    turned = [ref[...].T for ref in d_rows]
    for chunk in range(count // unit):
        columns = slice(chunk * unit, (chunk + 1) * unit)
        grad = sum(nn(turned[b], active[b][:, columns]) for b in range(blocks)).astype(BF16)
        if scatter:
            rows = outs[0].shape[2]
            for i in range(width // rows):
                part = grad[i * rows : (i + 1) * rows]
                scatter_store((outs[0], outs[1], chunk, slot_y_first), me, i, part)
        else:
            outs[0][:, columns] = grad


def up_grads_kernel(place, *refs, blocks, scatter):
    rows_all, d_hidden, outs = refs[:blocks], refs[blocks : 2 * blocks], refs[2 * blocks :]
    bias = outs[-1]
    me = place[2]
    width, count = rows_all[0].shape[1], bias.shape[1]
    unit = min(width, count)
    turned = [ref[...].T for ref in rows_all]
    for chunk in range(count // unit):
        columns = slice(chunk * unit, (chunk + 1) * unit)
        grad = sum(nn(turned[b], d_hidden[b][:, columns]) for b in range(blocks)).astype(BF16)
        bias[:, columns] = sum(over_tokens(d_hidden[b][:, columns].astype(F32)) for b in range(blocks))
        if scatter:
            rows = outs[0].shape[2]
            for i in range(width // rows):
                part = grad[i * rows : (i + 1) * rows]
                scatter_store((outs[0], outs[1], chunk, slot_y_first), me, i, part)
        else:
            outs[0][:, columns] = grad


def proj_grads_kernel(place, d_attended, *refs, side, scatter):
    mixed, refs = refs[:side], refs[side:]
    spot, me = place[1], place[2]
    width = d_attended.shape[1]
    whole_grad = refs[-1]
    if side > GROUPS:
        whole_grad[...] = jnp.zeros_like(whole_grad)
    for e in range(side):
        other = spot ^ e
        first = pl.multiple_of((other % GROUPS) * WIDTH, WIDTH)
        grad = nn(mixed[e][...].T, d_attended[...]).astype(BF16)
        if side > GROUPS:
            grad = whole_grad[pl.ds(first, WIDTH), :] + jnp.where(other < GROUPS, grad, jnp.zeros_like(grad))
        whole_grad[pl.ds(first, WIDTH), :] = grad
    if not scatter:
        refs[0][...] = whole_grad[...]
        return
    _, _, own, sent, ready, done, _ = refs
    rows, chunk = own.shape[2], own.shape[1] - 1
    for i in range(width // rows):
        part = whole_grad[i * rows : (i + 1) * rows, :]
        scatter_store((ready.at[0], ready.at[1], 0, slot_y_first), me, i, part)
    copies = [
        pltpu.make_async_copy(ready.at[at, :, 0], out.at[:, chunk], done.at[at])
        for at, out in enumerate((own, sent))
    ]
    for copy in copies:
        copy.start()
    for copy in copies:
        copy.wait()


def qkv_grads_kernel(place, d_project, normed, *outs):
    grad = nn(d_project[...], normed[...]).astype(BF16).T
    plane, slice_of = place[0], place[3]
    rows = outs[0].shape[1]
    if len(outs[0].shape) == 3 and outs[0].shape[0] == PLANES:
        for at in range(PLANES):
            distance = plane ^ at
            slot = (distance % 2) * 2 + distance // 2
            halves = [grad[(2 * at + half) * rows : (2 * at + half + 1) * rows] for half in range(2)]
            outs[0][slot] = jnp.where(slice_of == 0, halves[0], halves[1])
            outs[1][slot] = jnp.where(slice_of == 0, halves[1], halves[0])
    else:
        for at in range(PLANES):
            part = grad[at * rows : (at + 1) * rows]
            distance = plane ^ at

            @pl.when(distance % 2 == 0)
            def _():
                outs[0][distance // 2] = part

            @pl.when(distance % 2 == 1)
            def _():
                outs[1][distance // 2] = part


def normed_backward_kernel(d_project, weight, *refs, blocks):
    tokens, (kept, sent, sums) = refs[:blocks], refs[blocks:]
    count = tokens[0].shape[0]
    d_shift = jnp.zeros((1, weight.shape[0]), F32)
    d_xhat = jnp.zeros((1, weight.shape[0]), F32)
    for block in range(blocks):
        part = nt(d_project[:, block * count : (block + 1) * count].T, weight[...])
        (sent if block % 2 else kept)[block // 2] = part.astype(BF16)
        xhat, _ = standardize(tokens[block][...].astype(F32))
        d_shift = d_shift + over_tokens(part)
        d_xhat = d_xhat + over_tokens(part * xhat)
    sums[0:1, :] = d_shift
    sums[1:2, :] = d_xhat
    sums[2:8, :] = jnp.zeros((6, weight.shape[0]), F32)


def middle_kernel(place, gathered, vectors, upstream, scale, attended, middle, d_own, *refs, others, chunks, slots):
    arrived, refs = refs[:others], refs[others:]
    d_mixed, (d_middle, d_attended, sums, weights, copied) = refs[:-5], refs[-5:]
    spot = place[1]
    copies = fetch(gathered, chunks, weights, copied)
    width = middle.shape[1]
    d_normed = d_own[...]
    for ref in arrived:
        d_normed = d_normed + ref[...].astype(F32)
    xhat, root = standardize(middle[...])
    d_result = upstream[...].astype(F32) * scale[...]
    d_after = d_result + pull_norm(d_normed, vectors[GAINS_TWO : GAINS_TWO + 1], xhat, root)
    d_middle[...] = d_after
    low = (vectors[GATE_ONE : GATE_ONE + 1] * d_after).astype(BF16)
    d_attended[...] = low
    for copy in copies:
        copy.wait()
    for e in range(len(d_mixed)):
        rows_here = group_rows(weights, (spot ^ e) % GROUPS, place[2] if slots else None)
        d_mixed[e][...] = nt(low, rows_here).astype(BF16)
    sums[0:1, :] = over_tokens(d_after * attended[...])
    sums[1:2, :] = over_tokens(d_normed)
    sums[2:3, :] = over_tokens(d_normed * xhat)
    sums[3:8, :] = jnp.zeros((5, width), F32)


def output_kernel(vectors, upstream, scale, middle, own, *refs, others):
    arrived, (result, sums) = refs[:others], refs[others:]
    output = own[...] + vectors[BIAS_DOWN : BIAS_DOWN + 1]
    for ref in arrived:
        output = output + ref[...].astype(F32)
    gate = vectors[GATE_TWO : GATE_TWO + 1]
    result[...] = (middle[...] + gate * output).astype(BF16)
    d_result = upstream[...].astype(F32) * scale[...]
    sums[0:1, :] = over_tokens(d_result * output)
    sums[1:2, :] = over_tokens(gate * d_result)
    sums[2:8, :] = jnp.zeros((6, middle.shape[1]), F32)


def tokens_kernel(vectors, tokens, d_middle, own, arrived, d_tokens):
    xhat, root = standardize(tokens[...].astype(F32))
    d_normed = own[...].astype(F32) + arrived[...].astype(F32)
    back = pull_norm(d_normed, vectors[GAINS_ONE : GAINS_ONE + 1], xhat, root)
    d_tokens[...] = (d_middle[...] + back).astype(BF16)


def forward_kernel(place, *refs, blocks, halves):
    tokens, refs = refs[:blocks], refs[blocks:]
    count = 2 if halves else PLANES
    weights, refs = refs[:count], refs[count:]
    (vectors, cosine, sines), refs = refs[:3], refs[3:]
    gain, shift = vectors[GAINS_ONE : GAINS_ONE + 1], vectors[SHIFT_ONE : SHIFT_ONE + 1]
    mixed, refs = refs[:blocks], refs[blocks:]
    heads, log_total, normed, weight, keys, mixed_turned = refs
    plane = place[0]
    rows = weights[0].shape[-2]
    count = tokens[0].shape[0]
    if halves:
        for half in range(2):
            for distance in range(PLANES):
                first = pl.multiple_of((plane ^ distance) * 2 * rows + (place[3] ^ half) * rows, 16)
                weight[pl.ds(first, rows), :] = weights[half][distance]
    else:
        for distance in range(PLANES):
            first = pl.multiple_of((plane ^ distance) * rows, 8)
            weight[pl.ds(first, rows), :] = weights[distance][...]
    for block in range(blocks):
        xhat, _ = standardize(tokens[block][...].astype(F32))
        normed[block * count : (block + 1) * count, :] = (xhat * gain + shift).astype(BF16)
    project = nt(weight[...].T, normed[...])
    cos, sin = cosine[...], sines[...]
    half = HEAD // 2
    for part in range(2):
        for head in range(PER_GROUP):
            start = part * WIDTH + head * HEAD
            first, second = project[start : start + half], project[start + half : start + HEAD]
            turned = jnp.concatenate([first * cos - second * sin, second * cos + first * sin], 0).astype(BF16)
            if part == 0:
                turned = turned * jnp.asarray(SCALING, BF16)
            else:
                keys[head] = turned.T
            heads[start : start + HEAD, :] = turned
    heads[2 * WIDTH :, :] = project[2 * WIDTH :].astype(BF16)
    length = heads.shape[1]
    for head in range(PER_GROUP):
        start = head * HEAD

        def queries_step(step, carry):
            columns = pl.ds(pl.multiple_of(step * QUERY_BLOCK, QUERY_BLOCK), QUERY_BLOCK)
            scores = nn(keys[head], heads[start : start + HEAD, columns])
            peak = jnp.max(scores, 0, keepdims=True)
            exps = jnp.exp(scores - peak)
            total = jnp.sum(exps, 0, keepdims=True)
            log_total[head : head + 1, columns] = peak + jnp.log(total)
            probs = (exps * (1.0 / total)).astype(BF16)
            values = heads[2 * WIDTH + start : 2 * WIDTH + start + HEAD, :]
            mixed_turned[start : start + HEAD, columns] = nn(values, probs).astype(BF16)
            return carry

        lax.fori_loop(0, length // QUERY_BLOCK, queries_step, 0, unroll=True)
    for block in range(blocks):
        mixed[block][...] = mixed_turned[:, block * count : (block + 1) * count].T


def backward_kernel(*refs, blocks):
    d_mixed, refs = refs[:blocks], refs[blocks:]
    (heads, log_total, cosine, sines), refs = refs[:4], refs[4:]
    d_project, d_turned, d_keys, d_values, keys, values = refs
    count = d_mixed[0].shape[0]
    length = heads.shape[1]
    for block in range(blocks):
        d_turned[:, block * count : (block + 1) * count] = d_mixed[block][...].T
    cos, sin = cosine[...], sines[...]
    half = HEAD // 2
    d_keys[...] = jnp.zeros_like(d_keys)
    d_values[...] = jnp.zeros_like(d_values)
    for head in range(PER_GROUP):
        start = head * HEAD
        keys_turned = heads.at[WIDTH + start : WIDTH + start + HEAD]
        keys[...] = keys_turned[...].T
        values[...] = heads[2 * WIDTH + start : 2 * WIDTH + start + HEAD, :].T

        def queries_step(step, carry):
            columns = pl.ds(pl.multiple_of(step * QUERY_BLOCK, QUERY_BLOCK), QUERY_BLOCK)
            queries = heads[start : start + HEAD, columns]
            incoming = d_turned[start : start + HEAD, columns]
            scores = nn(keys[...], queries)
            probs = jnp.exp(scores - log_total[head : head + 1, columns])
            d_probs = nn(values[...], incoming)
            delta = jnp.sum(probs * d_probs, 0, keepdims=True)
            d_scores = (probs * (d_probs - delta)).astype(BF16)
            d_values[start : start + HEAD, :] += nt(incoming, probs.astype(BF16))
            d_keys[start : start + HEAD, :] += nt(queries, d_scores)
            d_queries = nn(keys_turned[...], d_scores) * SCALING
            first, second = d_queries[:half], d_queries[half:]
            cos_here, sin_here = cosine[:, columns], sines[:, columns]
            d_project[start : start + half, columns] = (first * cos_here + second * sin_here).astype(BF16)
            d_project[start + half : start + HEAD, columns] = (second * cos_here - first * sin_here).astype(BF16)
            return carry

        lax.fori_loop(0, length // QUERY_BLOCK, queries_step, 0, unroll=True)
        first, second = d_keys[start : start + half, :], d_keys[start + half : start + HEAD, :]
        d_project[WIDTH + start : WIDTH + start + half, :] = (first * cos + second * sin).astype(BF16)
        d_project[WIDTH + start + half : WIDTH + start + HEAD, :] = (second * cos - first * sin).astype(BF16)
    d_project[2 * WIDTH :, :] = d_values[...].astype(BF16)


def attend_forward(place, tokens, weights, vectors, cosine, sines, halves):
    blocks, (count, width) = len(tokens), tokens[0].shape
    length = blocks * count
    columns = weights[0].shape[-1]
    outs = call(
        functools.partial(forward_kernel, blocks=blocks, halves=halves),
        "attend_forward",
        [*tokens, *weights, vectors, cosine, sines],
        [place],
        [shape_of((count, WIDTH), BF16)] * blocks
        + [
            shape_of((columns, length), BF16),
            shape_of((8, length), F32),
            shape_of((length, width), BF16),
            shape_of((width, columns), BF16),
        ],
        [pltpu.VMEM((PER_GROUP, length, HEAD), BF16), pltpu.VMEM((WIDTH, length), BF16)],
        us=15.0,
    )
    return outs[:blocks], outs[blocks:]


def attend_backward(d_mixed, heads, log_total, cosine, sines):
    blocks, length = len(d_mixed), heads.shape[1]
    (d_project,) = call(
        functools.partial(backward_kernel, blocks=blocks),
        "attend_backward",
        [*d_mixed, heads, log_total, cosine, sines],
        [],
        [shape_of((3 * WIDTH, length), BF16)],
        [
            pltpu.VMEM((WIDTH, length), BF16),
            pltpu.VMEM((WIDTH, length), F32),
            pltpu.VMEM((WIDTH, length), F32),
            pltpu.VMEM((length, HEAD), BF16),
            pltpu.VMEM((length, HEAD), BF16),
        ],
        us=18.0,
    )
    return d_project


def after(values, *others):
    return lax.optimization_barrier((values, others))[0]


def add(left, right):
    return (left.astype(F32) + right.astype(F32)).astype(BF16)


def pick(stack, index):
    return lax.dynamic_index_in_dim(stack, index, 0, keepdims=False)


def bits_of(count):
    return [1 << bit for bit in range(count.bit_length() - 1)]


def body(
    tokens,
    upstream,
    token_mask,
    time_index,
    weight_index,
    time_table,
    weight_grid,
    w_ada,
    b_ada,
    gain_one,
    gain_two,
    w_qkv,
    w_proj,
    w_up,
    b_up,
    w_down,
    b_down,
    *,
    n,
    m,
):
    side = n // PLANES
    me = lax.axis_index("seq")
    plane, spot = me // side, me % side
    slice_of = lax.axis_index("mlp")
    place = jnp.stack([plane, spot, me, slice_of]).astype(jnp.int32)
    shard, width = tokens.shape[2], tokens.shape[3]
    rows = w_qkv.shape[0]
    hidden_count = w_up.shape[1]
    grid_size = time_table.shape[0]
    ada_columns = w_ada.shape[1]
    count = PLANES * shard
    unit = min(width, hidden_count)
    hidden_chunks, width_chunks = hidden_count // unit, width // unit
    pairwise = rows % 16 == 0 and side == GROUPS and unit == width and m == 2
    z_bits, y_bit, core_bit = (2 * side, side), 2, 1

    def swap(value, distance):
        return lax.ppermute(value, "seq", [(i, i ^ distance) for i in range(n)])

    def swap_mlp(value, distance):
        return lax.ppermute(value, "mlp", [(i, i ^ distance) for i in range(m)])

    def between_planes(pieces):
        return [pieces[0]] + [swap(pieces[d], d * side) for d in range(1, PLANES)]

    def in_plane(pieces):
        return [pieces[0]] + [swap(pieces[e], e) for e in range(1, side)]

    def in_order(blocks, axis):
        halves = jnp.stack(blocks)
        for bit in bits_of(len(blocks)):
            here = halves.reshape((len(blocks) // (2 * bit), 2, bit) + halves.shape[1:])
            halves = jnp.where((axis & bit) != 0, here[:, ::-1], here).reshape(halves.shape)
        return halves

    def for_plane(values):
        return [pick(values, jnp.minimum(plane ^ d, MICRO - 1)) for d in range(PLANES)]

    def columns_of(value):
        return [value[:, at : at + unit] for at in range(0, value.shape[1], unit)]

    line = [value[None] for value in (b_ada, gain_one, gain_two, b_down)]
    small_count = -(-MICRO * (ada_columns + rows + shard) // 128) * 128
    first_shapes = [shape_of((2 * hidden_chunks + width_chunks, rows, unit), BF16), shape_of((1, small_count), F32)]
    first_shapes += [shape_of((rows, 3 * WIDTH), BF16)] * side + [shape_of((shard, width), BF16)] * (2 * PLANES)
    packed, small, *pieces = call(
        prepare_kernel,
        "prepare",
        [tokens[:, 0], upstream[:, 0], w_qkv, w_up, w_down.T, w_proj, time_table, w_ada.T, *line, token_mask[:, 0]],
        [place, time_index[:, 0]],
        first_shapes,
        us=4.0,
    )
    group_columns, token_pieces, upstream_pieces = pieces[:side], pieces[side : side + PLANES], pieces[side + PLANES :]

    token_arrived = between_planes(token_pieces)

    received = jnp.stack(after(in_plane(group_columns), token_arrived[1]))
    weight_block = jnp.concatenate([pick(received, spot ^ at) for at in range(side)], 0)
    if pairwise:
        weight_block = pick(weight_block.reshape(2, width // 8, 3 * WIDTH), slice_of)
    weight_blocks = {0: weight_block}
    for bit in (2, 1):
        for known in list(weight_blocks):
            weight_blocks[known | bit] = swap(weight_blocks[known], bit * side)
    weight_blocks = [weight_blocks[at] for at in range(PLANES)]
    far_block = weight_blocks[2]
    own_upstream = between_planes(after(upstream_pieces, weight_blocks[1], weight_blocks[3]))
    if pairwise:
        weight_blocks = jnp.stack(weight_blocks)
        weight_blocks = [weight_blocks, swap_mlp(weight_blocks, 1)]

    for bit in bits_of(n)[:-1]:
        small = jnp.concatenate([small, swap(small, bit)], 0)
    arrived, small = lax.optimization_barrier((token_arrived, after(small, far_block)))
    own_low = jnp.concatenate(arrived, 0)
    token_blocks = {0: own_low}
    for bit in reversed(bits_of(side)):
        for known in list(token_blocks):
            mine = token_blocks[known]
            if bit < side // 2:
                mine = after(mine, token_blocks[side // 2])
            token_blocks[known | bit] = swap(mine, bit)
    token_blocks = [token_blocks[at] for at in range(side)]

    gathered = lax.all_gather(after(packed, token_arrived, far_block), "seq", axis=0)
    if not pairwise:
        gathered = gathered.transpose(1, 0, 2, 3).reshape(-1, GROUPS, WIDTH, unit).transpose(1, 0, 2, 3)
    blocks_shape = (gathered.shape[0],) + gathered.shape[2:]
    proj_chunks = list(range(2 * hidden_chunks, 2 * hidden_chunks + width_chunks))

    def weight_scratch(number):
        return [pltpu.VMEM((number,) + blocks_shape, BF16), pltpu.SemaphoreType.DMA((number,))]

    for bit in bits_of(n)[-1:]:
        small = jnp.concatenate([small, swap(small, bit)], 0)
    vectors, scale = call(
        vectors_kernel,
        "vectors",
        [small],
        [place, weight_index[:, 0], weight_grid],
        [shape_of((16, width), F32), shape_of((count, 1), F32)],
        [pltpu.VMEM((8, count), F32)],
    )

    order = ((plane ^ jnp.arange(PLANES))[None, :] * side + (spot ^ jnp.arange(side))[:, None]) * shard
    positions = (order[:, :, None] + jnp.arange(shard)).reshape(1, -1).astype(F32)
    frequency = 10000.0 ** (-jnp.arange(0, HEAD, 2).astype(F32) / HEAD)
    angles = frequency[:, None] * positions
    cosine, sines = jnp.cos(angles), jnp.sin(angles)

    mixed_blocks, kept = attend_forward(
        after(place, own_upstream), token_blocks, weight_blocks, vectors, cosine, sines, pairwise
    )

    full_ada = lax.all_gather(after(w_ada, gathered), "seq", axis=0)

    mixed_blocks = in_plane(mixed_blocks)

    own_upstream = jnp.concatenate(own_upstream, 0)
    d_rows = ((own_upstream.astype(F32) * scale) * vectors[GATE_TWO][None]).astype(BF16)
    d_rows = [d_rows] + [swap_mlp(d_rows, d) for d in range(1, m)]

    attended, middle, normed_two = call(
        functools.partial(project_kernel, chunks=proj_chunks, slots=False),
        "project",
        [own_low, vectors, *mixed_blocks],
        [place],
        [shape_of((count, width), F32), shape_of((count, width), F32), shape_of((count, width), BF16)],
        weight_scratch(width_chunks),
        us=3.0,
        far=[gathered],
    )
    rows_all = [normed_two] + [swap_mlp(normed_two, d) for d in range(1, m)]
    bias_up = b_up.astype(F32)[None]
    fed = [
        call(
            feed_kernel,
            "feed_forward",
            [rows_all[d], d_rows[d], bias_up],
            [],
            [shape_of((count, width), BF16 if d else F32)] * 2 + [shape_of((count, hidden_count), BF16)] * 2,
            weight_scratch(2 * hidden_chunks),
            us=6.0,
            far=[gathered],
        )
        for d in range(m)
    ]
    d_arrived = [swap_mlp(fed[d][1], d) for d in range(1, m)]
    out_arrived = [swap_mlp(fed[d][0], d) for d in range(1, m)]
    slots = n // 2
    if pairwise:
        down_shapes = [shape_of((slots, hidden_chunks, rows, unit), BF16)] * 2
    else:
        down_shapes = [shape_of((width, hidden_count), BF16)]
    if pairwise:
        up_shapes = [shape_of((slots, hidden_chunks + width_chunks, rows, unit), BF16)] * 2
    else:
        up_shapes = [shape_of((width, hidden_count), BF16)]
    down_grads = call(
        functools.partial(down_grads_kernel, blocks=m, scatter=pairwise),
        "down_gradients",
        [*d_rows, *[f[2] for f in fed]],
        [place],
        down_shapes,
        us=6.0,
    )
    *up_grads, bias_up_sum = call(
        functools.partial(up_grads_kernel, blocks=m, scatter=pairwise),
        "up_gradients",
        [*rows_all, *[f[3] for f in fed]],
        [place],
        up_shapes + [shape_of((1, hidden_count), F32)],
        us=5.0,
    )
    d_arrived, down_grads, full_ada, *up_grads = lax.optimization_barrier(
        (d_arrived, down_grads, full_ada, *up_grads)
    )
    middle_outs = call(
        functools.partial(middle_kernel, others=m - 1, chunks=proj_chunks, slots=False),
        "middle_backward",
        [vectors, own_upstream, scale, attended, middle, fed[0][1], *d_arrived],
        [place],
        [shape_of((count, WIDTH), BF16)] * side
        + [shape_of((count, width), F32), shape_of((count, width), BF16), shape_of((8, width), F32)],
        weight_scratch(width_chunks),
        us=4.0,
        far=[gathered],
    )
    d_mixed_blocks, (d_middle, d_attended, middle_sums) = middle_outs[:side], middle_outs[side:]

    d_mixed_blocks = in_plane(d_mixed_blocks)
    if side > GROUPS:
        share = (spot < GROUPS).astype(BF16)
        d_mixed_blocks = [block * share for block in d_mixed_blocks]

    anywhere = pl.BlockSpec(memory_space=pl.ANY)
    proj_grads = pl.pallas_call(
        functools.partial(proj_grads_kernel, side=side, scatter=pairwise),
        out_shape=up_shapes if pairwise else [shape_of((width, width), BF16)],
        in_specs=[SMEM] + [VMEM] * (1 + side) + ([anywhere] * 2 if pairwise else []),
        out_specs=[anywhere] * 2 if pairwise else [VMEM],
        scratch_shapes=(
            [pltpu.VMEM((2, slots, 1, rows, unit), BF16), pltpu.SemaphoreType.DMA((2,))] if pairwise else []
        )
        + [pltpu.VMEM((width, width), BF16)],
        input_output_aliases={2 + side: 0, 3 + side: 1} if pairwise else {},
        compiler_params=pltpu.CompilerParams(vmem_limit_bytes=56 * 1024 * 1024),
        cost_estimate=pl.CostEstimate(flops=2 * 10**9, bytes_accessed=4 * 10**6, transcendentals=0),
        name="proj_gradients",
    )(place, d_attended, *mixed_blocks, *(up_grads if pairwise else []))

    def add_halves(own, arrived):
        half = own.shape[0] // 2
        return add(own[:half], arrived[:half]), add(own[half:], arrived[half:])

    def back_to_tokens(value):
        received = between_planes([value[d * shard : (d + 1) * shard] for d in range(PLANES)])
        received = jnp.stack(received)
        return jnp.stack([pick(received, plane ^ at) for at in range(MICRO)])[:, None]

    if pairwise:
        down_arrived = swap(down_grads[1], core_bit)
        proj_sent, out_arrived, down_arrived = lax.optimization_barrier((proj_grads[1], out_arrived, down_arrived))
        up_arrived = swap(proj_sent, core_bit)
        down_own, down_sent = add_halves(down_grads[0], down_arrived)

    result, output_sums = call(
        functools.partial(output_kernel, others=m - 1),
        "output",
        [vectors, own_upstream, scale, middle, fed[0][0], *out_arrived],
        [],
        [shape_of((count, width), BF16), shape_of((8, width), F32)],
    )
    if pairwise:
        up_own, up_sent = add_halves(proj_grads[0], after(up_arrived, result, *d_mixed_blocks))
        up_sent, down_sent, result, *d_mixed_blocks = lax.optimization_barrier(
            (up_sent, down_sent, result, *d_mixed_blocks)
        )
    result = back_to_tokens(result)

    d_project = attend_backward(d_mixed_blocks, kept[0], kept[1], cosine, sines)
    if pairwise:
        up_arrived, down_arrived = swap(up_sent, y_bit), swap(down_sent, y_bit)
        d_project, result, down_arrived = lax.optimization_barrier((d_project, result, down_arrived))
    qkv_shape = (PLANES, width // 8, 3 * WIDTH) if pairwise else (2, width // PLANES, 3 * WIDTH)
    d_kept, d_sent, sums = call(
        functools.partial(normed_backward_kernel, blocks=side),
        "normed_backward",
        [d_project, kept[3], *token_blocks],
        [],
        [shape_of((side // 2, count, width), BF16)] * 2 + [shape_of((8, width), F32)],
        us=2.0,
    )
    d_project = after(d_project, d_sent, up_arrived) if pairwise else d_project
    grad_own, grad_sent = call(
        qkv_grads_kernel,
        "qkv_gradients",
        [d_project, kept[2]],
        [place],
        [shape_of(qkv_shape, BF16)] * 2,
        us=4.0,
    )

    arrived = after(swap(d_sent, 1), grad_sent)
    blocks = {2 * at: add(d_kept[at], arrived[at]) for at in range(side // 2)}
    if pairwise:
        up_arrived = after(up_arrived, blocks[y_bit])
        up_own, up_sent = add_halves(up_own, up_arrived)
        down_own, down_sent = add_halves(down_own, down_arrived)
        up_own = jnp.concatenate([up_own, down_own], 1)
        up_sent = jnp.concatenate([up_sent, down_sent], 1)
        grad_arrived = swap_mlp(grad_sent, 1)
    bias_up_rows = -(-hidden_count // width)
    bias_up_sum = jnp.pad(bias_up_sum, ((0, 0), (0, bias_up_rows * width - hidden_count)))
    small = jnp.concatenate(
        [sums[0:2], middle_sums[0:3], output_sums[0:2], bias_up_sum.reshape(-1, width)], 0
    )
    small = small + swap(small, 1)
    for bit in bits_of(side)[1:]:
        for at in [at for at in blocks if at & bit]:
            arrived = swap(blocks.pop(at), bit)
            if len(blocks) > 1:
                blocks[at ^ bit] = add(blocks[at ^ bit], arrived)
    if pairwise:
        grad_arrived = after(grad_arrived, arrived)
        grad_own, grad_sent = add_halves(grad_own, grad_arrived)
    small = after(small, arrived)
    for bit in bits_of(side)[1:]:
        small = small + swap(small, bit)
    near_arrived = swap(grad_sent, side)
    small = jnp.concatenate([after(small, near_arrived), vectors[SCALE_TWO][None]], 0)[None]
    for bit in bits_of(PLANES):
        small = jnp.concatenate([small, swap(small, bit * side)], 0)
    (d_tokens,) = call(
        tokens_kernel,
        "tokens_backward",
        [vectors, own_low, d_middle, blocks[0], after(arrived, grad_arrived) if pairwise else arrived],
        [],
        [shape_of((count, width), BF16)],
    )
    if pairwise:
        grad_own, grad_sent = add_halves(grad_own, after(near_arrived, d_tokens))
        far_arrived = swap(grad_sent, 2 * side)
        up_own, up_sent = add_halves(up_own, after(swap(up_sent, side), near_arrived))
        d_tokens = after(d_tokens, grad_sent, up_sent)
        far_arrived = after(far_arrived, up_sent)
    returned = back_to_tokens(d_tokens)

    if pairwise:
        up_parts = up_own[0].astype(F32) + swap(up_sent, 2 * side)[0].astype(F32)
        grad_up = jnp.concatenate([up_parts[at] for at in range(hidden_chunks)], -1)
        grad_proj = up_parts[hidden_chunks]
        down_parts = up_parts[hidden_chunks + 1 :]
    else:
        grads = jnp.stack(columns_of(up_grads[0]) + columns_of(proj_grads[0]) + columns_of(down_grads[0]))
        grads = grads.reshape(-1, n, rows, unit).transpose(1, 0, 2, 3)
        grads = lax.psum_scatter(grads, "seq", scatter_dimension=0, tiled=True)[0]

        def columns_from(start, number):
            return jnp.concatenate([grads[start + at] for at in range(number)], -1).astype(F32)

        grad_up = columns_from(0, hidden_chunks)
        grad_proj = columns_from(hidden_chunks, width_chunks)
        down_parts = grads[hidden_chunks + width_chunks :].astype(F32)
    for bit in bits_of(m):
        grad_proj = grad_proj + swap_mlp(grad_proj.astype(BF16), bit).astype(F32)

    arrived = near_arrived
    if pairwise:
        arrived = far_arrived
        total = grad_own[0].astype(F32) + arrived[0].astype(F32)
        by_spot = total.astype(BF16).reshape(2, rows, 3 * WIDTH)
        slices = [pick(by_spot, (spot ^ e) % 2) for e in range(side)]
    else:
        arrived = swap(add(grad_own[1], arrived[1]), 2 * side).astype(F32) + arrived[0].astype(F32)
        total = grad_own[0].astype(F32) + arrived
        by_spot = total.astype(BF16).reshape(side, rows, 3 * WIDTH)
        slices = [pick(by_spot, spot ^ e) for e in range(side)]
    received = jnp.stack(in_plane(slices))
    grad_qkv = jnp.stack([pick(received, spot ^ group) for group in range(GROUPS)])
    grad_qkv = grad_qkv.reshape(GROUPS, rows, 3, WIDTH).transpose(1, 2, 0, 3).reshape(rows, 3 * width)
    if pairwise:
        grad_qkv = jnp.where(spot // 2 == slice_of, grad_qkv, swap_mlp(grad_qkv, 1)).astype(F32)
    else:
        grad_qkv = grad_qkv.astype(F32)
        for bit in bits_of(m):
            grad_qkv = grad_qkv + swap_mlp(grad_qkv.astype(BF16), bit).astype(F32)

    grad_down = jnp.concatenate([down_parts[at] for at in range(hidden_chunks)], -1).T

    small = in_order(list(small), plane)[:MICRO]
    grad_bias_up = jnp.sum(small[:, 7 : 7 + bias_up_rows], 0).reshape(-1)[:hidden_count]
    d_shift_one, d_xhat_one, d_gate_one, d_shift_two, d_xhat_two, d_gate_two = [small[:, at] for at in range(6)]
    index_here = time_index[:, 0]
    vector_sums = jnp.stack(
        [
            jnp.sum((1.0 + vectors[SCALES_ALL : SCALES_ALL + MICRO]) * d_xhat_one, 0),
            jnp.sum((1.0 + small[:, -1]) * d_xhat_two, 0),
            jnp.sum(small[:, 6], 0),
            jnp.pad(index_here.astype(F32), (0, width - MICRO)),
        ]
    )
    d_scale_one, d_scale_two = vectors[GAIN_ONE] * d_xhat_one, vectors[GAIN_TWO] * d_xhat_two
    small = jnp.stack([d_shift_one, d_scale_one, d_gate_one, d_shift_two, d_scale_two, d_gate_two], 1)
    small = jnp.concatenate([small.reshape(6 * MICRO, width), vector_sums], 0)[None]
    for bit in bits_of(m):
        small = jnp.concatenate([small, swap_mlp(small, bit)], 0)
    at = 6 * MICRO
    d_modulation = small[:, :at].reshape(m * MICRO, n, ada_columns)
    vector_sums = jnp.sum(small[:, at : at + 3], 0)
    index_all = small[:, at + 3, :MICRO].reshape(-1).astype(jnp.int32)
    onehot = (index_all[:, None] == jnp.arange(grid_size)[None, :]).astype(BF16)
    cond = jnp.dot(onehot, time_table, preferred_element_type=F32)
    d_modulation_own = lax.dynamic_index_in_dim(d_modulation, me, 1, keepdims=False)
    grad_ada = jnp.dot(cond.T, d_modulation_own, precision=highest)
    grad_bias_ada = jnp.sum(d_modulation_own, 0)
    d_cond = jnp.einsum("bic,idc->bd", d_modulation, full_ada.astype(F32), precision=highest)
    table_rows = grid_size // n
    onehot_own = index_all[None, :] == (me * table_rows + jnp.arange(table_rows))[:, None]
    grad_table = jnp.dot(onehot_own.astype(F32), d_cond, precision=highest)
    vector_sums = lax.dynamic_slice_in_dim(vector_sums, me * rows, rows, 1)
    return (
        result,
        returned.astype(F32),
        grad_table,
        grad_ada,
        grad_bias_ada,
        vector_sums[0],
        vector_sums[1],
        grad_qkv,
        grad_proj,
        grad_up,
        grad_bias_up,
        grad_down,
        vector_sums[2],
    )


def solution(mesh):
    in_specs = (
        P(None, "mlp", "seq", None),
        P(None, "mlp", "seq", None),
        P(None, "mlp", "seq"),
        P(None, "mlp"),
        P(None, "mlp"),
        P(),
        P(),
        P(None, "seq"),
        P("seq"),
        P("seq"),
        P("seq"),
        P("seq", None),
        P("seq", None),
        P("seq", "mlp"),
        P("mlp"),
        P("mlp", "seq"),
        P("seq"),
    )
    out_specs = (
        P(None, "mlp", "seq", None),
        P(None, "mlp", "seq", None),
        P("seq", None),
        P(None, "seq"),
        P("seq"),
        P("seq"),
        P("seq"),
        P("seq", None),
        P("seq", None),
        P("seq", "mlp"),
        P("mlp"),
        P("mlp", "seq"),
        P("seq"),
    )
    run = functools.partial(body, n=mesh.shape["seq"], m=mesh.shape["mlp"])
    return jax.shard_map(run, mesh=mesh, in_specs=in_specs, out_specs=out_specs, check_vma=False)
```

```python
import functools
import math

import jax
import jax.numpy as jnp
from jax import lax
from jax.experimental import pallas as pl
from jax.experimental.pallas import tpu as pltpu
from jax.sharding import PartitionSpec as P

HEADS = 12
HEAD = 64
MICRO = 3
PLANES = 4
GROUPS = 4
PER_GROUP = HEADS // GROUPS
WIDTH = PER_GROUP * HEAD
QUERY_BLOCK = 256
SCALING = HEAD ** (-0.5)
BF16 = jnp.bfloat16
F32 = jnp.float32
highest = lax.Precision.HIGHEST
SLOPE = math.sqrt(2.0 / math.pi)
CUBIC = 0.044715

SHIFT_ONE, SCALE_ONE, GATE_ONE, SHIFT_TWO, SCALE_TWO, GATE_TWO, GAIN_ONE, GAIN_TWO, BIAS_DOWN = range(9)
SCALES_ALL, GAINS_ONE, GAINS_TWO = 9, 12, 13

VMEM = pl.BlockSpec(memory_space=pltpu.VMEM)
SMEM = pl.BlockSpec(memory_space=pltpu.SMEM)


def nn(left, right):
    return lax.dot_general(left, right, (((1,), (0,)), ((), ())), preferred_element_type=F32)


def nt(left, right):
    return lax.dot_general(left, right, (((1,), (1,)), ((), ())), preferred_element_type=F32)


def standardize(inputs):
    average = jnp.mean(inputs, -1, keepdims=True)
    centred = inputs - average
    spread = jnp.mean(centred * centred, -1, keepdims=True)
    root = lax.rsqrt(spread + 1e-06)
    return centred * root, root


def pull_norm(d_normed, gains, xhat, root):
    e = d_normed * gains
    return root * (e - jnp.mean(e, -1, keepdims=True) - xhat * jnp.mean(e * xhat, -1, keepdims=True))


def over_tokens(value):
    return jnp.sum(value, 0, keepdims=True)


def shape_of(dims, dtype):
    return jax.ShapeDtypeStruct(dims, dtype)


def call(kernel, name, operands, scalars, outs, scratch=(), us=1.0, far=()):
    moved = sum(math.prod(o.shape) * o.dtype.itemsize for o in list(operands) + list(outs))
    return pl.pallas_call(
        kernel,
        out_shape=list(outs),
        in_specs=[SMEM] * len(scalars) + [pl.BlockSpec(memory_space=pl.ANY)] * len(far) + [VMEM] * len(operands),
        out_specs=[VMEM] * len(outs),
        scratch_shapes=list(scratch),
        compiler_params=pltpu.CompilerParams(vmem_limit_bytes=56 * 1024 * 1024),
        cost_estimate=pl.CostEstimate(flops=int(us * 1e9), bytes_accessed=moved, transcendentals=0),
        name=name,
    )(*scalars, *far, *operands)


def fetch(gathered, chunks, weights, arrived):
    copies = [
        pltpu.make_async_copy(gathered.at[:, chunk], weights.at[at], arrived.at[at])
        for at, chunk in enumerate(chunks)
    ]
    for copy in copies:
        copy.start()
    return copies


def whole(weights, at):
    return weights[at].reshape(weights.shape[1] * weights.shape[2], weights.shape[3])


def group_rows(weights, group, me=None):
    blocks = WIDTH // weights.shape[2]
    if me is not None:
        return jnp.concatenate([weights[0, me ^ (group * blocks + at)] for at in range(blocks)], 0)
    parts = [
        weights[at, pl.ds(group * blocks, blocks)].reshape(WIDTH, weights.shape[3])
        for at in range(weights.shape[0])
    ]
    return parts[0] if len(parts) == 1 else jnp.concatenate(parts, -1)


def modulation(times, table, ada, b_ada, gain_one, gain_two, b_down, mask, small):
    columns = ada.shape[0]
    rows = gain_one.shape[1]
    at = lax.broadcasted_iota(jnp.int32, (8, table.shape[0]), 1)
    line = lax.broadcasted_iota(jnp.int32, (8, table.shape[0]), 0)
    wanted = jnp.where(line == 0, times[0], jnp.where(line == 1, times[1], times[2]))
    cond = nn((at == wanted).astype(F32).astype(BF16), table[...]).astype(BF16)
    part = nt(cond, ada[...]) + b_ada[...].astype(F32)
    small[...] = jnp.zeros_like(small)
    at = 0
    for s in range(MICRO):
        small[0:1, at : at + columns] = part[s : s + 1]
        at += columns
    for ref in (gain_one, gain_two, b_down):
        small[0:1, at : at + rows] = ref[...].astype(F32)
        at += rows
    for s in range(MICRO):
        small[0:1, at : at + mask.shape[1]] = mask[s : s + 1, :].astype(F32)
        at += mask.shape[1]


def prepare_kernel(
    place, times, tokens, upstream, w_qkv, w_up, down, w_proj, table, ada, b_ada, gain_one, gain_two, b_down, mask, *outs
):
    packed, small, outs = outs[0], outs[1], outs[2:]
    columns_out, token_out, upstream_out = outs[: -2 * PLANES], outs[-2 * PLANES : -PLANES], outs[-PLANES:]
    plane, spot = place[0], place[1]
    for d in range(PLANES):
        token_out[d][...] = tokens[jnp.minimum(plane ^ d, MICRO - 1)]
        upstream_out[d][...] = upstream[jnp.minimum(plane ^ d, MICRO - 1)]
    width = w_proj.shape[1]
    by_group = [
        jnp.concatenate([w_qkv[:, p * width + g * WIDTH : p * width + (g + 1) * WIDTH] for p in range(3)], -1)
        for g in range(GROUPS)
    ]
    for e, out in enumerate(columns_out):
        group = (spot ^ e) % GROUPS
        here = by_group[0]
        for g in range(1, GROUPS):
            here = jnp.where(group == g, by_group[g], here)
        out[...] = here
    unit = packed.shape[2]
    chunk = 0
    for value in (w_up[...], down[...], w_proj[...]):
        for at in range(0, value.shape[1], unit):
            packed[chunk] = value[:, at : at + unit]
            chunk += 1
    modulation(times, table, ada, b_ada, gain_one, gain_two, b_down, mask, small)


def vectors_kernel(place, weight_index, weight_grid, small, vectors, scale, line):
    n = small.shape[0]
    width = vectors.shape[1]
    columns, rows, shard = 6 * width // n, width // n, scale.shape[0] // PLANES
    plane, spot = place[0], place[1]
    side = n // PLANES
    me = plane * side + spot
    last = jnp.minimum(plane, MICRO - 1)

    def one_of(three):
        return jnp.where(last == 0, three[0], jnp.where(last == 1, three[1], three[2]))

    def pieces(first, size):
        start = first
        while start < first + size:
            stop = min(first + size, (start // width + 1) * width)
            yield start // width, start % width, start - first, stop - start
            start = stop

    vectors[...] = jnp.zeros_like(vectors)
    for i in range(n):
        here = small[pl.ds(me ^ i, 1), :]
        each = [here[:, s * columns : (s + 1) * columns] for s in range(MICRO)]
        mine = one_of(each)
        for part, column, offset, size in pieces(i * columns, columns):
            vectors[part : part + 1, column : column + size] = mine[:, offset : offset + size]
            if part == SCALE_ONE:
                for s in range(MICRO):
                    vectors[SCALES_ALL + s : SCALES_ALL + s + 1, column : column + size] = each[s][
                        :, offset : offset + size
                    ]
        for row in (GAIN_ONE, GAIN_TWO, BIAS_DOWN):
            start = MICRO * columns + (row - GAIN_ONE) * rows
            vectors[row : row + 1, i * rows : (i + 1) * rows] = here[:, start : start + rows]
    for to, gain, by in ((GAINS_ONE, GAIN_ONE, SCALE_ONE), (GAINS_TWO, GAIN_TWO, SCALE_TWO)):
        vectors[to : to + 1, :] = vectors[gain : gain + 1, :] * (1.0 + vectors[by : by + 1, :])
    line[...] = jnp.zeros_like(line)
    for d in range(PLANES):
        here = small[d * side : d * side + 1, :]
        start = MICRO * (columns + rows)
        three = [here[:, start + s * shard : start + (s + 1) * shard] for s in range(MICRO)]
        line[0:1, d * shard : (d + 1) * shard] = one_of(three)
    weight = jnp.where(plane < MICRO, weight_grid[weight_index[last]], 0.0)
    scale[...] = line[...].T[:, 0:1] * weight


def project_kernel(place, gathered, tokens, vectors, *refs, chunks, slots):
    side = len(refs) - 5
    mixed, (attended, middle, normed, weights, arrived) = refs[:side], refs[side:]
    spot = place[1]
    copies = fetch(gathered, chunks, weights, arrived)
    for copy in copies:
        copy.wait()
    total = jnp.zeros(attended.shape, F32)
    for e in range(side):
        other = spot ^ e
        block = mixed[e][...]
        if side > GROUPS:
            block = jnp.where(other < GROUPS, block, jnp.zeros_like(block))
        total = total + nn(block, group_rows(weights, other % GROUPS, place[2] if slots else None))
    attended[...] = total
    after = tokens[...].astype(F32) + vectors[GATE_ONE : GATE_ONE + 1] * total
    middle[...] = after
    xhat, _ = standardize(after)
    normed[...] = (xhat * vectors[GAINS_TWO : GAINS_TWO + 1] + vectors[SHIFT_TWO : SHIFT_TWO + 1]).astype(BF16)


def feed_kernel(gathered, rows, d_rows, bias, output, d_normed, active, d_hidden, weights, arrived):
    parts = weights.shape[0] // 2
    unit = weights.shape[3]
    order = [at for part in range(parts) for at in (part, parts + part)]
    copies = fetch(gathered, order, weights, arrived)
    out = jnp.zeros(output.shape, F32)
    back = jnp.zeros(output.shape, F32)
    for part in range(parts):
        columns = slice(part * unit, (part + 1) * unit)
        copies[2 * part].wait()
        up = whole(weights, 2 * part)
        u = nn(rows[...], up) + bias[:, columns]
        square = u * u
        bent = jnp.tanh(SLOPE * u * (1.0 + CUBIC * square))
        half = 0.5 * (1.0 + bent)
        on = (u * half).astype(BF16)
        active[:, columns] = on
        slope = half + 0.5 * u * (1.0 - bent * bent) * (SLOPE * (1.0 + 3.0 * CUBIC * square))
        copies[2 * part + 1].wait()
        down = whole(weights, 2 * part + 1)
        d_on = (nn(d_rows[...], down) * slope).astype(BF16)
        d_hidden[:, columns] = d_on
        out = out + nt(on, down)
        back = back + nt(d_on, up)
    output[...] = out.astype(output.dtype)
    d_normed[...] = back.astype(d_normed.dtype)


def scatter_store(refs, me, device, value):
    kept, sent, chunk, slot_of = refs
    distance = me ^ device
    slot = slot_of(distance)

    @pl.when(distance % 2 == 0)
    def _():
        kept[slot, chunk] = value

    @pl.when(distance % 2 == 1)
    def _():
        sent[slot, chunk] = value


def slot_y_first(distance):
    return ((distance >> 1) & 1) * 4 + ((distance >> 2) & 1) * 2 + ((distance >> 3) & 1)


def down_grads_kernel(place, *refs, blocks, scatter):
    d_rows, active, outs = refs[:blocks], refs[blocks : 2 * blocks], refs[2 * blocks :]
    me = place[2]
    width, count = d_rows[0].shape[1], active[0].shape[1]
    unit = min(width, count)
    turned = [ref[...].T for ref in d_rows]
    for chunk in range(count // unit):
        columns = slice(chunk * unit, (chunk + 1) * unit)
        grad = sum(nn(turned[b], active[b][:, columns]) for b in range(blocks)).astype(BF16)
        if scatter:
            rows = outs[0].shape[2]
            for i in range(width // rows):
                part = grad[i * rows : (i + 1) * rows]
                scatter_store((outs[0], outs[1], chunk, slot_y_first), me, i, part)
        else:
            outs[0][:, columns] = grad


def up_grads_kernel(place, *refs, blocks, scatter):
    rows_all, d_hidden, outs = refs[:blocks], refs[blocks : 2 * blocks], refs[2 * blocks :]
    bias = outs[-1]
    me = place[2]
    width, count = rows_all[0].shape[1], bias.shape[1]
    unit = min(width, count)
    turned = [ref[...].T for ref in rows_all]
    for chunk in range(count // unit):
        columns = slice(chunk * unit, (chunk + 1) * unit)
        grad = sum(nn(turned[b], d_hidden[b][:, columns]) for b in range(blocks)).astype(BF16)
        bias[:, columns] = sum(over_tokens(d_hidden[b][:, columns].astype(F32)) for b in range(blocks))
        if scatter:
            rows = outs[0].shape[2]
            for i in range(width // rows):
                part = grad[i * rows : (i + 1) * rows]
                scatter_store((outs[0], outs[1], chunk, slot_y_first), me, i, part)
        else:
            outs[0][:, columns] = grad


def proj_grads_kernel(place, d_attended, *refs, side, scatter):
    mixed, refs = refs[:side], refs[side:]
    spot, me = place[1], place[2]
    width = d_attended.shape[1]
    whole_grad = refs[-1]
    if side > GROUPS:
        whole_grad[...] = jnp.zeros_like(whole_grad)
    for e in range(side):
        other = spot ^ e
        first = pl.multiple_of((other % GROUPS) * WIDTH, WIDTH)
        grad = nn(mixed[e][...].T, d_attended[...]).astype(BF16)
        if side > GROUPS:
            grad = whole_grad[pl.ds(first, WIDTH), :] + jnp.where(other < GROUPS, grad, jnp.zeros_like(grad))
        whole_grad[pl.ds(first, WIDTH), :] = grad
    if not scatter:
        refs[0][...] = whole_grad[...]
        return
    _, _, own, sent, ready, done, _ = refs
    rows, chunk = own.shape[2], own.shape[1] - 1
    for i in range(width // rows):
        part = whole_grad[i * rows : (i + 1) * rows, :]
        scatter_store((ready.at[0], ready.at[1], 0, slot_y_first), me, i, part)
    copies = [
        pltpu.make_async_copy(ready.at[at, :, 0], out.at[:, chunk], done.at[at])
        for at, out in enumerate((own, sent))
    ]
    for copy in copies:
        copy.start()
    for copy in copies:
        copy.wait()


def qkv_grads_kernel(place, d_project, normed, *outs):
    grad = nn(d_project[...], normed[...]).astype(BF16).T
    plane, slice_of = place[0], place[3]
    rows = outs[0].shape[1]
    if len(outs[0].shape) == 3 and outs[0].shape[0] == PLANES:
        for at in range(PLANES):
            distance = plane ^ at
            slot = (distance % 2) * 2 + distance // 2
            halves = [grad[(2 * at + half) * rows : (2 * at + half + 1) * rows] for half in range(2)]
            outs[0][slot] = jnp.where(slice_of == 0, halves[0], halves[1])
            outs[1][slot] = jnp.where(slice_of == 0, halves[1], halves[0])
    else:
        for at in range(PLANES):
            part = grad[at * rows : (at + 1) * rows]
            distance = plane ^ at

            @pl.when(distance % 2 == 0)
            def _():
                outs[0][distance // 2] = part

            @pl.when(distance % 2 == 1)
            def _():
                outs[1][distance // 2] = part


def normed_backward_kernel(d_project, weight, *refs, blocks):
    tokens, (kept, sent, sums) = refs[:blocks], refs[blocks:]
    count = tokens[0].shape[0]
    d_shift = jnp.zeros((1, weight.shape[0]), F32)
    d_xhat = jnp.zeros((1, weight.shape[0]), F32)
    for block in range(blocks):
        part = nt(d_project[:, block * count : (block + 1) * count].T, weight[...])
        (sent if block % 2 else kept)[block // 2] = part.astype(BF16)
        xhat, _ = standardize(tokens[block][...].astype(F32))
        d_shift = d_shift + over_tokens(part)
        d_xhat = d_xhat + over_tokens(part * xhat)
    sums[0:1, :] = d_shift
    sums[1:2, :] = d_xhat
    sums[2:8, :] = jnp.zeros((6, weight.shape[0]), F32)


def middle_kernel(place, gathered, vectors, upstream, scale, attended, middle, d_own, *refs, others, chunks, slots):
    arrived, refs = refs[:others], refs[others:]
    d_mixed, (d_middle, d_attended, sums, weights, copied) = refs[:-5], refs[-5:]
    spot = place[1]
    copies = fetch(gathered, chunks, weights, copied)
    width = middle.shape[1]
    d_normed = d_own[...]
    for ref in arrived:
        d_normed = d_normed + ref[...].astype(F32)
    xhat, root = standardize(middle[...])
    d_result = upstream[...].astype(F32) * scale[...]
    d_after = d_result + pull_norm(d_normed, vectors[GAINS_TWO : GAINS_TWO + 1], xhat, root)
    d_middle[...] = d_after
    low = (vectors[GATE_ONE : GATE_ONE + 1] * d_after).astype(BF16)
    d_attended[...] = low
    for copy in copies:
        copy.wait()
    for e in range(len(d_mixed)):
        rows_here = group_rows(weights, (spot ^ e) % GROUPS, place[2] if slots else None)
        d_mixed[e][...] = nt(low, rows_here).astype(BF16)
    sums[0:1, :] = over_tokens(d_after * attended[...])
    sums[1:2, :] = over_tokens(d_normed)
    sums[2:3, :] = over_tokens(d_normed * xhat)
    sums[3:8, :] = jnp.zeros((5, width), F32)


def output_kernel(vectors, upstream, scale, middle, own, *refs, others):
    arrived, (result, sums) = refs[:others], refs[others:]
    output = own[...] + vectors[BIAS_DOWN : BIAS_DOWN + 1]
    for ref in arrived:
        output = output + ref[...].astype(F32)
    gate = vectors[GATE_TWO : GATE_TWO + 1]
    result[...] = (middle[...] + gate * output).astype(BF16)
    d_result = upstream[...].astype(F32) * scale[...]
    sums[0:1, :] = over_tokens(d_result * output)
    sums[1:2, :] = over_tokens(gate * d_result)
    sums[2:8, :] = jnp.zeros((6, middle.shape[1]), F32)


def tokens_kernel(vectors, tokens, d_middle, own, arrived, d_tokens):
    xhat, root = standardize(tokens[...].astype(F32))
    d_normed = own[...].astype(F32) + arrived[...].astype(F32)
    back = pull_norm(d_normed, vectors[GAINS_ONE : GAINS_ONE + 1], xhat, root)
    d_tokens[...] = (d_middle[...] + back).astype(BF16)


def forward_kernel(place, *refs, blocks, halves):
    tokens, refs = refs[:blocks], refs[blocks:]
    count = 2 if halves else PLANES
    weights, refs = refs[:count], refs[count:]
    (vectors, cosine, sines), refs = refs[:3], refs[3:]
    gain, shift = vectors[GAINS_ONE : GAINS_ONE + 1], vectors[SHIFT_ONE : SHIFT_ONE + 1]
    mixed, refs = refs[:blocks], refs[blocks:]
    heads, log_total, normed, weight, keys, mixed_turned = refs
    plane = place[0]
    rows = weights[0].shape[-2]
    count = tokens[0].shape[0]
    if halves:
        for half in range(2):
            for distance in range(PLANES):
                first = pl.multiple_of((plane ^ distance) * 2 * rows + (place[3] ^ half) * rows, 16)
                weight[pl.ds(first, rows), :] = weights[half][distance]
    else:
        for distance in range(PLANES):
            first = pl.multiple_of((plane ^ distance) * rows, 8)
            weight[pl.ds(first, rows), :] = weights[distance][...]
    for block in range(blocks):
        xhat, _ = standardize(tokens[block][...].astype(F32))
        normed[block * count : (block + 1) * count, :] = (xhat * gain + shift).astype(BF16)
    project = nt(weight[...].T, normed[...])
    cos, sin = cosine[...], sines[...]
    half = HEAD // 2
    for part in range(2):
        for head in range(PER_GROUP):
            start = part * WIDTH + head * HEAD
            first, second = project[start : start + half], project[start + half : start + HEAD]
            turned = jnp.concatenate([first * cos - second * sin, second * cos + first * sin], 0).astype(BF16)
            if part == 0:
                turned = turned * jnp.asarray(SCALING, BF16)
            else:
                keys[head] = turned.T
            heads[start : start + HEAD, :] = turned
    heads[2 * WIDTH :, :] = project[2 * WIDTH :].astype(BF16)
    length = heads.shape[1]
    for head in range(PER_GROUP):
        start = head * HEAD

        def queries_step(step, carry):
            columns = pl.ds(pl.multiple_of(step * QUERY_BLOCK, QUERY_BLOCK), QUERY_BLOCK)
            scores = nn(keys[head], heads[start : start + HEAD, columns])
            peak = jnp.max(scores, 0, keepdims=True)
            exps = jnp.exp(scores - peak)
            total = jnp.sum(exps, 0, keepdims=True)
            log_total[head : head + 1, columns] = peak + jnp.log(total)
            probs = (exps * (1.0 / total)).astype(BF16)
            values = heads[2 * WIDTH + start : 2 * WIDTH + start + HEAD, :]
            mixed_turned[start : start + HEAD, columns] = nn(values, probs).astype(BF16)
            return carry

        lax.fori_loop(0, length // QUERY_BLOCK, queries_step, 0, unroll=True)
    for block in range(blocks):
        mixed[block][...] = mixed_turned[:, block * count : (block + 1) * count].T


def backward_kernel(*refs, blocks):
    d_mixed, refs = refs[:blocks], refs[blocks:]
    (heads, log_total, cosine, sines), refs = refs[:4], refs[4:]
    d_project, d_turned, d_keys, d_values, keys, values = refs
    count = d_mixed[0].shape[0]
    length = heads.shape[1]
    for block in range(blocks):
        d_turned[:, block * count : (block + 1) * count] = d_mixed[block][...].T
    cos, sin = cosine[...], sines[...]
    half = HEAD // 2
    d_keys[...] = jnp.zeros_like(d_keys)
    d_values[...] = jnp.zeros_like(d_values)
    for head in range(PER_GROUP):
        start = head * HEAD
        keys_turned = heads.at[WIDTH + start : WIDTH + start + HEAD]
        keys[...] = keys_turned[...].T
        values[...] = heads[2 * WIDTH + start : 2 * WIDTH + start + HEAD, :].T

        def queries_step(step, carry):
            columns = pl.ds(pl.multiple_of(step * QUERY_BLOCK, QUERY_BLOCK), QUERY_BLOCK)
            queries = heads[start : start + HEAD, columns]
            incoming = d_turned[start : start + HEAD, columns]
            scores = nn(keys[...], queries)
            probs = jnp.exp(scores - log_total[head : head + 1, columns])
            d_probs = nn(values[...], incoming)
            delta = jnp.sum(probs * d_probs, 0, keepdims=True)
            d_scores = (probs * (d_probs - delta)).astype(BF16)
            d_values[start : start + HEAD, :] += nt(incoming, probs.astype(BF16))
            d_keys[start : start + HEAD, :] += nt(queries, d_scores)
            d_queries = nn(keys_turned[...], d_scores) * SCALING
            first, second = d_queries[:half], d_queries[half:]
            cos_here, sin_here = cosine[:, columns], sines[:, columns]
            d_project[start : start + half, columns] = (first * cos_here + second * sin_here).astype(BF16)
            d_project[start + half : start + HEAD, columns] = (second * cos_here - first * sin_here).astype(BF16)
            return carry

        lax.fori_loop(0, length // QUERY_BLOCK, queries_step, 0, unroll=True)
        first, second = d_keys[start : start + half, :], d_keys[start + half : start + HEAD, :]
        d_project[WIDTH + start : WIDTH + start + half, :] = (first * cos + second * sin).astype(BF16)
        d_project[WIDTH + start + half : WIDTH + start + HEAD, :] = (second * cos - first * sin).astype(BF16)
    d_project[2 * WIDTH :, :] = d_values[...].astype(BF16)


def attend_forward(place, tokens, weights, vectors, cosine, sines, halves):
    blocks, (count, width) = len(tokens), tokens[0].shape
    length = blocks * count
    columns = weights[0].shape[-1]
    outs = call(
        functools.partial(forward_kernel, blocks=blocks, halves=halves),
        "attend_forward",
        [*tokens, *weights, vectors, cosine, sines],
        [place],
        [shape_of((count, WIDTH), BF16)] * blocks
        + [
            shape_of((columns, length), BF16),
            shape_of((8, length), F32),
            shape_of((length, width), BF16),
            shape_of((width, columns), BF16),
        ],
        [pltpu.VMEM((PER_GROUP, length, HEAD), BF16), pltpu.VMEM((WIDTH, length), BF16)],
        us=15.0,
    )
    return outs[:blocks], outs[blocks:]


def attend_backward(d_mixed, heads, log_total, cosine, sines):
    blocks, length = len(d_mixed), heads.shape[1]
    (d_project,) = call(
        functools.partial(backward_kernel, blocks=blocks),
        "attend_backward",
        [*d_mixed, heads, log_total, cosine, sines],
        [],
        [shape_of((3 * WIDTH, length), BF16)],
        [
            pltpu.VMEM((WIDTH, length), BF16),
            pltpu.VMEM((WIDTH, length), F32),
            pltpu.VMEM((WIDTH, length), F32),
            pltpu.VMEM((length, HEAD), BF16),
            pltpu.VMEM((length, HEAD), BF16),
        ],
        us=18.0,
    )
    return d_project


def after(values, *others):
    return lax.optimization_barrier((values, others))[0]


def add(left, right):
    return (left.astype(F32) + right.astype(F32)).astype(BF16)


def pick(stack, index):
    return lax.dynamic_index_in_dim(stack, index, 0, keepdims=False)


def bits_of(count):
    return [1 << bit for bit in range(count.bit_length() - 1)]


def body(
    tokens,
    upstream,
    token_mask,
    time_index,
    weight_index,
    time_table,
    weight_grid,
    w_ada,
    b_ada,
    gain_one,
    gain_two,
    w_qkv,
    w_proj,
    w_up,
    b_up,
    w_down,
    b_down,
    *,
    n,
    m,
):
    side = n // PLANES
    me = lax.axis_index("seq")
    plane, spot = me // side, me % side
    slice_of = lax.axis_index("mlp")
    place = jnp.stack([plane, spot, me, slice_of]).astype(jnp.int32)
    shard, width = tokens.shape[2], tokens.shape[3]
    rows = w_qkv.shape[0]
    hidden_count = w_up.shape[1]
    grid_size = time_table.shape[0]
    ada_columns = w_ada.shape[1]
    count = PLANES * shard
    unit = min(width, hidden_count)
    hidden_chunks, width_chunks = hidden_count // unit, width // unit
    pairwise = rows % 16 == 0 and side == GROUPS and unit == width and m == 2
    z_bits, y_bit, core_bit = (2 * side, side), 2, 1

    def swap(value, distance):
        return lax.ppermute(value, "seq", [(i, i ^ distance) for i in range(n)])

    def swap_mlp(value, distance):
        return lax.ppermute(value, "mlp", [(i, i ^ distance) for i in range(m)])

    def between_planes(pieces):
        return [pieces[0]] + [swap(pieces[d], d * side) for d in range(1, PLANES)]

    def in_plane(pieces):
        return [pieces[0]] + [swap(pieces[e], e) for e in range(1, side)]

    def in_order(blocks, axis):
        halves = jnp.stack(blocks)
        for bit in bits_of(len(blocks)):
            here = halves.reshape((len(blocks) // (2 * bit), 2, bit) + halves.shape[1:])
            halves = jnp.where((axis & bit) != 0, here[:, ::-1], here).reshape(halves.shape)
        return halves

    def for_plane(values):
        return [pick(values, jnp.minimum(plane ^ d, MICRO - 1)) for d in range(PLANES)]

    def columns_of(value):
        return [value[:, at : at + unit] for at in range(0, value.shape[1], unit)]

    line = [value[None] for value in (b_ada, gain_one, gain_two, b_down)]
    small_count = -(-MICRO * (ada_columns + rows + shard) // 128) * 128
    first_shapes = [shape_of((2 * hidden_chunks + width_chunks, rows, unit), BF16), shape_of((1, small_count), F32)]
    first_shapes += [shape_of((rows, 3 * WIDTH), BF16)] * side + [shape_of((shard, width), BF16)] * (2 * PLANES)
    packed, small, *pieces = call(
        prepare_kernel,
        "prepare",
        [tokens[:, 0], upstream[:, 0], w_qkv, w_up, w_down.T, w_proj, time_table, w_ada.T, *line, token_mask[:, 0]],
        [place, time_index[:, 0]],
        first_shapes,
        us=4.0,
    )
    group_columns, token_pieces, upstream_pieces = pieces[:side], pieces[side : side + PLANES], pieces[side + PLANES :]

    token_arrived = between_planes(token_pieces)

    received = jnp.stack(after(in_plane(group_columns), token_arrived[1]))
    weight_block = jnp.concatenate([pick(received, spot ^ at) for at in range(side)], 0)
    if pairwise:
        weight_block = pick(weight_block.reshape(2, width // 8, 3 * WIDTH), slice_of)
    weight_blocks = {0: weight_block}
    for bit in (2, 1):
        for known in list(weight_blocks):
            weight_blocks[known | bit] = swap(weight_blocks[known], bit * side)
    weight_blocks = [weight_blocks[at] for at in range(PLANES)]
    far_block = weight_blocks[2]
    own_upstream = between_planes(after(upstream_pieces, weight_blocks[1], weight_blocks[3]))
    if pairwise:
        weight_blocks = jnp.stack(weight_blocks)
        weight_blocks = [weight_blocks, swap_mlp(weight_blocks, 1)]

    for bit in bits_of(n)[:-1]:
        small = jnp.concatenate([small, swap(small, bit)], 0)
    arrived, small = lax.optimization_barrier((token_arrived, after(small, far_block)))
    own_low = jnp.concatenate(arrived, 0)
    token_blocks = {0: own_low}
    for bit in reversed(bits_of(side)):
        for known in list(token_blocks):
            mine = token_blocks[known]
            if bit < side // 2:
                mine = after(mine, token_blocks[side // 2])
            token_blocks[known | bit] = swap(mine, bit)
    token_blocks = [token_blocks[at] for at in range(side)]

    gathered = lax.all_gather(after(packed, token_arrived, far_block), "seq", axis=0)
    if not pairwise:
        gathered = gathered.transpose(1, 0, 2, 3).reshape(-1, GROUPS, WIDTH, unit).transpose(1, 0, 2, 3)
    blocks_shape = (gathered.shape[0],) + gathered.shape[2:]
    proj_chunks = list(range(2 * hidden_chunks, 2 * hidden_chunks + width_chunks))

    def weight_scratch(number):
        return [pltpu.VMEM((number,) + blocks_shape, BF16), pltpu.SemaphoreType.DMA((number,))]

    for bit in bits_of(n)[-1:]:
        small = jnp.concatenate([small, swap(small, bit)], 0)
    vectors, scale = call(
        vectors_kernel,
        "vectors",
        [small],
        [place, weight_index[:, 0], weight_grid],
        [shape_of((16, width), F32), shape_of((count, 1), F32)],
        [pltpu.VMEM((8, count), F32)],
    )

    order = ((plane ^ jnp.arange(PLANES))[None, :] * side + (spot ^ jnp.arange(side))[:, None]) * shard
    positions = (order[:, :, None] + jnp.arange(shard)).reshape(1, -1).astype(F32)
    frequency = 10000.0 ** (-jnp.arange(0, HEAD, 2).astype(F32) / HEAD)
    angles = frequency[:, None] * positions
    cosine, sines = jnp.cos(angles), jnp.sin(angles)

    mixed_blocks, kept = attend_forward(
        after(place, own_upstream), token_blocks, weight_blocks, vectors, cosine, sines, pairwise
    )

    full_ada = lax.all_gather(after(w_ada, gathered), "seq", axis=0)

    mixed_blocks = in_plane(mixed_blocks)

    own_upstream = jnp.concatenate(own_upstream, 0)
    d_rows = ((own_upstream.astype(F32) * scale) * vectors[GATE_TWO][None]).astype(BF16)
    d_rows = [d_rows] + [swap_mlp(d_rows, d) for d in range(1, m)]

    attended, middle, normed_two = call(
        functools.partial(project_kernel, chunks=proj_chunks, slots=False),
        "project",
        [own_low, vectors, *mixed_blocks],
        [place],
        [shape_of((count, width), F32), shape_of((count, width), F32), shape_of((count, width), BF16)],
        weight_scratch(width_chunks),
        us=3.0,
        far=[gathered],
    )
    rows_all = [normed_two] + [swap_mlp(normed_two, d) for d in range(1, m)]
    bias_up = b_up.astype(F32)[None]
    fed = [
        call(
            feed_kernel,
            "feed_forward",
            [rows_all[d], d_rows[d], bias_up],
            [],
            [shape_of((count, width), BF16 if d else F32)] * 2 + [shape_of((count, hidden_count), BF16)] * 2,
            weight_scratch(2 * hidden_chunks),
            us=6.0,
            far=[gathered],
        )
        for d in range(m)
    ]
    d_arrived = [swap_mlp(fed[d][1], d) for d in range(1, m)]
    out_arrived = [swap_mlp(fed[d][0], d) for d in range(1, m)]
    slots = n // 2
    if pairwise:
        down_shapes = [shape_of((slots, hidden_chunks + width_chunks, rows, unit), BF16)] * 2
    else:
        down_shapes = [shape_of((width, hidden_count), BF16)]
    if pairwise:
        up_shapes = [shape_of((slots, hidden_chunks, rows, unit), BF16)] * 2
    else:
        up_shapes = [shape_of((width, hidden_count), BF16)]
    down_grads = call(
        functools.partial(down_grads_kernel, blocks=m, scatter=pairwise),
        "down_gradients",
        [*d_rows, *[f[2] for f in fed]],
        [place],
        down_shapes,
        us=6.0,
    )
    *up_grads, bias_up_sum = call(
        functools.partial(up_grads_kernel, blocks=m, scatter=pairwise),
        "up_gradients",
        [*rows_all, *[f[3] for f in fed]],
        [place],
        up_shapes + [shape_of((1, hidden_count), F32)],
        us=5.0,
    )
    d_arrived, down_grads, full_ada, *up_grads = lax.optimization_barrier(
        (d_arrived, down_grads, full_ada, *up_grads)
    )
    middle_outs = call(
        functools.partial(middle_kernel, others=m - 1, chunks=proj_chunks, slots=False),
        "middle_backward",
        [vectors, own_upstream, scale, attended, middle, fed[0][1], *d_arrived],
        [place],
        [shape_of((count, WIDTH), BF16)] * side
        + [shape_of((count, width), F32), shape_of((count, width), BF16), shape_of((8, width), F32)],
        weight_scratch(width_chunks),
        us=4.0,
        far=[gathered],
    )
    d_mixed_blocks, (d_middle, d_attended, middle_sums) = middle_outs[:side], middle_outs[side:]

    d_mixed_blocks = in_plane(d_mixed_blocks)
    if side > GROUPS:
        share = (spot < GROUPS).astype(BF16)
        d_mixed_blocks = [block * share for block in d_mixed_blocks]

    anywhere = pl.BlockSpec(memory_space=pl.ANY)
    proj_grads = pl.pallas_call(
        functools.partial(proj_grads_kernel, side=side, scatter=pairwise),
        out_shape=down_shapes if pairwise else [shape_of((width, width), BF16)],
        in_specs=[SMEM] + [VMEM] * (1 + side) + ([anywhere] * 2 if pairwise else []),
        out_specs=[anywhere] * 2 if pairwise else [VMEM],
        scratch_shapes=(
            [pltpu.VMEM((2, slots, 1, rows, unit), BF16), pltpu.SemaphoreType.DMA((2,))] if pairwise else []
        )
        + [pltpu.VMEM((width, width), BF16)],
        input_output_aliases={2 + side: 0, 3 + side: 1} if pairwise else {},
        compiler_params=pltpu.CompilerParams(vmem_limit_bytes=56 * 1024 * 1024),
        cost_estimate=pl.CostEstimate(flops=2 * 10**9, bytes_accessed=4 * 10**6, transcendentals=0),
        name="proj_gradients",
    )(place, d_attended, *mixed_blocks, *(down_grads if pairwise else []))

    def add_halves(own, arrived):
        half = own.shape[0] // 2
        return add(own[:half], arrived[:half]), add(own[half:], arrived[half:])

    def back_to_tokens(value):
        received = between_planes([value[d * shard : (d + 1) * shard] for d in range(PLANES)])
        received = jnp.stack(received)
        return jnp.stack([pick(received, plane ^ at) for at in range(MICRO)])[:, None]

    if pairwise:
        up_arrived = swap(up_grads[1], core_bit)
        down_sent, out_arrived, up_arrived = lax.optimization_barrier((proj_grads[1], out_arrived, up_arrived))
        up_own, up_sent = add_halves(up_grads[0], up_arrived)

    result, output_sums = call(
        functools.partial(output_kernel, others=m - 1),
        "output",
        [vectors, own_upstream, scale, middle, fed[0][0], *out_arrived],
        [],
        [shape_of((count, width), BF16), shape_of((8, width), F32)],
    )
    if pairwise:
        up_sent, down_sent, result, *d_mixed_blocks = lax.optimization_barrier(
            (up_sent, down_sent, result, *d_mixed_blocks)
        )
    result = back_to_tokens(result)

    d_project = attend_backward(d_mixed_blocks, kept[0], kept[1], cosine, sines)
    if pairwise:
        up_arrived, down_arrived = swap(up_sent, y_bit), swap(down_sent, core_bit)
        d_project, result, up_arrived, down_arrived = lax.optimization_barrier(
            (d_project, result, up_arrived, down_arrived)
        )
    qkv_shape = (PLANES, width // 8, 3 * WIDTH) if pairwise else (2, width // PLANES, 3 * WIDTH)
    d_kept, d_sent, sums = call(
        functools.partial(normed_backward_kernel, blocks=side),
        "normed_backward",
        [d_project, kept[3], *token_blocks],
        [],
        [shape_of((side // 2, count, width), BF16)] * 2 + [shape_of((8, width), F32)],
        us=2.0,
    )
    arrived = swap(d_sent, 1)
    if pairwise:
        up_own, up_sent = add_halves(up_own, after(up_arrived, d_sent))
        down_own, down_sent = add_halves(proj_grads[0], after(down_arrived, d_sent))
        up_near, down_beside = swap(up_sent, side), swap(down_sent, y_bit)
        arrived = after(arrived, up_sent, down_sent)
    blocks = {2 * at: add(d_kept[at], arrived[at]) for at in range(side // 2)}
    grad_own, grad_sent = call(
        qkv_grads_kernel,
        "qkv_gradients",
        [after(d_project, blocks[2]), kept[2]],
        [place],
        [shape_of(qkv_shape, BF16)] * 2,
        us=4.0,
    )
    if pairwise:
        grad_arrived = swap_mlp(grad_sent, 1)
    bias_up_rows = -(-hidden_count // width)
    bias_up_sum = jnp.pad(bias_up_sum, ((0, 0), (0, bias_up_rows * width - hidden_count)))
    small = jnp.concatenate(
        [sums[0:2], middle_sums[0:3], output_sums[0:2], bias_up_sum.reshape(-1, width)], 0
    )
    small = small + swap(small, 1)
    for bit in bits_of(side)[1:]:
        for at in [at for at in blocks if at & bit]:
            arrived = swap(blocks.pop(at), bit)
            if len(blocks) > 1:
                blocks[at ^ bit] = add(blocks[at ^ bit], arrived)
    if pairwise:
        grad_arrived = after(grad_arrived, arrived)
        grad_own, grad_sent = add_halves(grad_own, grad_arrived)
    small = after(small, arrived)
    for bit in bits_of(side)[1:]:
        small = small + swap(small, bit)
    near_arrived = swap(grad_sent, side)
    small = jnp.concatenate([small, vectors[SCALE_TWO][None]], 0)[None]
    for bit in bits_of(PLANES):
        small = jnp.concatenate([small, swap(small, bit * side)], 0)
    (d_tokens,) = call(
        tokens_kernel,
        "tokens_backward",
        [vectors, own_low, d_middle, blocks[0], after(arrived, grad_arrived, up_near, down_beside) if pairwise else arrived],
        [],
        [shape_of((count, width), BF16)],
    )
    if pairwise:
        grad_own, grad_sent = add_halves(grad_own, after(near_arrived, d_tokens))
        far_arrived = swap(grad_sent, 2 * side)
        up_own, up_sent = add_halves(up_own, after(up_near, d_tokens))
        down_own, down_sent = add_halves(down_own, down_beside)
        down_own, down_sent = add_halves(down_own, after(swap(down_sent, side), near_arrived))
        d_tokens = after(d_tokens, grad_sent, down_sent)
        far_arrived = after(far_arrived, down_sent)
    returned = back_to_tokens(d_tokens)

    if pairwise:
        up_parts = up_own[0].astype(F32) + swap(after(up_sent, returned), 2 * side)[0].astype(F32)
        grad_up = jnp.concatenate([up_parts[at] for at in range(hidden_chunks)], -1)
        down_parts = down_own[0].astype(F32) + swap(down_sent, 2 * side)[0].astype(F32)
        grad_proj = down_parts[hidden_chunks]
    else:
        grads = jnp.stack(columns_of(up_grads[0]) + columns_of(proj_grads[0]) + columns_of(down_grads[0]))
        grads = grads.reshape(-1, n, rows, unit).transpose(1, 0, 2, 3)
        grads = lax.psum_scatter(grads, "seq", scatter_dimension=0, tiled=True)[0]

        def columns_from(start, number):
            return jnp.concatenate([grads[start + at] for at in range(number)], -1).astype(F32)

        grad_up = columns_from(0, hidden_chunks)
        grad_proj = columns_from(hidden_chunks, width_chunks)
        down_parts = grads[hidden_chunks + width_chunks :].astype(F32)
    for bit in bits_of(m):
        grad_proj = grad_proj + swap_mlp(grad_proj.astype(BF16), bit).astype(F32)

    arrived = near_arrived
    if pairwise:
        arrived = far_arrived
        total = grad_own[0].astype(F32) + arrived[0].astype(F32)
        by_spot = total.astype(BF16).reshape(2, rows, 3 * WIDTH)
        slices = [pick(by_spot, (spot ^ e) % 2) for e in range(side)]
    else:
        arrived = swap(add(grad_own[1], arrived[1]), 2 * side).astype(F32) + arrived[0].astype(F32)
        total = grad_own[0].astype(F32) + arrived
        by_spot = total.astype(BF16).reshape(side, rows, 3 * WIDTH)
        slices = [pick(by_spot, spot ^ e) for e in range(side)]
    received = jnp.stack(in_plane(slices))
    grad_qkv = jnp.stack([pick(received, spot ^ group) for group in range(GROUPS)])
    grad_qkv = grad_qkv.reshape(GROUPS, rows, 3, WIDTH).transpose(1, 2, 0, 3).reshape(rows, 3 * width)
    if pairwise:
        grad_qkv = jnp.where(spot // 2 == slice_of, grad_qkv, swap_mlp(grad_qkv, 1)).astype(F32)
    else:
        grad_qkv = grad_qkv.astype(F32)
        for bit in bits_of(m):
            grad_qkv = grad_qkv + swap_mlp(grad_qkv.astype(BF16), bit).astype(F32)

    grad_down = jnp.concatenate([down_parts[at] for at in range(hidden_chunks)], -1).T

    small = in_order(list(small), plane)[:MICRO]
    grad_bias_up = jnp.sum(small[:, 7 : 7 + bias_up_rows], 0).reshape(-1)[:hidden_count]
    d_shift_one, d_xhat_one, d_gate_one, d_shift_two, d_xhat_two, d_gate_two = [small[:, at] for at in range(6)]
    index_here = time_index[:, 0]
    vector_sums = jnp.stack(
        [
            jnp.sum((1.0 + vectors[SCALES_ALL : SCALES_ALL + MICRO]) * d_xhat_one, 0),
            jnp.sum((1.0 + small[:, -1]) * d_xhat_two, 0),
            jnp.sum(small[:, 6], 0),
            jnp.pad(index_here.astype(F32), (0, width - MICRO)),
        ]
    )
    d_scale_one, d_scale_two = vectors[GAIN_ONE] * d_xhat_one, vectors[GAIN_TWO] * d_xhat_two
    small = jnp.stack([d_shift_one, d_scale_one, d_gate_one, d_shift_two, d_scale_two, d_gate_two], 1)
    small = jnp.concatenate([small.reshape(6 * MICRO, width), vector_sums], 0)[None]
    for bit in bits_of(m):
        small = jnp.concatenate([small, swap_mlp(small, bit)], 0)
    at = 6 * MICRO
    d_modulation = small[:, :at].reshape(m * MICRO, n, ada_columns)
    vector_sums = jnp.sum(small[:, at : at + 3], 0)
    index_all = small[:, at + 3, :MICRO].reshape(-1).astype(jnp.int32)
    onehot = (index_all[:, None] == jnp.arange(grid_size)[None, :]).astype(BF16)
    cond = jnp.dot(onehot, time_table, preferred_element_type=F32)
    d_modulation_own = lax.dynamic_index_in_dim(d_modulation, me, 1, keepdims=False)
    grad_ada = jnp.dot(cond.T, d_modulation_own, precision=highest)
    grad_bias_ada = jnp.sum(d_modulation_own, 0)
    d_cond = jnp.einsum("bic,idc->bd", d_modulation, full_ada.astype(F32), precision=highest)
    table_rows = grid_size // n
    onehot_own = index_all[None, :] == (me * table_rows + jnp.arange(table_rows))[:, None]
    grad_table = jnp.dot(onehot_own.astype(F32), d_cond, precision=highest)
    vector_sums = lax.dynamic_slice_in_dim(vector_sums, me * rows, rows, 1)
    return (
        result,
        returned.astype(F32),
        grad_table,
        grad_ada,
        grad_bias_ada,
        vector_sums[0],
        vector_sums[1],
        grad_qkv,
        grad_proj,
        grad_up,
        grad_bias_up,
        grad_down,
        vector_sums[2],
    )


def solution(mesh):
    in_specs = (
        P(None, "mlp", "seq", None),
        P(None, "mlp", "seq", None),
        P(None, "mlp", "seq"),
        P(None, "mlp"),
        P(None, "mlp"),
        P(),
        P(),
        P(None, "seq"),
        P("seq"),
        P("seq"),
        P("seq"),
        P("seq", None),
        P("seq", None),
        P("seq", "mlp"),
        P("mlp"),
        P("mlp", "seq"),
        P("seq"),
    )
    out_specs = (
        P(None, "mlp", "seq", None),
        P(None, "mlp", "seq", None),
        P("seq", None),
        P(None, "seq"),
        P("seq"),
        P("seq"),
        P("seq"),
        P("seq", None),
        P("seq", None),
        P("seq", "mlp"),
        P("mlp"),
        P("mlp", "seq"),
        P("seq"),
    )
    run = functools.partial(body, n=mesh.shape["seq"], m=mesh.shape["mlp"])
    return jax.shard_map(run, mesh=mesh, in_specs=in_specs, out_specs=out_specs, check_vma=False)
```

```python
import functools
import math

import jax
import jax.numpy as jnp
from jax import lax
from jax.experimental import pallas as pl
from jax.experimental.pallas import tpu as pltpu
from jax.sharding import PartitionSpec as P

HEADS = 12
HEAD = 64
MICRO = 3
PLANES = 4
GROUPS = 4
PER_GROUP = HEADS // GROUPS
WIDTH = PER_GROUP * HEAD
QUERY_BLOCK = 256
SCALING = HEAD ** (-0.5)
BF16 = jnp.bfloat16
F32 = jnp.float32
highest = lax.Precision.HIGHEST
SLOPE = math.sqrt(2.0 / math.pi)
CUBIC = 0.044715

SHIFT_ONE, SCALE_ONE, GATE_ONE, SHIFT_TWO, SCALE_TWO, GATE_TWO, GAIN_ONE, GAIN_TWO, BIAS_DOWN = range(9)
SCALES_ALL, GAINS_ONE, GAINS_TWO = 9, 12, 13

VMEM = pl.BlockSpec(memory_space=pltpu.VMEM)
SMEM = pl.BlockSpec(memory_space=pltpu.SMEM)


def nn(left, right):
    return lax.dot_general(left, right, (((1,), (0,)), ((), ())), preferred_element_type=F32)


def nt(left, right):
    return lax.dot_general(left, right, (((1,), (1,)), ((), ())), preferred_element_type=F32)


def standardize(inputs):
    average = jnp.mean(inputs, -1, keepdims=True)
    centred = inputs - average
    spread = jnp.mean(centred * centred, -1, keepdims=True)
    root = lax.rsqrt(spread + 1e-06)
    return centred * root, root


def pull_norm(d_normed, gains, xhat, root):
    e = d_normed * gains
    return root * (e - jnp.mean(e, -1, keepdims=True) - xhat * jnp.mean(e * xhat, -1, keepdims=True))


def over_tokens(value):
    return jnp.sum(value, 0, keepdims=True)


def shape_of(dims, dtype):
    return jax.ShapeDtypeStruct(dims, dtype)


def call(kernel, name, operands, scalars, outs, scratch=(), us=1.0, far=()):
    moved = sum(math.prod(o.shape) * o.dtype.itemsize for o in list(operands) + list(outs))
    return pl.pallas_call(
        kernel,
        out_shape=list(outs),
        in_specs=[SMEM] * len(scalars) + [pl.BlockSpec(memory_space=pl.ANY)] * len(far) + [VMEM] * len(operands),
        out_specs=[VMEM] * len(outs),
        scratch_shapes=list(scratch),
        compiler_params=pltpu.CompilerParams(vmem_limit_bytes=56 * 1024 * 1024),
        cost_estimate=pl.CostEstimate(flops=int(us * 1e9), bytes_accessed=moved, transcendentals=0),
        name=name,
    )(*scalars, *far, *operands)


def fetch(gathered, chunks, weights, arrived):
    copies = [
        pltpu.make_async_copy(gathered.at[:, chunk], weights.at[at], arrived.at[at])
        for at, chunk in enumerate(chunks)
    ]
    for copy in copies:
        copy.start()
    return copies


def whole(weights, at):
    return weights[at].reshape(weights.shape[1] * weights.shape[2], weights.shape[3])


def group_rows(weights, group, me=None):
    blocks = WIDTH // weights.shape[2]
    if me is not None:
        return jnp.concatenate([weights[0, me ^ (group * blocks + at)] for at in range(blocks)], 0)
    parts = [
        weights[at, pl.ds(group * blocks, blocks)].reshape(WIDTH, weights.shape[3])
        for at in range(weights.shape[0])
    ]
    return parts[0] if len(parts) == 1 else jnp.concatenate(parts, -1)


def modulation(times, table, ada, b_ada, gain_one, gain_two, b_down, mask, small):
    columns = ada.shape[0]
    rows = gain_one.shape[1]
    at = lax.broadcasted_iota(jnp.int32, (8, table.shape[0]), 1)
    line = lax.broadcasted_iota(jnp.int32, (8, table.shape[0]), 0)
    wanted = jnp.where(line == 0, times[0], jnp.where(line == 1, times[1], times[2]))
    cond = nn((at == wanted).astype(F32).astype(BF16), table[...]).astype(BF16)
    part = nt(cond, ada[...]) + b_ada[...].astype(F32)
    small[...] = jnp.zeros_like(small)
    at = 0
    for s in range(MICRO):
        small[0:1, at : at + columns] = part[s : s + 1]
        at += columns
    for ref in (gain_one, gain_two, b_down):
        small[0:1, at : at + rows] = ref[...].astype(F32)
        at += rows
    for s in range(MICRO):
        small[0:1, at : at + mask.shape[1]] = mask[s : s + 1, :].astype(F32)
        at += mask.shape[1]


def prepare_kernel(
    place, times, tokens, upstream, w_qkv, w_up, down, w_proj, table, ada, b_ada, gain_one, gain_two, b_down, mask, *outs
):
    packed, small, outs = outs[0], outs[1], outs[2:]
    columns_out, token_out, upstream_out = outs[: -2 * PLANES], outs[-2 * PLANES : -PLANES], outs[-PLANES:]
    plane, spot = place[0], place[1]
    for d in range(PLANES):
        token_out[d][...] = tokens[jnp.minimum(plane ^ d, MICRO - 1)]
        upstream_out[d][...] = upstream[jnp.minimum(plane ^ d, MICRO - 1)]
    width = w_proj.shape[1]
    by_group = [
        jnp.concatenate([w_qkv[:, p * width + g * WIDTH : p * width + (g + 1) * WIDTH] for p in range(3)], -1)
        for g in range(GROUPS)
    ]
    for e, out in enumerate(columns_out):
        group = (spot ^ e) % GROUPS
        here = by_group[0]
        for g in range(1, GROUPS):
            here = jnp.where(group == g, by_group[g], here)
        out[...] = here
    unit = packed.shape[2]
    chunk = 0
    for value in (w_up[...], down[...], w_proj[...]):
        for at in range(0, value.shape[1], unit):
            packed[chunk] = value[:, at : at + unit]
            chunk += 1
    modulation(times, table, ada, b_ada, gain_one, gain_two, b_down, mask, small)


def vectors_kernel(place, weight_index, weight_grid, small, vectors, scale, line):
    n = small.shape[0]
    width = vectors.shape[1]
    columns, rows, shard = 6 * width // n, width // n, scale.shape[0] // PLANES
    plane, spot = place[0], place[1]
    side = n // PLANES
    me = plane * side + spot
    last = jnp.minimum(plane, MICRO - 1)

    def one_of(three):
        return jnp.where(last == 0, three[0], jnp.where(last == 1, three[1], three[2]))

    def pieces(first, size):
        start = first
        while start < first + size:
            stop = min(first + size, (start // width + 1) * width)
            yield start // width, start % width, start - first, stop - start
            start = stop

    vectors[...] = jnp.zeros_like(vectors)
    for i in range(n):
        here = small[pl.ds(me ^ i, 1), :]
        each = [here[:, s * columns : (s + 1) * columns] for s in range(MICRO)]
        mine = one_of(each)
        for part, column, offset, size in pieces(i * columns, columns):
            vectors[part : part + 1, column : column + size] = mine[:, offset : offset + size]
            if part == SCALE_ONE:
                for s in range(MICRO):
                    vectors[SCALES_ALL + s : SCALES_ALL + s + 1, column : column + size] = each[s][
                        :, offset : offset + size
                    ]
        for row in (GAIN_ONE, GAIN_TWO, BIAS_DOWN):
            start = MICRO * columns + (row - GAIN_ONE) * rows
            vectors[row : row + 1, i * rows : (i + 1) * rows] = here[:, start : start + rows]
    for to, gain, by in ((GAINS_ONE, GAIN_ONE, SCALE_ONE), (GAINS_TWO, GAIN_TWO, SCALE_TWO)):
        vectors[to : to + 1, :] = vectors[gain : gain + 1, :] * (1.0 + vectors[by : by + 1, :])
    line[...] = jnp.zeros_like(line)
    for d in range(PLANES):
        here = small[d * side : d * side + 1, :]
        start = MICRO * (columns + rows)
        three = [here[:, start + s * shard : start + (s + 1) * shard] for s in range(MICRO)]
        line[0:1, d * shard : (d + 1) * shard] = one_of(three)
    weight = jnp.where(plane < MICRO, weight_grid[weight_index[last]], 0.0)
    scale[...] = line[...].T[:, 0:1] * weight


def project_kernel(place, gathered, tokens, vectors, *refs, chunks, slots):
    side = len(refs) - 5
    mixed, (attended, middle, normed, weights, arrived) = refs[:side], refs[side:]
    spot = place[1]
    copies = fetch(gathered, chunks, weights, arrived)
    for copy in copies:
        copy.wait()
    total = jnp.zeros(attended.shape, F32)
    for e in range(side):
        other = spot ^ e
        block = mixed[e][...]
        if side > GROUPS:
            block = jnp.where(other < GROUPS, block, jnp.zeros_like(block))
        total = total + nn(block, group_rows(weights, other % GROUPS, place[2] if slots else None))
    attended[...] = total
    after = tokens[...].astype(F32) + vectors[GATE_ONE : GATE_ONE + 1] * total
    middle[...] = after
    xhat, _ = standardize(after)
    normed[...] = (xhat * vectors[GAINS_TWO : GAINS_TWO + 1] + vectors[SHIFT_TWO : SHIFT_TWO + 1]).astype(BF16)


def feed_kernel(gathered, rows, d_rows, bias, output, d_normed, active, d_hidden, weights, arrived):
    parts = weights.shape[0] // 2
    unit = weights.shape[3]
    order = [at for part in range(parts) for at in (part, parts + part)]
    copies = fetch(gathered, order, weights, arrived)
    out = jnp.zeros(output.shape, F32)
    back = jnp.zeros(output.shape, F32)
    for part in range(parts):
        columns = slice(part * unit, (part + 1) * unit)
        copies[2 * part].wait()
        up = whole(weights, 2 * part)
        u = nn(rows[...], up) + bias[:, columns]
        square = u * u
        bent = jnp.tanh(SLOPE * u * (1.0 + CUBIC * square))
        half = 0.5 * (1.0 + bent)
        on = (u * half).astype(BF16)
        active[:, columns] = on
        slope = half + 0.5 * u * (1.0 - bent * bent) * (SLOPE * (1.0 + 3.0 * CUBIC * square))
        copies[2 * part + 1].wait()
        down = whole(weights, 2 * part + 1)
        d_on = (nn(d_rows[...], down) * slope).astype(BF16)
        d_hidden[:, columns] = d_on
        out = out + nt(on, down)
        back = back + nt(d_on, up)
    output[...] = out.astype(output.dtype)
    d_normed[...] = back.astype(d_normed.dtype)


def scatter_store(refs, me, device, value):
    kept, sent, chunk, slot_of = refs
    distance = me ^ device
    slot = slot_of(distance)

    @pl.when(distance % 2 == 0)
    def _():
        kept[slot, chunk] = value

    @pl.when(distance % 2 == 1)
    def _():
        sent[slot, chunk] = value


def slot_y_first(distance):
    return ((distance >> 1) & 1) * 4 + ((distance >> 2) & 1) * 2 + ((distance >> 3) & 1)


def down_grads_kernel(place, *refs, blocks, scatter):
    d_rows, active, outs = refs[:blocks], refs[blocks : 2 * blocks], refs[2 * blocks :]
    me = place[2]
    width, count = d_rows[0].shape[1], active[0].shape[1]
    unit = min(width, count)
    turned = [ref[...].T for ref in d_rows]
    for chunk in range(count // unit):
        columns = slice(chunk * unit, (chunk + 1) * unit)
        grad = sum(nn(turned[b], active[b][:, columns]) for b in range(blocks)).astype(BF16)
        if scatter:
            rows = outs[0].shape[2]
            for i in range(width // rows):
                part = grad[i * rows : (i + 1) * rows]
                scatter_store((outs[0], outs[1], chunk, slot_y_first), me, i, part)
        else:
            outs[0][:, columns] = grad


def up_grads_kernel(place, *refs, blocks, scatter):
    rows_all, d_hidden, outs = refs[:blocks], refs[blocks : 2 * blocks], refs[2 * blocks :]
    bias = outs[-1]
    me = place[2]
    width, count = rows_all[0].shape[1], bias.shape[1]
    unit = min(width, count)
    turned = [ref[...].T for ref in rows_all]
    for chunk in range(count // unit):
        columns = slice(chunk * unit, (chunk + 1) * unit)
        grad = sum(nn(turned[b], d_hidden[b][:, columns]) for b in range(blocks)).astype(BF16)
        bias[:, columns] = sum(over_tokens(d_hidden[b][:, columns].astype(F32)) for b in range(blocks))
        if scatter:
            rows = outs[0].shape[2]
            for i in range(width // rows):
                part = grad[i * rows : (i + 1) * rows]
                scatter_store((outs[0], outs[1], chunk, slot_y_first), me, i, part)
        else:
            outs[0][:, columns] = grad


def proj_grads_kernel(place, d_attended, *refs, side, scatter):
    mixed, refs = refs[:side], refs[side:]
    spot, me = place[1], place[2]
    width = d_attended.shape[1]
    whole_grad = refs[-1]
    if side > GROUPS:
        whole_grad[...] = jnp.zeros_like(whole_grad)
    for e in range(side):
        other = spot ^ e
        first = pl.multiple_of((other % GROUPS) * WIDTH, WIDTH)
        grad = nn(mixed[e][...].T, d_attended[...]).astype(BF16)
        if side > GROUPS:
            grad = whole_grad[pl.ds(first, WIDTH), :] + jnp.where(other < GROUPS, grad, jnp.zeros_like(grad))
        whole_grad[pl.ds(first, WIDTH), :] = grad
    if not scatter:
        refs[0][...] = whole_grad[...]
        return
    _, _, own, sent, ready, done, _ = refs
    rows, chunk = own.shape[2], own.shape[1] - 1
    for i in range(width // rows):
        part = whole_grad[i * rows : (i + 1) * rows, :]
        scatter_store((ready.at[0], ready.at[1], 0, slot_y_first), me, i, part)
    copies = [
        pltpu.make_async_copy(ready.at[at, :, 0], out.at[:, chunk], done.at[at])
        for at, out in enumerate((own, sent))
    ]
    for copy in copies:
        copy.start()
    for copy in copies:
        copy.wait()


def qkv_grads_kernel(place, d_project, normed, *outs):
    grad = nn(d_project[...], normed[...]).astype(BF16).T
    plane, slice_of = place[0], place[3]
    rows = outs[0].shape[1]
    if len(outs[0].shape) == 3 and outs[0].shape[0] == PLANES:
        for at in range(PLANES):
            distance = plane ^ at
            slot = (distance % 2) * 2 + distance // 2
            halves = [grad[(2 * at + half) * rows : (2 * at + half + 1) * rows] for half in range(2)]
            outs[0][slot] = jnp.where(slice_of == 0, halves[0], halves[1])
            outs[1][slot] = jnp.where(slice_of == 0, halves[1], halves[0])
    else:
        for at in range(PLANES):
            part = grad[at * rows : (at + 1) * rows]
            distance = plane ^ at

            @pl.when(distance % 2 == 0)
            def _():
                outs[0][distance // 2] = part

            @pl.when(distance % 2 == 1)
            def _():
                outs[1][distance // 2] = part


def normed_backward_kernel(d_project, weight, *refs, blocks):
    tokens, (kept, sent, sums) = refs[:blocks], refs[blocks:]
    count = tokens[0].shape[0]
    d_shift = jnp.zeros((1, weight.shape[0]), F32)
    d_xhat = jnp.zeros((1, weight.shape[0]), F32)
    for block in range(blocks):
        part = nt(d_project[:, block * count : (block + 1) * count].T, weight[...])
        (sent if block % 2 else kept)[block // 2] = part.astype(BF16)
        xhat, _ = standardize(tokens[block][...].astype(F32))
        d_shift = d_shift + over_tokens(part)
        d_xhat = d_xhat + over_tokens(part * xhat)
    sums[0:1, :] = d_shift
    sums[1:2, :] = d_xhat
    sums[2:8, :] = jnp.zeros((6, weight.shape[0]), F32)


def middle_kernel(place, gathered, vectors, upstream, scale, attended, middle, d_own, *refs, others, chunks, slots):
    arrived, refs = refs[:others], refs[others:]
    d_mixed, (d_middle, d_attended, sums, weights, copied) = refs[:-5], refs[-5:]
    spot = place[1]
    copies = fetch(gathered, chunks, weights, copied)
    width = middle.shape[1]
    d_normed = d_own[...]
    for ref in arrived:
        d_normed = d_normed + ref[...].astype(F32)
    xhat, root = standardize(middle[...])
    d_result = upstream[...].astype(F32) * scale[...]
    d_after = d_result + pull_norm(d_normed, vectors[GAINS_TWO : GAINS_TWO + 1], xhat, root)
    d_middle[...] = d_after
    low = (vectors[GATE_ONE : GATE_ONE + 1] * d_after).astype(BF16)
    d_attended[...] = low
    for copy in copies:
        copy.wait()
    for e in range(len(d_mixed)):
        rows_here = group_rows(weights, (spot ^ e) % GROUPS, place[2] if slots else None)
        d_mixed[e][...] = nt(low, rows_here).astype(BF16)
    sums[0:1, :] = over_tokens(d_after * attended[...])
    sums[1:2, :] = over_tokens(d_normed)
    sums[2:3, :] = over_tokens(d_normed * xhat)
    sums[3:8, :] = jnp.zeros((5, width), F32)


def output_kernel(vectors, upstream, scale, middle, own, *refs, others):
    arrived, (result, sums) = refs[:others], refs[others:]
    output = own[...] + vectors[BIAS_DOWN : BIAS_DOWN + 1]
    for ref in arrived:
        output = output + ref[...].astype(F32)
    gate = vectors[GATE_TWO : GATE_TWO + 1]
    result[...] = (middle[...] + gate * output).astype(BF16)
    d_result = upstream[...].astype(F32) * scale[...]
    sums[0:1, :] = over_tokens(d_result * output)
    sums[1:2, :] = over_tokens(gate * d_result)
    sums[2:8, :] = jnp.zeros((6, middle.shape[1]), F32)


def tokens_kernel(vectors, tokens, d_middle, own, arrived, d_tokens):
    xhat, root = standardize(tokens[...].astype(F32))
    d_normed = own[...].astype(F32) + arrived[...].astype(F32)
    back = pull_norm(d_normed, vectors[GAINS_ONE : GAINS_ONE + 1], xhat, root)
    d_tokens[...] = (d_middle[...] + back).astype(BF16)


def forward_kernel(place, *refs, blocks, halves):
    tokens, refs = refs[:blocks], refs[blocks:]
    count = 2 if halves else PLANES
    weights, refs = refs[:count], refs[count:]
    (vectors, cosine, sines), refs = refs[:3], refs[3:]
    gain, shift = vectors[GAINS_ONE : GAINS_ONE + 1], vectors[SHIFT_ONE : SHIFT_ONE + 1]
    mixed, refs = refs[:blocks], refs[blocks:]
    heads, log_total, normed, weight, keys, mixed_turned = refs
    plane = place[0]
    rows = weights[0].shape[-2]
    count = tokens[0].shape[0]
    if halves:
        for half in range(2):
            for distance in range(PLANES):
                first = pl.multiple_of((plane ^ distance) * 2 * rows + (place[3] ^ half) * rows, 16)
                weight[pl.ds(first, rows), :] = weights[half][distance]
    else:
        for distance in range(PLANES):
            first = pl.multiple_of((plane ^ distance) * rows, 8)
            weight[pl.ds(first, rows), :] = weights[distance][...]
    for block in range(blocks):
        xhat, _ = standardize(tokens[block][...].astype(F32))
        normed[block * count : (block + 1) * count, :] = (xhat * gain + shift).astype(BF16)
    project = nt(weight[...].T, normed[...])
    cos, sin = cosine[...], sines[...]
    half = HEAD // 2
    for part in range(2):
        for head in range(PER_GROUP):
            start = part * WIDTH + head * HEAD
            first, second = project[start : start + half], project[start + half : start + HEAD]
            turned = jnp.concatenate([first * cos - second * sin, second * cos + first * sin], 0).astype(BF16)
            if part == 0:
                turned = turned * jnp.asarray(SCALING, BF16)
            else:
                keys[head] = turned.T
            heads[start : start + HEAD, :] = turned
    heads[2 * WIDTH :, :] = project[2 * WIDTH :].astype(BF16)
    length = heads.shape[1]
    for head in range(PER_GROUP):
        start = head * HEAD

        def queries_step(step, carry):
            columns = pl.ds(pl.multiple_of(step * QUERY_BLOCK, QUERY_BLOCK), QUERY_BLOCK)
            scores = nn(keys[head], heads[start : start + HEAD, columns])
            peak = jnp.max(scores, 0, keepdims=True)
            exps = jnp.exp(scores - peak)
            total = jnp.sum(exps, 0, keepdims=True)
            log_total[head : head + 1, columns] = peak + jnp.log(total)
            probs = (exps * (1.0 / total)).astype(BF16)
            values = heads[2 * WIDTH + start : 2 * WIDTH + start + HEAD, :]
            mixed_turned[start : start + HEAD, columns] = nn(values, probs).astype(BF16)
            return carry

        lax.fori_loop(0, length // QUERY_BLOCK, queries_step, 0, unroll=True)
    for block in range(blocks):
        mixed[block][...] = mixed_turned[:, block * count : (block + 1) * count].T


def backward_kernel(*refs, blocks):
    d_mixed, refs = refs[:blocks], refs[blocks:]
    (heads, log_total, cosine, sines), refs = refs[:4], refs[4:]
    d_project, d_turned, d_keys, d_values, keys, values = refs
    count = d_mixed[0].shape[0]
    length = heads.shape[1]
    for block in range(blocks):
        d_turned[:, block * count : (block + 1) * count] = d_mixed[block][...].T
    cos, sin = cosine[...], sines[...]
    half = HEAD // 2
    d_keys[...] = jnp.zeros_like(d_keys)
    d_values[...] = jnp.zeros_like(d_values)
    for head in range(PER_GROUP):
        start = head * HEAD
        keys_turned = heads.at[WIDTH + start : WIDTH + start + HEAD]
        keys[...] = keys_turned[...].T
        values[...] = heads[2 * WIDTH + start : 2 * WIDTH + start + HEAD, :].T

        def queries_step(step, carry):
            columns = pl.ds(pl.multiple_of(step * QUERY_BLOCK, QUERY_BLOCK), QUERY_BLOCK)
            queries = heads[start : start + HEAD, columns]
            incoming = d_turned[start : start + HEAD, columns]
            scores = nn(keys[...], queries)
            probs = jnp.exp(scores - log_total[head : head + 1, columns])
            d_probs = nn(values[...], incoming)
            delta = jnp.sum(probs * d_probs, 0, keepdims=True)
            d_scores = (probs * (d_probs - delta)).astype(BF16)
            d_values[start : start + HEAD, :] += nt(incoming, probs.astype(BF16))
            d_keys[start : start + HEAD, :] += nt(queries, d_scores)
            d_queries = nn(keys_turned[...], d_scores) * SCALING
            first, second = d_queries[:half], d_queries[half:]
            cos_here, sin_here = cosine[:, columns], sines[:, columns]
            d_project[start : start + half, columns] = (first * cos_here + second * sin_here).astype(BF16)
            d_project[start + half : start + HEAD, columns] = (second * cos_here - first * sin_here).astype(BF16)
            return carry

        lax.fori_loop(0, length // QUERY_BLOCK, queries_step, 0, unroll=True)
        first, second = d_keys[start : start + half, :], d_keys[start + half : start + HEAD, :]
        d_project[WIDTH + start : WIDTH + start + half, :] = (first * cos + second * sin).astype(BF16)
        d_project[WIDTH + start + half : WIDTH + start + HEAD, :] = (second * cos - first * sin).astype(BF16)
    d_project[2 * WIDTH :, :] = d_values[...].astype(BF16)


def attend_forward(place, tokens, weights, vectors, cosine, sines, halves):
    blocks, (count, width) = len(tokens), tokens[0].shape
    length = blocks * count
    columns = weights[0].shape[-1]
    outs = call(
        functools.partial(forward_kernel, blocks=blocks, halves=halves),
        "attend_forward",
        [*tokens, *weights, vectors, cosine, sines],
        [place],
        [shape_of((count, WIDTH), BF16)] * blocks
        + [
            shape_of((columns, length), BF16),
            shape_of((8, length), F32),
            shape_of((length, width), BF16),
            shape_of((width, columns), BF16),
        ],
        [pltpu.VMEM((PER_GROUP, length, HEAD), BF16), pltpu.VMEM((WIDTH, length), BF16)],
        us=15.0,
    )
    return outs[:blocks], outs[blocks:]


def attend_backward(d_mixed, heads, log_total, cosine, sines):
    blocks, length = len(d_mixed), heads.shape[1]
    (d_project,) = call(
        functools.partial(backward_kernel, blocks=blocks),
        "attend_backward",
        [*d_mixed, heads, log_total, cosine, sines],
        [],
        [shape_of((3 * WIDTH, length), BF16)],
        [
            pltpu.VMEM((WIDTH, length), BF16),
            pltpu.VMEM((WIDTH, length), F32),
            pltpu.VMEM((WIDTH, length), F32),
            pltpu.VMEM((length, HEAD), BF16),
            pltpu.VMEM((length, HEAD), BF16),
        ],
        us=18.0,
    )
    return d_project


def after(values, *others):
    return lax.optimization_barrier((values, others))[0]


def add(left, right):
    return (left.astype(F32) + right.astype(F32)).astype(BF16)


def pick(stack, index):
    return lax.dynamic_index_in_dim(stack, index, 0, keepdims=False)


def bits_of(count):
    return [1 << bit for bit in range(count.bit_length() - 1)]


def body(
    tokens,
    upstream,
    token_mask,
    time_index,
    weight_index,
    time_table,
    weight_grid,
    w_ada,
    b_ada,
    gain_one,
    gain_two,
    w_qkv,
    w_proj,
    w_up,
    b_up,
    w_down,
    b_down,
    *,
    n,
    m,
):
    side = n // PLANES
    me = lax.axis_index("seq")
    plane, spot = me // side, me % side
    slice_of = lax.axis_index("mlp")
    place = jnp.stack([plane, spot, me, slice_of]).astype(jnp.int32)
    shard, width = tokens.shape[2], tokens.shape[3]
    rows = w_qkv.shape[0]
    hidden_count = w_up.shape[1]
    grid_size = time_table.shape[0]
    ada_columns = w_ada.shape[1]
    count = PLANES * shard
    unit = min(width, hidden_count)
    hidden_chunks, width_chunks = hidden_count // unit, width // unit
    pairwise = rows % 16 == 0 and side == GROUPS and unit == width and m == 2
    z_bits, y_bit, core_bit = (2 * side, side), 2, 1

    def swap(value, distance):
        return lax.ppermute(value, "seq", [(i, i ^ distance) for i in range(n)])

    def swap_mlp(value, distance):
        return lax.ppermute(value, "mlp", [(i, i ^ distance) for i in range(m)])

    def between_planes(pieces):
        return [pieces[0]] + [swap(pieces[d], d * side) for d in range(1, PLANES)]

    def in_plane(pieces):
        return [pieces[0]] + [swap(pieces[e], e) for e in range(1, side)]

    def in_order(blocks, axis):
        halves = jnp.stack(blocks)
        for bit in bits_of(len(blocks)):
            here = halves.reshape((len(blocks) // (2 * bit), 2, bit) + halves.shape[1:])
            halves = jnp.where((axis & bit) != 0, here[:, ::-1], here).reshape(halves.shape)
        return halves

    def for_plane(values):
        return [pick(values, jnp.minimum(plane ^ d, MICRO - 1)) for d in range(PLANES)]

    def columns_of(value):
        return [value[:, at : at + unit] for at in range(0, value.shape[1], unit)]

    line = [value[None] for value in (b_ada, gain_one, gain_two, b_down)]
    small_count = -(-MICRO * (ada_columns + rows + shard) // 128) * 128
    first_shapes = [shape_of((2 * hidden_chunks + width_chunks, rows, unit), BF16), shape_of((1, small_count), F32)]
    first_shapes += [shape_of((rows, 3 * WIDTH), BF16)] * side + [shape_of((shard, width), BF16)] * (2 * PLANES)
    packed, small, *pieces = call(
        prepare_kernel,
        "prepare",
        [tokens[:, 0], upstream[:, 0], w_qkv, w_up, w_down.T, w_proj, time_table, w_ada.T, *line, token_mask[:, 0]],
        [place, time_index[:, 0]],
        first_shapes,
        us=4.0,
    )
    group_columns, token_pieces, upstream_pieces = pieces[:side], pieces[side : side + PLANES], pieces[side + PLANES :]

    token_arrived = between_planes(token_pieces)

    received = jnp.stack(after(in_plane(group_columns), token_arrived[1]))
    weight_block = jnp.concatenate([pick(received, spot ^ at) for at in range(side)], 0)
    if pairwise:
        weight_block = pick(weight_block.reshape(2, width // 8, 3 * WIDTH), slice_of)
    weight_blocks = {0: weight_block}
    for bit in (2, 1):
        for known in list(weight_blocks):
            weight_blocks[known | bit] = swap(weight_blocks[known], bit * side)
    weight_blocks = [weight_blocks[at] for at in range(PLANES)]
    far_block = weight_blocks[2]
    own_upstream = between_planes(after(upstream_pieces, weight_blocks[1], weight_blocks[3]))
    if pairwise:
        weight_blocks = jnp.stack(weight_blocks)
        weight_blocks = [weight_blocks, swap_mlp(weight_blocks, 1)]

    for bit in bits_of(n)[:-1]:
        small = jnp.concatenate([small, swap(small, bit)], 0)
    arrived, small = lax.optimization_barrier((token_arrived, after(small, far_block)))
    own_low = jnp.concatenate(arrived, 0)
    token_blocks = {0: own_low}
    for bit in reversed(bits_of(side)):
        for known in list(token_blocks):
            mine = token_blocks[known]
            if bit < side // 2:
                mine = after(mine, token_blocks[side // 2])
            token_blocks[known | bit] = swap(mine, bit)
    token_blocks = [token_blocks[at] for at in range(side)]

    gathered = lax.all_gather(after(packed, token_arrived, far_block), "seq", axis=0)
    if not pairwise:
        gathered = gathered.transpose(1, 0, 2, 3).reshape(-1, GROUPS, WIDTH, unit).transpose(1, 0, 2, 3)
    blocks_shape = (gathered.shape[0],) + gathered.shape[2:]
    proj_chunks = list(range(2 * hidden_chunks, 2 * hidden_chunks + width_chunks))

    def weight_scratch(number):
        return [pltpu.VMEM((number,) + blocks_shape, BF16), pltpu.SemaphoreType.DMA((number,))]

    for bit in bits_of(n)[-1:]:
        small = jnp.concatenate([small, swap(small, bit)], 0)
    vectors, scale = call(
        vectors_kernel,
        "vectors",
        [small],
        [place, weight_index[:, 0], weight_grid],
        [shape_of((16, width), F32), shape_of((count, 1), F32)],
        [pltpu.VMEM((8, count), F32)],
    )

    order = ((plane ^ jnp.arange(PLANES))[None, :] * side + (spot ^ jnp.arange(side))[:, None]) * shard
    positions = (order[:, :, None] + jnp.arange(shard)).reshape(1, -1).astype(F32)
    frequency = 10000.0 ** (-jnp.arange(0, HEAD, 2).astype(F32) / HEAD)
    angles = frequency[:, None] * positions
    cosine, sines = jnp.cos(angles), jnp.sin(angles)

    mixed_blocks, kept = attend_forward(
        after(place, own_upstream), token_blocks, weight_blocks, vectors, cosine, sines, pairwise
    )

    full_ada = lax.all_gather(after(w_ada, gathered), "seq", axis=0)

    mixed_blocks = in_plane(mixed_blocks)

    own_upstream = jnp.concatenate(own_upstream, 0)
    d_rows = ((own_upstream.astype(F32) * scale) * vectors[GATE_TWO][None]).astype(BF16)
    d_rows = [d_rows] + [swap_mlp(d_rows, d) for d in range(1, m)]

    attended, middle, normed_two = call(
        functools.partial(project_kernel, chunks=proj_chunks, slots=False),
        "project",
        [own_low, vectors, *mixed_blocks],
        [place],
        [shape_of((count, width), F32), shape_of((count, width), F32), shape_of((count, width), BF16)],
        weight_scratch(width_chunks),
        us=3.0,
        far=[gathered],
    )
    rows_all = [normed_two] + [swap_mlp(normed_two, d) for d in range(1, m)]
    bias_up = b_up.astype(F32)[None]
    fed = [
        call(
            feed_kernel,
            "feed_forward",
            [rows_all[d], d_rows[d], bias_up],
            [],
            [shape_of((count, width), BF16 if d else F32)] * 2 + [shape_of((count, hidden_count), BF16)] * 2,
            weight_scratch(2 * hidden_chunks),
            us=6.0,
            far=[gathered],
        )
        for d in range(m)
    ]
    d_arrived = [swap_mlp(fed[d][1], d) for d in range(1, m)]
    out_arrived = [swap_mlp(fed[d][0], d) for d in range(1, m)]
    slots = n // 2
    if pairwise:
        down_shapes = [shape_of((slots, hidden_chunks + width_chunks, rows, unit), BF16)] * 2
    else:
        down_shapes = [shape_of((width, hidden_count), BF16)]
    if pairwise:
        up_shapes = [shape_of((slots, hidden_chunks, rows, unit), BF16)] * 2
    else:
        up_shapes = [shape_of((width, hidden_count), BF16)]
    down_grads = call(
        functools.partial(down_grads_kernel, blocks=m, scatter=pairwise),
        "down_gradients",
        [*d_rows, *[f[2] for f in fed]],
        [place],
        down_shapes,
        us=6.0,
    )
    *up_grads, bias_up_sum = call(
        functools.partial(up_grads_kernel, blocks=m, scatter=pairwise),
        "up_gradients",
        [*rows_all, *[f[3] for f in fed]],
        [place],
        up_shapes + [shape_of((1, hidden_count), F32)],
        us=5.0,
    )
    d_arrived, down_grads, full_ada, *up_grads = lax.optimization_barrier(
        (d_arrived, down_grads, full_ada, *up_grads)
    )
    middle_outs = call(
        functools.partial(middle_kernel, others=m - 1, chunks=proj_chunks, slots=False),
        "middle_backward",
        [vectors, own_upstream, scale, attended, middle, fed[0][1], *d_arrived],
        [place],
        [shape_of((count, WIDTH), BF16)] * side
        + [shape_of((count, width), F32), shape_of((count, width), BF16), shape_of((8, width), F32)],
        weight_scratch(width_chunks),
        us=4.0,
        far=[gathered],
    )
    d_mixed_blocks, (d_middle, d_attended, middle_sums) = middle_outs[:side], middle_outs[side:]

    d_mixed_blocks = in_plane(d_mixed_blocks)
    if side > GROUPS:
        share = (spot < GROUPS).astype(BF16)
        d_mixed_blocks = [block * share for block in d_mixed_blocks]

    anywhere = pl.BlockSpec(memory_space=pl.ANY)
    proj_grads = pl.pallas_call(
        functools.partial(proj_grads_kernel, side=side, scatter=pairwise),
        out_shape=down_shapes if pairwise else [shape_of((width, width), BF16)],
        in_specs=[SMEM] + [VMEM] * (1 + side) + ([anywhere] * 2 if pairwise else []),
        out_specs=[anywhere] * 2 if pairwise else [VMEM],
        scratch_shapes=(
            [pltpu.VMEM((2, slots, 1, rows, unit), BF16), pltpu.SemaphoreType.DMA((2,))] if pairwise else []
        )
        + [pltpu.VMEM((width, width), BF16)],
        input_output_aliases={2 + side: 0, 3 + side: 1} if pairwise else {},
        compiler_params=pltpu.CompilerParams(vmem_limit_bytes=56 * 1024 * 1024),
        cost_estimate=pl.CostEstimate(flops=2 * 10**9, bytes_accessed=4 * 10**6, transcendentals=0),
        name="proj_gradients",
    )(place, d_attended, *mixed_blocks, *(down_grads if pairwise else []))

    def add_halves(own, arrived):
        half = own.shape[0] // 2
        return add(own[:half], arrived[:half]), add(own[half:], arrived[half:])

    def back_to_tokens(value, *others):
        received = between_planes([value[d * shard : (d + 1) * shard] for d in range(PLANES)])
        received = after(received, *others) if others else received
        received = jnp.stack(received)
        return jnp.stack([pick(received, plane ^ at) for at in range(MICRO)])[:, None]

    if pairwise:
        up_arrived = swap(up_grads[1], core_bit)
        down_sent, out_arrived, up_arrived = lax.optimization_barrier((proj_grads[1], out_arrived, up_arrived))
        up_own, up_sent = add_halves(up_grads[0], up_arrived)

    result, output_sums = call(
        functools.partial(output_kernel, others=m - 1),
        "output",
        [vectors, own_upstream, scale, middle, fed[0][0], *out_arrived],
        [],
        [shape_of((count, width), BF16), shape_of((8, width), F32)],
    )
    if pairwise:
        up_sent, down_sent, result, *d_mixed_blocks = lax.optimization_barrier(
            (up_sent, down_sent, result, *d_mixed_blocks)
        )
    result = back_to_tokens(result)

    d_project = attend_backward(d_mixed_blocks, kept[0], kept[1], cosine, sines)
    if pairwise:
        up_arrived, down_arrived = swap(up_sent, y_bit), swap(down_sent, core_bit)
        d_project, result, up_arrived, down_arrived = lax.optimization_barrier(
            (d_project, result, up_arrived, down_arrived)
        )
    qkv_shape = (PLANES, width // 8, 3 * WIDTH) if pairwise else (2, width // PLANES, 3 * WIDTH)
    d_kept, d_sent, sums = call(
        functools.partial(normed_backward_kernel, blocks=side),
        "normed_backward",
        [d_project, kept[3], *token_blocks],
        [],
        [shape_of((side // 2, count, width), BF16)] * 2 + [shape_of((8, width), F32)],
        us=2.0,
    )
    arrived = swap(d_sent, 1)
    if pairwise:
        up_own, up_sent = add_halves(up_own, after(up_arrived, d_sent))
        down_own, down_sent = add_halves(proj_grads[0], after(down_arrived, d_sent))
        up_near = swap(up_sent, side)
        arrived = after(arrived, up_sent, down_sent)
    blocks = {2 * at: add(d_kept[at], arrived[at]) for at in range(side // 2)}
    grad_own, grad_sent = call(
        qkv_grads_kernel,
        "qkv_gradients",
        [after(d_project, blocks[2]), kept[2]],
        [place],
        [shape_of(qkv_shape, BF16)] * 2,
        us=4.0,
    )
    if pairwise:
        grad_arrived = swap_mlp(after(grad_sent, up_near), 1)
    bias_up_rows = -(-hidden_count // width)
    bias_up_sum = jnp.pad(bias_up_sum, ((0, 0), (0, bias_up_rows * width - hidden_count)))
    small = jnp.concatenate(
        [sums[0:2], middle_sums[0:3], output_sums[0:2], bias_up_sum.reshape(-1, width)], 0
    )
    small = small + swap(small, 1)
    for bit in bits_of(side)[1:]:
        for at in [at for at in blocks if at & bit]:
            arrived = swap(blocks.pop(at), bit)
            if len(blocks) > 1:
                blocks[at ^ bit] = add(blocks[at ^ bit], arrived)
    if pairwise:
        down_beside = swap(after(down_sent, arrived), y_bit)
        grad_arrived = after(grad_arrived, arrived)
        grad_own, grad_sent = add_halves(grad_own, grad_arrived)
    small = after(small, arrived)
    for bit in bits_of(side)[1:]:
        small = small + swap(small, bit)
    near_arrived = swap(grad_sent, side)
    small = jnp.concatenate([small, vectors[SCALE_TWO][None]], 0)[None]
    for bit in bits_of(PLANES):
        small = jnp.concatenate([small, swap(small, bit * side)], 0)
    (d_tokens,) = call(
        tokens_kernel,
        "tokens_backward",
        [vectors, own_low, d_middle, blocks[0], after(arrived, grad_arrived) if pairwise else arrived],
        [],
        [shape_of((count, width), BF16)],
    )
    if pairwise:
        grad_own, grad_sent = add_halves(grad_own, after(near_arrived, d_tokens))
        far_arrived = swap(grad_sent, 2 * side)
        up_own, up_sent = add_halves(up_own, after(up_near, d_tokens))
        down_own, down_sent = add_halves(down_own, after(down_beside, near_arrived))
        d_tokens = after(d_tokens, grad_sent)
        far_arrived, beside_sent = after(far_arrived, down_sent), down_sent
        down_own, down_sent = add_halves(down_own, after(swap(down_sent, side), far_arrived))
    returned = back_to_tokens(d_tokens, *([beside_sent] if pairwise else []))

    if pairwise:
        up_parts = up_own[0].astype(F32) + swap(after(up_sent, returned), 2 * side)[0].astype(F32)
        grad_up = jnp.concatenate([up_parts[at] for at in range(hidden_chunks)], -1)
        down_parts = down_own[0].astype(F32) + swap(down_sent, 2 * side)[0].astype(F32)
        grad_proj = down_parts[hidden_chunks]
    else:
        grads = jnp.stack(columns_of(up_grads[0]) + columns_of(proj_grads[0]) + columns_of(down_grads[0]))
        grads = grads.reshape(-1, n, rows, unit).transpose(1, 0, 2, 3)
        grads = lax.psum_scatter(grads, "seq", scatter_dimension=0, tiled=True)[0]

        def columns_from(start, number):
            return jnp.concatenate([grads[start + at] for at in range(number)], -1).astype(F32)

        grad_up = columns_from(0, hidden_chunks)
        grad_proj = columns_from(hidden_chunks, width_chunks)
        down_parts = grads[hidden_chunks + width_chunks :].astype(F32)
    for bit in bits_of(m):
        grad_proj = grad_proj + swap_mlp(grad_proj.astype(BF16), bit).astype(F32)

    arrived = near_arrived
    if pairwise:
        arrived = far_arrived
        total = grad_own[0].astype(F32) + arrived[0].astype(F32)
        by_spot = total.astype(BF16).reshape(2, rows, 3 * WIDTH)
        slices = [pick(by_spot, (spot ^ e) % 2) for e in range(side)]
    else:
        arrived = swap(add(grad_own[1], arrived[1]), 2 * side).astype(F32) + arrived[0].astype(F32)
        total = grad_own[0].astype(F32) + arrived
        by_spot = total.astype(BF16).reshape(side, rows, 3 * WIDTH)
        slices = [pick(by_spot, spot ^ e) for e in range(side)]
    received = in_plane(slices)
    received = jnp.stack(after(received, down_sent) if pairwise else received)
    grad_qkv = jnp.stack([pick(received, spot ^ group) for group in range(GROUPS)])
    grad_qkv = grad_qkv.reshape(GROUPS, rows, 3, WIDTH).transpose(1, 2, 0, 3).reshape(rows, 3 * width)
    if pairwise:
        grad_qkv = jnp.where(spot // 2 == slice_of, grad_qkv, swap_mlp(grad_qkv, 1)).astype(F32)
    else:
        grad_qkv = grad_qkv.astype(F32)
        for bit in bits_of(m):
            grad_qkv = grad_qkv + swap_mlp(grad_qkv.astype(BF16), bit).astype(F32)

    grad_down = jnp.concatenate([down_parts[at] for at in range(hidden_chunks)], -1).T

    small = in_order(list(small), plane)[:MICRO]
    grad_bias_up = jnp.sum(small[:, 7 : 7 + bias_up_rows], 0).reshape(-1)[:hidden_count]
    d_shift_one, d_xhat_one, d_gate_one, d_shift_two, d_xhat_two, d_gate_two = [small[:, at] for at in range(6)]
    index_here = time_index[:, 0]
    vector_sums = jnp.stack(
        [
            jnp.sum((1.0 + vectors[SCALES_ALL : SCALES_ALL + MICRO]) * d_xhat_one, 0),
            jnp.sum((1.0 + small[:, -1]) * d_xhat_two, 0),
            jnp.sum(small[:, 6], 0),
            jnp.pad(index_here.astype(F32), (0, width - MICRO)),
        ]
    )
    d_scale_one, d_scale_two = vectors[GAIN_ONE] * d_xhat_one, vectors[GAIN_TWO] * d_xhat_two
    small = jnp.stack([d_shift_one, d_scale_one, d_gate_one, d_shift_two, d_scale_two, d_gate_two], 1)
    small = jnp.concatenate([small.reshape(6 * MICRO, width), vector_sums], 0)[None]
    for bit in bits_of(m):
        small = jnp.concatenate([small, swap_mlp(small, bit)], 0)
    at = 6 * MICRO
    d_modulation = small[:, :at].reshape(m * MICRO, n, ada_columns)
    vector_sums = jnp.sum(small[:, at : at + 3], 0)
    index_all = small[:, at + 3, :MICRO].reshape(-1).astype(jnp.int32)
    onehot = (index_all[:, None] == jnp.arange(grid_size)[None, :]).astype(BF16)
    cond = jnp.dot(onehot, time_table, preferred_element_type=F32)
    d_modulation_own = lax.dynamic_index_in_dim(d_modulation, me, 1, keepdims=False)
    grad_ada = jnp.dot(cond.T, d_modulation_own, precision=highest)
    grad_bias_ada = jnp.sum(d_modulation_own, 0)
    d_cond = jnp.einsum("bic,idc->bd", d_modulation, full_ada.astype(F32), precision=highest)
    table_rows = grid_size // n
    onehot_own = index_all[None, :] == (me * table_rows + jnp.arange(table_rows))[:, None]
    grad_table = jnp.dot(onehot_own.astype(F32), d_cond, precision=highest)
    vector_sums = lax.dynamic_slice_in_dim(vector_sums, me * rows, rows, 1)
    return (
        result,
        returned.astype(F32),
        grad_table,
        grad_ada,
        grad_bias_ada,
        vector_sums[0],
        vector_sums[1],
        grad_qkv,
        grad_proj,
        grad_up,
        grad_bias_up,
        grad_down,
        vector_sums[2],
    )


def solution(mesh):
    in_specs = (
        P(None, "mlp", "seq", None),
        P(None, "mlp", "seq", None),
        P(None, "mlp", "seq"),
        P(None, "mlp"),
        P(None, "mlp"),
        P(),
        P(),
        P(None, "seq"),
        P("seq"),
        P("seq"),
        P("seq"),
        P("seq", None),
        P("seq", None),
        P("seq", "mlp"),
        P("mlp"),
        P("mlp", "seq"),
        P("seq"),
    )
    out_specs = (
        P(None, "mlp", "seq", None),
        P(None, "mlp", "seq", None),
        P("seq", None),
        P(None, "seq"),
        P("seq"),
        P("seq"),
        P("seq"),
        P("seq", None),
        P("seq", None),
        P("seq", "mlp"),
        P("mlp"),
        P("mlp", "seq"),
        P("seq"),
    )
    run = functools.partial(body, n=mesh.shape["seq"], m=mesh.shape["mlp"])
    return jax.shard_map(run, mesh=mesh, in_specs=in_specs, out_specs=out_specs, check_vma=False)
```

```python
import functools
import math

import jax
import jax.numpy as jnp
from jax import lax
from jax.experimental import pallas as pl
from jax.experimental.pallas import tpu as pltpu
from jax.sharding import PartitionSpec as P

HEADS = 12
HEAD = 64
MICRO = 3
PLANES = 4
GROUPS = 4
PER_GROUP = HEADS // GROUPS
WIDTH = PER_GROUP * HEAD
QUERY_BLOCK = 256
SCALING = HEAD ** (-0.5)
BF16 = jnp.bfloat16
F32 = jnp.float32
highest = lax.Precision.HIGHEST
SLOPE = math.sqrt(2.0 / math.pi)
CUBIC = 0.044715

SHIFT_ONE, SCALE_ONE, GATE_ONE, SHIFT_TWO, SCALE_TWO, GATE_TWO, GAIN_ONE, GAIN_TWO, BIAS_DOWN = range(9)
SCALES_ALL, GAINS_ONE, GAINS_TWO = 9, 12, 13

VMEM = pl.BlockSpec(memory_space=pltpu.VMEM)
SMEM = pl.BlockSpec(memory_space=pltpu.SMEM)


def nn(left, right):
    return lax.dot_general(left, right, (((1,), (0,)), ((), ())), preferred_element_type=F32)


def nt(left, right):
    return lax.dot_general(left, right, (((1,), (1,)), ((), ())), preferred_element_type=F32)


def standardize(inputs):
    average = jnp.mean(inputs, -1, keepdims=True)
    centred = inputs - average
    spread = jnp.mean(centred * centred, -1, keepdims=True)
    root = lax.rsqrt(spread + 1e-06)
    return centred * root, root


def pull_norm(d_normed, gains, xhat, root):
    e = d_normed * gains
    return root * (e - jnp.mean(e, -1, keepdims=True) - xhat * jnp.mean(e * xhat, -1, keepdims=True))


def over_tokens(value):
    return jnp.sum(value, 0, keepdims=True)


def shape_of(dims, dtype):
    return jax.ShapeDtypeStruct(dims, dtype)


def call(kernel, name, operands, scalars, outs, scratch=(), us=1.0, far=()):
    moved = sum(math.prod(o.shape) * o.dtype.itemsize for o in list(operands) + list(outs))
    return pl.pallas_call(
        kernel,
        out_shape=list(outs),
        in_specs=[SMEM] * len(scalars) + [pl.BlockSpec(memory_space=pl.ANY)] * len(far) + [VMEM] * len(operands),
        out_specs=[VMEM] * len(outs),
        scratch_shapes=list(scratch),
        compiler_params=pltpu.CompilerParams(vmem_limit_bytes=56 * 1024 * 1024),
        cost_estimate=pl.CostEstimate(flops=int(us * 1e9), bytes_accessed=moved, transcendentals=0),
        name=name,
    )(*scalars, *far, *operands)


def fetch(gathered, chunks, weights, arrived):
    copies = [
        pltpu.make_async_copy(gathered.at[:, chunk], weights.at[at], arrived.at[at])
        for at, chunk in enumerate(chunks)
    ]
    for copy in copies:
        copy.start()
    return copies


def whole(weights, at):
    return weights[at].reshape(weights.shape[1] * weights.shape[2], weights.shape[3])


def group_rows(weights, group, me=None):
    blocks = WIDTH // weights.shape[2]
    if me is not None:
        return jnp.concatenate([weights[0, me ^ (group * blocks + at)] for at in range(blocks)], 0)
    parts = [
        weights[at, pl.ds(group * blocks, blocks)].reshape(WIDTH, weights.shape[3])
        for at in range(weights.shape[0])
    ]
    return parts[0] if len(parts) == 1 else jnp.concatenate(parts, -1)


def modulation(times, table, ada, b_ada, gain_one, gain_two, b_down, mask, small):
    columns = ada.shape[0]
    rows = gain_one.shape[1]
    at = lax.broadcasted_iota(jnp.int32, (8, table.shape[0]), 1)
    line = lax.broadcasted_iota(jnp.int32, (8, table.shape[0]), 0)
    wanted = jnp.where(line == 0, times[0], jnp.where(line == 1, times[1], times[2]))
    cond = nn((at == wanted).astype(F32).astype(BF16), table[...]).astype(BF16)
    part = nt(cond, ada[...]) + b_ada[...].astype(F32)
    small[...] = jnp.zeros_like(small)
    at = 0
    for s in range(MICRO):
        small[0:1, at : at + columns] = part[s : s + 1]
        at += columns
    for ref in (gain_one, gain_two, b_down):
        small[0:1, at : at + rows] = ref[...].astype(F32)
        at += rows
    for s in range(MICRO):
        small[0:1, at : at + mask.shape[1]] = mask[s : s + 1, :].astype(F32)
        at += mask.shape[1]


def prepare_kernel(
    place, times, tokens, upstream, w_qkv, w_up, down, w_proj, table, ada, b_ada, gain_one, gain_two, b_down, mask, *outs
):
    packed, small, outs = outs[0], outs[1], outs[2:]
    columns_out, token_out, upstream_out = outs[: -2 * PLANES], outs[-2 * PLANES : -PLANES], outs[-PLANES:]
    plane, spot = place[0], place[1]
    for d in range(PLANES):
        token_out[d][...] = tokens[jnp.minimum(plane ^ d, MICRO - 1)]
        upstream_out[d][...] = upstream[jnp.minimum(plane ^ d, MICRO - 1)]
    width = w_proj.shape[1]
    by_group = [
        jnp.concatenate([w_qkv[:, p * width + g * WIDTH : p * width + (g + 1) * WIDTH] for p in range(3)], -1)
        for g in range(GROUPS)
    ]
    for e, out in enumerate(columns_out):
        group = (spot ^ e) % GROUPS
        here = by_group[0]
        for g in range(1, GROUPS):
            here = jnp.where(group == g, by_group[g], here)
        out[...] = here
    unit = packed.shape[2]
    chunk = 0
    for value in (w_up[...], down[...], w_proj[...]):
        for at in range(0, value.shape[1], unit):
            packed[chunk] = value[:, at : at + unit]
            chunk += 1
    modulation(times, table, ada, b_ada, gain_one, gain_two, b_down, mask, small)


def vectors_kernel(place, weight_index, weight_grid, small, vectors, scale, line):
    n = small.shape[0]
    width = vectors.shape[1]
    columns, rows, shard = 6 * width // n, width // n, scale.shape[0] // PLANES
    plane, spot = place[0], place[1]
    side = n // PLANES
    me = plane * side + spot
    last = jnp.minimum(plane, MICRO - 1)

    def one_of(three):
        return jnp.where(last == 0, three[0], jnp.where(last == 1, three[1], three[2]))

    def pieces(first, size):
        start = first
        while start < first + size:
            stop = min(first + size, (start // width + 1) * width)
            yield start // width, start % width, start - first, stop - start
            start = stop

    vectors[...] = jnp.zeros_like(vectors)
    for i in range(n):
        here = small[pl.ds(me ^ i, 1), :]
        each = [here[:, s * columns : (s + 1) * columns] for s in range(MICRO)]
        mine = one_of(each)
        for part, column, offset, size in pieces(i * columns, columns):
            vectors[part : part + 1, column : column + size] = mine[:, offset : offset + size]
            if part == SCALE_ONE:
                for s in range(MICRO):
                    vectors[SCALES_ALL + s : SCALES_ALL + s + 1, column : column + size] = each[s][
                        :, offset : offset + size
                    ]
        for row in (GAIN_ONE, GAIN_TWO, BIAS_DOWN):
            start = MICRO * columns + (row - GAIN_ONE) * rows
            vectors[row : row + 1, i * rows : (i + 1) * rows] = here[:, start : start + rows]
    for to, gain, by in ((GAINS_ONE, GAIN_ONE, SCALE_ONE), (GAINS_TWO, GAIN_TWO, SCALE_TWO)):
        vectors[to : to + 1, :] = vectors[gain : gain + 1, :] * (1.0 + vectors[by : by + 1, :])
    line[...] = jnp.zeros_like(line)
    for d in range(PLANES):
        here = small[d * side : d * side + 1, :]
        start = MICRO * (columns + rows)
        three = [here[:, start + s * shard : start + (s + 1) * shard] for s in range(MICRO)]
        line[0:1, d * shard : (d + 1) * shard] = one_of(three)
    weight = jnp.where(plane < MICRO, weight_grid[weight_index[last]], 0.0)
    scale[...] = line[...].T[:, 0:1] * weight


def project_kernel(place, gathered, tokens, vectors, *refs, chunks, slots):
    side = len(refs) - 5
    mixed, (attended, middle, normed, weights, arrived) = refs[:side], refs[side:]
    spot = place[1]
    copies = fetch(gathered, chunks, weights, arrived)
    for copy in copies:
        copy.wait()
    total = jnp.zeros(attended.shape, F32)
    for e in range(side):
        other = spot ^ e
        block = mixed[e][...]
        if side > GROUPS:
            block = jnp.where(other < GROUPS, block, jnp.zeros_like(block))
        total = total + nn(block, group_rows(weights, other % GROUPS, place[2] if slots else None))
    attended[...] = total
    after = tokens[...].astype(F32) + vectors[GATE_ONE : GATE_ONE + 1] * total
    middle[...] = after
    xhat, _ = standardize(after)
    normed[...] = (xhat * vectors[GAINS_TWO : GAINS_TWO + 1] + vectors[SHIFT_TWO : SHIFT_TWO + 1]).astype(BF16)


def feed_kernel(gathered, rows, d_rows, bias, output, d_normed, active, d_hidden, weights, arrived):
    parts = weights.shape[0] // 2
    unit = weights.shape[3]
    order = [at for part in range(parts) for at in (part, parts + part)]
    copies = fetch(gathered, order, weights, arrived)
    out = jnp.zeros(output.shape, F32)
    back = jnp.zeros(output.shape, F32)
    for part in range(parts):
        columns = slice(part * unit, (part + 1) * unit)
        copies[2 * part].wait()
        up = whole(weights, 2 * part)
        u = nn(rows[...], up) + bias[:, columns]
        square = u * u
        bent = jnp.tanh(SLOPE * u * (1.0 + CUBIC * square))
        half = 0.5 * (1.0 + bent)
        on = (u * half).astype(BF16)
        active[:, columns] = on
        slope = half + 0.5 * u * (1.0 - bent * bent) * (SLOPE * (1.0 + 3.0 * CUBIC * square))
        copies[2 * part + 1].wait()
        down = whole(weights, 2 * part + 1)
        d_on = (nn(d_rows[...], down) * slope).astype(BF16)
        d_hidden[:, columns] = d_on
        out = out + nt(on, down)
        back = back + nt(d_on, up)
    output[...] = out.astype(output.dtype)
    d_normed[...] = back.astype(d_normed.dtype)


def scatter_store(refs, me, device, value):
    kept, sent, chunk, slot_of = refs
    distance = me ^ device
    slot = slot_of(distance)

    @pl.when(distance % 2 == 0)
    def _():
        kept[slot, chunk] = value

    @pl.when(distance % 2 == 1)
    def _():
        sent[slot, chunk] = value


def slot_y_first(distance):
    return ((distance >> 1) & 1) * 4 + ((distance >> 2) & 1) * 2 + ((distance >> 3) & 1)


def down_grads_kernel(place, *refs, blocks, scatter):
    d_rows, active, outs = refs[:blocks], refs[blocks : 2 * blocks], refs[2 * blocks :]
    me = place[2]
    width, count = d_rows[0].shape[1], active[0].shape[1]
    unit = min(width, count)
    turned = [ref[...].T for ref in d_rows]
    for chunk in range(count // unit):
        columns = slice(chunk * unit, (chunk + 1) * unit)
        grad = sum(nn(turned[b], active[b][:, columns]) for b in range(blocks)).astype(BF16)
        if scatter:
            rows = outs[0].shape[2]
            for i in range(width // rows):
                part = grad[i * rows : (i + 1) * rows]
                scatter_store((outs[0], outs[1], chunk, slot_y_first), me, i, part)
        else:
            outs[0][:, columns] = grad


def up_grads_kernel(place, *refs, blocks, scatter):
    rows_all, d_hidden, outs = refs[:blocks], refs[blocks : 2 * blocks], refs[2 * blocks :]
    bias = outs[-1]
    me = place[2]
    width, count = rows_all[0].shape[1], bias.shape[1]
    unit = min(width, count)
    turned = [ref[...].T for ref in rows_all]
    for chunk in range(count // unit):
        columns = slice(chunk * unit, (chunk + 1) * unit)
        grad = sum(nn(turned[b], d_hidden[b][:, columns]) for b in range(blocks)).astype(BF16)
        bias[:, columns] = sum(over_tokens(d_hidden[b][:, columns].astype(F32)) for b in range(blocks))
        if scatter:
            rows = outs[0].shape[2]
            for i in range(width // rows):
                part = grad[i * rows : (i + 1) * rows]
                scatter_store((outs[0], outs[1], chunk, slot_y_first), me, i, part)
        else:
            outs[0][:, columns] = grad


def proj_grads_kernel(place, d_attended, *refs, side, scatter):
    mixed, refs = refs[:side], refs[side:]
    spot, me = place[1], place[2]
    width = d_attended.shape[1]
    whole_grad = refs[-1]
    if side > GROUPS:
        whole_grad[...] = jnp.zeros_like(whole_grad)
    for e in range(side):
        other = spot ^ e
        first = pl.multiple_of((other % GROUPS) * WIDTH, WIDTH)
        grad = nn(mixed[e][...].T, d_attended[...]).astype(BF16)
        if side > GROUPS:
            grad = whole_grad[pl.ds(first, WIDTH), :] + jnp.where(other < GROUPS, grad, jnp.zeros_like(grad))
        whole_grad[pl.ds(first, WIDTH), :] = grad
    if not scatter:
        refs[0][...] = whole_grad[...]
        return
    _, _, own, sent, ready, done, _ = refs
    rows, chunk = own.shape[2], own.shape[1] - 1
    for i in range(width // rows):
        part = whole_grad[i * rows : (i + 1) * rows, :]
        scatter_store((ready.at[0], ready.at[1], 0, slot_y_first), me, i, part)
    copies = [
        pltpu.make_async_copy(ready.at[at, :, 0], out.at[:, chunk], done.at[at])
        for at, out in enumerate((own, sent))
    ]
    for copy in copies:
        copy.start()
    for copy in copies:
        copy.wait()


def qkv_grads_kernel(place, d_project, normed, *outs):
    grad = nn(d_project[...], normed[...]).astype(BF16).T
    plane, slice_of = place[0], place[3]
    rows = outs[0].shape[1]
    if len(outs[0].shape) == 3 and outs[0].shape[0] == PLANES:
        for at in range(PLANES):
            distance = plane ^ at
            slot = (distance % 2) * 2 + distance // 2
            halves = [grad[(2 * at + half) * rows : (2 * at + half + 1) * rows] for half in range(2)]
            outs[0][slot] = jnp.where(slice_of == 0, halves[0], halves[1])
            outs[1][slot] = jnp.where(slice_of == 0, halves[1], halves[0])
    else:
        for at in range(PLANES):
            part = grad[at * rows : (at + 1) * rows]
            distance = plane ^ at

            @pl.when(distance % 2 == 0)
            def _():
                outs[0][distance // 2] = part

            @pl.when(distance % 2 == 1)
            def _():
                outs[1][distance // 2] = part


def normed_backward_kernel(d_project, weight, *refs, blocks):
    tokens, (kept, sent, sums) = refs[:blocks], refs[blocks:]
    count = tokens[0].shape[0]
    d_shift = jnp.zeros((1, weight.shape[0]), F32)
    d_xhat = jnp.zeros((1, weight.shape[0]), F32)
    for block in range(blocks):
        part = nt(d_project[:, block * count : (block + 1) * count].T, weight[...])
        (sent if block % 2 else kept)[block // 2] = part.astype(BF16)
        xhat, _ = standardize(tokens[block][...].astype(F32))
        d_shift = d_shift + over_tokens(part)
        d_xhat = d_xhat + over_tokens(part * xhat)
    sums[0:1, :] = d_shift
    sums[1:2, :] = d_xhat
    sums[2:8, :] = jnp.zeros((6, weight.shape[0]), F32)


def middle_kernel(place, gathered, vectors, upstream, scale, attended, middle, d_own, *refs, others, chunks, slots):
    arrived, refs = refs[:others], refs[others:]
    d_mixed, (d_middle, d_attended, sums, weights, copied) = refs[:-5], refs[-5:]
    spot = place[1]
    copies = fetch(gathered, chunks, weights, copied)
    width = middle.shape[1]
    d_normed = d_own[...]
    for ref in arrived:
        d_normed = d_normed + ref[...].astype(F32)
    xhat, root = standardize(middle[...])
    d_result = upstream[...].astype(F32) * scale[...]
    d_after = d_result + pull_norm(d_normed, vectors[GAINS_TWO : GAINS_TWO + 1], xhat, root)
    d_middle[...] = d_after
    low = (vectors[GATE_ONE : GATE_ONE + 1] * d_after).astype(BF16)
    d_attended[...] = low
    for copy in copies:
        copy.wait()
    for e in range(len(d_mixed)):
        rows_here = group_rows(weights, (spot ^ e) % GROUPS, place[2] if slots else None)
        d_mixed[e][...] = nt(low, rows_here).astype(BF16)
    sums[0:1, :] = over_tokens(d_after * attended[...])
    sums[1:2, :] = over_tokens(d_normed)
    sums[2:3, :] = over_tokens(d_normed * xhat)
    sums[3:8, :] = jnp.zeros((5, width), F32)


def output_kernel(vectors, upstream, scale, middle, own, *refs, others):
    arrived, (result, sums) = refs[:others], refs[others:]
    output = own[...] + vectors[BIAS_DOWN : BIAS_DOWN + 1]
    for ref in arrived:
        output = output + ref[...].astype(F32)
    gate = vectors[GATE_TWO : GATE_TWO + 1]
    result[...] = (middle[...] + gate * output).astype(BF16)
    d_result = upstream[...].astype(F32) * scale[...]
    sums[0:1, :] = over_tokens(d_result * output)
    sums[1:2, :] = over_tokens(gate * d_result)
    sums[2:8, :] = jnp.zeros((6, middle.shape[1]), F32)


def tokens_kernel(vectors, tokens, d_middle, own, arrived, d_tokens):
    xhat, root = standardize(tokens[...].astype(F32))
    d_normed = own[...].astype(F32) + arrived[...].astype(F32)
    back = pull_norm(d_normed, vectors[GAINS_ONE : GAINS_ONE + 1], xhat, root)
    d_tokens[...] = (d_middle[...] + back).astype(BF16)


def forward_kernel(place, *refs, blocks, halves):
    tokens, refs = refs[:blocks], refs[blocks:]
    count = 2 if halves else PLANES
    weights, refs = refs[:count], refs[count:]
    (vectors, cosine, sines), refs = refs[:3], refs[3:]
    gain, shift = vectors[GAINS_ONE : GAINS_ONE + 1], vectors[SHIFT_ONE : SHIFT_ONE + 1]
    mixed, refs = refs[:blocks], refs[blocks:]
    heads, log_total, normed, weight, keys, mixed_turned = refs
    plane = place[0]
    rows = weights[0].shape[-2]
    count = tokens[0].shape[0]
    if halves:
        for half in range(2):
            for distance in range(PLANES):
                first = pl.multiple_of((plane ^ distance) * 2 * rows + (place[3] ^ half) * rows, 16)
                weight[pl.ds(first, rows), :] = weights[half][distance]
    else:
        for distance in range(PLANES):
            first = pl.multiple_of((plane ^ distance) * rows, 8)
            weight[pl.ds(first, rows), :] = weights[distance][...]
    for block in range(blocks):
        xhat, _ = standardize(tokens[block][...].astype(F32))
        normed[block * count : (block + 1) * count, :] = (xhat * gain + shift).astype(BF16)
    project = nt(weight[...].T, normed[...])
    cos, sin = cosine[...], sines[...]
    half = HEAD // 2
    for part in range(2):
        for head in range(PER_GROUP):
            start = part * WIDTH + head * HEAD
            first, second = project[start : start + half], project[start + half : start + HEAD]
            turned = jnp.concatenate([first * cos - second * sin, second * cos + first * sin], 0).astype(BF16)
            if part == 0:
                turned = turned * jnp.asarray(SCALING, BF16)
            else:
                keys[head] = turned.T
            heads[start : start + HEAD, :] = turned
    heads[2 * WIDTH :, :] = project[2 * WIDTH :].astype(BF16)
    length = heads.shape[1]
    for head in range(PER_GROUP):
        start = head * HEAD

        def queries_step(step, carry):
            columns = pl.ds(pl.multiple_of(step * QUERY_BLOCK, QUERY_BLOCK), QUERY_BLOCK)
            scores = nn(keys[head], heads[start : start + HEAD, columns])
            peak = jnp.max(scores, 0, keepdims=True)
            exps = jnp.exp(scores - peak)
            total = jnp.sum(exps, 0, keepdims=True)
            log_total[head : head + 1, columns] = peak + jnp.log(total)
            probs = (exps * (1.0 / total)).astype(BF16)
            values = heads[2 * WIDTH + start : 2 * WIDTH + start + HEAD, :]
            mixed_turned[start : start + HEAD, columns] = nn(values, probs).astype(BF16)
            return carry

        lax.fori_loop(0, length // QUERY_BLOCK, queries_step, 0, unroll=True)
    for block in range(blocks):
        mixed[block][...] = mixed_turned[:, block * count : (block + 1) * count].T


def backward_kernel(*refs, blocks):
    d_mixed, refs = refs[:blocks], refs[blocks:]
    (heads, log_total, cosine, sines), refs = refs[:4], refs[4:]
    d_project, d_turned, d_keys, d_values, keys, values = refs
    count = d_mixed[0].shape[0]
    length = heads.shape[1]
    for block in range(blocks):
        d_turned[:, block * count : (block + 1) * count] = d_mixed[block][...].T
    cos, sin = cosine[...], sines[...]
    half = HEAD // 2
    d_keys[...] = jnp.zeros_like(d_keys)
    d_values[...] = jnp.zeros_like(d_values)
    for head in range(PER_GROUP):
        start = head * HEAD
        keys_turned = heads.at[WIDTH + start : WIDTH + start + HEAD]
        keys[...] = keys_turned[...].T
        values[...] = heads[2 * WIDTH + start : 2 * WIDTH + start + HEAD, :].T

        def queries_step(step, carry):
            columns = pl.ds(pl.multiple_of(step * QUERY_BLOCK, QUERY_BLOCK), QUERY_BLOCK)
            queries = heads[start : start + HEAD, columns]
            incoming = d_turned[start : start + HEAD, columns]
            scores = nn(keys[...], queries)
            probs = jnp.exp(scores - log_total[head : head + 1, columns])
            d_probs = nn(values[...], incoming)
            delta = jnp.sum(probs * d_probs, 0, keepdims=True)
            d_scores = (probs * (d_probs - delta)).astype(BF16)
            d_values[start : start + HEAD, :] += nt(incoming, probs.astype(BF16))
            d_keys[start : start + HEAD, :] += nt(queries, d_scores)
            d_queries = nn(keys_turned[...], d_scores) * SCALING
            first, second = d_queries[:half], d_queries[half:]
            cos_here, sin_here = cosine[:, columns], sines[:, columns]
            d_project[start : start + half, columns] = (first * cos_here + second * sin_here).astype(BF16)
            d_project[start + half : start + HEAD, columns] = (second * cos_here - first * sin_here).astype(BF16)
            return carry

        lax.fori_loop(0, length // QUERY_BLOCK, queries_step, 0, unroll=True)
        first, second = d_keys[start : start + half, :], d_keys[start + half : start + HEAD, :]
        d_project[WIDTH + start : WIDTH + start + half, :] = (first * cos + second * sin).astype(BF16)
        d_project[WIDTH + start + half : WIDTH + start + HEAD, :] = (second * cos - first * sin).astype(BF16)
    d_project[2 * WIDTH :, :] = d_values[...].astype(BF16)


def attend_forward(place, tokens, weights, vectors, cosine, sines, halves):
    blocks, (count, width) = len(tokens), tokens[0].shape
    length = blocks * count
    columns = weights[0].shape[-1]
    outs = call(
        functools.partial(forward_kernel, blocks=blocks, halves=halves),
        "attend_forward",
        [*tokens, *weights, vectors, cosine, sines],
        [place],
        [shape_of((count, WIDTH), BF16)] * blocks
        + [
            shape_of((columns, length), BF16),
            shape_of((8, length), F32),
            shape_of((length, width), BF16),
            shape_of((width, columns), BF16),
        ],
        [pltpu.VMEM((PER_GROUP, length, HEAD), BF16), pltpu.VMEM((WIDTH, length), BF16)],
        us=15.0,
    )
    return outs[:blocks], outs[blocks:]


def attend_backward(d_mixed, heads, log_total, cosine, sines):
    blocks, length = len(d_mixed), heads.shape[1]
    (d_project,) = call(
        functools.partial(backward_kernel, blocks=blocks),
        "attend_backward",
        [*d_mixed, heads, log_total, cosine, sines],
        [],
        [shape_of((3 * WIDTH, length), BF16)],
        [
            pltpu.VMEM((WIDTH, length), BF16),
            pltpu.VMEM((WIDTH, length), F32),
            pltpu.VMEM((WIDTH, length), F32),
            pltpu.VMEM((length, HEAD), BF16),
            pltpu.VMEM((length, HEAD), BF16),
        ],
        us=18.0,
    )
    return d_project


def after(values, *others):
    return lax.optimization_barrier((values, others))[0]


def add(left, right):
    return (left.astype(F32) + right.astype(F32)).astype(BF16)


def pick(stack, index):
    return lax.dynamic_index_in_dim(stack, index, 0, keepdims=False)


def bits_of(count):
    return [1 << bit for bit in range(count.bit_length() - 1)]


def body(
    tokens,
    upstream,
    token_mask,
    time_index,
    weight_index,
    time_table,
    weight_grid,
    w_ada,
    b_ada,
    gain_one,
    gain_two,
    w_qkv,
    w_proj,
    w_up,
    b_up,
    w_down,
    b_down,
    *,
    n,
    m,
):
    side = n // PLANES
    me = lax.axis_index("seq")
    plane, spot = me // side, me % side
    slice_of = lax.axis_index("mlp")
    place = jnp.stack([plane, spot, me, slice_of]).astype(jnp.int32)
    shard, width = tokens.shape[2], tokens.shape[3]
    rows = w_qkv.shape[0]
    hidden_count = w_up.shape[1]
    grid_size = time_table.shape[0]
    ada_columns = w_ada.shape[1]
    count = PLANES * shard
    unit = min(width, hidden_count)
    hidden_chunks, width_chunks = hidden_count // unit, width // unit
    pairwise = rows % 16 == 0 and side == GROUPS and unit == width and m == 2
    z_bits, y_bit, core_bit = (2 * side, side), 2, 1

    def swap(value, distance):
        return lax.ppermute(value, "seq", [(i, i ^ distance) for i in range(n)])

    def swap_mlp(value, distance):
        return lax.ppermute(value, "mlp", [(i, i ^ distance) for i in range(m)])

    def between_planes(pieces):
        return [pieces[0]] + [swap(pieces[d], d * side) for d in range(1, PLANES)]

    def in_plane(pieces):
        return [pieces[0]] + [swap(pieces[e], e) for e in range(1, side)]

    def in_order(blocks, axis):
        halves = jnp.stack(blocks)
        for bit in bits_of(len(blocks)):
            here = halves.reshape((len(blocks) // (2 * bit), 2, bit) + halves.shape[1:])
            halves = jnp.where((axis & bit) != 0, here[:, ::-1], here).reshape(halves.shape)
        return halves

    def for_plane(values):
        return [pick(values, jnp.minimum(plane ^ d, MICRO - 1)) for d in range(PLANES)]

    def columns_of(value):
        return [value[:, at : at + unit] for at in range(0, value.shape[1], unit)]

    line = [value[None] for value in (b_ada, gain_one, gain_two, b_down)]
    small_count = -(-MICRO * (ada_columns + rows + shard) // 128) * 128
    first_shapes = [shape_of((2 * hidden_chunks + width_chunks, rows, unit), BF16), shape_of((1, small_count), F32)]
    first_shapes += [shape_of((rows, 3 * WIDTH), BF16)] * side + [shape_of((shard, width), BF16)] * (2 * PLANES)
    packed, small, *pieces = call(
        prepare_kernel,
        "prepare",
        [tokens[:, 0], upstream[:, 0], w_qkv, w_up, w_down.T, w_proj, time_table, w_ada.T, *line, token_mask[:, 0]],
        [place, time_index[:, 0]],
        first_shapes,
        us=4.0,
    )
    group_columns, token_pieces, upstream_pieces = pieces[:side], pieces[side : side + PLANES], pieces[side + PLANES :]

    token_arrived = between_planes(token_pieces)

    received = jnp.stack(after(in_plane(group_columns), token_arrived[1]))
    weight_block = jnp.concatenate([pick(received, spot ^ at) for at in range(side)], 0)
    if pairwise:
        weight_block = pick(weight_block.reshape(2, width // 8, 3 * WIDTH), slice_of)
    weight_blocks = {0: weight_block}
    for bit in (2, 1):
        for known in list(weight_blocks):
            weight_blocks[known | bit] = swap(weight_blocks[known], bit * side)
    weight_blocks = [weight_blocks[at] for at in range(PLANES)]
    far_block = weight_blocks[2]
    own_upstream = between_planes(after(upstream_pieces, weight_blocks[1], weight_blocks[3]))
    if pairwise:
        weight_blocks = jnp.stack(weight_blocks)
        weight_blocks = [weight_blocks, swap_mlp(weight_blocks, 1)]

    for bit in bits_of(n)[:-1]:
        small = jnp.concatenate([small, swap(small, bit)], 0)
    arrived, small = lax.optimization_barrier((token_arrived, after(small, far_block)))
    own_low = jnp.concatenate(arrived, 0)
    token_blocks = {0: own_low}
    for bit in reversed(bits_of(side)):
        for known in list(token_blocks):
            mine = token_blocks[known]
            if bit < side // 2:
                mine = after(mine, token_blocks[side // 2])
            token_blocks[known | bit] = swap(mine, bit)
    token_blocks = [token_blocks[at] for at in range(side)]

    gathered = lax.all_gather(after(packed, token_arrived, far_block), "seq", axis=0)
    if not pairwise:
        gathered = gathered.transpose(1, 0, 2, 3).reshape(-1, GROUPS, WIDTH, unit).transpose(1, 0, 2, 3)
    blocks_shape = (gathered.shape[0],) + gathered.shape[2:]
    proj_chunks = list(range(2 * hidden_chunks, 2 * hidden_chunks + width_chunks))

    def weight_scratch(number):
        return [pltpu.VMEM((number,) + blocks_shape, BF16), pltpu.SemaphoreType.DMA((number,))]

    for bit in bits_of(n)[-1:]:
        small = jnp.concatenate([small, swap(small, bit)], 0)
    vectors, scale = call(
        vectors_kernel,
        "vectors",
        [small],
        [place, weight_index[:, 0], weight_grid],
        [shape_of((16, width), F32), shape_of((count, 1), F32)],
        [pltpu.VMEM((8, count), F32)],
    )

    order = ((plane ^ jnp.arange(PLANES))[None, :] * side + (spot ^ jnp.arange(side))[:, None]) * shard
    positions = (order[:, :, None] + jnp.arange(shard)).reshape(1, -1).astype(F32)
    frequency = 10000.0 ** (-jnp.arange(0, HEAD, 2).astype(F32) / HEAD)
    angles = frequency[:, None] * positions
    cosine, sines = jnp.cos(angles), jnp.sin(angles)

    mixed_blocks, kept = attend_forward(
        after(place, own_upstream), token_blocks, weight_blocks, vectors, cosine, sines, pairwise
    )

    full_ada = lax.all_gather(after(w_ada, gathered), "seq", axis=0)

    mixed_blocks = in_plane(mixed_blocks)

    own_upstream = jnp.concatenate(own_upstream, 0)
    d_rows = ((own_upstream.astype(F32) * scale) * vectors[GATE_TWO][None]).astype(BF16)
    d_rows = [d_rows] + [swap_mlp(d_rows, d) for d in range(1, m)]

    attended, middle, normed_two = call(
        functools.partial(project_kernel, chunks=proj_chunks, slots=False),
        "project",
        [own_low, vectors, *mixed_blocks],
        [place],
        [shape_of((count, width), F32), shape_of((count, width), F32), shape_of((count, width), BF16)],
        weight_scratch(width_chunks),
        us=3.0,
        far=[gathered],
    )
    rows_all = [normed_two] + [swap_mlp(normed_two, d) for d in range(1, m)]
    bias_up = b_up.astype(F32)[None]
    fed = [
        call(
            feed_kernel,
            "feed_forward",
            [rows_all[d], d_rows[d], bias_up],
            [],
            [shape_of((count, width), BF16 if d else F32)] * 2 + [shape_of((count, hidden_count), BF16)] * 2,
            weight_scratch(2 * hidden_chunks),
            us=6.0,
            far=[gathered],
        )
        for d in range(m)
    ]
    d_arrived = [swap_mlp(fed[d][1], d) for d in range(1, m)]
    out_arrived = [swap_mlp(fed[d][0], d) for d in range(1, m)]
    slots = n // 2
    if pairwise:
        down_shapes = [shape_of((slots, hidden_chunks + width_chunks, rows, unit), BF16)] * 2
    else:
        down_shapes = [shape_of((width, hidden_count), BF16)]
    if pairwise:
        up_shapes = [shape_of((slots, hidden_chunks, rows, unit), BF16)] * 2
    else:
        up_shapes = [shape_of((width, hidden_count), BF16)]
    down_grads = call(
        functools.partial(down_grads_kernel, blocks=m, scatter=pairwise),
        "down_gradients",
        [*d_rows, *[f[2] for f in fed]],
        [place],
        down_shapes,
        us=6.0,
    )
    *up_grads, bias_up_sum = call(
        functools.partial(up_grads_kernel, blocks=m, scatter=pairwise),
        "up_gradients",
        [*rows_all, *[f[3] for f in fed]],
        [place],
        up_shapes + [shape_of((1, hidden_count), F32)],
        us=5.0,
    )
    d_arrived, down_grads, full_ada, *up_grads = lax.optimization_barrier(
        (d_arrived, down_grads, full_ada, *up_grads)
    )
    middle_outs = call(
        functools.partial(middle_kernel, others=m - 1, chunks=proj_chunks, slots=False),
        "middle_backward",
        [vectors, own_upstream, scale, attended, middle, fed[0][1], *d_arrived],
        [place],
        [shape_of((count, WIDTH), BF16)] * side
        + [shape_of((count, width), F32), shape_of((count, width), BF16), shape_of((8, width), F32)],
        weight_scratch(width_chunks),
        us=4.0,
        far=[gathered],
    )
    d_mixed_blocks, (d_middle, d_attended, middle_sums) = middle_outs[:side], middle_outs[side:]

    d_mixed_blocks = in_plane(d_mixed_blocks)
    if side > GROUPS:
        share = (spot < GROUPS).astype(BF16)
        d_mixed_blocks = [block * share for block in d_mixed_blocks]

    anywhere = pl.BlockSpec(memory_space=pl.ANY)
    proj_grads = pl.pallas_call(
        functools.partial(proj_grads_kernel, side=side, scatter=pairwise),
        out_shape=down_shapes if pairwise else [shape_of((width, width), BF16)],
        in_specs=[SMEM] + [VMEM] * (1 + side) + ([anywhere] * 2 if pairwise else []),
        out_specs=[anywhere] * 2 if pairwise else [VMEM],
        scratch_shapes=(
            [pltpu.VMEM((2, slots, 1, rows, unit), BF16), pltpu.SemaphoreType.DMA((2,))] if pairwise else []
        )
        + [pltpu.VMEM((width, width), BF16)],
        input_output_aliases={2 + side: 0, 3 + side: 1} if pairwise else {},
        compiler_params=pltpu.CompilerParams(vmem_limit_bytes=56 * 1024 * 1024),
        cost_estimate=pl.CostEstimate(flops=2 * 10**9, bytes_accessed=4 * 10**6, transcendentals=0),
        name="proj_gradients",
    )(place, d_attended, *mixed_blocks, *(down_grads if pairwise else []))

    def add_halves(own, arrived):
        half = own.shape[0] // 2
        return add(own[:half], arrived[:half]), add(own[half:], arrived[half:])

    def back_to_tokens(value, *others):
        received = between_planes([value[d * shard : (d + 1) * shard] for d in range(PLANES)])
        received = after(received, *others) if others else received
        received = jnp.stack(received)
        return jnp.stack([pick(received, plane ^ at) for at in range(MICRO)])[:, None]

    if pairwise:
        up_arrived = swap(up_grads[1], core_bit)
        down_sent, out_arrived, up_arrived = lax.optimization_barrier((proj_grads[1], out_arrived, up_arrived))
        up_own, up_sent = add_halves(up_grads[0], up_arrived)

    result, output_sums = call(
        functools.partial(output_kernel, others=m - 1),
        "output",
        [vectors, own_upstream, scale, middle, fed[0][0], *out_arrived],
        [],
        [shape_of((count, width), BF16), shape_of((8, width), F32)],
    )
    if pairwise:
        up_sent, down_sent, result, *d_mixed_blocks = lax.optimization_barrier(
            (up_sent, down_sent, result, *d_mixed_blocks)
        )
    result = back_to_tokens(result)

    d_project = attend_backward(d_mixed_blocks, kept[0], kept[1], cosine, sines)
    if pairwise:
        up_arrived, down_arrived = swap(up_sent, y_bit), swap(down_sent, core_bit)
        d_project, result, up_arrived, down_arrived = lax.optimization_barrier(
            (d_project, result, up_arrived, down_arrived)
        )
    qkv_shape = (PLANES, width // 8, 3 * WIDTH) if pairwise else (2, width // PLANES, 3 * WIDTH)
    d_kept, d_sent, sums = call(
        functools.partial(normed_backward_kernel, blocks=side),
        "normed_backward",
        [d_project, kept[3], *token_blocks],
        [],
        [shape_of((side // 2, count, width), BF16)] * 2 + [shape_of((8, width), F32)],
        us=2.0,
    )
    arrived = swap(d_sent, 1)
    if pairwise:
        up_own, up_sent = add_halves(up_own, after(up_arrived, d_sent))
        down_own, down_sent = add_halves(proj_grads[0], after(down_arrived, d_sent))
        up_near = swap(up_sent, side)
        arrived = after(arrived, up_sent, down_sent)
    blocks = {2 * at: add(d_kept[at], arrived[at]) for at in range(side // 2)}
    grad_own, grad_sent = call(
        qkv_grads_kernel,
        "qkv_gradients",
        [after(d_project, blocks[2]), kept[2]],
        [place],
        [shape_of(qkv_shape, BF16)] * 2,
        us=4.0,
    )
    if pairwise:
        grad_arrived = swap_mlp(after(grad_sent, up_near), 1)
    bias_up_rows = -(-hidden_count // width)
    bias_up_sum = jnp.pad(bias_up_sum, ((0, 0), (0, bias_up_rows * width - hidden_count)))
    small = jnp.concatenate(
        [sums[0:2], middle_sums[0:3], output_sums[0:2], bias_up_sum.reshape(-1, width)], 0
    )
    small = small + swap(small, 1)
    for bit in bits_of(side)[1:]:
        for at in [at for at in blocks if at & bit]:
            arrived = swap(blocks.pop(at), bit)
            if len(blocks) > 1:
                blocks[at ^ bit] = add(blocks[at ^ bit], arrived)
    if pairwise:
        down_beside = swap(after(down_sent, arrived), y_bit)
        grad_arrived = after(grad_arrived, arrived)
        grad_own, grad_sent = add_halves(grad_own, grad_arrived)
    small = after(small, arrived)
    for bit in bits_of(side)[1:]:
        small = small + swap(small, bit)
    near_arrived = swap(grad_sent, side)
    small = jnp.concatenate([small, vectors[SCALE_TWO][None]], 0)[None]
    for bit in bits_of(PLANES):
        small = jnp.concatenate([small, swap(small, bit * side)], 0)
    (d_tokens,) = call(
        tokens_kernel,
        "tokens_backward",
        [vectors, own_low, d_middle, blocks[0], after(arrived, grad_arrived) if pairwise else arrived],
        [],
        [shape_of((count, width), BF16)],
    )
    if pairwise:
        grad_own, grad_sent = add_halves(grad_own, after(near_arrived, d_tokens))
        far_arrived = swap(grad_sent, 2 * side)
        up_own, up_sent = add_halves(up_own, after(up_near, d_tokens))
        down_own, down_sent = add_halves(down_own, after(down_beside, near_arrived))
        d_tokens = after(d_tokens, grad_sent)
        far_arrived, beside_sent = after(far_arrived, down_sent), down_sent
        far_done = far_arrived
        down_own, down_sent = add_halves(down_own, after(swap(down_sent, side), far_arrived))
    returned = back_to_tokens(d_tokens, *([beside_sent] if pairwise else []))

    if pairwise:
        up_parts = up_own[0].astype(F32) + after(swap(after(up_sent, far_done), 2 * side), down_sent)[0].astype(F32)
        grad_up = jnp.concatenate([up_parts[at] for at in range(hidden_chunks)], -1)
        down_parts = down_own[0].astype(F32) + swap(down_sent, 2 * side)[0].astype(F32)
        grad_proj = down_parts[hidden_chunks]
    else:
        grads = jnp.stack(columns_of(up_grads[0]) + columns_of(proj_grads[0]) + columns_of(down_grads[0]))
        grads = grads.reshape(-1, n, rows, unit).transpose(1, 0, 2, 3)
        grads = lax.psum_scatter(grads, "seq", scatter_dimension=0, tiled=True)[0]

        def columns_from(start, number):
            return jnp.concatenate([grads[start + at] for at in range(number)], -1).astype(F32)

        grad_up = columns_from(0, hidden_chunks)
        grad_proj = columns_from(hidden_chunks, width_chunks)
        down_parts = grads[hidden_chunks + width_chunks :].astype(F32)
    for bit in bits_of(m):
        grad_proj = grad_proj + swap_mlp(grad_proj.astype(BF16), bit).astype(F32)

    arrived = near_arrived
    if pairwise:
        arrived = far_arrived
        total = grad_own[0].astype(F32) + arrived[0].astype(F32)
        by_spot = total.astype(BF16).reshape(2, rows, 3 * WIDTH)
        slices = [pick(by_spot, (spot ^ e) % 2) for e in range(side)]
    else:
        arrived = swap(add(grad_own[1], arrived[1]), 2 * side).astype(F32) + arrived[0].astype(F32)
        total = grad_own[0].astype(F32) + arrived
        by_spot = total.astype(BF16).reshape(side, rows, 3 * WIDTH)
        slices = [pick(by_spot, spot ^ e) for e in range(side)]
    received = in_plane(slices)
    received = jnp.stack(after(received, down_sent) if pairwise else received)
    grad_qkv = jnp.stack([pick(received, spot ^ group) for group in range(GROUPS)])
    grad_qkv = grad_qkv.reshape(GROUPS, rows, 3, WIDTH).transpose(1, 2, 0, 3).reshape(rows, 3 * width)
    if pairwise:
        grad_qkv = jnp.where(spot // 2 == slice_of, grad_qkv, swap_mlp(grad_qkv, 1)).astype(F32)
    else:
        grad_qkv = grad_qkv.astype(F32)
        for bit in bits_of(m):
            grad_qkv = grad_qkv + swap_mlp(grad_qkv.astype(BF16), bit).astype(F32)

    grad_down = jnp.concatenate([down_parts[at] for at in range(hidden_chunks)], -1).T

    small = in_order(list(small), plane)[:MICRO]
    grad_bias_up = jnp.sum(small[:, 7 : 7 + bias_up_rows], 0).reshape(-1)[:hidden_count]
    d_shift_one, d_xhat_one, d_gate_one, d_shift_two, d_xhat_two, d_gate_two = [small[:, at] for at in range(6)]
    index_here = time_index[:, 0]
    vector_sums = jnp.stack(
        [
            jnp.sum((1.0 + vectors[SCALES_ALL : SCALES_ALL + MICRO]) * d_xhat_one, 0),
            jnp.sum((1.0 + small[:, -1]) * d_xhat_two, 0),
            jnp.sum(small[:, 6], 0),
            jnp.pad(index_here.astype(F32), (0, width - MICRO)),
        ]
    )
    d_scale_one, d_scale_two = vectors[GAIN_ONE] * d_xhat_one, vectors[GAIN_TWO] * d_xhat_two
    small = jnp.stack([d_shift_one, d_scale_one, d_gate_one, d_shift_two, d_scale_two, d_gate_two], 1)
    small = jnp.concatenate([small.reshape(6 * MICRO, width), vector_sums], 0)[None]
    for bit in bits_of(m):
        small = jnp.concatenate([small, swap_mlp(small, bit)], 0)
    small = after(small, grad_sent) if pairwise else small
    at = 6 * MICRO
    d_modulation = small[:, :at].reshape(m * MICRO, n, ada_columns)
    vector_sums = jnp.sum(small[:, at : at + 3], 0)
    index_all = small[:, at + 3, :MICRO].reshape(-1).astype(jnp.int32)
    onehot = (index_all[:, None] == jnp.arange(grid_size)[None, :]).astype(BF16)
    cond = jnp.dot(onehot, time_table, preferred_element_type=F32)
    d_modulation_own = lax.dynamic_index_in_dim(d_modulation, me, 1, keepdims=False)
    grad_ada = jnp.dot(cond.T, d_modulation_own, precision=highest)
    grad_bias_ada = jnp.sum(d_modulation_own, 0)
    d_cond = jnp.einsum("bic,idc->bd", d_modulation, full_ada.astype(F32), precision=highest)
    table_rows = grid_size // n
    onehot_own = index_all[None, :] == (me * table_rows + jnp.arange(table_rows))[:, None]
    grad_table = jnp.dot(onehot_own.astype(F32), d_cond, precision=highest)
    vector_sums = lax.dynamic_slice_in_dim(vector_sums, me * rows, rows, 1)
    return (
        result,
        returned.astype(F32),
        grad_table,
        grad_ada,
        grad_bias_ada,
        vector_sums[0],
        vector_sums[1],
        grad_qkv,
        grad_proj,
        grad_up,
        grad_bias_up,
        grad_down,
        vector_sums[2],
    )


def solution(mesh):
    in_specs = (
        P(None, "mlp", "seq", None),
        P(None, "mlp", "seq", None),
        P(None, "mlp", "seq"),
        P(None, "mlp"),
        P(None, "mlp"),
        P(),
        P(),
        P(None, "seq"),
        P("seq"),
        P("seq"),
        P("seq"),
        P("seq", None),
        P("seq", None),
        P("seq", "mlp"),
        P("mlp"),
        P("mlp", "seq"),
        P("seq"),
    )
    out_specs = (
        P(None, "mlp", "seq", None),
        P(None, "mlp", "seq", None),
        P("seq", None),
        P(None, "seq"),
        P("seq"),
        P("seq"),
        P("seq"),
        P("seq", None),
        P("seq", None),
        P("seq", "mlp"),
        P("mlp"),
        P("mlp", "seq"),
        P("seq"),
    )
    run = functools.partial(body, n=mesh.shape["seq"], m=mesh.shape["mlp"])
    return jax.shard_map(run, mesh=mesh, in_specs=in_specs, out_specs=out_specs, check_vma=False)
```

```python
import functools
import math

import jax
import jax.numpy as jnp
from jax import lax
from jax.experimental import pallas as pl
from jax.experimental.pallas import tpu as pltpu
from jax.sharding import PartitionSpec as P

HEADS = 12
HEAD = 64
MICRO = 3
PLANES = 4
GROUPS = 4
PER_GROUP = HEADS // GROUPS
WIDTH = PER_GROUP * HEAD
QUERY_BLOCK = 256
SCALING = HEAD ** (-0.5)
BF16 = jnp.bfloat16
F32 = jnp.float32
highest = lax.Precision.HIGHEST
SLOPE = math.sqrt(2.0 / math.pi)
CUBIC = 0.044715

SHIFT_ONE, SCALE_ONE, GATE_ONE, SHIFT_TWO, SCALE_TWO, GATE_TWO, GAIN_ONE, GAIN_TWO, BIAS_DOWN = range(9)
SCALES_ALL, GAINS_ONE, GAINS_TWO = 9, 12, 13

VMEM = pl.BlockSpec(memory_space=pltpu.VMEM)
SMEM = pl.BlockSpec(memory_space=pltpu.SMEM)


def nn(left, right):
    return lax.dot_general(left, right, (((1,), (0,)), ((), ())), preferred_element_type=F32)


def nt(left, right):
    return lax.dot_general(left, right, (((1,), (1,)), ((), ())), preferred_element_type=F32)


def standardize(inputs):
    average = jnp.mean(inputs, -1, keepdims=True)
    centred = inputs - average
    spread = jnp.mean(centred * centred, -1, keepdims=True)
    root = lax.rsqrt(spread + 1e-06)
    return centred * root, root


def pull_norm(d_normed, gains, xhat, root):
    e = d_normed * gains
    return root * (e - jnp.mean(e, -1, keepdims=True) - xhat * jnp.mean(e * xhat, -1, keepdims=True))


def over_tokens(value):
    return jnp.sum(value, 0, keepdims=True)


def shape_of(dims, dtype):
    return jax.ShapeDtypeStruct(dims, dtype)


def call(kernel, name, operands, scalars, outs, scratch=(), us=1.0, far=()):
    moved = sum(math.prod(o.shape) * o.dtype.itemsize for o in list(operands) + list(outs))
    return pl.pallas_call(
        kernel,
        out_shape=list(outs),
        in_specs=[SMEM] * len(scalars) + [pl.BlockSpec(memory_space=pl.ANY)] * len(far) + [VMEM] * len(operands),
        out_specs=[VMEM] * len(outs),
        scratch_shapes=list(scratch),
        compiler_params=pltpu.CompilerParams(vmem_limit_bytes=56 * 1024 * 1024),
        cost_estimate=pl.CostEstimate(flops=int(us * 1e9), bytes_accessed=moved, transcendentals=0),
        name=name,
    )(*scalars, *far, *operands)


def fetch(gathered, chunks, weights, arrived):
    copies = [
        pltpu.make_async_copy(gathered.at[:, chunk], weights.at[at], arrived.at[at])
        for at, chunk in enumerate(chunks)
    ]
    for copy in copies:
        copy.start()
    return copies


def whole(weights, at):
    return weights[at].reshape(weights.shape[1] * weights.shape[2], weights.shape[3])


def group_rows(weights, group, me=None):
    blocks = WIDTH // weights.shape[2]
    if me is not None:
        return jnp.concatenate([weights[0, me ^ (group * blocks + at)] for at in range(blocks)], 0)
    parts = [
        weights[at, pl.ds(group * blocks, blocks)].reshape(WIDTH, weights.shape[3])
        for at in range(weights.shape[0])
    ]
    return parts[0] if len(parts) == 1 else jnp.concatenate(parts, -1)


def modulation(times, table, ada, b_ada, gain_one, gain_two, b_down, mask, small):
    columns = ada.shape[0]
    rows = gain_one.shape[1]
    at = lax.broadcasted_iota(jnp.int32, (8, table.shape[0]), 1)
    line = lax.broadcasted_iota(jnp.int32, (8, table.shape[0]), 0)
    wanted = jnp.where(line == 0, times[0], jnp.where(line == 1, times[1], times[2]))
    cond = nn((at == wanted).astype(F32).astype(BF16), table[...]).astype(BF16)
    part = nt(cond, ada[...]) + b_ada[...].astype(F32)
    small[...] = jnp.zeros_like(small)
    at = 0
    for s in range(MICRO):
        small[0:1, at : at + columns] = part[s : s + 1]
        at += columns
    for ref in (gain_one, gain_two, b_down):
        small[0:1, at : at + rows] = ref[...].astype(F32)
        at += rows
    for s in range(MICRO):
        small[0:1, at : at + mask.shape[1]] = mask[s : s + 1, :].astype(F32)
        at += mask.shape[1]


def prepare_kernel(
    place, times, tokens, upstream, w_qkv, w_up, down, w_proj, table, ada, b_ada, gain_one, gain_two, b_down, mask, *outs
):
    packed, small, outs = outs[0], outs[1], outs[2:]
    columns_out, token_out, upstream_out = outs[: -2 * PLANES], outs[-2 * PLANES : -PLANES], outs[-PLANES:]
    plane, spot = place[0], place[1]
    for d in range(PLANES):
        token_out[d][...] = tokens[jnp.minimum(plane ^ d, MICRO - 1)]
        upstream_out[d][...] = upstream[jnp.minimum(plane ^ d, MICRO - 1)]
    width = w_proj.shape[1]
    by_group = [
        jnp.concatenate([w_qkv[:, p * width + g * WIDTH : p * width + (g + 1) * WIDTH] for p in range(3)], -1)
        for g in range(GROUPS)
    ]
    for e, out in enumerate(columns_out):
        group = (spot ^ e) % GROUPS
        here = by_group[0]
        for g in range(1, GROUPS):
            here = jnp.where(group == g, by_group[g], here)
        out[...] = here
    unit = packed.shape[2]
    chunk = 0
    for value in (w_up[...], down[...], w_proj[...]):
        for at in range(0, value.shape[1], unit):
            packed[chunk] = value[:, at : at + unit]
            chunk += 1
    modulation(times, table, ada, b_ada, gain_one, gain_two, b_down, mask, small)


def vectors_kernel(place, weight_index, weight_grid, small, vectors, scale, line):
    n = small.shape[0]
    width = vectors.shape[1]
    columns, rows, shard = 6 * width // n, width // n, scale.shape[0] // PLANES
    plane, spot = place[0], place[1]
    side = n // PLANES
    me = plane * side + spot
    last = jnp.minimum(plane, MICRO - 1)

    def one_of(three):
        return jnp.where(last == 0, three[0], jnp.where(last == 1, three[1], three[2]))

    def pieces(first, size):
        start = first
        while start < first + size:
            stop = min(first + size, (start // width + 1) * width)
            yield start // width, start % width, start - first, stop - start
            start = stop

    vectors[...] = jnp.zeros_like(vectors)
    for i in range(n):
        here = small[pl.ds(me ^ i, 1), :]
        each = [here[:, s * columns : (s + 1) * columns] for s in range(MICRO)]
        mine = one_of(each)
        for part, column, offset, size in pieces(i * columns, columns):
            vectors[part : part + 1, column : column + size] = mine[:, offset : offset + size]
            if part == SCALE_ONE:
                for s in range(MICRO):
                    vectors[SCALES_ALL + s : SCALES_ALL + s + 1, column : column + size] = each[s][
                        :, offset : offset + size
                    ]
        for row in (GAIN_ONE, GAIN_TWO, BIAS_DOWN):
            start = MICRO * columns + (row - GAIN_ONE) * rows
            vectors[row : row + 1, i * rows : (i + 1) * rows] = here[:, start : start + rows]
    for to, gain, by in ((GAINS_ONE, GAIN_ONE, SCALE_ONE), (GAINS_TWO, GAIN_TWO, SCALE_TWO)):
        vectors[to : to + 1, :] = vectors[gain : gain + 1, :] * (1.0 + vectors[by : by + 1, :])
    line[...] = jnp.zeros_like(line)
    for d in range(PLANES):
        here = small[d * side : d * side + 1, :]
        start = MICRO * (columns + rows)
        three = [here[:, start + s * shard : start + (s + 1) * shard] for s in range(MICRO)]
        line[0:1, d * shard : (d + 1) * shard] = one_of(three)
    weight = jnp.where(plane < MICRO, weight_grid[weight_index[last]], 0.0)
    scale[...] = line[...].T[:, 0:1] * weight


def project_kernel(place, gathered, tokens, vectors, *refs, chunks, slots):
    side = len(refs) - 5
    mixed, (attended, middle, normed, weights, arrived) = refs[:side], refs[side:]
    spot = place[1]
    copies = fetch(gathered, chunks, weights, arrived)
    for copy in copies:
        copy.wait()
    total = jnp.zeros(attended.shape, F32)
    for e in range(side):
        other = spot ^ e
        block = mixed[e][...]
        if side > GROUPS:
            block = jnp.where(other < GROUPS, block, jnp.zeros_like(block))
        total = total + nn(block, group_rows(weights, other % GROUPS, place[2] if slots else None))
    attended[...] = total
    after = tokens[...].astype(F32) + vectors[GATE_ONE : GATE_ONE + 1] * total
    middle[...] = after
    xhat, _ = standardize(after)
    normed[...] = (xhat * vectors[GAINS_TWO : GAINS_TWO + 1] + vectors[SHIFT_TWO : SHIFT_TWO + 1]).astype(BF16)


def feed_kernel(gathered, rows, d_rows, bias, output, d_normed, active, d_hidden, weights, arrived):
    parts = weights.shape[0] // 2
    unit = weights.shape[3]
    order = [at for part in range(parts) for at in (part, parts + part)]
    copies = fetch(gathered, order, weights, arrived)
    out = jnp.zeros(output.shape, F32)
    back = jnp.zeros(output.shape, F32)
    for part in range(parts):
        columns = slice(part * unit, (part + 1) * unit)
        copies[2 * part].wait()
        up = whole(weights, 2 * part)
        u = nn(rows[...], up) + bias[:, columns]
        square = u * u
        bent = jnp.tanh(SLOPE * u * (1.0 + CUBIC * square))
        half = 0.5 * (1.0 + bent)
        on = (u * half).astype(BF16)
        active[:, columns] = on
        slope = half + 0.5 * u * (1.0 - bent * bent) * (SLOPE * (1.0 + 3.0 * CUBIC * square))
        copies[2 * part + 1].wait()
        down = whole(weights, 2 * part + 1)
        d_on = (nn(d_rows[...], down) * slope).astype(BF16)
        d_hidden[:, columns] = d_on
        out = out + nt(on, down)
        back = back + nt(d_on, up)
    output[...] = out.astype(output.dtype)
    d_normed[...] = back.astype(d_normed.dtype)


def scatter_store(refs, me, device, value):
    kept, sent, chunk, slot_of = refs
    distance = me ^ device
    slot = slot_of(distance)

    @pl.when(distance % 2 == 0)
    def _():
        kept[slot, chunk] = value

    @pl.when(distance % 2 == 1)
    def _():
        sent[slot, chunk] = value


def slot_y_first(distance):
    return ((distance >> 1) & 1) * 4 + ((distance >> 2) & 1) * 2 + ((distance >> 3) & 1)


def down_grads_kernel(place, *refs, blocks, scatter):
    d_rows, active, outs = refs[:blocks], refs[blocks : 2 * blocks], refs[2 * blocks :]
    me = place[2]
    width, count = d_rows[0].shape[1], active[0].shape[1]
    unit = min(width, count)
    turned = [ref[...].T for ref in d_rows]
    for chunk in range(count // unit):
        columns = slice(chunk * unit, (chunk + 1) * unit)
        grad = sum(nn(turned[b], active[b][:, columns]) for b in range(blocks)).astype(BF16)
        if scatter:
            rows = outs[0].shape[2]
            for i in range(width // rows):
                part = grad[i * rows : (i + 1) * rows]
                scatter_store((outs[0], outs[1], chunk, slot_y_first), me, i, part)
        else:
            outs[0][:, columns] = grad


def up_grads_kernel(place, *refs, blocks, scatter):
    rows_all, d_hidden, outs = refs[:blocks], refs[blocks : 2 * blocks], refs[2 * blocks :]
    bias = outs[-1]
    me = place[2]
    width, count = rows_all[0].shape[1], bias.shape[1]
    unit = min(width, count)
    turned = [ref[...].T for ref in rows_all]
    for chunk in range(count // unit):
        columns = slice(chunk * unit, (chunk + 1) * unit)
        grad = sum(nn(turned[b], d_hidden[b][:, columns]) for b in range(blocks)).astype(BF16)
        bias[:, columns] = sum(over_tokens(d_hidden[b][:, columns].astype(F32)) for b in range(blocks))
        if scatter:
            rows = outs[0].shape[2]
            for i in range(width // rows):
                part = grad[i * rows : (i + 1) * rows]
                scatter_store((outs[0], outs[1], chunk, slot_y_first), me, i, part)
        else:
            outs[0][:, columns] = grad


def proj_grads_kernel(place, d_attended, *refs, side, scatter):
    mixed, refs = refs[:side], refs[side:]
    spot, me = place[1], place[2]
    width = d_attended.shape[1]
    whole_grad = refs[-1]
    if side > GROUPS:
        whole_grad[...] = jnp.zeros_like(whole_grad)
    for e in range(side):
        other = spot ^ e
        first = pl.multiple_of((other % GROUPS) * WIDTH, WIDTH)
        grad = nn(mixed[e][...].T, d_attended[...]).astype(BF16)
        if side > GROUPS:
            grad = whole_grad[pl.ds(first, WIDTH), :] + jnp.where(other < GROUPS, grad, jnp.zeros_like(grad))
        whole_grad[pl.ds(first, WIDTH), :] = grad
    if not scatter:
        refs[0][...] = whole_grad[...]
        return
    _, _, own, sent, ready, done, _ = refs
    rows, chunk = own.shape[2], own.shape[1] - 1
    for i in range(width // rows):
        part = whole_grad[i * rows : (i + 1) * rows, :]
        scatter_store((ready.at[0], ready.at[1], 0, slot_y_first), me, i, part)
    copies = [
        pltpu.make_async_copy(ready.at[at, :, 0], out.at[:, chunk], done.at[at])
        for at, out in enumerate((own, sent))
    ]
    for copy in copies:
        copy.start()
    for copy in copies:
        copy.wait()


def qkv_grads_kernel(place, d_project, normed, *outs):
    grad = nn(d_project[...], normed[...]).astype(BF16).T
    plane, slice_of = place[0], place[3]
    rows = outs[0].shape[1]
    if len(outs[0].shape) == 3 and outs[0].shape[0] == PLANES:
        for at in range(PLANES):
            distance = plane ^ at
            slot = (distance % 2) * 2 + distance // 2
            halves = [grad[(2 * at + half) * rows : (2 * at + half + 1) * rows] for half in range(2)]
            outs[0][slot] = jnp.where(slice_of == 0, halves[0], halves[1])
            outs[1][slot] = jnp.where(slice_of == 0, halves[1], halves[0])
    else:
        for at in range(PLANES):
            part = grad[at * rows : (at + 1) * rows]
            distance = plane ^ at

            @pl.when(distance % 2 == 0)
            def _():
                outs[0][distance // 2] = part

            @pl.when(distance % 2 == 1)
            def _():
                outs[1][distance // 2] = part


def normed_backward_kernel(d_project, weight, *refs, blocks):
    tokens, (kept, sent, sums) = refs[:blocks], refs[blocks:]
    count = tokens[0].shape[0]
    d_shift = jnp.zeros((1, weight.shape[0]), F32)
    d_xhat = jnp.zeros((1, weight.shape[0]), F32)
    for block in range(blocks):
        part = nt(d_project[:, block * count : (block + 1) * count].T, weight[...])
        (sent if block % 2 else kept)[block // 2] = part.astype(BF16)
        xhat, _ = standardize(tokens[block][...].astype(F32))
        d_shift = d_shift + over_tokens(part)
        d_xhat = d_xhat + over_tokens(part * xhat)
    sums[0:1, :] = d_shift
    sums[1:2, :] = d_xhat
    sums[2:8, :] = jnp.zeros((6, weight.shape[0]), F32)


def middle_kernel(place, gathered, vectors, upstream, scale, attended, middle, d_own, *refs, others, chunks, slots):
    arrived, refs = refs[:others], refs[others:]
    d_mixed, (d_middle, d_attended, sums, weights, copied) = refs[:-5], refs[-5:]
    spot = place[1]
    copies = fetch(gathered, chunks, weights, copied)
    width = middle.shape[1]
    d_normed = d_own[...]
    for ref in arrived:
        d_normed = d_normed + ref[...].astype(F32)
    xhat, root = standardize(middle[...])
    d_result = upstream[...].astype(F32) * scale[...]
    d_after = d_result + pull_norm(d_normed, vectors[GAINS_TWO : GAINS_TWO + 1], xhat, root)
    d_middle[...] = d_after
    low = (vectors[GATE_ONE : GATE_ONE + 1] * d_after).astype(BF16)
    d_attended[...] = low
    for copy in copies:
        copy.wait()
    for e in range(len(d_mixed)):
        rows_here = group_rows(weights, (spot ^ e) % GROUPS, place[2] if slots else None)
        d_mixed[e][...] = nt(low, rows_here).astype(BF16)
    sums[0:1, :] = over_tokens(d_after * attended[...])
    sums[1:2, :] = over_tokens(d_normed)
    sums[2:3, :] = over_tokens(d_normed * xhat)
    sums[3:8, :] = jnp.zeros((5, width), F32)


def output_kernel(vectors, upstream, scale, middle, own, *refs, others):
    arrived, (result, sums) = refs[:others], refs[others:]
    output = own[...] + vectors[BIAS_DOWN : BIAS_DOWN + 1]
    for ref in arrived:
        output = output + ref[...].astype(F32)
    gate = vectors[GATE_TWO : GATE_TWO + 1]
    result[...] = (middle[...] + gate * output).astype(BF16)
    d_result = upstream[...].astype(F32) * scale[...]
    sums[0:1, :] = over_tokens(d_result * output)
    sums[1:2, :] = over_tokens(gate * d_result)
    sums[2:8, :] = jnp.zeros((6, middle.shape[1]), F32)


def tokens_kernel(vectors, tokens, d_middle, own, arrived, d_tokens):
    xhat, root = standardize(tokens[...].astype(F32))
    d_normed = own[...].astype(F32) + arrived[...].astype(F32)
    back = pull_norm(d_normed, vectors[GAINS_ONE : GAINS_ONE + 1], xhat, root)
    d_tokens[...] = (d_middle[...] + back).astype(BF16)


def forward_kernel(place, *refs, blocks, halves):
    tokens, refs = refs[:blocks], refs[blocks:]
    count = 2 if halves else PLANES
    weights, refs = refs[:count], refs[count:]
    (vectors, cosine, sines), refs = refs[:3], refs[3:]
    gain, shift = vectors[GAINS_ONE : GAINS_ONE + 1], vectors[SHIFT_ONE : SHIFT_ONE + 1]
    mixed, refs = refs[:blocks], refs[blocks:]
    heads, log_total, normed, weight, keys, mixed_turned = refs
    plane = place[0]
    rows = weights[0].shape[-2]
    count = tokens[0].shape[0]
    if halves:
        for half in range(2):
            for distance in range(PLANES):
                first = pl.multiple_of((plane ^ distance) * 2 * rows + (place[3] ^ half) * rows, 16)
                weight[pl.ds(first, rows), :] = weights[half][distance]
    else:
        for distance in range(PLANES):
            first = pl.multiple_of((plane ^ distance) * rows, 8)
            weight[pl.ds(first, rows), :] = weights[distance][...]
    for block in range(blocks):
        xhat, _ = standardize(tokens[block][...].astype(F32))
        normed[block * count : (block + 1) * count, :] = (xhat * gain + shift).astype(BF16)
    project = nt(weight[...].T, normed[...])
    cos, sin = cosine[...], sines[...]
    half = HEAD // 2
    for part in range(2):
        for head in range(PER_GROUP):
            start = part * WIDTH + head * HEAD
            first, second = project[start : start + half], project[start + half : start + HEAD]
            turned = jnp.concatenate([first * cos - second * sin, second * cos + first * sin], 0).astype(BF16)
            if part == 0:
                turned = turned * jnp.asarray(SCALING, BF16)
            else:
                keys[head] = turned.T
            heads[start : start + HEAD, :] = turned
    heads[2 * WIDTH :, :] = project[2 * WIDTH :].astype(BF16)
    length = heads.shape[1]
    for head in range(PER_GROUP):
        start = head * HEAD

        def queries_step(step, carry):
            columns = pl.ds(pl.multiple_of(step * QUERY_BLOCK, QUERY_BLOCK), QUERY_BLOCK)
            scores = nn(keys[head], heads[start : start + HEAD, columns])
            peak = jnp.max(scores, 0, keepdims=True)
            exps = jnp.exp(scores - peak)
            total = jnp.sum(exps, 0, keepdims=True)
            log_total[head : head + 1, columns] = peak + jnp.log(total)
            probs = (exps * (1.0 / total)).astype(BF16)
            values = heads[2 * WIDTH + start : 2 * WIDTH + start + HEAD, :]
            mixed_turned[start : start + HEAD, columns] = nn(values, probs).astype(BF16)
            return carry

        lax.fori_loop(0, length // QUERY_BLOCK, queries_step, 0, unroll=True)
    for block in range(blocks):
        mixed[block][...] = mixed_turned[:, block * count : (block + 1) * count].T


def backward_kernel(*refs, blocks):
    d_mixed, refs = refs[:blocks], refs[blocks:]
    (heads, log_total, cosine, sines), refs = refs[:4], refs[4:]
    d_project, d_turned, d_keys, d_values, keys, values = refs
    count = d_mixed[0].shape[0]
    length = heads.shape[1]
    for block in range(blocks):
        d_turned[:, block * count : (block + 1) * count] = d_mixed[block][...].T
    cos, sin = cosine[...], sines[...]
    half = HEAD // 2
    d_keys[...] = jnp.zeros_like(d_keys)
    d_values[...] = jnp.zeros_like(d_values)
    for head in range(PER_GROUP):
        start = head * HEAD
        keys_turned = heads.at[WIDTH + start : WIDTH + start + HEAD]
        keys[...] = keys_turned[...].T
        values[...] = heads[2 * WIDTH + start : 2 * WIDTH + start + HEAD, :].T

        def queries_step(step, carry):
            columns = pl.ds(pl.multiple_of(step * QUERY_BLOCK, QUERY_BLOCK), QUERY_BLOCK)
            queries = heads[start : start + HEAD, columns]
            incoming = d_turned[start : start + HEAD, columns]
            scores = nn(keys[...], queries)
            probs = jnp.exp(scores - log_total[head : head + 1, columns])
            d_probs = nn(values[...], incoming)
            delta = jnp.sum(probs * d_probs, 0, keepdims=True)
            d_scores = (probs * (d_probs - delta)).astype(BF16)
            d_values[start : start + HEAD, :] += nt(incoming, probs.astype(BF16))
            d_keys[start : start + HEAD, :] += nt(queries, d_scores)
            d_queries = nn(keys_turned[...], d_scores) * SCALING
            first, second = d_queries[:half], d_queries[half:]
            cos_here, sin_here = cosine[:, columns], sines[:, columns]
            d_project[start : start + half, columns] = (first * cos_here + second * sin_here).astype(BF16)
            d_project[start + half : start + HEAD, columns] = (second * cos_here - first * sin_here).astype(BF16)
            return carry

        lax.fori_loop(0, length // QUERY_BLOCK, queries_step, 0, unroll=True)
        first, second = d_keys[start : start + half, :], d_keys[start + half : start + HEAD, :]
        d_project[WIDTH + start : WIDTH + start + half, :] = (first * cos + second * sin).astype(BF16)
        d_project[WIDTH + start + half : WIDTH + start + HEAD, :] = (second * cos - first * sin).astype(BF16)
    d_project[2 * WIDTH :, :] = d_values[...].astype(BF16)


def attend_forward(place, tokens, weights, vectors, cosine, sines, halves):
    blocks, (count, width) = len(tokens), tokens[0].shape
    length = blocks * count
    columns = weights[0].shape[-1]
    outs = call(
        functools.partial(forward_kernel, blocks=blocks, halves=halves),
        "attend_forward",
        [*tokens, *weights, vectors, cosine, sines],
        [place],
        [shape_of((count, WIDTH), BF16)] * blocks
        + [
            shape_of((columns, length), BF16),
            shape_of((8, length), F32),
            shape_of((length, width), BF16),
            shape_of((width, columns), BF16),
        ],
        [pltpu.VMEM((PER_GROUP, length, HEAD), BF16), pltpu.VMEM((WIDTH, length), BF16)],
        us=15.0,
    )
    return outs[:blocks], outs[blocks:]


def attend_backward(d_mixed, heads, log_total, cosine, sines):
    blocks, length = len(d_mixed), heads.shape[1]
    (d_project,) = call(
        functools.partial(backward_kernel, blocks=blocks),
        "attend_backward",
        [*d_mixed, heads, log_total, cosine, sines],
        [],
        [shape_of((3 * WIDTH, length), BF16)],
        [
            pltpu.VMEM((WIDTH, length), BF16),
            pltpu.VMEM((WIDTH, length), F32),
            pltpu.VMEM((WIDTH, length), F32),
            pltpu.VMEM((length, HEAD), BF16),
            pltpu.VMEM((length, HEAD), BF16),
        ],
        us=18.0,
    )
    return d_project


def after(values, *others):
    return lax.optimization_barrier((values, others))[0]


def add(left, right):
    return (left.astype(F32) + right.astype(F32)).astype(BF16)


def pick(stack, index):
    return lax.dynamic_index_in_dim(stack, index, 0, keepdims=False)


def bits_of(count):
    return [1 << bit for bit in range(count.bit_length() - 1)]


def body(
    tokens,
    upstream,
    token_mask,
    time_index,
    weight_index,
    time_table,
    weight_grid,
    w_ada,
    b_ada,
    gain_one,
    gain_two,
    w_qkv,
    w_proj,
    w_up,
    b_up,
    w_down,
    b_down,
    *,
    n,
    m,
):
    side = n // PLANES
    me = lax.axis_index("seq")
    plane, spot = me // side, me % side
    slice_of = lax.axis_index("mlp")
    place = jnp.stack([plane, spot, me, slice_of]).astype(jnp.int32)
    shard, width = tokens.shape[2], tokens.shape[3]
    rows = w_qkv.shape[0]
    hidden_count = w_up.shape[1]
    grid_size = time_table.shape[0]
    ada_columns = w_ada.shape[1]
    count = PLANES * shard
    unit = min(width, hidden_count)
    hidden_chunks, width_chunks = hidden_count // unit, width // unit
    pairwise = rows % 16 == 0 and side == GROUPS and unit == width and m == 2
    z_bits, y_bit, core_bit = (2 * side, side), 2, 1

    def swap(value, distance):
        return lax.ppermute(value, "seq", [(i, i ^ distance) for i in range(n)])

    def swap_mlp(value, distance):
        return lax.ppermute(value, "mlp", [(i, i ^ distance) for i in range(m)])

    def between_planes(pieces):
        return [pieces[0]] + [swap(pieces[d], d * side) for d in range(1, PLANES)]

    def in_plane(pieces):
        return [pieces[0]] + [swap(pieces[e], e) for e in range(1, side)]

    def in_order(blocks, axis):
        halves = jnp.stack(blocks)
        for bit in bits_of(len(blocks)):
            here = halves.reshape((len(blocks) // (2 * bit), 2, bit) + halves.shape[1:])
            halves = jnp.where((axis & bit) != 0, here[:, ::-1], here).reshape(halves.shape)
        return halves

    def for_plane(values):
        return [pick(values, jnp.minimum(plane ^ d, MICRO - 1)) for d in range(PLANES)]

    def columns_of(value):
        return [value[:, at : at + unit] for at in range(0, value.shape[1], unit)]

    line = [value[None] for value in (b_ada, gain_one, gain_two, b_down)]
    small_count = -(-MICRO * (ada_columns + rows + shard) // 128) * 128
    first_shapes = [shape_of((2 * hidden_chunks + width_chunks, rows, unit), BF16), shape_of((1, small_count), F32)]
    first_shapes += [shape_of((rows, 3 * WIDTH), BF16)] * side + [shape_of((shard, width), BF16)] * (2 * PLANES)
    packed, small, *pieces = call(
        prepare_kernel,
        "prepare",
        [tokens[:, 0], upstream[:, 0], w_qkv, w_up, w_down.T, w_proj, time_table, w_ada.T, *line, token_mask[:, 0]],
        [place, time_index[:, 0]],
        first_shapes,
        us=4.0,
    )
    group_columns, token_pieces, upstream_pieces = pieces[:side], pieces[side : side + PLANES], pieces[side + PLANES :]

    token_arrived = between_planes(token_pieces)

    received = jnp.stack(after(in_plane(group_columns), token_arrived[1]))
    weight_block = jnp.concatenate([pick(received, spot ^ at) for at in range(side)], 0)
    if pairwise:
        weight_block = pick(weight_block.reshape(2, width // 8, 3 * WIDTH), slice_of)
    weight_blocks = {0: weight_block}
    for bit in (2, 1):
        for known in list(weight_blocks):
            weight_blocks[known | bit] = swap(weight_blocks[known], bit * side)
    weight_blocks = [weight_blocks[at] for at in range(PLANES)]
    far_block = weight_blocks[2]
    own_upstream = between_planes(after(upstream_pieces, weight_blocks[1], weight_blocks[3]))
    if pairwise:
        weight_blocks = jnp.stack(weight_blocks)
        weight_blocks = [weight_blocks, swap_mlp(weight_blocks, 1)]

    for bit in bits_of(n)[:-1]:
        small = jnp.concatenate([small, swap(small, bit)], 0)
    arrived, small = lax.optimization_barrier((token_arrived, after(small, far_block)))
    own_low = jnp.concatenate(arrived, 0)
    token_blocks = {0: own_low}
    for bit in reversed(bits_of(side)):
        for known in list(token_blocks):
            mine = token_blocks[known]
            if bit < side // 2:
                mine = after(mine, token_blocks[side // 2])
            token_blocks[known | bit] = swap(mine, bit)
    token_blocks = [token_blocks[at] for at in range(side)]

    gathered = lax.all_gather(after(packed, token_arrived, far_block), "seq", axis=0)
    if not pairwise:
        gathered = gathered.transpose(1, 0, 2, 3).reshape(-1, GROUPS, WIDTH, unit).transpose(1, 0, 2, 3)
    blocks_shape = (gathered.shape[0],) + gathered.shape[2:]
    proj_chunks = list(range(2 * hidden_chunks, 2 * hidden_chunks + width_chunks))

    def weight_scratch(number):
        return [pltpu.VMEM((number,) + blocks_shape, BF16), pltpu.SemaphoreType.DMA((number,))]

    for bit in bits_of(n)[-1:]:
        small = jnp.concatenate([small, swap(small, bit)], 0)
    vectors, scale = call(
        vectors_kernel,
        "vectors",
        [small],
        [place, weight_index[:, 0], weight_grid],
        [shape_of((16, width), F32), shape_of((count, 1), F32)],
        [pltpu.VMEM((8, count), F32)],
    )

    order = ((plane ^ jnp.arange(PLANES))[None, :] * side + (spot ^ jnp.arange(side))[:, None]) * shard
    positions = (order[:, :, None] + jnp.arange(shard)).reshape(1, -1).astype(F32)
    frequency = 10000.0 ** (-jnp.arange(0, HEAD, 2).astype(F32) / HEAD)
    angles = frequency[:, None] * positions
    cosine, sines = jnp.cos(angles), jnp.sin(angles)

    mixed_blocks, kept = attend_forward(
        after(place, own_upstream), token_blocks, weight_blocks, vectors, cosine, sines, pairwise
    )

    full_ada = lax.all_gather(after(w_ada, gathered), "seq", axis=0)

    mixed_blocks = in_plane(mixed_blocks)

    own_upstream = jnp.concatenate(own_upstream, 0)
    d_rows = ((own_upstream.astype(F32) * scale) * vectors[GATE_TWO][None]).astype(BF16)
    d_rows = [d_rows] + [swap_mlp(d_rows, d) for d in range(1, m)]

    attended, middle, normed_two = call(
        functools.partial(project_kernel, chunks=proj_chunks, slots=False),
        "project",
        [own_low, vectors, *mixed_blocks],
        [place],
        [shape_of((count, width), F32), shape_of((count, width), F32), shape_of((count, width), BF16)],
        weight_scratch(width_chunks),
        us=3.0,
        far=[gathered],
    )
    rows_all = [normed_two] + [swap_mlp(normed_two, d) for d in range(1, m)]
    bias_up = b_up.astype(F32)[None]
    fed = [
        call(
            feed_kernel,
            "feed_forward",
            [rows_all[d], d_rows[d], bias_up],
            [],
            [shape_of((count, width), BF16 if d else F32)] * 2 + [shape_of((count, hidden_count), BF16)] * 2,
            weight_scratch(2 * hidden_chunks),
            us=6.0,
            far=[gathered],
        )
        for d in range(m)
    ]
    d_arrived = [swap_mlp(fed[d][1], d) for d in range(1, m)]
    out_arrived = [swap_mlp(fed[d][0], d) for d in range(1, m)]
    slots = n // 2
    if pairwise:
        down_shapes = [shape_of((slots, hidden_chunks + width_chunks, rows, unit), BF16)] * 2
    else:
        down_shapes = [shape_of((width, hidden_count), BF16)]
    if pairwise:
        up_shapes = [shape_of((slots, hidden_chunks, rows, unit), BF16)] * 2
    else:
        up_shapes = [shape_of((width, hidden_count), BF16)]
    down_grads = call(
        functools.partial(down_grads_kernel, blocks=m, scatter=pairwise),
        "down_gradients",
        [*d_rows, *[f[2] for f in fed]],
        [place],
        down_shapes,
        us=6.0,
    )
    *up_grads, bias_up_sum = call(
        functools.partial(up_grads_kernel, blocks=m, scatter=pairwise),
        "up_gradients",
        [*rows_all, *[f[3] for f in fed]],
        [place],
        up_shapes + [shape_of((1, hidden_count), F32)],
        us=5.0,
    )
    d_arrived, down_grads, full_ada, *up_grads = lax.optimization_barrier(
        (d_arrived, down_grads, full_ada, *up_grads)
    )
    middle_outs = call(
        functools.partial(middle_kernel, others=m - 1, chunks=proj_chunks, slots=False),
        "middle_backward",
        [vectors, own_upstream, scale, attended, middle, fed[0][1], *d_arrived],
        [place],
        [shape_of((count, WIDTH), BF16)] * side
        + [shape_of((count, width), F32), shape_of((count, width), BF16), shape_of((8, width), F32)],
        weight_scratch(width_chunks),
        us=4.0,
        far=[gathered],
    )
    d_mixed_blocks, (d_middle, d_attended, middle_sums) = middle_outs[:side], middle_outs[side:]

    d_mixed_blocks = in_plane(d_mixed_blocks)
    if side > GROUPS:
        share = (spot < GROUPS).astype(BF16)
        d_mixed_blocks = [block * share for block in d_mixed_blocks]

    anywhere = pl.BlockSpec(memory_space=pl.ANY)
    proj_grads = pl.pallas_call(
        functools.partial(proj_grads_kernel, side=side, scatter=pairwise),
        out_shape=down_shapes if pairwise else [shape_of((width, width), BF16)],
        in_specs=[SMEM] + [VMEM] * (1 + side) + ([anywhere] * 2 if pairwise else []),
        out_specs=[anywhere] * 2 if pairwise else [VMEM],
        scratch_shapes=(
            [pltpu.VMEM((2, slots, 1, rows, unit), BF16), pltpu.SemaphoreType.DMA((2,))] if pairwise else []
        )
        + [pltpu.VMEM((width, width), BF16)],
        input_output_aliases={2 + side: 0, 3 + side: 1} if pairwise else {},
        compiler_params=pltpu.CompilerParams(vmem_limit_bytes=56 * 1024 * 1024),
        cost_estimate=pl.CostEstimate(flops=2 * 10**9, bytes_accessed=4 * 10**6, transcendentals=0),
        name="proj_gradients",
    )(place, d_attended, *mixed_blocks, *(down_grads if pairwise else []))

    def add_halves(own, arrived):
        half = own.shape[0] // 2
        return add(own[:half], arrived[:half]), add(own[half:], arrived[half:])

    def back_to_tokens(value, *others):
        received = between_planes([value[d * shard : (d + 1) * shard] for d in range(PLANES)])
        received = after(received, *others) if others else received
        received = jnp.stack(received)
        return jnp.stack([pick(received, plane ^ at) for at in range(MICRO)])[:, None]

    if pairwise:
        up_arrived = swap(up_grads[1], core_bit)
        down_sent, out_arrived, up_arrived = lax.optimization_barrier((proj_grads[1], out_arrived, up_arrived))
        up_own, up_sent = add_halves(up_grads[0], up_arrived)

    result, output_sums = call(
        functools.partial(output_kernel, others=m - 1),
        "output",
        [vectors, own_upstream, scale, middle, fed[0][0], *out_arrived],
        [],
        [shape_of((count, width), BF16), shape_of((8, width), F32)],
    )
    if pairwise:
        up_sent, down_sent, result, *d_mixed_blocks = lax.optimization_barrier(
            (up_sent, down_sent, result, *d_mixed_blocks)
        )
    result = back_to_tokens(result)

    d_project = attend_backward(d_mixed_blocks, kept[0], kept[1], cosine, sines)
    if pairwise:
        up_arrived, down_arrived = swap(up_sent, y_bit), swap(down_sent, core_bit)
        d_project, result, up_arrived, down_arrived = lax.optimization_barrier(
            (d_project, result, up_arrived, down_arrived)
        )
    qkv_shape = (PLANES, width // 8, 3 * WIDTH) if pairwise else (2, width // PLANES, 3 * WIDTH)
    d_kept, d_sent, sums = call(
        functools.partial(normed_backward_kernel, blocks=side),
        "normed_backward",
        [d_project, kept[3], *token_blocks],
        [],
        [shape_of((side // 2, count, width), BF16)] * 2 + [shape_of((8, width), F32)],
        us=2.0,
    )
    arrived = swap(d_sent, 1)
    if pairwise:
        up_own, up_sent = add_halves(up_own, after(up_arrived, d_sent))
        down_own, down_sent = add_halves(proj_grads[0], after(down_arrived, d_sent))
        up_near = swap(up_sent, side)
        arrived = after(arrived, up_sent, down_sent)
    blocks = {2 * at: add(d_kept[at], arrived[at]) for at in range(side // 2)}
    grad_own, grad_sent = call(
        qkv_grads_kernel,
        "qkv_gradients",
        [after(d_project, blocks[2]), kept[2]],
        [place],
        [shape_of(qkv_shape, BF16)] * 2,
        us=4.0,
    )
    if pairwise:
        grad_arrived = swap_mlp(after(grad_sent, up_near), 1)
    bias_up_rows = -(-hidden_count // width)
    bias_up_sum = jnp.pad(bias_up_sum, ((0, 0), (0, bias_up_rows * width - hidden_count)))
    small = jnp.concatenate(
        [sums[0:2], middle_sums[0:3], output_sums[0:2], bias_up_sum.reshape(-1, width)], 0
    )
    small = small + swap(small, 1)
    for bit in bits_of(side)[1:]:
        for at in [at for at in blocks if at & bit]:
            arrived = swap(blocks.pop(at), bit)
            if len(blocks) > 1:
                blocks[at ^ bit] = add(blocks[at ^ bit], arrived)
    if pairwise:
        down_beside = swap(after(down_sent, arrived), y_bit)
        grad_arrived = after(grad_arrived, arrived)
        grad_own, grad_sent = add_halves(grad_own, grad_arrived)
    small = after(small, arrived)
    for bit in bits_of(side)[1:]:
        small = small + swap(small, bit)
    near_arrived = swap(grad_sent, side)
    small = jnp.concatenate([small, vectors[SCALE_TWO][None]], 0)[None]
    for bit in bits_of(PLANES):
        small = jnp.concatenate([small, swap(small, bit * side)], 0)
    (d_tokens,) = call(
        tokens_kernel,
        "tokens_backward",
        [vectors, own_low, d_middle, blocks[0], after(arrived, grad_arrived) if pairwise else arrived],
        [],
        [shape_of((count, width), BF16)],
    )
    if pairwise:
        grad_own, grad_sent = add_halves(grad_own, after(near_arrived, d_tokens))
        far_arrived = swap(grad_sent, 2 * side)
        up_own, up_sent = add_halves(up_own, after(up_near, d_tokens))
        down_own, down_sent = add_halves(down_own, after(down_beside, near_arrived))
        d_tokens = after(d_tokens, grad_sent)
        far_arrived, beside_sent = after(far_arrived, down_sent), down_sent
        far_done = far_arrived
        down_own, down_sent = add_halves(down_own, after(swap(down_sent, side), far_arrived))
    returned = back_to_tokens(d_tokens, *([beside_sent] if pairwise else []))

    if pairwise:
        up_parts = up_own[0].astype(F32) + after(swap(after(up_sent, far_done), 2 * side), down_sent)[0].astype(F32)
        grad_up = jnp.concatenate([up_parts[at] for at in range(hidden_chunks)], -1)
        down_parts = down_own[0].astype(F32) + swap(down_sent, 2 * side)[0].astype(F32)
        grad_proj = down_parts[hidden_chunks]
    else:
        grads = jnp.stack(columns_of(up_grads[0]) + columns_of(proj_grads[0]) + columns_of(down_grads[0]))
        grads = grads.reshape(-1, n, rows, unit).transpose(1, 0, 2, 3)
        grads = lax.psum_scatter(grads, "seq", scatter_dimension=0, tiled=True)[0]

        def columns_from(start, number):
            return jnp.concatenate([grads[start + at] for at in range(number)], -1).astype(F32)

        grad_up = columns_from(0, hidden_chunks)
        grad_proj = columns_from(hidden_chunks, width_chunks)
        down_parts = grads[hidden_chunks + width_chunks :].astype(F32)
    for bit in bits_of(m):
        grad_proj = grad_proj + swap_mlp(grad_proj.astype(BF16), bit).astype(F32)

    arrived = near_arrived
    if pairwise:
        arrived = far_arrived
        total = grad_own[0].astype(F32) + arrived[0].astype(F32)
        by_spot = total.astype(BF16).reshape(2, rows, 3 * WIDTH)
        slices = [pick(by_spot, (spot ^ e) % 2) for e in range(side)]
    else:
        arrived = swap(add(grad_own[1], arrived[1]), 2 * side).astype(F32) + arrived[0].astype(F32)
        total = grad_own[0].astype(F32) + arrived
        by_spot = total.astype(BF16).reshape(side, rows, 3 * WIDTH)
        slices = [pick(by_spot, spot ^ e) for e in range(side)]
    received = in_plane(slices)
    received = jnp.stack(after(received, down_sent) if pairwise else received)
    grad_qkv = jnp.stack([pick(received, spot ^ group) for group in range(GROUPS)])
    grad_qkv = grad_qkv.reshape(GROUPS, rows, 3, WIDTH).transpose(1, 2, 0, 3).reshape(rows, 3 * width)
    if pairwise:
        grad_qkv = jnp.where(spot // 2 == slice_of, grad_qkv, swap_mlp(grad_qkv, 1)).astype(F32)
    else:
        grad_qkv = grad_qkv.astype(F32)
        for bit in bits_of(m):
            grad_qkv = grad_qkv + swap_mlp(grad_qkv.astype(BF16), bit).astype(F32)

    grad_down = jnp.concatenate([down_parts[at] for at in range(hidden_chunks)], -1).T

    small = in_order(list(small), plane)[:MICRO]
    grad_bias_up = jnp.sum(small[:, 7 : 7 + bias_up_rows], 0).reshape(-1)[:hidden_count]
    d_shift_one, d_xhat_one, d_gate_one, d_shift_two, d_xhat_two, d_gate_two = [small[:, at] for at in range(6)]
    index_here = time_index[:, 0]
    vector_sums = jnp.stack(
        [
            jnp.sum((1.0 + vectors[SCALES_ALL : SCALES_ALL + MICRO]) * d_xhat_one, 0),
            jnp.sum((1.0 + small[:, -1]) * d_xhat_two, 0),
            jnp.sum(small[:, 6], 0),
            jnp.pad(index_here.astype(F32), (0, width - MICRO)),
        ]
    )
    d_scale_one, d_scale_two = vectors[GAIN_ONE] * d_xhat_one, vectors[GAIN_TWO] * d_xhat_two
    small = jnp.stack([d_shift_one, d_scale_one, d_gate_one, d_shift_two, d_scale_two, d_gate_two], 1)
    small = jnp.concatenate([small.reshape(6 * MICRO, width), vector_sums], 0)[None]
    for bit in bits_of(m):
        small = jnp.concatenate([small, swap_mlp(small, bit)], 0)
    small = after(small, grad_sent, beside_sent) if pairwise else small
    at = 6 * MICRO
    d_modulation = small[:, :at].reshape(m * MICRO, n, ada_columns)
    vector_sums = jnp.sum(small[:, at : at + 3], 0)
    index_all = small[:, at + 3, :MICRO].reshape(-1).astype(jnp.int32)
    onehot = (index_all[:, None] == jnp.arange(grid_size)[None, :]).astype(BF16)
    cond = jnp.dot(onehot, time_table, preferred_element_type=F32)
    d_modulation_own = lax.dynamic_index_in_dim(d_modulation, me, 1, keepdims=False)
    grad_ada = jnp.dot(cond.T, d_modulation_own, precision=highest)
    grad_bias_ada = jnp.sum(d_modulation_own, 0)
    d_cond = jnp.einsum("bic,idc->bd", d_modulation, full_ada.astype(F32), precision=highest)
    table_rows = grid_size // n
    onehot_own = index_all[None, :] == (me * table_rows + jnp.arange(table_rows))[:, None]
    grad_table = jnp.dot(onehot_own.astype(F32), d_cond, precision=highest)
    vector_sums = lax.dynamic_slice_in_dim(vector_sums, me * rows, rows, 1)
    return (
        result,
        returned.astype(F32),
        grad_table,
        grad_ada,
        grad_bias_ada,
        vector_sums[0],
        vector_sums[1],
        grad_qkv,
        grad_proj,
        grad_up,
        grad_bias_up,
        grad_down,
        vector_sums[2],
    )


def solution(mesh):
    in_specs = (
        P(None, "mlp", "seq", None),
        P(None, "mlp", "seq", None),
        P(None, "mlp", "seq"),
        P(None, "mlp"),
        P(None, "mlp"),
        P(),
        P(),
        P(None, "seq"),
        P("seq"),
        P("seq"),
        P("seq"),
        P("seq", None),
        P("seq", None),
        P("seq", "mlp"),
        P("mlp"),
        P("mlp", "seq"),
        P("seq"),
    )
    out_specs = (
        P(None, "mlp", "seq", None),
        P(None, "mlp", "seq", None),
        P("seq", None),
        P(None, "seq"),
        P("seq"),
        P("seq"),
        P("seq"),
        P("seq", None),
        P("seq", None),
        P("seq", "mlp"),
        P("mlp"),
        P("mlp", "seq"),
        P("seq"),
    )
    run = functools.partial(body, n=mesh.shape["seq"], m=mesh.shape["mlp"])
    return jax.shard_map(run, mesh=mesh, in_specs=in_specs, out_specs=out_specs, check_vma=False)
```
